32 devices in a mesh: dp: 16 (over z, y, x), tensor: 2 (over core).
Axes of the slice: x: 2, y: 2, z: 4, core: 2. Of those that a mesh axis runs over, the one named last changes fastest.
Arguments:
- tokens: bfloat16 [8192, 1024], P('dp', 'tensor'), may hold values from -6 to 6
- cotangent: bfloat16 [8192, 1024], P('dp', 'tensor'), may hold values from -6 to 6
- w_in: bfloat16 [4096, 1024], P(('dp', 'tensor')), may hold values from -0.1875 to 0.1875
- b_in: bfloat16 [4096], P(('dp', 'tensor')), may hold values from -4 to 4
- w_out: bfloat16 [4096, 1024], P(('dp', 'tensor')), may hold values from -0.09375 to 0.09375
Outputs:
- mixed: bfloat16 [8192, 1024], P('dp', 'tensor')
- grad_in: float32 [4096, 1024], P(('dp', 'tensor'))
The draws below stay inside these ranges and needn't reach their ends.
All inputs are finite; a program needn't handle non-finite values.
Results may differ from the reference program's by a relative error of at most 0.017.
Values may be sent and summed in bfloat16 or wider, within the bound.
No kernel may reach another device: no remote copies, remote signals or barrier semaphores. Data moves between devices by JAX's collectives and lax.ppermute only.
A program may use at most 64 MiB of HBM per device.

```python
import math
import jax
import jax.numpy as jnp
from jax import lax

D = 1024
FF = 4096
TOKENS = 8192
N_DP = 16
N_TENSOR = 2


def levels(key, shape, split, low, largest):
    level = 1.0
    for axis_at, shards_of in split:
        heights = jax.random.uniform(jax.random.fold_in(jax.random.fold_in(key, 6), axis_at), (shards_of,), jnp.float32, low / len(split), largest / len(split))
        level = level * jnp.repeat(jnp.exp(heights), shape[axis_at] // shards_of).reshape((-1,) + (1,) * (len(shape) - 1 - axis_at))
    return level


def normal_values(rng, dims, deviation, most, pieces=(), held_as=jnp.bfloat16):
    drawn = deviation * jax.random.normal(rng, dims, jnp.float32)
    if pieces:
        drawn = drawn * levels(rng, dims, pieces, -0.22, 0.18)
    return jnp.clip(drawn, -most, most).astype(held_as)


def setup_inputs(seed: int = 0) -> dict:
    keys = jax.random.split(jax.random.key(seed), 6)
    return {
        "tokens": normal_values(keys[0], (TOKENS, D), 1.0, 6.0, ((0, 16), (1, 2))),
        "cotangent": normal_values(keys[1], (TOKENS, D), 1.0, 6.0, ((0, 16), (1, 2))),
        "w_in": normal_values(keys[2], (FF, D), D ** -0.5, 0.1875, ((0, 32),)),
        "b_in": normal_values(keys[3], (FF,), 1.0, 4.0, ((0, 32),)),
        "w_out": normal_values(keys[4], (FF, D), FF ** -0.5, 0.09375, ((0, 32),)),
    }


def gelu_parts(value):
    coeff = 0.7978845608
    inner = coeff * (value + 0.044715 * value * value * value)
    tangent = jnp.tanh(inner)
    result = 0.5 * value * (1.0 + tangent)
    slope = 0.5 * (1.0 + tangent) + 0.5 * value * (1.0 - tangent * tangent) * coeff * (1.0 + 3.0 * 0.044715 * value * value)
    return (result, slope)

def reference(tokens, cotangent, w_in, b_in, w_out):
    contract_last = (((1,), (1,)), ((), ()))
    contract_first = (((0,), (0,)), ((), ()))
    owned = FF // (N_TENSOR * N_DP)
    units = FF // N_TENSOR
    in_groups = w_in.reshape(N_DP, N_TENSOR, owned, D).transpose(1, 0, 2, 3).reshape(N_TENSOR, units, D)
    out_groups = w_out.reshape(N_DP, N_TENSOR, owned, D).transpose(1, 0, 2, 3).reshape(N_TENSOR, units, D)
    bias_groups = b_in.reshape(N_DP, N_TENSOR, owned).transpose(1, 0, 2).reshape(N_TENSOR, units)

    def step(total, items):
        in_rows, bias_rows, out_rows = items
        pre = lax.dot_general(tokens, in_rows, contract_last, preferred_element_type=jnp.float32) + bias_rows.astype(jnp.float32)
        act_value, slope = gelu_parts(pre)
        act = act_value.astype(jnp.bfloat16)
        part = jnp.dot(act, out_rows, preferred_element_type=jnp.float32).astype(jnp.bfloat16)
        part = lax.optimization_barrier(part).astype(jnp.float32)
        dact = lax.dot_general(cotangent, out_rows, contract_last, preferred_element_type=jnp.float32)
        dpre = (dact * slope).astype(jnp.bfloat16)
        grad = lax.dot_general(dpre, tokens, contract_first, preferred_element_type=jnp.float32)
        return (total + part, grad)
    total, grads = lax.scan(step, jnp.zeros((TOKENS, D), jnp.float32), (in_groups, bias_groups, out_groups))
    grad_in = grads.reshape(N_TENSOR, N_DP, owned, D).transpose(1, 0, 2, 3).reshape(FF, D)
    grad_in = grad_in * (1.0 / math.sqrt(TOKENS))
    return (total.astype(jnp.bfloat16), grad_in)
```

```python
import math

import jax
import jax.numpy as jnp
from jax import lax
from jax.sharding import Mesh, PartitionSpec as P


def gelu_parts(value):
    coeff = 0.7978845608
    inner = coeff * (value + 0.044715 * value * value * value)
    tangent = jnp.tanh(inner)
    result = 0.5 * value * (1.0 + tangent)
    slope = 0.5 * (1.0 + tangent) + 0.5 * value * (1.0 - tangent * tangent) * coeff * (
        1.0 + 3.0 * 0.044715 * value * value
    )
    return (result, slope)


NEAR = 4
CONTRACT_LAST = (((1,), (1,)), ((), ()))
CONTRACT_FIRST = (((0,), (0,)), ((), ()))


def on_device(tokens, cotangent, w_in, b_in, w_out):
    far = lax.axis_size("far")
    near = lax.axis_size("near")
    tensor = lax.axis_size("tensor")
    rows, feats = tokens.shape
    owned, width = w_in.shape
    scale = 1.0 / math.sqrt(rows * far * near)
    bias_rows = jnp.pad(b_in.reshape(1, owned), ((0, 15), (0, width - owned)))
    weights = lax.all_gather(jnp.concatenate([w_in, w_out, bias_rows], 0), "far", axis=0)
    in_rows = weights[:, :owned].reshape(far * owned, width)
    proj_rows = weights[:, owned : 2 * owned].reshape(far * owned, width)
    bias = weights[:, 2 * owned, :owned].reshape(far * owned).astype(jnp.float32)
    tok = lax.all_gather(tokens, ("near", "tensor"), axis=0).reshape(near, tensor, rows, feats)
    cot = lax.all_gather(cotangent, ("near", "tensor"), axis=0).reshape(near, tensor, rows, feats)
    tok_full = tok.transpose(0, 2, 1, 3).reshape(near * rows, width)
    cot_full = cot.transpose(0, 2, 1, 3).reshape(near * rows, width)
    pre = lax.dot_general(
        tok_full, in_rows, CONTRACT_LAST, preferred_element_type=jnp.float32
    ) + bias
    act_value, slope = gelu_parts(pre)
    act = act_value.astype(jnp.bfloat16)
    term = jnp.dot(act, proj_rows, preferred_element_type=jnp.float32).astype(jnp.bfloat16)
    term = term.reshape(near, rows, tensor, feats).transpose(0, 2, 1, 3)
    mixed = lax.psum_scatter(
        term.reshape(near * tensor, rows, feats), ("near", "tensor"), scatter_dimension=0
    )
    dact = lax.dot_general(cot_full, proj_rows, CONTRACT_LAST, preferred_element_type=jnp.float32)
    dpre = (dact * slope).astype(jnp.bfloat16)
    grad = lax.dot_general(dpre, tok_full, CONTRACT_FIRST, preferred_element_type=jnp.float32)
    grad_sum = lax.psum_scatter(grad.astype(jnp.bfloat16), "far", scatter_dimension=0, tiled=True)
    return (mixed, grad_sum.astype(jnp.float32) * scale)


def solution(mesh):
    dp, tensor = mesh.shape["dp"], mesh.shape["tensor"]
    fine = Mesh(mesh.devices.reshape(dp // NEAR, NEAR, tensor), ("far", "near", "tensor"))
    rows = ("far", "near")
    owners = ("far", "near", "tensor")
    in_specs = (P(rows, "tensor"), P(rows, "tensor"), P(owners, None), P(owners), P(owners, None))
    out_specs = (P(rows, "tensor"), P(owners, None))
    return jax.shard_map(
        on_device, mesh=fine, in_specs=in_specs, out_specs=out_specs, check_vma=False
    )
```

```python
import functools
import math

import jax
import jax.numpy as jnp
from jax import lax
from jax.experimental import pallas as pl
from jax.experimental.pallas import tpu as pltpu
from jax.sharding import Mesh, PartitionSpec as P

NEAR = 4
AXES = ("far", "y", "x", "core")
CONTRACT_LAST = (((1,), (1,)), ((), ()))
CONTRACT_FIRST = (((0,), (0,)), ((), ()))
VMEM_LIMIT = 56 * 1024 * 1024


def gelu_parts(value):
    coeff = 0.7978845608
    inner = coeff * (value + 0.044715 * value * value * value)
    tangent = jnp.tanh(inner)
    result = 0.5 * value * (1.0 + tangent)
    slope = 0.5 * (1.0 + tangent) + 0.5 * value * (1.0 - tangent * tangent) * coeff * (
        1.0 + 3.0 * 0.044715 * value * value
    )
    return (result, slope)


def on_device_any(tokens, cotangent, w_in, b_in, w_out):
    far, near, tensor = lax.axis_size("far"), lax.axis_size("near"), lax.axis_size("tensor")
    rows, feats = tokens.shape
    owned, width = w_in.shape
    scale = 1.0 / math.sqrt(rows * far * near)
    bias_rows = jnp.pad(b_in.reshape(1, owned), ((0, 15), (0, width - owned)))
    weights = lax.all_gather(jnp.concatenate([w_in, w_out, bias_rows], 0), "far", axis=0)
    in_rows = weights[:, :owned].reshape(far * owned, width)
    proj_rows = weights[:, owned : 2 * owned].reshape(far * owned, width)
    bias = weights[:, 2 * owned, :owned].reshape(far * owned).astype(jnp.float32)
    tok = lax.all_gather(tokens, ("near", "tensor"), axis=0).reshape(near, tensor, rows, feats)
    cot = lax.all_gather(cotangent, ("near", "tensor"), axis=0).reshape(near, tensor, rows, feats)
    tok_full = tok.transpose(0, 2, 1, 3).reshape(near * rows, width)
    cot_full = cot.transpose(0, 2, 1, 3).reshape(near * rows, width)
    pre = lax.dot_general(
        tok_full, in_rows, CONTRACT_LAST, preferred_element_type=jnp.float32
    ) + bias
    act_value, slope = gelu_parts(pre)
    act = act_value.astype(jnp.bfloat16)
    term = jnp.dot(act, proj_rows, preferred_element_type=jnp.float32).astype(jnp.bfloat16)
    term = term.reshape(near, rows, tensor, feats).transpose(0, 2, 1, 3)
    mixed = lax.psum_scatter(
        term.reshape(near * tensor, rows, feats), ("near", "tensor"), scatter_dimension=0
    )
    dact = lax.dot_general(cot_full, proj_rows, CONTRACT_LAST, preferred_element_type=jnp.float32)
    dpre = (dact * slope).astype(jnp.bfloat16)
    grad = lax.dot_general(dpre, tok_full, CONTRACT_FIRST, preferred_element_type=jnp.float32)
    grad_sum = lax.psum_scatter(grad.astype(jnp.bfloat16), "far", scatter_dimension=0, tiled=True)
    return (mixed, grad_sum.astype(jnp.float32) * scale)


def backward_kernel(far, owned, part, feats, *refs):
    blocks = NEAR
    tok_refs = refs[: 2 * blocks]
    w_refs = refs[2 * blocks : 2 * blocks + 2 * far]
    act_ref, mine_ref, other_ref = refs[2 * blocks + 2 * far : 2 * blocks + 2 * far + 3]
    tok, cot, w_in, w_out, bias, dpre, tok_sem, cot_sem, in_sem, out_sem, bias_sem = refs[
        2 * blocks + 2 * far + 3 :
    ]
    core = lax.axis_index("core")
    tok_copies, cot_copies, in_copies, out_copies, bias_copies = [], [], [], [], []
    for at, ref in enumerate(w_refs):
        in_copies.append(
            pltpu.make_async_copy(
                ref.at[pl.ds(0, owned)], w_in.at[pl.ds(at * owned, owned)], in_sem.at[at]
            )
        )
        bias_copies.append(
            pltpu.make_async_copy(
                ref.at[pl.ds(2 * owned, 16), pl.ds(0, owned)],
                bias.at[:, pl.ds(at * owned, owned)],
                bias_sem.at[at],
            )
        )
        out_copies.append(
            pltpu.make_async_copy(
                ref.at[pl.ds(owned, owned)], w_out.at[pl.ds(at * owned, owned)], out_sem.at[at]
            )
        )
    for at, ref in enumerate(tok_refs):
        block, shift = at // 2, at % 2
        source = lax.rem(core + shift, 2)
        columns = pl.ds(pl.multiple_of(source * feats, feats), feats)
        spot = pl.ds(block * part, part)
        tok_copies.append(
            pltpu.make_async_copy(ref.at[0], tok.at[spot, columns], tok_sem.at[at])
        )
        cot_copies.append(
            pltpu.make_async_copy(ref.at[1], cot.at[spot, columns], cot_sem.at[at])
        )
    for copy in in_copies + bias_copies + tok_copies + out_copies + cot_copies:
        copy.start()
    for copy in in_copies + bias_copies + tok_copies + out_copies + cot_copies:
        copy.wait()

    @pl.loop(0, blocks)
    def _(block):
        spot = pl.ds(pl.multiple_of(block * part, part), part)
        pre = lax.dot_general(
            tok[spot, :], w_in[...], CONTRACT_LAST, preferred_element_type=jnp.float32
        ) + bias[0:1, :].astype(jnp.float32)
        value, slope = gelu_parts(pre)
        act_ref[spot, :] = value.astype(jnp.bfloat16)
        dact = lax.dot_general(
            cot[spot, :], w_out[...], CONTRACT_LAST, preferred_element_type=jnp.float32
        )
        dpre[spot, :] = (dact * slope).astype(jnp.bfloat16)

    @pl.loop(0, far)
    def _(at):
        units = pl.ds(pl.multiple_of(at * 2 * owned, 2 * owned), 2 * owned)
        grad = lax.dot_general(
            dpre[:, units], tok[...], CONTRACT_FIRST, preferred_element_type=jnp.float32
        ).astype(jnp.bfloat16)
        mine_ref[at] = grad[:owned]
        other_ref[at] = grad[owned:]


def project_kernel(far, owned, part, feats, *refs):
    act_ref = refs[0]
    w_refs = refs[1 : 1 + 2 * far]
    out_refs = refs[1 + 2 * far : 1 + 2 * far + 2 * NEAR]
    w_out, out_sem = refs[1 + 2 * far + 2 * NEAR :]
    core = lax.axis_index("core")
    copies = []
    for at, ref in enumerate(w_refs):
        copies.append(
            pltpu.make_async_copy(
                ref.at[pl.ds(owned, owned)], w_out.at[pl.ds(at * owned, owned)], out_sem.at[at]
            )
        )
    for copy in copies:
        copy.start()
    for copy in copies:
        copy.wait()
    for shift in range(2):
        half = lax.rem(core + shift, 2)
        columns = pl.ds(pl.multiple_of(half * feats, feats), feats)
        for block in range(NEAR):
            out_refs[2 * block + shift][...] = jnp.dot(
                act_ref[pl.ds(block * part, part), :],
                w_out[:, columns],
                preferred_element_type=jnp.float32,
            ).astype(jnp.bfloat16)


def pair_kernel(far, mine_ref, other_ref, *out_refs):
    for at in range(far):
        out_refs[at][...] = (
            mine_ref[at].astype(jnp.float32) + other_ref[at].astype(jnp.float32)
        ).astype(jnp.bfloat16)


def sum_kernel(part, *refs):
    out_ref = refs[-1]
    core = lax.axis_index("core")
    for shift in range(2):
        total = refs[shift][...].astype(jnp.float32)
        for block in range(1, NEAR):
            total = total + refs[2 * block + shift][...].astype(jnp.float32)
        spot = pl.ds(pl.multiple_of(lax.rem(core + shift, 2) * part, part), part)
        out_ref[spot, :] = total.astype(jnp.bfloat16)


def vmem(count):
    return [pl.BlockSpec(memory_space=pltpu.VMEM)] * count


def anywhere(count):
    return [pl.BlockSpec(memory_space=pl.ANY)] * count


def bf16(*shape):
    return jax.ShapeDtypeStruct(shape, jnp.bfloat16)


def on_device_pairs(sizes, tokens, cotangent, w_in, b_in, w_out):
    far = sizes[0]
    rows, feats = tokens.shape
    owned, width = w_in.shape
    part = rows // 2
    units = far * 2 * owned
    count = NEAR * part
    scale = 1.0 / math.sqrt(rows * far * NEAR)
    core = lax.axis_index("core")
    params = pltpu.CompilerParams(vmem_limit_bytes=VMEM_LIMIT)

    def move(value, d_far=0, d_y=0, d_x=0, d_core=0):
        pairs = []
        for f in range(far):
            for y in range(2):
                for x in range(2):
                    for c in range(2):
                        there = ((f + d_far) % far, (y + d_y) % 2, (x + d_x) % 2, (c + d_core) % 2)
                        here = ((f * 2 + y) * 2 + x) * 2 + c
                        pairs.append((here, ((there[0] * 2 + there[1]) * 2 + there[2]) * 2 + there[3]))
        return lax.ppermute(value, AXES, pairs)

    pieces = []
    for shift in range(2):
        start = lax.rem(core + shift, 2) * part
        pieces.append(
            jnp.stack(
                [
                    lax.dynamic_slice_in_dim(tokens, start, part, 0),
                    lax.dynamic_slice_in_dim(cotangent, start, part, 0),
                ]
            )
        )
    bias_rows = jnp.pad(b_in.reshape(1, owned), ((0, 15), (0, width - owned)))
    own_w = jnp.concatenate([w_in, w_out, bias_rows], 0)

    x_same = move(pieces[0], d_x=1)
    y_cross = move(pieces[1], d_y=1, d_core=1)
    lines = [own_w] + [move(own_w, d_far=k) for k in range(1, far)]
    x_cross = move(pieces[1], d_x=1, d_core=1)
    y_same = move(pieces[0], d_y=1)
    own_cross = move(pieces[1], d_core=1)
    d_same = move(x_same, d_y=1)
    d_cross = move(y_cross, d_x=1)
    toks = [pieces[0], own_cross, x_same, x_cross, y_same, y_cross, d_same, d_cross]
    weights = []
    for line in lines:
        weights += [line, move(line, d_core=1)]

    dma = pltpu.SemaphoreType.DMA
    act, mine, other = pl.pallas_call(
        functools.partial(backward_kernel, far, owned, part, feats),
        out_shape=(bf16(count, units), bf16(far, owned, width), bf16(far, owned, width)),
        in_specs=anywhere(len(toks) + len(weights)),
        out_specs=vmem(3),
        scratch_shapes=[
            pltpu.VMEM((count, width), jnp.bfloat16),
            pltpu.VMEM((count, width), jnp.bfloat16),
            pltpu.VMEM((units, width), jnp.bfloat16),
            pltpu.VMEM((units, width), jnp.bfloat16),
            pltpu.VMEM((16, units), jnp.bfloat16),
            pltpu.VMEM((count, units), jnp.bfloat16),
            dma((len(toks),)),
            dma((len(toks),)),
            dma((len(weights),)),
            dma((len(weights),)),
            dma((len(weights),)),
        ],
        compiler_params=params,
        cost_estimate=pl.CostEstimate(
            flops=6 * count * units * width, bytes_accessed=14 * count * width, transcendentals=0
        ),
        name="backward",
    )(*toks, *weights)
    other = move(other, d_core=1)

    terms = pl.pallas_call(
        functools.partial(project_kernel, far, owned, part, feats),
        out_shape=[bf16(part, feats)] * (2 * NEAR),
        in_specs=vmem(1) + anywhere(len(weights)),
        out_specs=vmem(2 * NEAR),
        scratch_shapes=[pltpu.VMEM((units, width), jnp.bfloat16), dma((len(weights),))],
        compiler_params=params,
        cost_estimate=pl.CostEstimate(
            flops=2 * count * units * width, bytes_accessed=6 * count * width, transcendentals=0
        ),
        name="project",
    )(act, *weights)
    sent = []
    for block, (d_x, d_y) in enumerate(((0, 0), (1, 0), (0, 1), (1, 1))):
        for shift in range(2):
            term = terms[2 * block + shift]
            if block or shift:
                term = move(term, d_x=d_x, d_y=d_y, d_core=shift)
            sent.append(term)

    sums = pl.pallas_call(
        functools.partial(pair_kernel, far),
        out_shape=[bf16(owned, width)] * far,
        in_specs=vmem(2),
        out_specs=vmem(far),
        compiler_params=params,
        name="pair_sum",
    )(mine, other)
    total = sums[0].astype(jnp.float32)
    for k in range(1, far):
        total = total + move(sums[k], d_far=-k).astype(jnp.float32)
    mixed = pl.pallas_call(
        functools.partial(sum_kernel, part),
        out_shape=bf16(rows, feats),
        in_specs=vmem(2 * NEAR),
        out_specs=pl.BlockSpec(memory_space=pltpu.VMEM),
        compiler_params=params,
        name="mixed_sum",
    )(*sent)
    return (mixed, total * scale)


def solution(mesh):
    dp, tensor = mesh.shape["dp"], mesh.shape["tensor"]
    far = dp // NEAR
    if tensor == 2 and far <= 4:
        fine = Mesh(mesh.devices.reshape(far, 2, 2, tensor), AXES)
        rows, owners, halves = ("far", "y", "x"), AXES, "core"
        body = functools.partial(on_device_pairs, (far,))
    else:
        fine = Mesh(mesh.devices.reshape(far, NEAR, tensor), ("far", "near", "tensor"))
        rows, owners, halves = ("far", "near"), ("far", "near", "tensor"), "tensor"
        body = on_device_any
    in_specs = (P(rows, halves), P(rows, halves), P(owners, None), P(owners), P(owners, None))
    out_specs = (P(rows, halves), P(owners, None))
    return jax.shard_map(
        body, mesh=fine, in_specs=in_specs, out_specs=out_specs, check_vma=False
    )
```

```python
import functools
import math

import jax
import jax.numpy as jnp
from jax import lax
from jax.experimental import pallas as pl
from jax.experimental.pallas import tpu as pltpu
from jax.sharding import Mesh, PartitionSpec as P

NEAR = 4
AXES = ("far", "y", "x", "core")
CONTRACT_LAST = (((1,), (1,)), ((), ()))
CONTRACT_FIRST = (((0,), (0,)), ((), ()))
VMEM_LIMIT = 28 * 1024 * 1024


def gelu_parts(value):
    coeff = 0.7978845608
    inner = coeff * (value + 0.044715 * value * value * value)
    tangent = jnp.tanh(inner)
    result = 0.5 * value * (1.0 + tangent)
    slope = 0.5 * (1.0 + tangent) + 0.5 * value * (1.0 - tangent * tangent) * coeff * (
        1.0 + 3.0 * 0.044715 * value * value
    )
    return (result, slope)


def on_device_any(tokens, cotangent, w_in, b_in, w_out):
    far, near, tensor = lax.axis_size("far"), lax.axis_size("near"), lax.axis_size("tensor")
    rows, feats = tokens.shape
    owned, width = w_in.shape
    scale = 1.0 / math.sqrt(rows * far * near)
    bias_rows = jnp.pad(b_in.reshape(1, owned), ((0, 15), (0, width - owned)))
    weights = lax.all_gather(jnp.concatenate([w_in, w_out, bias_rows], 0), "far", axis=0)
    in_rows = weights[:, :owned].reshape(far * owned, width)
    proj_rows = weights[:, owned : 2 * owned].reshape(far * owned, width)
    bias = weights[:, 2 * owned, :owned].reshape(far * owned).astype(jnp.float32)
    tok = lax.all_gather(tokens, ("near", "tensor"), axis=0).reshape(near, tensor, rows, feats)
    cot = lax.all_gather(cotangent, ("near", "tensor"), axis=0).reshape(near, tensor, rows, feats)
    tok_full = tok.transpose(0, 2, 1, 3).reshape(near * rows, width)
    cot_full = cot.transpose(0, 2, 1, 3).reshape(near * rows, width)
    pre = lax.dot_general(
        tok_full, in_rows, CONTRACT_LAST, preferred_element_type=jnp.float32
    ) + bias
    act_value, slope = gelu_parts(pre)
    act = act_value.astype(jnp.bfloat16)
    term = jnp.dot(act, proj_rows, preferred_element_type=jnp.float32).astype(jnp.bfloat16)
    term = term.reshape(near, rows, tensor, feats).transpose(0, 2, 1, 3)
    mixed = lax.psum_scatter(
        term.reshape(near * tensor, rows, feats), ("near", "tensor"), scatter_dimension=0
    )
    dact = lax.dot_general(cot_full, proj_rows, CONTRACT_LAST, preferred_element_type=jnp.float32)
    dpre = (dact * slope).astype(jnp.bfloat16)
    grad = lax.dot_general(dpre, tok_full, CONTRACT_FIRST, preferred_element_type=jnp.float32)
    grad_sum = lax.psum_scatter(grad.astype(jnp.bfloat16), "far", scatter_dimension=0, tiled=True)
    return (mixed, grad_sum.astype(jnp.float32) * scale)


def weight_copies(ref, at, owned, w_in, w_out, bias, sem):
    spot = pl.ds(at * owned, owned)
    return [
        pltpu.make_async_copy(ref.at[pl.ds(0, owned)], w_in.at[spot], sem.at[at, 0]),
        pltpu.make_async_copy(ref.at[pl.ds(owned, owned)], w_out.at[spot], sem.at[at, 1]),
        pltpu.make_async_copy(
            ref.at[pl.ds(2 * owned, 16), pl.ds(0, owned)], bias.at[:, spot], sem.at[at, 2]
        ),
    ]


def forward_kernel(owned, rows, feats, *refs):
    piece_refs, w_refs = refs[:10], refs[10:14]
    mine_ref, other_ref, dpre_ref = refs[14:17]
    tok, cot, w_in, w_out, bias, tok_sem, cot_sem, w_sem = refs[17:]
    core = lax.axis_index("core")
    w_copies = []
    for at, ref in enumerate(w_refs):
        w_copies += weight_copies(ref, at, owned, w_in, w_out, bias, w_sem)
    for copy in w_copies:
        copy.start()
    copies = token_copies(core, rows, feats, piece_refs, tok, tok_sem, 0)
    cot_copies = token_copies(core, rows, feats, piece_refs, cot, cot_sem, 1)
    for block in range(NEAR):
        for copy in copies[block] + cot_copies[block]:
            copy.start()
    for copy in w_copies:
        copy.wait()
    own_half = pl.ds(pl.multiple_of(core * feats, feats), feats)
    other_half = pl.ds(pl.multiple_of((1 - core) * feats, feats), feats)
    step = rows // 2
    for block in range(NEAR):
        for copy in copies[block] + cot_copies[block]:
            copy.wait()

        @pl.loop(0, 2)
        def _(sub):
            start = pl.multiple_of(block * rows + sub * step, step)
            spot = pl.ds(start, step)
            pre = lax.dot_general(
                tok[spot, :], w_in[...], CONTRACT_LAST, preferred_element_type=jnp.float32
            ) + bias[0:1, :].astype(jnp.float32)
            value, slope = gelu_parts(pre)
            act = value.astype(jnp.bfloat16)
            dact = lax.dot_general(
                cot[spot, :], w_out[...], CONTRACT_LAST, preferred_element_type=jnp.float32
            )
            dpre_ref[spot, :] = (dact * slope).astype(jnp.bfloat16)
            mine_ref[spot, :] = jnp.dot(
                act, w_out[:, own_half], preferred_element_type=jnp.float32
            ).astype(jnp.bfloat16)
            other_ref[spot, :] = jnp.dot(
                act, w_out[:, other_half], preferred_element_type=jnp.float32
            ).astype(jnp.bfloat16)


def token_copies(core, rows, feats, piece_refs, whole, sems, which):
    blocks = []
    for block in range(NEAR):
        copies = []
        for shift in range(2):
            if block < NEAR - 1:
                source = piece_refs[2 * block + shift].at[which]
            else:
                source = piece_refs[6 + 2 * which + shift]
            columns = pl.ds(pl.multiple_of(lax.rem(core + shift, 2) * feats, feats), feats)
            copies.append(
                pltpu.make_async_copy(
                    source,
                    whole.at[pl.ds(block * rows, rows), columns],
                    sems.at[2 * block + shift],
                )
            )
        blocks.append(copies)
    return blocks


def gradient_kernel(owned, rows, feats, *refs):
    dpre_ref, piece_refs, out_refs = refs[0], refs[1:11], refs[11:15]
    tok, tok_sem = refs[15:]
    core = lax.axis_index("core")
    copies = token_copies(core, rows, feats, piece_refs, tok, tok_sem, 0)
    for block in range(NEAR):
        for copy in copies[block]:
            copy.start()
    for block in range(NEAR):
        for copy in copies[block]:
            copy.wait()
    for at in range(0, 4, 2):
        grad = lax.dot_general(
            dpre_ref[:, at * owned : (at + 2) * owned],
            tok[...],
            CONTRACT_FIRST,
            preferred_element_type=jnp.float32,
        ).astype(jnp.bfloat16)
        out_refs[at][...] = grad[:owned]
        out_refs[at + 1][...] = grad[owned:]


def pair_kernel(rows, mine_ref, other_ref, *out_refs):
    for block in range(NEAR):
        spot = pl.ds(block * rows, rows)
        out_refs[block][...] = (
            mine_ref[spot, :].astype(jnp.float32) + other_ref[spot, :].astype(jnp.float32)
        ).astype(jnp.bfloat16)


def vmem(count):
    return [pl.BlockSpec(memory_space=pltpu.VMEM)] * count


def anywhere(count):
    return [pl.BlockSpec(memory_space=pl.ANY)] * count


def bf16(*shape):
    return jax.ShapeDtypeStruct(shape, jnp.bfloat16)


def permute(value, there):
    pairs = []
    for f in range(4):
        for y in range(2):
            for x in range(2):
                for c in range(2):
                    to = there(f, y, x, c)
                    here = ((f * 2 + y) * 2 + x) * 2 + c
                    pairs.append((here, ((to[0] * 2 + to[1]) * 2 + to[2]) * 2 + to[3]))
    return lax.ppermute(value, AXES, pairs)


def to_x(value):
    return permute(value, lambda f, y, x, c: (f, y, 1 - x, c))


def to_y(value):
    return permute(value, lambda f, y, x, c: (f, 1 - y, x, c))


def to_diagonal(value):
    return permute(value, lambda f, y, x, c: (f, 1 - y, 1 - x, c))


def to_core(value):
    return permute(value, lambda f, y, x, c: (f, y, x, 1 - c))


def to_far(value, flip):
    return permute(value, lambda f, y, x, c: (f ^ flip, y, x, c))


def on_device_lines(tokens, cotangent, w_in, b_in, w_out):
    rows, feats = tokens.shape
    owned, width = w_in.shape
    units = 4 * owned
    count = NEAR * rows
    scale = 1.0 / math.sqrt(4 * count)
    params = pltpu.CompilerParams(vmem_limit_bytes=VMEM_LIMIT)
    dma = pltpu.SemaphoreType.DMA

    own = jnp.stack([tokens, cotangent])
    bias_rows = jnp.pad(b_in.reshape(1, owned), ((0, 15), (0, width - owned)))
    own_w = jnp.concatenate([w_in, w_out, bias_rows], 0)

    from_x = to_x(own)
    from_y = to_y(own)
    w_two = to_far(own_w, 2)
    w_one = to_far(own_w, 1)
    own_other = to_core(own)
    from_x, from_y, w_two, w_one, own_other = lax.optimization_barrier(
        (from_x, from_y, w_two, w_one, own_other)
    )
    diag_tok = to_y(from_x[0])
    diag_cot = to_x(from_y[1])
    w_three = to_far(w_two, 1)
    x_other = to_core(from_x)
    y_other = to_core(from_y)
    pieces = [own, own_other, from_x, x_other, from_y, y_other]
    pieces += [diag_tok, to_core(diag_tok), diag_cot, to_core(diag_cot)]
    weights = [own_w, w_one, w_two, w_three]

    mine, other, dpre = pl.pallas_call(
        functools.partial(forward_kernel, owned, rows, feats),
        out_shape=(bf16(count, feats), bf16(count, feats), bf16(count, units)),
        in_specs=anywhere(len(pieces) + len(weights)),
        out_specs=vmem(3),
        scratch_shapes=[
            pltpu.VMEM((count, width), jnp.bfloat16),
            pltpu.VMEM((count, width), jnp.bfloat16),
            pltpu.VMEM((units, width), jnp.bfloat16),
            pltpu.VMEM((units, width), jnp.bfloat16),
            pltpu.VMEM((16, units), jnp.bfloat16),
            dma((2 * NEAR,)),
            dma((2 * NEAR,)),
            dma((4, 3)),
        ],
        compiler_params=params,
        cost_estimate=pl.CostEstimate(
            flops=6 * count * units * width, bytes_accessed=8 * count * width, transcendentals=0
        ),
        name="forward",
    )(*pieces, *weights)
    received = to_core(other)

    grads = pl.pallas_call(
        functools.partial(gradient_kernel, owned, rows, feats),
        out_shape=[bf16(owned, width)] * 4,
        in_specs=vmem(1) + anywhere(len(pieces)),
        out_specs=vmem(4),
        scratch_shapes=[pltpu.VMEM((count, width), jnp.bfloat16), dma((2 * NEAR,))],
        compiler_params=params,
        cost_estimate=pl.CostEstimate(
            flops=2 * count * units * width, bytes_accessed=4 * count * width, transcendentals=0
        ),
        name="gradient",
    )(dpre, *pieces)
    grad_one = to_far(grads[1], 1)
    grad_two = to_far(grads[2], 2)
    grad_three = to_far(grads[3], 3)

    sums = pl.pallas_call(
        functools.partial(pair_kernel, rows),
        out_shape=[bf16(rows, feats)] * NEAR,
        in_specs=vmem(2),
        out_specs=vmem(NEAR),
        compiler_params=params,
        name="pair_sum",
    )(mine, received)
    mixed_x = to_x(sums[1])
    mixed_y = to_y(sums[2])
    last, grad_one = lax.optimization_barrier((sums[3], grad_one))
    mixed_diag = to_diagonal(last)
    mixed = (
        sums[0].astype(jnp.float32)
        + mixed_x.astype(jnp.float32)
        + mixed_y.astype(jnp.float32)
        + mixed_diag.astype(jnp.float32)
    ).astype(jnp.bfloat16)
    total = (
        grads[0].astype(jnp.float32)
        + grad_one.astype(jnp.float32)
        + grad_two.astype(jnp.float32)
        + grad_three.astype(jnp.float32)
    )
    return (mixed, total * scale)


def solution(mesh):
    dp, tensor = mesh.shape["dp"], mesh.shape["tensor"]
    far = dp // NEAR
    if tensor == 2 and far == 4:
        fine = Mesh(mesh.devices.reshape(far, 2, 2, tensor), AXES)
        rows, owners, halves = ("far", "y", "x"), AXES, "core"
        body = on_device_lines
    else:
        fine = Mesh(mesh.devices.reshape(far, NEAR, tensor), ("far", "near", "tensor"))
        rows, owners, halves = ("far", "near"), ("far", "near", "tensor"), "tensor"
        body = on_device_any
    in_specs = (P(rows, halves), P(rows, halves), P(owners, None), P(owners), P(owners, None))
    out_specs = (P(rows, halves), P(owners, None))
    return jax.shard_map(
        body, mesh=fine, in_specs=in_specs, out_specs=out_specs, check_vma=False
    )
```

```python
import functools
import math

import jax
import jax.numpy as jnp
from jax import lax
from jax.experimental import pallas as pl
from jax.experimental.pallas import tpu as pltpu
from jax.sharding import Mesh, PartitionSpec as P

NEAR = 4
AXES = ("far", "y", "x", "core")
CONTRACT_LAST = (((1,), (1,)), ((), ()))
CONTRACT_FIRST = (((0,), (0,)), ((), ()))
VMEM_LIMIT = 28 * 1024 * 1024


def gelu_parts(value):
    coeff = 0.7978845608
    inner = coeff * (value + 0.044715 * value * value * value)
    tangent = jnp.tanh(inner)
    result = 0.5 * value * (1.0 + tangent)
    slope = 0.5 * (1.0 + tangent) + 0.5 * value * (1.0 - tangent * tangent) * coeff * (
        1.0 + 3.0 * 0.044715 * value * value
    )
    return (result, slope)


def on_device_any(tokens, cotangent, w_in, b_in, w_out):
    far, near, tensor = lax.axis_size("far"), lax.axis_size("near"), lax.axis_size("tensor")
    rows, feats = tokens.shape
    owned, width = w_in.shape
    scale = 1.0 / math.sqrt(rows * far * near)
    bias_rows = jnp.pad(b_in.reshape(1, owned), ((0, 15), (0, width - owned)))
    weights = lax.all_gather(jnp.concatenate([w_in, w_out, bias_rows], 0), "far", axis=0)
    in_rows = weights[:, :owned].reshape(far * owned, width)
    proj_rows = weights[:, owned : 2 * owned].reshape(far * owned, width)
    bias = weights[:, 2 * owned, :owned].reshape(far * owned).astype(jnp.float32)
    tok = lax.all_gather(tokens, ("near", "tensor"), axis=0).reshape(near, tensor, rows, feats)
    cot = lax.all_gather(cotangent, ("near", "tensor"), axis=0).reshape(near, tensor, rows, feats)
    tok_full = tok.transpose(0, 2, 1, 3).reshape(near * rows, width)
    cot_full = cot.transpose(0, 2, 1, 3).reshape(near * rows, width)
    pre = lax.dot_general(
        tok_full, in_rows, CONTRACT_LAST, preferred_element_type=jnp.float32
    ) + bias
    act_value, slope = gelu_parts(pre)
    act = act_value.astype(jnp.bfloat16)
    term = jnp.dot(act, proj_rows, preferred_element_type=jnp.float32).astype(jnp.bfloat16)
    term = term.reshape(near, rows, tensor, feats).transpose(0, 2, 1, 3)
    mixed = lax.psum_scatter(
        term.reshape(near * tensor, rows, feats), ("near", "tensor"), scatter_dimension=0
    )
    dact = lax.dot_general(cot_full, proj_rows, CONTRACT_LAST, preferred_element_type=jnp.float32)
    dpre = (dact * slope).astype(jnp.bfloat16)
    grad = lax.dot_general(dpre, tok_full, CONTRACT_FIRST, preferred_element_type=jnp.float32)
    grad_sum = lax.psum_scatter(grad.astype(jnp.bfloat16), "far", scatter_dimension=0, tiled=True)
    return (mixed, grad_sum.astype(jnp.float32) * scale)


def weight_copies(ref, at, owned, w_in, w_out, bias, sem):
    spot = pl.ds(at * owned, owned)
    return [
        pltpu.make_async_copy(ref.at[pl.ds(0, owned)], w_in.at[spot], sem.at[at, 0]),
        pltpu.make_async_copy(ref.at[pl.ds(owned, owned)], w_out.at[spot], sem.at[at, 1]),
        pltpu.make_async_copy(
            ref.at[pl.ds(2 * owned, 16), pl.ds(0, owned)], bias.at[:, spot], sem.at[at, 2]
        ),
    ]


def forward_kernel(owned, rows, feats, *refs):
    piece_refs, w_refs = refs[:10], refs[10:14]
    mine_ref, other_ref, dpre_ref = refs[14:17]
    tok, cot, w_in, w_out, bias, tok_sem, cot_sem, w_sem = refs[17:]
    core = lax.axis_index("core")
    w_copies = []
    for at, ref in enumerate(w_refs):
        w_copies += weight_copies(ref, at, owned, w_in, w_out, bias, w_sem)
    for copy in w_copies:
        copy.start()
    copies = token_copies(core, rows, feats, piece_refs, tok, tok_sem, 0)
    cot_copies = token_copies(core, rows, feats, piece_refs, cot, cot_sem, 1)
    for block in range(NEAR):
        for copy in copies[block] + cot_copies[block]:
            copy.start()
    for copy in w_copies:
        copy.wait()
    own_half = pl.ds(pl.multiple_of(core * feats, feats), feats)
    other_half = pl.ds(pl.multiple_of((1 - core) * feats, feats), feats)
    step = rows // 2
    for block in range(NEAR):
        for copy in copies[block] + cot_copies[block]:
            copy.wait()

        @pl.loop(0, 2)
        def _(sub):
            start = pl.multiple_of(block * rows + sub * step, step)
            spot = pl.ds(start, step)
            pre = lax.dot_general(
                tok[spot, :], w_in[...], CONTRACT_LAST, preferred_element_type=jnp.float32
            ) + bias[0:1, :].astype(jnp.float32)
            value, slope = gelu_parts(pre)
            act = value.astype(jnp.bfloat16)
            dact = lax.dot_general(
                cot[spot, :], w_out[...], CONTRACT_LAST, preferred_element_type=jnp.float32
            )
            dpre_ref[spot, :] = (dact * slope).astype(jnp.bfloat16)
            mine_ref[spot, :] = jnp.dot(
                act, w_out[:, own_half], preferred_element_type=jnp.float32
            ).astype(jnp.bfloat16)
            other_ref[spot, :] = jnp.dot(
                act, w_out[:, other_half], preferred_element_type=jnp.float32
            ).astype(jnp.bfloat16)


def token_copies(core, rows, feats, piece_refs, whole, sems, which):
    blocks = []
    for block in range(NEAR):
        copies = []
        for shift in range(2):
            if block < NEAR - 1:
                source = piece_refs[2 * block + shift].at[which]
            else:
                source = piece_refs[6 + 2 * which + shift]
            columns = pl.ds(pl.multiple_of(lax.rem(core + shift, 2) * feats, feats), feats)
            copies.append(
                pltpu.make_async_copy(
                    source,
                    whole.at[pl.ds(block * rows, rows), columns],
                    sems.at[2 * block + shift],
                )
            )
        blocks.append(copies)
    return blocks


def gradient_kernel(owned, rows, feats, *refs):
    dpre_ref, piece_refs = refs[0], refs[1:11]
    keep_ref, send_ref, tok, tok_sem = refs[11:]
    core = lax.axis_index("core")
    copies = token_copies(core, rows, feats, piece_refs, tok, tok_sem, 0)
    for block in range(NEAR):
        for copy in copies[block]:
            copy.start()
    for block in range(NEAR):
        for copy in copies[block]:
            copy.wait()
    for at in range(0, 4, 2):
        grad = lax.dot_general(
            dpre_ref[:, at * owned : (at + 2) * owned],
            tok[...],
            CONTRACT_FIRST,
            preferred_element_type=jnp.float32,
        ).astype(jnp.bfloat16)
        keep_ref[at // 2] = grad[:owned]
        send_ref[at // 2] = grad[owned:]


def pair_kernel(rows, mine_ref, other_ref, *out_refs):
    for block in range(NEAR):
        spot = pl.ds(block * rows, rows)
        out_refs[block][...] = (
            mine_ref[spot, :].astype(jnp.float32) + other_ref[spot, :].astype(jnp.float32)
        ).astype(jnp.bfloat16)


def vmem(count):
    return [pl.BlockSpec(memory_space=pltpu.VMEM)] * count


def anywhere(count):
    return [pl.BlockSpec(memory_space=pl.ANY)] * count


def bf16(*shape):
    return jax.ShapeDtypeStruct(shape, jnp.bfloat16)


def permute(value, there):
    pairs = []
    for f in range(4):
        for y in range(2):
            for x in range(2):
                for c in range(2):
                    to = there(f, y, x, c)
                    here = ((f * 2 + y) * 2 + x) * 2 + c
                    pairs.append((here, ((to[0] * 2 + to[1]) * 2 + to[2]) * 2 + to[3]))
    return lax.ppermute(value, AXES, pairs)


def to_x(value):
    return permute(value, lambda f, y, x, c: (f, y, 1 - x, c))


def to_y(value):
    return permute(value, lambda f, y, x, c: (f, 1 - y, x, c))


def to_diagonal(value):
    return permute(value, lambda f, y, x, c: (f, 1 - y, 1 - x, c))


def to_core(value):
    return permute(value, lambda f, y, x, c: (f, y, x, 1 - c))


def to_far(value, flip):
    return permute(value, lambda f, y, x, c: (f ^ flip, y, x, c))


def on_device_lines(tokens, cotangent, w_in, b_in, w_out):
    rows, feats = tokens.shape
    owned, width = w_in.shape
    units = 4 * owned
    count = NEAR * rows
    scale = 1.0 / math.sqrt(4 * count)
    params = pltpu.CompilerParams(vmem_limit_bytes=VMEM_LIMIT)
    dma = pltpu.SemaphoreType.DMA

    own = jnp.stack([tokens, cotangent])
    bias_rows = jnp.pad(b_in.reshape(1, owned), ((0, 15), (0, width - owned)))
    own_w = jnp.concatenate([w_in, w_out, bias_rows], 0)
    w_two = to_far(own_w, 2)
    from_x = to_x(own)
    from_y = to_y(own)
    w_one = to_far(own_w, 1)
    own_other = to_core(own)
    from_x, from_y, w_two, w_one, own_other = lax.optimization_barrier(
        (from_x, from_y, w_two, w_one, own_other)
    )
    diag_tok = to_y(from_x[0])
    diag_cot = to_x(from_y[1])
    w_three = to_far(w_two, 1)
    x_other = to_core(from_x)
    y_other = to_core(from_y)
    pieces = [own, own_other, from_x, x_other, from_y, y_other]
    pieces += [diag_tok, to_core(diag_tok), diag_cot, to_core(diag_cot)]
    weights = [own_w, w_one, w_two, w_three]

    mine, other, dpre = pl.pallas_call(
        functools.partial(forward_kernel, owned, rows, feats),
        out_shape=(bf16(count, feats), bf16(count, feats), bf16(count, units)),
        in_specs=anywhere(len(pieces) + len(weights)),
        out_specs=vmem(3),
        scratch_shapes=[
            pltpu.VMEM((count, width), jnp.bfloat16),
            pltpu.VMEM((count, width), jnp.bfloat16),
            pltpu.VMEM((units, width), jnp.bfloat16),
            pltpu.VMEM((units, width), jnp.bfloat16),
            pltpu.VMEM((16, units), jnp.bfloat16),
            dma((2 * NEAR,)),
            dma((2 * NEAR,)),
            dma((4, 3)),
        ],
        compiler_params=params,
        cost_estimate=pl.CostEstimate(
            flops=6 * count * units * width, bytes_accessed=8 * count * width, transcendentals=0
        ),
        name="forward",
    )(*pieces, *weights)
    received = to_core(other)

    keep, send = pl.pallas_call(
        functools.partial(gradient_kernel, owned, rows, feats),
        out_shape=[bf16(2, owned, width)] * 2,
        in_specs=vmem(1) + anywhere(len(pieces)),
        out_specs=vmem(2),
        scratch_shapes=[pltpu.VMEM((count, width), jnp.bfloat16), dma((2 * NEAR,))],
        compiler_params=params,
        cost_estimate=pl.CostEstimate(
            flops=2 * count * units * width, bytes_accessed=4 * count * width, transcendentals=0
        ),
        name="gradient",
    )(dpre, *pieces)
    sent = to_far(send, 1)

    sums = pl.pallas_call(
        functools.partial(pair_kernel, rows),
        out_shape=[bf16(rows, feats)] * NEAR,
        in_specs=vmem(2),
        out_specs=vmem(NEAR),
        compiler_params=params,
        name="pair_sum",
    )(mine, received)
    mixed_x = to_x(sums[1])
    mixed_y = to_y(sums[2])
    mixed_diag = to_diagonal(sums[3])
    keep, _ = lax.optimization_barrier((keep, sums[0]))
    pair = keep.astype(jnp.float32) + sent.astype(jnp.float32)
    grad_two = to_far(pair[1].astype(jnp.bfloat16), 2)
    mixed = (
        sums[0].astype(jnp.float32)
        + mixed_x.astype(jnp.float32)
        + mixed_y.astype(jnp.float32)
        + mixed_diag.astype(jnp.float32)
    ).astype(jnp.bfloat16)
    return (mixed, (pair[0] + grad_two.astype(jnp.float32)) * scale)


def solution(mesh):
    dp, tensor = mesh.shape["dp"], mesh.shape["tensor"]
    far = dp // NEAR
    if tensor == 2 and far == 4:
        fine = Mesh(mesh.devices.reshape(far, 2, 2, tensor), AXES)
        rows, owners, halves = ("far", "y", "x"), AXES, "core"
        body = on_device_lines
    else:
        fine = Mesh(mesh.devices.reshape(far, NEAR, tensor), ("far", "near", "tensor"))
        rows, owners, halves = ("far", "near"), ("far", "near", "tensor"), "tensor"
        body = on_device_any
    in_specs = (P(rows, halves), P(rows, halves), P(owners, None), P(owners), P(owners, None))
    out_specs = (P(rows, halves), P(owners, None))
    return jax.shard_map(
        body, mesh=fine, in_specs=in_specs, out_specs=out_specs, check_vma=False
    )
```

```python
import functools
import math

import jax
import jax.numpy as jnp
from jax import lax
from jax.experimental import pallas as pl
from jax.experimental.pallas import tpu as pltpu
from jax.sharding import Mesh, PartitionSpec as P

NEAR = 4
AXES = ("far", "y", "x", "core")
CONTRACT_LAST = (((1,), (1,)), ((), ()))
CONTRACT_FIRST = (((0,), (0,)), ((), ()))
VMEM_LIMIT = 28 * 1024 * 1024


def gelu_parts(value):
    coeff = 0.7978845608
    inner = coeff * (value + 0.044715 * value * value * value)
    tangent = jnp.tanh(inner)
    result = 0.5 * value * (1.0 + tangent)
    slope = 0.5 * (1.0 + tangent) + 0.5 * value * (1.0 - tangent * tangent) * coeff * (
        1.0 + 3.0 * 0.044715 * value * value
    )
    return (result, slope)


def on_device_any(tokens, cotangent, w_in, b_in, w_out):
    far, near, tensor = lax.axis_size("far"), lax.axis_size("near"), lax.axis_size("tensor")
    rows, feats = tokens.shape
    owned, width = w_in.shape
    scale = 1.0 / math.sqrt(rows * far * near)
    bias_rows = jnp.pad(b_in.reshape(1, owned), ((0, 15), (0, width - owned)))
    weights = lax.all_gather(jnp.concatenate([w_in, w_out, bias_rows], 0), "far", axis=0)
    in_rows = weights[:, :owned].reshape(far * owned, width)
    proj_rows = weights[:, owned : 2 * owned].reshape(far * owned, width)
    bias = weights[:, 2 * owned, :owned].reshape(far * owned).astype(jnp.float32)
    tok = lax.all_gather(tokens, ("near", "tensor"), axis=0).reshape(near, tensor, rows, feats)
    cot = lax.all_gather(cotangent, ("near", "tensor"), axis=0).reshape(near, tensor, rows, feats)
    tok_full = tok.transpose(0, 2, 1, 3).reshape(near * rows, width)
    cot_full = cot.transpose(0, 2, 1, 3).reshape(near * rows, width)
    pre = lax.dot_general(
        tok_full, in_rows, CONTRACT_LAST, preferred_element_type=jnp.float32
    ) + bias
    act_value, slope = gelu_parts(pre)
    act = act_value.astype(jnp.bfloat16)
    term = jnp.dot(act, proj_rows, preferred_element_type=jnp.float32).astype(jnp.bfloat16)
    term = term.reshape(near, rows, tensor, feats).transpose(0, 2, 1, 3)
    mixed = lax.psum_scatter(
        term.reshape(near * tensor, rows, feats), ("near", "tensor"), scatter_dimension=0
    )
    dact = lax.dot_general(cot_full, proj_rows, CONTRACT_LAST, preferred_element_type=jnp.float32)
    dpre = (dact * slope).astype(jnp.bfloat16)
    grad = lax.dot_general(dpre, tok_full, CONTRACT_FIRST, preferred_element_type=jnp.float32)
    grad_sum = lax.psum_scatter(grad.astype(jnp.bfloat16), "far", scatter_dimension=0, tiled=True)
    return (mixed, grad_sum.astype(jnp.float32) * scale)


def half_columns(core, shift, feats):
    return pl.ds(pl.multiple_of(lax.rem(core + shift, 2) * feats, feats), feats)


def side_by_side(core, pair, whole, start, sem):
    rows, feats = pair[0].shape
    return [
        pltpu.make_async_copy(
            pair[shift],
            whole.at[pl.ds(start, rows), half_columns(core, shift, feats)],
            sem.at[shift],
        )
        for shift in range(2)
    ]


def weight_copies(refs, owned, w_in, w_out, bias, sem):
    ins, outs = [], []
    for at, ref in enumerate(refs):
        spot = pl.ds(at * owned, owned)
        ins.append(pltpu.make_async_copy(ref.at[pl.ds(0, owned)], w_in.at[spot], sem.at[0, at]))
        ins.append(
            pltpu.make_async_copy(
                ref.at[pl.ds(2 * owned, 16), pl.ds(0, owned)], bias.at[:, spot], sem.at[1, at]
            )
        )
        outs.append(
            pltpu.make_async_copy(ref.at[pl.ds(owned, owned)], w_out.at[spot], sem.at[2, at])
        )
    return ins, outs


def run(copies, what):
    for copy in copies:
        getattr(copy, what)()


def activate(tok, w_in, bias):
    pre = lax.dot_general(
        tok, w_in, CONTRACT_LAST, preferred_element_type=jnp.float32
    ) + bias.astype(jnp.float32)
    return gelu_parts(pre)


def dot_last(left, right):
    return lax.dot_general(left, right, CONTRACT_LAST, preferred_element_type=jnp.float32)


def early_kernel(owned, *refs):
    blocks = NEAR - 1
    pair_refs, w_refs = refs[: 2 * blocks], refs[2 * blocks : 2 * blocks + 3]
    act_ref, dpre_ref, tok, cot = refs[2 * blocks + 3 : 2 * blocks + 7]
    w_in, w_out, bias, tok_sem, cot_sem, w_sem = refs[2 * blocks + 7 :]
    core = lax.axis_index("core")
    rows = pair_refs[0].shape[1]
    ins, outs = weight_copies(w_refs, owned, w_in, w_out, bias, w_sem)
    loads = []
    for block in range(blocks):
        first, second = pair_refs[2 * block], pair_refs[2 * block + 1]
        loads.append(
            side_by_side(core, (first.at[0], second.at[0]), tok, block * rows, tok_sem.at[block])
            + side_by_side(core, (first.at[1], second.at[1]), cot, block * rows, cot_sem.at[block])
        )
    run(ins + outs, "start")
    for load in loads:
        run(load, "start")
    run(ins + outs, "wait")
    step = rows // 2
    for block, load in enumerate(loads):
        run(load, "wait")

        @pl.loop(0, 2)
        def _(sub):
            spot = pl.ds(pl.multiple_of(block * rows + sub * step, step), step)
            value, slope = activate(tok[spot, :], w_in[...], bias[0:1, :])
            act_ref[spot, :] = value.astype(jnp.bfloat16)
            dact = dot_last(cot[spot, :], w_out[...])
            dpre_ref[spot, :] = (dact * slope).astype(jnp.bfloat16)


def output_kernel(owned, *refs):
    early_act, tok, diag_refs, w_refs = refs[0], refs[1], refs[2:4], refs[4:8]
    mine_ref, other_ref, slope_ref, slope_diag_ref, tok_diag, w_out = refs[8:14]
    act, w_in, bias, act_sem, tok_sem, w_sem = refs[14:]
    core = lax.axis_index("core")
    rows, feats = diag_refs[0].shape
    early_rows, early_units = early_act.shape
    ins, outs = weight_copies(w_refs, owned, w_in, w_out, bias, w_sem)
    load = side_by_side(core, diag_refs, tok_diag, 0, tok_sem)
    moved = pltpu.make_async_copy(
        early_act, act.at[pl.ds(0, early_rows), pl.ds(0, early_units)], act_sem
    )
    run(ins + load + [moved] + outs, "start")
    run(ins, "wait")
    rest = slice(early_units, early_units + owned)
    step = rows // 2

    @pl.loop(0, early_rows // rows)
    def _(block):
        spot = pl.ds(pl.multiple_of(block * rows, rows), rows)
        value, slope = activate(tok[spot, :], w_in[rest, :], bias[0:1, rest])
        act[spot, rest] = value.astype(jnp.bfloat16)
        slope_ref[spot, :] = slope

    run(load, "wait")

    @pl.loop(0, 2)
    def _(sub):
        spot = pl.ds(pl.multiple_of(sub * step, step), step)
        value, slope = activate(tok_diag[spot, :], w_in[...], bias[0:1, :])
        act[pl.ds(pl.multiple_of(early_rows + sub * step, step), step), :] = value.astype(
            jnp.bfloat16
        )
        slope_diag_ref[spot, :] = slope

    run([moved] + outs, "wait")

    @pl.loop(0, NEAR)
    def _(block):
        spot = pl.ds(pl.multiple_of(block * rows, rows), rows)
        for shift, ref in enumerate((mine_ref, other_ref)):
            ref[spot, :] = jnp.dot(
                act[spot, :],
                w_out[:, half_columns(core, shift, feats)],
                preferred_element_type=jnp.float32,
            ).astype(jnp.bfloat16)


def gradient_kernel(owned, *refs):
    early_dpre, tok, tok_diag, cot, slope, slope_diag, w_out, diag_refs = refs[:7] + (refs[7:9],)
    own_ref, one_ref, two_ref, three_ref, cot_diag, dpre, dpre_sem, cot_sem = refs[9:]
    core = lax.axis_index("core")
    rows = diag_refs[0].shape[0]
    early_rows, early_units = early_dpre.shape
    load = side_by_side(core, diag_refs, cot_diag, 0, cot_sem)
    moved = pltpu.make_async_copy(
        early_dpre, dpre.at[pl.ds(0, early_rows), pl.ds(0, early_units)], dpre_sem
    )
    run(load + [moved], "start")
    rest = slice(early_units, early_units + owned)
    step = rows // 2

    @pl.loop(0, early_rows // rows)
    def _(block):
        spot = pl.ds(pl.multiple_of(block * rows, rows), rows)
        dact = dot_last(cot[spot, :], w_out[rest, :])
        dpre[spot, rest] = (dact * slope[spot, :]).astype(jnp.bfloat16)

    run(load, "wait")

    @pl.loop(0, 2)
    def _(sub):
        spot = pl.ds(pl.multiple_of(sub * step, step), step)
        dact = dot_last(cot_diag[spot, :], w_out[...])
        dpre[pl.ds(pl.multiple_of(early_rows + sub * step, step), step), :] = (
            dact * slope_diag[spot, :]
        ).astype(jnp.bfloat16)

    run([moved], "wait")
    for at, (first_ref, second_ref) in ((0, (own_ref, one_ref)), (2, (two_ref, three_ref))):
        units = slice(at * owned, (at + 2) * owned)
        grad = lax.dot_general(
            dpre[:early_rows, units], tok[...], CONTRACT_FIRST, preferred_element_type=jnp.float32
        ) + lax.dot_general(
            dpre[early_rows:, units],
            tok_diag[...],
            CONTRACT_FIRST,
            preferred_element_type=jnp.float32,
        )
        first_ref[...] = grad[:owned].astype(jnp.bfloat16)
        second_ref[...] = grad[owned:].astype(jnp.bfloat16)


def pair_kernel(rows, mine_ref, other_ref, *out_refs):
    for block in range(NEAR):
        spot = pl.ds(block * rows, rows)
        out_refs[block][...] = (
            mine_ref[spot, :].astype(jnp.float32) + other_ref[spot, :].astype(jnp.float32)
        ).astype(jnp.bfloat16)


def vmem(count):
    return [pl.BlockSpec(memory_space=pltpu.VMEM)] * count


def anywhere(count):
    return [pl.BlockSpec(memory_space=pl.ANY)] * count


def bf16(*shape):
    return jax.ShapeDtypeStruct(shape, jnp.bfloat16)


def permute(value, there):
    pairs = []
    for f in range(4):
        for y in range(2):
            for x in range(2):
                for c in range(2):
                    to = there(f, y, x, c)
                    here = ((f * 2 + y) * 2 + x) * 2 + c
                    pairs.append((here, ((to[0] * 2 + to[1]) * 2 + to[2]) * 2 + to[3]))
    return lax.ppermute(value, AXES, pairs)


def to_x(value):
    return permute(value, lambda f, y, x, c: (f, y, 1 - x, c))


def to_y(value):
    return permute(value, lambda f, y, x, c: (f, 1 - y, x, c))


def to_diagonal(value):
    return permute(value, lambda f, y, x, c: (f, 1 - y, 1 - x, c))


def to_core(value):
    return permute(value, lambda f, y, x, c: (f, y, x, 1 - c))


def to_far(value, flip):
    return permute(value, lambda f, y, x, c: (f ^ flip, y, x, c))


def on_device_lines(tokens, cotangent, w_in, b_in, w_out):
    rows, feats = tokens.shape
    owned, width = w_in.shape
    units = 4 * owned
    count = NEAR * rows
    scale = 1.0 / math.sqrt(4 * count)
    params = pltpu.CompilerParams(vmem_limit_bytes=VMEM_LIMIT)
    dma = pltpu.SemaphoreType.DMA
    barrier = lax.optimization_barrier
    early_rows, early_units = (NEAR - 1) * rows, 3 * owned

    def f32(*shape):
        return jax.ShapeDtypeStruct(shape, jnp.float32)

    def cost(flops, traffic):
        return pl.CostEstimate(flops=flops, bytes_accessed=traffic, transcendentals=0)

    bias_rows = jnp.pad(b_in.reshape(1, owned), ((0, 15), (0, width - owned)))
    own_w = jnp.concatenate([w_in, w_out, bias_rows], 0)
    own_w, tokens, cotangent = barrier((own_w, tokens, cotangent))
    own = jnp.stack([tokens, cotangent])
    w_two, w_one = to_far(own_w, 2), to_far(own_w, 1)
    from_x, from_y = to_x(own), to_y(own)
    own_other = to_core(own)
    from_x, from_y, w_two, w_one, own_other = barrier((from_x, from_y, w_two, w_one, own_other))
    tok_diag, cot_diag = to_y(from_x[0]), to_x(from_y[1])
    w_three = to_far(w_two, 1)
    x_other, y_other = to_core(from_x), to_core(from_y)
    early_w = [own_w, w_one, w_two]
    early_act, early_dpre, tok, cot = pl.pallas_call(
        functools.partial(early_kernel, owned),
        out_shape=(
            bf16(early_rows, early_units),
            bf16(early_rows, early_units),
            bf16(early_rows, width),
            bf16(early_rows, width),
        ),
        in_specs=anywhere(2 * (NEAR - 1) + 3),
        out_specs=vmem(4),
        scratch_shapes=[
            pltpu.VMEM((early_units, width), jnp.bfloat16),
            pltpu.VMEM((early_units, width), jnp.bfloat16),
            pltpu.VMEM((16, early_units), jnp.bfloat16),
            dma((NEAR - 1, 2)),
            dma((NEAR - 1, 2)),
            dma((3, 3)),
        ],
        compiler_params=params,
        cost_estimate=cost(4 * early_rows * early_units * width, 8 * early_rows * width),
        name="early",
    )(own, own_other, from_x, x_other, from_y, y_other, *early_w)
    tok_diag, cot_diag, early_act = barrier((tok_diag, cot_diag, early_act))
    tok_diag_other, cot_diag_other = barrier((to_core(tok_diag), to_core(cot_diag)))

    mine, other, slope, slope_diag, tok_last, w_out_all = pl.pallas_call(
        functools.partial(output_kernel, owned),
        out_shape=(
            bf16(count, feats),
            bf16(count, feats),
            f32(early_rows, owned),
            f32(rows, units),
            bf16(rows, width),
            bf16(units, width),
        ),
        in_specs=vmem(2) + anywhere(6),
        out_specs=vmem(6),
        scratch_shapes=[
            pltpu.VMEM((count, units), jnp.bfloat16),
            pltpu.VMEM((units, width), jnp.bfloat16),
            pltpu.VMEM((16, units), jnp.bfloat16),
            dma,
            dma((2,)),
            dma((3, 4)),
        ],
        compiler_params=params,
        cost_estimate=cost(4 * count * units * width, 4 * count * width),
        name="output",
    )(early_act, tok, tok_diag, tok_diag_other, *early_w, w_three)
    received = to_core(other)

    grad_own, grad_one, grad_two, grad_three = pl.pallas_call(
        functools.partial(gradient_kernel, owned),
        out_shape=[bf16(owned, width)] * 4,
        in_specs=vmem(7) + anywhere(2),
        out_specs=vmem(4),
        scratch_shapes=[
            pltpu.VMEM((rows, width), jnp.bfloat16),
            pltpu.VMEM((count, units), jnp.bfloat16),
            dma,
            dma((2,)),
        ],
        compiler_params=params,
        cost_estimate=cost(4 * count * units * width, 4 * count * width),
        name="gradient",
    )(
        early_dpre, tok, tok_last, cot, slope, slope_diag, w_out_all, cot_diag, cot_diag_other
    )
    relayed = to_far(grad_three, 1)
    from_one = to_far(grad_one, 1)

    sums = pl.pallas_call(
        functools.partial(pair_kernel, rows),
        out_shape=[bf16(rows, feats)] * NEAR,
        in_specs=vmem(2),
        out_specs=vmem(NEAR),
        compiler_params=params,
        name="pair_sum",
    )(mine, received)
    mixed_x, mixed_y, mixed_diag = to_x(sums[1]), to_y(sums[2]), to_diagonal(sums[3])
    grad_two, _ = barrier((grad_two, sums[0]))
    from_two = to_far(
        (grad_two.astype(jnp.float32) + relayed.astype(jnp.float32)).astype(jnp.bfloat16), 2
    )
    total = (
        grad_own.astype(jnp.float32)
        + from_one.astype(jnp.float32)
        + from_two.astype(jnp.float32)
    )
    mixed = (
        sums[0].astype(jnp.float32)
        + mixed_x.astype(jnp.float32)
        + mixed_y.astype(jnp.float32)
        + mixed_diag.astype(jnp.float32)
    ).astype(jnp.bfloat16)
    return (mixed, total * scale)


def solution(mesh):
    dp, tensor = mesh.shape["dp"], mesh.shape["tensor"]
    far = dp // NEAR
    if tensor == 2 and far == 4:
        fine = Mesh(mesh.devices.reshape(far, 2, 2, tensor), AXES)
        rows, owners, halves = ("far", "y", "x"), AXES, "core"
        body = on_device_lines
    else:
        fine = Mesh(mesh.devices.reshape(far, NEAR, tensor), ("far", "near", "tensor"))
        rows, owners, halves = ("far", "near"), ("far", "near", "tensor"), "tensor"
        body = on_device_any
    in_specs = (P(rows, halves), P(rows, halves), P(owners, None), P(owners), P(owners, None))
    out_specs = (P(rows, halves), P(owners, None))
    return jax.shard_map(
        body, mesh=fine, in_specs=in_specs, out_specs=out_specs, check_vma=False
    )
```

```python
import functools
import math

import jax
import jax.numpy as jnp
from jax import lax
from jax.experimental import pallas as pl
from jax.experimental.pallas import tpu as pltpu
from jax.sharding import Mesh, PartitionSpec as P

NEAR = 4
AXES = ("far", "y", "x", "core")
CONTRACT_LAST = (((1,), (1,)), ((), ()))
CONTRACT_FIRST = (((0,), (0,)), ((), ()))
VMEM_LIMIT = 28 * 1024 * 1024


def gelu_parts(value):
    coeff = 0.7978845608
    inner = coeff * (value + 0.044715 * value * value * value)
    tangent = jnp.tanh(inner)
    result = 0.5 * value * (1.0 + tangent)
    slope = 0.5 * (1.0 + tangent) + 0.5 * value * (1.0 - tangent * tangent) * coeff * (
        1.0 + 3.0 * 0.044715 * value * value
    )
    return (result, slope)


def on_device_any(tokens, cotangent, w_in, b_in, w_out):
    far, near, tensor = lax.axis_size("far"), lax.axis_size("near"), lax.axis_size("tensor")
    rows, feats = tokens.shape
    owned, width = w_in.shape
    scale = 1.0 / math.sqrt(rows * far * near)
    bias_rows = jnp.pad(b_in.reshape(1, owned), ((0, 15), (0, width - owned)))
    weights = lax.all_gather(jnp.concatenate([w_in, w_out, bias_rows], 0), "far", axis=0)
    in_rows = weights[:, :owned].reshape(far * owned, width)
    proj_rows = weights[:, owned : 2 * owned].reshape(far * owned, width)
    bias = weights[:, 2 * owned, :owned].reshape(far * owned).astype(jnp.float32)
    tok = lax.all_gather(tokens, ("near", "tensor"), axis=0).reshape(near, tensor, rows, feats)
    cot = lax.all_gather(cotangent, ("near", "tensor"), axis=0).reshape(near, tensor, rows, feats)
    tok_full = tok.transpose(0, 2, 1, 3).reshape(near * rows, width)
    cot_full = cot.transpose(0, 2, 1, 3).reshape(near * rows, width)
    pre = lax.dot_general(
        tok_full, in_rows, CONTRACT_LAST, preferred_element_type=jnp.float32
    ) + bias
    act_value, slope = gelu_parts(pre)
    act = act_value.astype(jnp.bfloat16)
    term = jnp.dot(act, proj_rows, preferred_element_type=jnp.float32).astype(jnp.bfloat16)
    term = term.reshape(near, rows, tensor, feats).transpose(0, 2, 1, 3)
    mixed = lax.psum_scatter(
        term.reshape(near * tensor, rows, feats), ("near", "tensor"), scatter_dimension=0
    )
    dact = lax.dot_general(cot_full, proj_rows, CONTRACT_LAST, preferred_element_type=jnp.float32)
    dpre = (dact * slope).astype(jnp.bfloat16)
    grad = lax.dot_general(dpre, tok_full, CONTRACT_FIRST, preferred_element_type=jnp.float32)
    grad_sum = lax.psum_scatter(grad.astype(jnp.bfloat16), "far", scatter_dimension=0, tiled=True)
    return (mixed, grad_sum.astype(jnp.float32) * scale)


def half_columns(core, shift, feats):
    return pl.ds(pl.multiple_of(lax.rem(core + shift, 2) * feats, feats), feats)


def side_by_side(core, pair, whole, start, sem):
    rows, feats = pair[0].shape
    return [
        pltpu.make_async_copy(
            pair[shift],
            whole.at[pl.ds(start, rows), half_columns(core, shift, feats)],
            sem.at[shift],
        )
        for shift in range(2)
    ]


def weight_copies(refs, owned, w_in, w_out, bias, sem):
    ins, outs = [], []
    for at, ref in enumerate(refs):
        spot = pl.ds(at * owned, owned)
        ins.append(pltpu.make_async_copy(ref.at[pl.ds(0, owned)], w_in.at[spot], sem.at[0, at]))
        ins.append(
            pltpu.make_async_copy(
                ref.at[pl.ds(2 * owned, 16), pl.ds(0, owned)], bias.at[:, spot], sem.at[1, at]
            )
        )
        outs.append(
            pltpu.make_async_copy(ref.at[pl.ds(owned, owned)], w_out.at[spot], sem.at[2, at])
        )
    return ins, outs


def run(copies, what):
    for copy in copies:
        getattr(copy, what)()


def activate(tok, w_in, bias):
    pre = lax.dot_general(
        tok, w_in, CONTRACT_LAST, preferred_element_type=jnp.float32
    ) + bias.astype(jnp.float32)
    return gelu_parts(pre)


def dot_last(left, right):
    return lax.dot_general(left, right, CONTRACT_LAST, preferred_element_type=jnp.float32)


def early_kernel(owned, *refs):
    blocks = NEAR - 1
    pair_refs, w_refs = refs[: 2 * blocks], refs[2 * blocks : 2 * blocks + 3]
    act_ref, dpre_ref, mixed_ref, grad_ref, tok, cot = refs[2 * blocks + 3 : 2 * blocks + 9]
    w_in, w_out, bias, dpre, tok_sem, cot_sem, w_sem = refs[2 * blocks + 9 :]
    core = lax.axis_index("core")
    rows = pair_refs[0].shape[1]
    two = 2 * owned
    ins, outs = weight_copies(w_refs, owned, w_in, w_out, bias, w_sem)
    loads = []
    for block in range(blocks):
        first, second = pair_refs[2 * block], pair_refs[2 * block + 1]
        loads.append(
            side_by_side(core, (first.at[0], second.at[0]), tok, block * rows, tok_sem.at[block])
            + side_by_side(core, (first.at[1], second.at[1]), cot, block * rows, cot_sem.at[block])
        )
    run(ins + outs, "start")
    for load in loads:
        run(load, "start")
    run(ins + outs, "wait")
    step = rows // 2
    for block, load in enumerate(loads):
        run(load, "wait")

        @pl.loop(0, 2)
        def _(sub):
            spot = pl.ds(pl.multiple_of(block * rows + sub * step, step), step)
            value, slope = activate(tok[spot, :], w_in[...], bias[0:1, :])
            act = value.astype(jnp.bfloat16)
            act_ref[spot, :] = act[:, two:]
            dact = dot_last(cot[spot, :], w_out[...])
            terms = (dact * slope).astype(jnp.bfloat16)
            dpre[spot, :] = terms[:, :two]
            dpre_ref[spot, :] = terms[:, two:]
            mixed_ref[spot, :] = jnp.dot(
                act[:, :two], w_out[:two, :], preferred_element_type=jnp.float32
            )

    grad_ref[...] = dot_first(dpre[...], tok[...])


def dot_first(left, right):
    return lax.dot_general(left, right, CONTRACT_FIRST, preferred_element_type=jnp.float32)


def output_kernel(owned, *refs):
    early_act, tok, early_mixed, w_refs = refs[0], refs[1], refs[2], refs[3:7]
    mine_ref, other_ref, slope_ref, w_in, w_out, bias = refs[7:13]
    act, act_sem, w_sem = refs[13:]
    core = lax.axis_index("core")
    early_rows, feats = mine_ref.shape
    two = 2 * owned
    ins, outs = weight_copies(w_refs, owned, w_in, w_out, bias, w_sem)
    moved = pltpu.make_async_copy(early_act, act.at[:, pl.ds(0, owned)], act_sem)
    run(ins + outs + [moved], "start")
    run(ins + outs + [moved], "wait")
    rest = slice(3 * owned, 4 * owned)
    step = early_rows // 3

    @pl.loop(0, 3)
    def _(block):
        spot = pl.ds(pl.multiple_of(block * step, step), step)
        value, slope = activate(tok[spot, :], w_in[rest, :], bias[0:1, rest])
        act[spot, owned:] = value.astype(jnp.bfloat16)
        slope_ref[spot, :] = slope
        for shift, ref in enumerate((mine_ref, other_ref)):
            half = half_columns(core, shift, feats)
            ref[spot, :] = (
                early_mixed[spot, half]
                + jnp.dot(act[spot, :], w_out[two:, half], preferred_element_type=jnp.float32)
            ).astype(jnp.bfloat16)


def diagonal_kernel(*refs):
    w_in, w_out, bias, diag_refs = refs[0], refs[1], refs[2], refs[3:5]
    mine_ref, other_ref, slope_ref, tok_diag, tok_sem = refs[5:]
    core = lax.axis_index("core")
    rows, feats = diag_refs[0].shape
    load = side_by_side(core, diag_refs, tok_diag, 0, tok_sem)
    run(load, "start")
    run(load, "wait")
    step = rows // 2

    @pl.loop(0, 2)
    def _(sub):
        spot = pl.ds(pl.multiple_of(sub * step, step), step)
        value, slope = activate(tok_diag[spot, :], w_in[...], bias[0:1, :])
        act = value.astype(jnp.bfloat16)
        slope_ref[spot, :] = slope
        for shift, ref in enumerate((mine_ref, other_ref)):
            ref[spot, :] = jnp.dot(
                act, w_out[:, half_columns(core, shift, feats)], preferred_element_type=jnp.float32
            ).astype(jnp.bfloat16)


def gradient_kernel(owned, *refs):
    early_dpre, early_grad, tok, tok_diag, cot, slope, slope_diag, w_out = refs[:8]
    diag_refs = refs[8:10]
    own_ref, one_ref, two_ref, three_ref, cot_diag, dpre, dpre_diag, dpre_sem, cot_sem = refs[10:]
    core = lax.axis_index("core")
    rows = diag_refs[0].shape[0]
    early_rows = early_dpre.shape[0]
    two = 2 * owned
    load = side_by_side(core, diag_refs, cot_diag, 0, cot_sem)
    moved = pltpu.make_async_copy(early_dpre, dpre.at[:, pl.ds(0, owned)], dpre_sem)
    run(load + [moved], "start")
    rest = slice(3 * owned, 4 * owned)

    @pl.loop(0, early_rows // rows)
    def _(block):
        spot = pl.ds(pl.multiple_of(block * rows, rows), rows)
        dact = dot_last(cot[spot, :], w_out[rest, :])
        dpre[spot, owned:] = (dact * slope[spot, :]).astype(jnp.bfloat16)

    run(load + [moved], "wait")
    dpre_diag[...] = (dot_last(cot_diag[...], w_out[...]) * slope_diag[...]).astype(jnp.bfloat16)
    grad = dot_first(dpre[...], tok[...]) + dot_first(dpre_diag[:, two:], tok_diag[...])
    two_ref[...] = grad[:owned].astype(jnp.bfloat16)
    three_ref[...] = grad[owned:].astype(jnp.bfloat16)
    grad = early_grad[...] + dot_first(dpre_diag[:, :two], tok_diag[...])
    own_ref[...] = grad[:owned].astype(jnp.bfloat16)
    one_ref[...] = grad[owned:].astype(jnp.bfloat16)


def pair_kernel(rows, mine_ref, other_ref, *out_refs):
    for block, ref in enumerate(out_refs):
        spot = pl.ds(block * rows, rows)
        ref[...] = (
            mine_ref[spot, :].astype(jnp.float32) + other_ref[spot, :].astype(jnp.float32)
        ).astype(jnp.bfloat16)


def vmem(count):
    return [pl.BlockSpec(memory_space=pltpu.VMEM)] * count


def anywhere(count):
    return [pl.BlockSpec(memory_space=pl.ANY)] * count


def bf16(*shape):
    return jax.ShapeDtypeStruct(shape, jnp.bfloat16)


def permute(value, there):
    pairs = []
    for f in range(4):
        for y in range(2):
            for x in range(2):
                for c in range(2):
                    to = there(f, y, x, c)
                    here = ((f * 2 + y) * 2 + x) * 2 + c
                    pairs.append((here, ((to[0] * 2 + to[1]) * 2 + to[2]) * 2 + to[3]))
    return lax.ppermute(value, AXES, pairs)


def to_x(value):
    return permute(value, lambda f, y, x, c: (f, y, 1 - x, c))


def to_y(value):
    return permute(value, lambda f, y, x, c: (f, 1 - y, x, c))


def to_diagonal(value):
    return permute(value, lambda f, y, x, c: (f, 1 - y, 1 - x, c))


def to_core(value):
    return permute(value, lambda f, y, x, c: (f, y, x, 1 - c))


def to_far(value, flip):
    return permute(value, lambda f, y, x, c: (f ^ flip, y, x, c))


def on_device_lines(tokens, cotangent, w_in, b_in, w_out):
    rows, feats = tokens.shape
    owned, width = w_in.shape
    units = 4 * owned
    count = NEAR * rows
    scale = 1.0 / math.sqrt(4 * count)
    params = pltpu.CompilerParams(vmem_limit_bytes=VMEM_LIMIT)
    dma = pltpu.SemaphoreType.DMA
    barrier = lax.optimization_barrier
    early_rows = (NEAR - 1) * rows

    def f32(*shape):
        return jax.ShapeDtypeStruct(shape, jnp.float32)

    def cost(flops, traffic):
        return pl.CostEstimate(flops=flops, bytes_accessed=traffic, transcendentals=0)

    bias_rows = jnp.pad(b_in.reshape(1, owned), ((0, 15), (0, width - owned)))
    own_w = jnp.concatenate([w_in, w_out, bias_rows], 0)
    own_w, tokens, cotangent = barrier((own_w, tokens, cotangent))
    own = jnp.stack([tokens, cotangent])
    w_two, w_one = to_far(own_w, 2), to_far(own_w, 1)
    from_x, from_y = to_x(own), to_y(own)
    own_other = to_core(own)
    tok_diag, cot_diag = to_y(from_x[0]), to_x(from_y[1])
    from_x, from_y, own_other, w_one, w_two = barrier((from_x, from_y, own_other, w_one, w_two))
    x_other, y_other = to_core(from_x), to_core(from_y)
    w_three = to_far(w_two, 1)
    early_w = [own_w, w_one, w_two]
    early_act, early_dpre, early_mixed, early_grad, tok, cot = pl.pallas_call(
        functools.partial(early_kernel, owned),
        out_shape=(
            bf16(early_rows, owned),
            bf16(early_rows, owned),
            f32(early_rows, width),
            f32(2 * owned, width),
            bf16(early_rows, width),
            bf16(early_rows, width),
        ),
        in_specs=anywhere(2 * (NEAR - 1) + 3),
        out_specs=vmem(6),
        scratch_shapes=[
            pltpu.VMEM((3 * owned, width), jnp.bfloat16),
            pltpu.VMEM((3 * owned, width), jnp.bfloat16),
            pltpu.VMEM((16, 3 * owned), jnp.bfloat16),
            pltpu.VMEM((early_rows, 2 * owned), jnp.bfloat16),
            dma((NEAR - 1, 2)),
            dma((NEAR - 1, 2)),
            dma((3, 3)),
        ],
        compiler_params=params,
        cost_estimate=cost(early_rows * units, early_rows),
        name="early",
    )(own, own_other, from_x, x_other, from_y, y_other, *early_w)
    tok_diag, cot_diag, early_act = barrier((tok_diag, cot_diag, early_act))
    tok_diag_other, cot_diag_other = to_core(tok_diag), to_core(cot_diag)

    mine, other, slope, w_in_all, w_out_all, bias = pl.pallas_call(
        functools.partial(output_kernel, owned),
        out_shape=(
            bf16(early_rows, feats),
            bf16(early_rows, feats),
            f32(early_rows, owned),
            bf16(units, width),
            bf16(units, width),
            bf16(16, units),
        ),
        in_specs=vmem(3) + anywhere(4),
        out_specs=vmem(6),
        scratch_shapes=[pltpu.VMEM((early_rows, 2 * owned), jnp.bfloat16), dma, dma((3, 4))],
        compiler_params=params,
        cost_estimate=cost(8 * early_rows * units * width, 4 * count * width),
        name="output",
    )(early_act, tok, early_mixed, *early_w, w_three)
    received = to_core(other)

    tok_diag_other, cot_diag_other, w_in_all = barrier((tok_diag_other, cot_diag_other, w_in_all))
    mine_diag, other_diag, slope_diag, tok_last = pl.pallas_call(
        diagonal_kernel,
        out_shape=(bf16(rows, feats), bf16(rows, feats), f32(rows, units), bf16(rows, width)),
        in_specs=vmem(3) + anywhere(2),
        out_specs=vmem(4),
        scratch_shapes=[dma((2,))],
        compiler_params=params,
        cost_estimate=cost(48 * rows * units * width, 4 * rows * width),
        name="diagonal",
    )(w_in_all, w_out_all, bias, tok_diag, tok_diag_other)
    received_diag = to_core(other_diag)

    mine, slope_diag = barrier((mine, slope_diag))
    sums = pl.pallas_call(
        functools.partial(pair_kernel, rows),
        out_shape=[bf16(rows, feats)] * (NEAR - 1),
        in_specs=vmem(2),
        out_specs=vmem(NEAR - 1),
        compiler_params=params,
        name="pair_sum",
    )(mine, received)
    mixed_x, mixed_y = to_x(sums[1]), to_y(sums[2])
    early_grad, mixed_own = barrier((early_grad, sums[0]))

    grad_own, grad_one, grad_two, grad_three = pl.pallas_call(
        functools.partial(gradient_kernel, owned),
        out_shape=[bf16(owned, width)] * 4,
        in_specs=vmem(8) + anywhere(2),
        out_specs=vmem(4),
        scratch_shapes=[
            pltpu.VMEM((rows, width), jnp.bfloat16),
            pltpu.VMEM((early_rows, 2 * owned), jnp.bfloat16),
            pltpu.VMEM((rows, units), jnp.bfloat16),
            dma,
            dma((2,)),
        ],
        compiler_params=params,
        cost_estimate=cost(early_rows * units, early_rows),
        name="gradient",
    )(
        early_dpre, early_grad, tok, tok_last, cot, slope, slope_diag, w_out_all,
        cot_diag, cot_diag_other,
    )
    relayed = to_far(grad_three, 1)
    from_one = to_far(grad_one, 1)

    mine_diag, grad_own = barrier((mine_diag, grad_own))
    (sum_diag,) = pl.pallas_call(
        functools.partial(pair_kernel, rows),
        out_shape=[bf16(rows, feats)],
        in_specs=vmem(2),
        out_specs=vmem(1),
        compiler_params=params,
        name="pair_sum_diagonal",
    )(mine_diag, received_diag)
    mixed_diag = to_diagonal(sum_diag)
    grad_two, mixed_x, mixed_y, _ = barrier((grad_two, mixed_x, mixed_y, sum_diag))
    from_two = to_far(
        (grad_two.astype(jnp.float32) + relayed.astype(jnp.float32)).astype(jnp.bfloat16), 2
    )
    total = (
        grad_own.astype(jnp.float32)
        + from_one.astype(jnp.float32)
        + from_two.astype(jnp.float32)
    )
    mixed = (
        mixed_own.astype(jnp.float32)
        + mixed_x.astype(jnp.float32)
        + mixed_y.astype(jnp.float32)
        + mixed_diag.astype(jnp.float32)
    ).astype(jnp.bfloat16)
    return (mixed, total * scale)


def solution(mesh):
    dp, tensor = mesh.shape["dp"], mesh.shape["tensor"]
    far = dp // NEAR
    if tensor == 2 and far == 4:
        fine = Mesh(mesh.devices.reshape(far, 2, 2, tensor), AXES)
        rows, owners, halves = ("far", "y", "x"), AXES, "core"
        body = on_device_lines
    else:
        fine = Mesh(mesh.devices.reshape(far, NEAR, tensor), ("far", "near", "tensor"))
        rows, owners, halves = ("far", "near"), ("far", "near", "tensor"), "tensor"
        body = on_device_any
    in_specs = (P(rows, halves), P(rows, halves), P(owners, None), P(owners), P(owners, None))
    out_specs = (P(rows, halves), P(owners, None))
    return jax.shard_map(
        body, mesh=fine, in_specs=in_specs, out_specs=out_specs, check_vma=False
    )
```

```python
import functools
import math

import jax
import jax.numpy as jnp
from jax import lax
from jax.experimental import pallas as pl
from jax.experimental.pallas import tpu as pltpu
from jax.sharding import Mesh, PartitionSpec as P

NEAR = 4
AXES = ("far", "y", "x", "core")
CONTRACT_LAST = (((1,), (1,)), ((), ()))
CONTRACT_FIRST = (((0,), (0,)), ((), ()))
VMEM_LIMIT = 28 * 1024 * 1024
OWN_COST = 10**10
PLANE_COST = 10**10


def gelu_parts(value):
    coeff = 0.7978845608
    inner = coeff * (value + 0.044715 * value * value * value)
    tangent = jnp.tanh(inner)
    result = 0.5 * value * (1.0 + tangent)
    slope = 0.5 * (1.0 + tangent) + 0.5 * value * (1.0 - tangent * tangent) * coeff * (
        1.0 + 3.0 * 0.044715 * value * value
    )
    return (result, slope)


def on_device_any(tokens, cotangent, w_in, b_in, w_out):
    far, near, tensor = lax.axis_size("far"), lax.axis_size("near"), lax.axis_size("tensor")
    rows, feats = tokens.shape
    owned, width = w_in.shape
    scale = 1.0 / math.sqrt(rows * far * near)
    bias_rows = jnp.pad(b_in.reshape(1, owned), ((0, 15), (0, width - owned)))
    weights = lax.all_gather(jnp.concatenate([w_in, w_out, bias_rows], 0), "far", axis=0)
    in_rows = weights[:, :owned].reshape(far * owned, width)
    proj_rows = weights[:, owned : 2 * owned].reshape(far * owned, width)
    bias = weights[:, 2 * owned, :owned].reshape(far * owned).astype(jnp.float32)
    tok = lax.all_gather(tokens, ("near", "tensor"), axis=0).reshape(near, tensor, rows, feats)
    cot = lax.all_gather(cotangent, ("near", "tensor"), axis=0).reshape(near, tensor, rows, feats)
    tok_full = tok.transpose(0, 2, 1, 3).reshape(near * rows, width)
    cot_full = cot.transpose(0, 2, 1, 3).reshape(near * rows, width)
    pre = lax.dot_general(
        tok_full, in_rows, CONTRACT_LAST, preferred_element_type=jnp.float32
    ) + bias
    act_value, slope = gelu_parts(pre)
    act = act_value.astype(jnp.bfloat16)
    term = jnp.dot(act, proj_rows, preferred_element_type=jnp.float32).astype(jnp.bfloat16)
    term = term.reshape(near, rows, tensor, feats).transpose(0, 2, 1, 3)
    mixed = lax.psum_scatter(
        term.reshape(near * tensor, rows, feats), ("near", "tensor"), scatter_dimension=0
    )
    dact = lax.dot_general(cot_full, proj_rows, CONTRACT_LAST, preferred_element_type=jnp.float32)
    dpre = (dact * slope).astype(jnp.bfloat16)
    grad = lax.dot_general(dpre, tok_full, CONTRACT_FIRST, preferred_element_type=jnp.float32)
    grad_sum = lax.psum_scatter(grad.astype(jnp.bfloat16), "far", scatter_dimension=0, tiled=True)
    return (mixed, grad_sum.astype(jnp.float32) * scale)


def half_columns(core, shift, feats):
    return pl.ds(pl.multiple_of(lax.rem(core + shift, 2) * feats, feats), feats)


def side_by_side(core, pair, whole, start, sem):
    rows, feats = pair[0].shape
    return [
        pltpu.make_async_copy(
            pair[shift],
            whole.at[pl.ds(start, rows), half_columns(core, shift, feats)],
            sem.at[shift],
        )
        for shift in range(2)
    ]


def weight_copies(refs, owned, w_in, w_out, bias, sem):
    ins, outs = [], []
    for at, ref in enumerate(refs):
        spot = pl.ds(at * owned, owned)
        ins.append(pltpu.make_async_copy(ref.at[pl.ds(0, owned)], w_in.at[spot], sem.at[0, at]))
        ins.append(
            pltpu.make_async_copy(
                ref.at[pl.ds(2 * owned, 16), pl.ds(0, owned)], bias.at[:, spot], sem.at[1, at]
            )
        )
        outs.append(
            pltpu.make_async_copy(ref.at[pl.ds(owned, owned)], w_out.at[spot], sem.at[2, at])
        )
    return ins, outs


def run(copies, what):
    for copy in copies:
        getattr(copy, what)()


def activate(tok, w_in, bias):
    pre = lax.dot_general(
        tok, w_in, CONTRACT_LAST, preferred_element_type=jnp.float32
    ) + bias.astype(jnp.float32)
    return gelu_parts(pre)


def dot_last(left, right):
    return lax.dot_general(left, right, CONTRACT_LAST, preferred_element_type=jnp.float32)


def dot_first(left, right):
    return lax.dot_general(left, right, CONTRACT_FIRST, preferred_element_type=jnp.float32)


def early_block(start, step, tok, cot, w_in, w_out, bias, two, act_ref, dpre_ref, mixed_ref, dpre):
    @pl.loop(0, 2)
    def _(sub):
        spot = pl.ds(pl.multiple_of(start + sub * step, step), step)
        value, slope = activate(tok[spot, :], w_in[...], bias[0:1, :])
        act = value.astype(jnp.bfloat16)
        act_ref[spot, :] = act[:, two:]
        dact = dot_last(cot[spot, :], w_out[...])
        terms = (dact * slope).astype(jnp.bfloat16)
        dpre[spot, :] = terms[:, :two]
        dpre_ref[spot, :] = terms[:, two:]
        mixed_ref[spot, :] = jnp.dot(
            act[:, :two], w_out[:two, :], preferred_element_type=jnp.float32
        )


def own_kernel(owned, *refs):
    own_ref, other_ref, w_refs = refs[0], refs[1], refs[2:5]
    act_ref, dpre_ref, mixed_ref, grad_ref, tok, cot, w_in, w_out, bias = refs[5:14]
    dpre, tok_sem, cot_sem, w_sem = refs[14:]
    core = lax.axis_index("core")
    rows = own_ref.shape[1]
    ins, outs = weight_copies(w_refs, owned, w_in, w_out, bias, w_sem)
    load = side_by_side(core, (own_ref.at[0], other_ref.at[0]), tok, 0, tok_sem)
    load += side_by_side(core, (own_ref.at[1], other_ref.at[1]), cot, 0, cot_sem)
    run(ins + outs + load, "start")
    run(ins + outs + load, "wait")
    early_block(
        0, rows // 2, tok, cot, w_in, w_out, bias, 2 * owned, act_ref, dpre_ref, mixed_ref, dpre
    )
    grad_ref[...] = dot_first(dpre[...], tok[...])


def early_kernel(owned, *refs):
    pair_refs, w_in, w_out, bias, grad_own_ref = refs[:4], refs[4], refs[5], refs[6], refs[7]
    act_ref, dpre_ref, mixed_ref, grad_ref, tok, cot = refs[8:14]
    dpre, tok_sem, cot_sem = refs[14:]
    core = lax.axis_index("core")
    rows = pair_refs[0].shape[1]
    loads = []
    for block in range(2):
        first, second = pair_refs[2 * block], pair_refs[2 * block + 1]
        loads.append(
            side_by_side(core, (first.at[0], second.at[0]), tok, block * rows, tok_sem.at[block])
            + side_by_side(core, (first.at[1], second.at[1]), cot, block * rows, cot_sem.at[block])
        )
    for load in loads:
        run(load, "start")
    for block, load in enumerate(loads):
        run(load, "wait")
        early_block(
            block * rows, rows // 2, tok, cot, w_in, w_out, bias, 2 * owned,
            act_ref, dpre_ref, mixed_ref, dpre,
        )
    grad_ref[...] = grad_own_ref[...] + dot_first(dpre[...], tok[...])


def output_kernel(owned, *refs):
    groups = (refs[0:3], refs[3:6])
    w_in, w_out, bias, w_three = refs[6:10]
    mine_ref, other_ref, slope_ref, w_in_all, w_out_all, bias_all = refs[10:16]
    w_last, sem = refs[16:]
    core = lax.axis_index("core")
    feats = mine_ref.shape[1]
    two, three = 2 * owned, 3 * owned
    first, last = pl.ds(0, three), pl.ds(three, owned)
    copies = [
        pltpu.make_async_copy(w_in, w_in_all.at[first], sem.at[0]),
        pltpu.make_async_copy(w_three.at[pl.ds(0, owned)], w_in_all.at[last], sem.at[1]),
        pltpu.make_async_copy(w_out, w_out_all.at[first], sem.at[2]),
        pltpu.make_async_copy(w_three.at[pl.ds(owned, owned)], w_out_all.at[last], sem.at[3]),
    ]
    run(copies, "start")
    bias_last = w_three[two : two + 16, :owned]
    bias_all[:, :three] = bias[...]
    bias_all[:, three:] = bias_last
    w_last[:owned, :] = w_out[two:, :]
    w_last[owned:, :] = w_three[owned:two, :]
    start = 0
    for act_two, tok, early_mixed in groups:
        rows = tok.shape[0]
        step = rows // 2

        @pl.loop(0, 2)
        def _(sub):
            here = pl.ds(pl.multiple_of(sub * step, step), step)
            spot = pl.ds(pl.multiple_of(start + sub * step, step), step)
            value, slope = activate(tok[here, :], w_three[:owned, :], bias_last[0:1, :])
            slope_ref[spot, :] = slope
            act = jnp.concatenate([act_two[here, :], value.astype(jnp.bfloat16)], axis=1)
            for shift, ref in enumerate((mine_ref, other_ref)):
                half = half_columns(core, shift, feats)
                ref[spot, :] = (
                    early_mixed[here, half]
                    + jnp.dot(act, w_last[:, half], preferred_element_type=jnp.float32)
                ).astype(jnp.bfloat16)

        start += rows
    run(copies, "wait")


def diagonal_kernel(*refs):
    w_in, w_out, bias, diag_refs = refs[0], refs[1], refs[2], refs[3:5]
    mine_ref, other_ref, slope_ref, tok_diag, tok_sem = refs[5:]
    core = lax.axis_index("core")
    rows, feats = diag_refs[0].shape
    load = side_by_side(core, diag_refs, tok_diag, 0, tok_sem)
    run(load, "start")
    run(load, "wait")
    step = rows // 2

    @pl.loop(0, 2)
    def _(sub):
        spot = pl.ds(pl.multiple_of(sub * step, step), step)
        value, slope = activate(tok_diag[spot, :], w_in[...], bias[0:1, :])
        act = value.astype(jnp.bfloat16)
        slope_ref[spot, :] = slope
        for shift, ref in enumerate((mine_ref, other_ref)):
            ref[spot, :] = jnp.dot(
                act, w_out[:, half_columns(core, shift, feats)], preferred_element_type=jnp.float32
            ).astype(jnp.bfloat16)


def gradient_kernel(owned, *refs):
    groups = (refs[0:3], refs[3:6])
    early_grad, tok_diag, slope, slope_diag, w_out = refs[6:11]
    diag_refs = refs[11:13]
    own_ref, one_ref, two_ref, three_ref, cot_diag, dpre_diag, cot_sem = refs[13:]
    core = lax.axis_index("core")
    two = 2 * owned
    load = side_by_side(core, diag_refs, cot_diag, 0, cot_sem)
    run(load, "start")
    start, grad = 0, None
    for dpre_two, tok, cot in groups:
        rows = tok.shape[0]
        dact = dot_last(cot[...], w_out[3 * owned :, :])
        last = (dact * slope[pl.ds(start, rows), :]).astype(jnp.bfloat16)
        terms = dot_first(jnp.concatenate([dpre_two[...], last], axis=1), tok[...])
        grad = terms if grad is None else grad + terms
        start += rows
    run(load, "wait")
    dpre_diag[...] = (dot_last(cot_diag[...], w_out[...]) * slope_diag[...]).astype(jnp.bfloat16)
    grad = grad + dot_first(dpre_diag[:, two:], tok_diag[...])
    two_ref[...] = grad[:owned].astype(jnp.bfloat16)
    three_ref[...] = grad[owned:].astype(jnp.bfloat16)
    grad = early_grad[...] + dot_first(dpre_diag[:, :two], tok_diag[...])
    own_ref[...] = grad[:owned].astype(jnp.bfloat16)
    one_ref[...] = grad[owned:].astype(jnp.bfloat16)


def pair_kernel(rows, mine_ref, other_ref, *out_refs):
    for block, ref in enumerate(out_refs):
        spot = pl.ds(block * rows, rows)
        ref[...] = (
            mine_ref[spot, :].astype(jnp.float32) + other_ref[spot, :].astype(jnp.float32)
        ).astype(jnp.bfloat16)


def plane_kernel(own_ref, x_ref, y_ref, out_ref):
    out_ref[...] = (
        own_ref[...].astype(jnp.float32)
        + x_ref[...].astype(jnp.float32)
        + y_ref[...].astype(jnp.float32)
    )


def vmem(count):
    return [pl.BlockSpec(memory_space=pltpu.VMEM)] * count


def anywhere(count):
    return [pl.BlockSpec(memory_space=pl.ANY)] * count


def bf16(*shape):
    return jax.ShapeDtypeStruct(shape, jnp.bfloat16)


def permute(value, there):
    pairs = []
    for f in range(4):
        for y in range(2):
            for x in range(2):
                for c in range(2):
                    to = there(f, y, x, c)
                    here = ((f * 2 + y) * 2 + x) * 2 + c
                    pairs.append((here, ((to[0] * 2 + to[1]) * 2 + to[2]) * 2 + to[3]))
    return lax.ppermute(value, AXES, pairs)


def to_x(value):
    return permute(value, lambda f, y, x, c: (f, y, 1 - x, c))


def to_y(value):
    return permute(value, lambda f, y, x, c: (f, 1 - y, x, c))


def to_diagonal(value):
    return permute(value, lambda f, y, x, c: (f, 1 - y, 1 - x, c))


def to_core(value):
    return permute(value, lambda f, y, x, c: (f, y, x, 1 - c))


def to_far(value, flip):
    return permute(value, lambda f, y, x, c: (f ^ flip, y, x, c))


def on_device_lines(tokens, cotangent, w_in, b_in, w_out):
    rows, feats = tokens.shape
    owned, width = w_in.shape
    units = 4 * owned
    count = NEAR * rows
    scale = 1.0 / math.sqrt(4 * count)
    params = pltpu.CompilerParams(vmem_limit_bytes=VMEM_LIMIT)
    dma = pltpu.SemaphoreType.DMA
    barrier = lax.optimization_barrier
    early_rows = (NEAR - 1) * rows

    def f32(*shape):
        return jax.ShapeDtypeStruct(shape, jnp.float32)

    def cost(flops, traffic):
        return pl.CostEstimate(flops=flops, bytes_accessed=traffic, transcendentals=0)

    bias_rows = jnp.pad(b_in.reshape(1, owned), ((0, 15), (0, width - owned)))
    own_w = jnp.concatenate([w_in, w_out, bias_rows], 0)
    own_w, tokens, cotangent = barrier((own_w, tokens, cotangent))
    own = jnp.stack([tokens, cotangent])
    w_two, w_one = to_far(own_w, 2), to_far(own_w, 1)
    from_x, from_y = to_x(own), to_y(own)
    own_other = to_core(own)
    w_three = to_far(w_two, 1)

    def early_shapes(here):
        return (
            bf16(here, owned),
            bf16(here, owned),
            f32(here, width),
            f32(2 * owned, width),
            bf16(here, width),
            bf16(here, width),
        )

    act_own, dpre_own, mixed_terms_own, grad_terms, tok_own, cot_own, w_in_three, w_out_three, bias = (
        pl.pallas_call(
            functools.partial(own_kernel, owned),
            out_shape=early_shapes(rows)
            + (bf16(3 * owned, width), bf16(3 * owned, width), bf16(16, 3 * owned)),
            in_specs=anywhere(5),
            out_specs=vmem(9),
            scratch_shapes=[
                pltpu.VMEM((rows, 2 * owned), jnp.bfloat16),
                dma((2,)),
                dma((2,)),
                dma((3, 3)),
            ],
            compiler_params=params,
            cost_estimate=cost(OWN_COST, rows),
            name="own",
        )(own, own_other, own_w, w_one, w_two)
    )
    from_x, from_y, grad_terms = barrier((from_x, from_y, grad_terms))
    tok_diag, cot_diag = to_y(from_x[0]), to_x(from_y[1])
    x_other, y_other = to_core(from_x), to_core(from_y)
    act_near, dpre_near, mixed_terms_near, grad_terms, tok_near, cot_near = pl.pallas_call(
        functools.partial(early_kernel, owned),
        out_shape=early_shapes(2 * rows),
        in_specs=anywhere(4) + vmem(4),
        out_specs=vmem(6),
        scratch_shapes=[
            pltpu.VMEM((2 * rows, 2 * owned), jnp.bfloat16),
            dma((2, 2)),
            dma((2, 2)),
        ],
        compiler_params=params,
        cost_estimate=cost(early_rows * units, early_rows),
        name="early",
    )(from_x, x_other, from_y, y_other, w_in_three, w_out_three, bias, grad_terms)
    tok_diag, cot_diag, act_near = barrier((tok_diag, cot_diag, act_near))
    tok_diag_other, cot_diag_other = to_core(tok_diag), to_core(cot_diag)

    mine, other, slope, w_in_all, w_out_all, bias = pl.pallas_call(
        functools.partial(output_kernel, owned),
        out_shape=(
            bf16(early_rows, feats),
            bf16(early_rows, feats),
            f32(early_rows, owned),
            bf16(units, width),
            bf16(units, width),
            bf16(16, units),
        ),
        in_specs=vmem(10),
        out_specs=vmem(6),
        scratch_shapes=[pltpu.VMEM((2 * owned, width), jnp.bfloat16), dma((4,))],
        compiler_params=params,
        cost_estimate=cost(8 * early_rows * units * width, 4 * count * width),
        name="output",
    )(
        act_own, tok_own, mixed_terms_own, act_near, tok_near, mixed_terms_near,
        w_in_three, w_out_three, bias, w_three,
    )
    received = to_core(other)

    tok_diag_other, cot_diag_other, w_in_all = barrier((tok_diag_other, cot_diag_other, w_in_all))
    mine_diag, other_diag, slope_diag, tok_last = pl.pallas_call(
        diagonal_kernel,
        out_shape=(bf16(rows, feats), bf16(rows, feats), f32(rows, units), bf16(rows, width)),
        in_specs=vmem(3) + anywhere(2),
        out_specs=vmem(4),
        scratch_shapes=[dma((2,))],
        compiler_params=params,
        cost_estimate=cost(48 * rows * units * width, 4 * rows * width),
        name="diagonal",
    )(w_in_all, w_out_all, bias, tok_diag, tok_diag_other)
    received_diag = to_core(other_diag)

    mine, slope_diag = barrier((mine, slope_diag))
    sums = pl.pallas_call(
        functools.partial(pair_kernel, rows),
        out_shape=[bf16(rows, feats)] * (NEAR - 1),
        in_specs=vmem(2),
        out_specs=vmem(NEAR - 1),
        compiler_params=params,
        name="pair_sum",
    )(mine, received)
    mixed_x, mixed_y = to_x(sums[1]), to_y(sums[2])
    grad_terms, mixed_own = barrier((grad_terms, sums[0]))

    grad_own, grad_one, grad_two, grad_three = pl.pallas_call(
        functools.partial(gradient_kernel, owned),
        out_shape=[bf16(owned, width)] * 4,
        in_specs=vmem(11) + anywhere(2),
        out_specs=vmem(4),
        scratch_shapes=[
            pltpu.VMEM((rows, width), jnp.bfloat16),
            pltpu.VMEM((rows, units), jnp.bfloat16),
            dma((2,)),
        ],
        compiler_params=params,
        cost_estimate=cost(early_rows * units, early_rows),
        name="gradient",
    )(
        dpre_own, tok_own, cot_own, dpre_near, tok_near, cot_near,
        grad_terms, tok_last, slope, slope_diag, w_out_all, cot_diag, cot_diag_other,
    )
    relayed = to_far(grad_three, 1)
    from_one = to_far(grad_one, 1)

    mine_diag, grad_own = barrier((mine_diag, grad_own))
    (sum_diag,) = pl.pallas_call(
        functools.partial(pair_kernel, rows),
        out_shape=[bf16(rows, feats)],
        in_specs=vmem(2),
        out_specs=vmem(1),
        compiler_params=params,
        name="pair_sum_diagonal",
    )(mine_diag, received_diag)
    mixed_diag = to_diagonal(sum_diag)
    grad_two, _ = barrier((grad_two, sum_diag))
    from_two = to_far(
        (grad_two.astype(jnp.float32) + relayed.astype(jnp.float32)).astype(jnp.bfloat16), 2
    )
    total = (
        grad_own.astype(jnp.float32)
        + from_one.astype(jnp.float32)
        + from_two.astype(jnp.float32)
    )
    mixed = pl.pallas_call(
        plane_kernel,
        out_shape=f32(rows, feats),
        in_specs=vmem(3),
        out_specs=pl.BlockSpec(memory_space=pltpu.VMEM),
        compiler_params=params,
        cost_estimate=cost(PLANE_COST, rows),
        name="plane_sum",
    )(mixed_own, mixed_x, mixed_y)
    mixed = (mixed + mixed_diag.astype(jnp.float32)).astype(jnp.bfloat16)
    return (mixed, total * scale)


def solution(mesh):
    dp, tensor = mesh.shape["dp"], mesh.shape["tensor"]
    far = dp // NEAR
    if tensor == 2 and far == 4:
        fine = Mesh(mesh.devices.reshape(far, 2, 2, tensor), AXES)
        rows, owners, halves = ("far", "y", "x"), AXES, "core"
        body = on_device_lines
    else:
        fine = Mesh(mesh.devices.reshape(far, NEAR, tensor), ("far", "near", "tensor"))
        rows, owners, halves = ("far", "near"), ("far", "near", "tensor"), "tensor"
        body = on_device_any
    in_specs = (P(rows, halves), P(rows, halves), P(owners, None), P(owners), P(owners, None))
    out_specs = (P(rows, halves), P(owners, None))
    return jax.shard_map(
        body, mesh=fine, in_specs=in_specs, out_specs=out_specs, check_vma=False
    )
```

```python
import functools
import math

import jax
import jax.numpy as jnp
from jax import lax
from jax.experimental import pallas as pl
from jax.experimental.pallas import tpu as pltpu
from jax.sharding import Mesh, PartitionSpec as P

NEAR = 4
AXES = ("far", "y", "x", "core")
CONTRACT_LAST = (((1,), (1,)), ((), ()))
CONTRACT_FIRST = (((0,), (0,)), ((), ()))
VMEM_LIMIT = 28 * 1024 * 1024
PLANE_COST = 10**10
EXTRA = 48


def gelu_parts(value):
    coeff = 0.7978845608
    inner = coeff * (value + 0.044715 * value * value * value)
    tangent = jnp.tanh(inner)
    result = 0.5 * value * (1.0 + tangent)
    slope = 0.5 * (1.0 + tangent) + 0.5 * value * (1.0 - tangent * tangent) * coeff * (
        1.0 + 3.0 * 0.044715 * value * value
    )
    return (result, slope)


def on_device_any(tokens, cotangent, w_in, b_in, w_out):
    far, near, tensor = lax.axis_size("far"), lax.axis_size("near"), lax.axis_size("tensor")
    rows, feats = tokens.shape
    owned, width = w_in.shape
    scale = 1.0 / math.sqrt(rows * far * near)
    bias_rows = jnp.pad(b_in.reshape(1, owned), ((0, 15), (0, width - owned)))
    weights = lax.all_gather(jnp.concatenate([w_in, w_out, bias_rows], 0), "far", axis=0)
    in_rows = weights[:, :owned].reshape(far * owned, width)
    proj_rows = weights[:, owned : 2 * owned].reshape(far * owned, width)
    bias = weights[:, 2 * owned, :owned].reshape(far * owned).astype(jnp.float32)
    tok = lax.all_gather(tokens, ("near", "tensor"), axis=0).reshape(near, tensor, rows, feats)
    cot = lax.all_gather(cotangent, ("near", "tensor"), axis=0).reshape(near, tensor, rows, feats)
    tok_full = tok.transpose(0, 2, 1, 3).reshape(near * rows, width)
    cot_full = cot.transpose(0, 2, 1, 3).reshape(near * rows, width)
    pre = lax.dot_general(
        tok_full, in_rows, CONTRACT_LAST, preferred_element_type=jnp.float32
    ) + bias
    act_value, slope = gelu_parts(pre)
    act = act_value.astype(jnp.bfloat16)
    term = jnp.dot(act, proj_rows, preferred_element_type=jnp.float32).astype(jnp.bfloat16)
    term = term.reshape(near, rows, tensor, feats).transpose(0, 2, 1, 3)
    mixed = lax.psum_scatter(
        term.reshape(near * tensor, rows, feats), ("near", "tensor"), scatter_dimension=0
    )
    dact = lax.dot_general(cot_full, proj_rows, CONTRACT_LAST, preferred_element_type=jnp.float32)
    dpre = (dact * slope).astype(jnp.bfloat16)
    grad = lax.dot_general(dpre, tok_full, CONTRACT_FIRST, preferred_element_type=jnp.float32)
    grad_sum = lax.psum_scatter(grad.astype(jnp.bfloat16), "far", scatter_dimension=0, tiled=True)
    return (mixed, grad_sum.astype(jnp.float32) * scale)


def half_columns(core, shift, feats):
    return pl.ds(pl.multiple_of(lax.rem(core + shift, 2) * feats, feats), feats)


def side_by_side(core, pair, whole, start, sem):
    rows, feats = pair[0].shape
    return [
        pltpu.make_async_copy(
            pair[shift],
            whole.at[pl.ds(start, rows), half_columns(core, shift, feats)],
            sem.at[shift],
        )
        for shift in range(2)
    ]


def weight_copies(refs, owned, w_in, w_out, bias, sem):
    ins, outs = [], []
    for at, ref in enumerate(refs):
        spot = pl.ds(at * owned, owned)
        ins.append(pltpu.make_async_copy(ref.at[pl.ds(0, owned)], w_in.at[spot], sem.at[0, at]))
        ins.append(
            pltpu.make_async_copy(
                ref.at[pl.ds(2 * owned, 16), pl.ds(0, owned)], bias.at[:, spot], sem.at[1, at]
            )
        )
        outs.append(
            pltpu.make_async_copy(ref.at[pl.ds(owned, owned)], w_out.at[spot], sem.at[2, at])
        )
    return ins, outs


def run(copies, what):
    for copy in copies:
        getattr(copy, what)()


def activate(tok, w_in, bias):
    pre = lax.dot_general(
        tok, w_in, CONTRACT_LAST, preferred_element_type=jnp.float32
    ) + bias.astype(jnp.float32)
    return gelu_parts(pre)


def dot_last(left, right):
    return lax.dot_general(left, right, CONTRACT_LAST, preferred_element_type=jnp.float32)


def dot_first(left, right):
    return lax.dot_general(left, right, CONTRACT_FIRST, preferred_element_type=jnp.float32)


def early_block(start, step, tok, cot, w_in, w_out, bias, two, act_ref, dpre_ref, mixed_ref, dpre):
    @pl.loop(0, 2)
    def _(sub):
        spot = pl.ds(pl.multiple_of(start + sub * step, step), step)
        value, slope = activate(tok[spot, :], w_in[...], bias[0:1, :])
        act = value.astype(jnp.bfloat16)
        act_ref[spot, :] = act[:, two:]
        dact = dot_last(cot[spot, :], w_out[...])
        terms = (dact * slope).astype(jnp.bfloat16)
        dpre[spot, :] = terms[:, :two]
        dpre_ref[spot, :] = terms[:, two:]
        mixed_ref[spot, :] = jnp.dot(
            act[:, :two], w_out[:two, :], preferred_element_type=jnp.float32
        )


def early_kernel(owned, *refs):
    pair_refs, w_refs = refs[:6], refs[6:9]
    act_ref, dpre_ref, mixed_ref, grad_ref, tok, cot, w_in, w_out, bias = refs[9:18]
    dpre, tok_sem, cot_sem, w_sem = refs[18:]
    core = lax.axis_index("core")
    rows = pair_refs[0].shape[1]
    ins, outs = weight_copies(w_refs, owned, w_in, w_out, bias, w_sem)
    loads = []
    for block in range(NEAR - 1):
        first, second = pair_refs[2 * block], pair_refs[2 * block + 1]
        loads.append(
            side_by_side(core, (first.at[0], second.at[0]), tok, block * rows, tok_sem.at[block])
            + side_by_side(core, (first.at[1], second.at[1]), cot, block * rows, cot_sem.at[block])
        )
    run(ins + outs, "start")
    for load in loads:
        run(load, "start")
    run(ins + outs, "wait")
    for block, load in enumerate(loads):
        run(load, "wait")
        early_block(
            block * rows, rows // 2, tok, cot, w_in, w_out, bias, 2 * owned,
            act_ref, dpre_ref, mixed_ref, dpre,
        )
    grad_ref[...] = dot_first(dpre[...], tok[...])


def output_kernel(owned, *refs):
    act_two, tok, early_mixed, w_in, w_out, bias, w_three = refs[:7]
    mine_ref, other_ref, slope_ref, w_in_all, w_out_all, bias_all = refs[7:13]
    w_last, sem = refs[13:]
    core = lax.axis_index("core")
    feats = mine_ref.shape[1]
    two, three = 2 * owned, 3 * owned
    first, last = pl.ds(0, three), pl.ds(three, owned)
    copies = [
        pltpu.make_async_copy(w_in, w_in_all.at[first], sem.at[0]),
        pltpu.make_async_copy(w_three.at[pl.ds(0, owned)], w_in_all.at[last], sem.at[1]),
        pltpu.make_async_copy(w_out, w_out_all.at[first], sem.at[2]),
        pltpu.make_async_copy(w_three.at[pl.ds(owned, owned)], w_out_all.at[last], sem.at[3]),
    ]
    run(copies, "start")
    bias_last = w_three[two : two + 16, :owned]
    bias_all[:, :three] = bias[...]
    bias_all[:, three:] = bias_last
    w_last[:owned, :] = w_out[two:, :]
    w_last[owned:, :] = w_three[owned:two, :]
    step = tok.shape[0] // 6

    @pl.loop(0, 6)
    def _(sub):
        spot = pl.ds(pl.multiple_of(sub * step, step), step)
        value, slope = activate(tok[spot, :], w_three[:owned, :], bias_last[0:1, :])
        slope_ref[spot, :] = slope
        act = jnp.concatenate([act_two[spot, :], value.astype(jnp.bfloat16)], axis=1)
        for shift, ref in enumerate((mine_ref, other_ref)):
            half = half_columns(core, shift, feats)
            ref[spot, :] = (
                early_mixed[spot, half]
                + jnp.dot(act, w_last[:, half], preferred_element_type=jnp.float32)
            ).astype(jnp.bfloat16)

    run(copies, "wait")


def diagonal_kernel(*refs):
    w_in, w_out, bias = refs[:3]
    mine_ref, other_ref, slope_ref, tok_diag, tok_sem = refs[5:]
    core = lax.axis_index("core")
    rows, feats = mine_ref.shape
    diag_refs = [ref.at[pl.ds(0, rows)] for ref in refs[3:5]]
    load = side_by_side(core, diag_refs, tok_diag, 0, tok_sem)
    run(load, "start")
    run(load, "wait")
    step = rows // 2

    @pl.loop(0, 2)
    def _(sub):
        spot = pl.ds(pl.multiple_of(sub * step, step), step)
        value, slope = activate(tok_diag[spot, :], w_in[...], bias[0:1, :])
        act = value.astype(jnp.bfloat16)
        slope_ref[spot, :] = slope
        for shift, ref in enumerate((mine_ref, other_ref)):
            ref[spot, :] = jnp.dot(
                act, w_out[:, half_columns(core, shift, feats)], preferred_element_type=jnp.float32
            ).astype(jnp.bfloat16)


def gradient_kernel(owned, *refs):
    dpre_two, tok, cot, early_grad, tok_diag, slope, slope_diag, w_out = refs[:8]
    own_ref, one_ref, two_ref, three_ref, cot_diag, dpre_diag, cot_sem = refs[10:]
    diag_refs = [ref.at[pl.ds(EXTRA, cot_diag.shape[0])] for ref in refs[8:10]]
    core = lax.axis_index("core")
    two = 2 * owned
    load = side_by_side(core, diag_refs, cot_diag, 0, cot_sem)
    run(load, "start")
    dact = dot_last(cot[...], w_out[3 * owned :, :])
    last = (dact * slope[...]).astype(jnp.bfloat16)
    grad = dot_first(jnp.concatenate([dpre_two[...], last], axis=1), tok[...])
    run(load, "wait")
    dpre_diag[...] = (dot_last(cot_diag[...], w_out[...]) * slope_diag[...]).astype(jnp.bfloat16)
    grad = grad + dot_first(dpre_diag[:, two:], tok_diag[...])
    two_ref[...] = grad[:owned].astype(jnp.bfloat16)
    three_ref[...] = grad[owned:].astype(jnp.bfloat16)
    grad = early_grad[...] + dot_first(dpre_diag[:, :two], tok_diag[...])
    own_ref[...] = grad[:owned].astype(jnp.bfloat16)
    one_ref[...] = grad[owned:].astype(jnp.bfloat16)


def pair_kernel(rows, mine_ref, other_ref, *out_refs):
    for block, ref in enumerate(out_refs):
        spot = pl.ds(block * rows, rows)
        ref[...] = (
            mine_ref[spot, :].astype(jnp.float32) + other_ref[spot, :].astype(jnp.float32)
        ).astype(jnp.bfloat16)


def plane_kernel(own_ref, x_ref, y_ref, out_ref):
    out_ref[...] = (
        own_ref[...].astype(jnp.float32)
        + x_ref[...].astype(jnp.float32)
        + y_ref[...].astype(jnp.float32)
    )


def vmem(count):
    return [pl.BlockSpec(memory_space=pltpu.VMEM)] * count


def anywhere(count):
    return [pl.BlockSpec(memory_space=pl.ANY)] * count


def bf16(*shape):
    return jax.ShapeDtypeStruct(shape, jnp.bfloat16)


def permute(value, there):
    pairs = []
    for f in range(4):
        for y in range(2):
            for x in range(2):
                for c in range(2):
                    to = there(f, y, x, c)
                    here = ((f * 2 + y) * 2 + x) * 2 + c
                    pairs.append((here, ((to[0] * 2 + to[1]) * 2 + to[2]) * 2 + to[3]))
    return lax.ppermute(value, AXES, pairs)


def to_x(value):
    return permute(value, lambda f, y, x, c: (f, y, 1 - x, c))


def to_y(value):
    return permute(value, lambda f, y, x, c: (f, 1 - y, x, c))


def to_diagonal(value):
    return permute(value, lambda f, y, x, c: (f, 1 - y, 1 - x, c))


def to_core(value):
    return permute(value, lambda f, y, x, c: (f, y, x, 1 - c))


def to_far(value, flip):
    return permute(value, lambda f, y, x, c: (f ^ flip, y, x, c))


def on_device_lines(tokens, cotangent, w_in, b_in, w_out):
    rows, feats = tokens.shape
    owned, width = w_in.shape
    units = 4 * owned
    count = NEAR * rows
    scale = 1.0 / math.sqrt(4 * count)
    params = pltpu.CompilerParams(vmem_limit_bytes=VMEM_LIMIT)
    dma = pltpu.SemaphoreType.DMA
    barrier = lax.optimization_barrier
    early_rows = (NEAR - 1) * rows

    def f32(*shape):
        return jax.ShapeDtypeStruct(shape, jnp.float32)

    def cost(flops, traffic):
        return pl.CostEstimate(flops=flops, bytes_accessed=traffic, transcendentals=0)

    bias_rows = jnp.pad(b_in.reshape(1, owned), ((0, 15), (0, width - owned)))
    own_w = jnp.concatenate([w_in, w_out, bias_rows], 0)
    own_w, tokens, cotangent = barrier((own_w, tokens, cotangent))
    own = jnp.stack([tokens, cotangent])
    w_two, w_one = to_far(own_w, 2), to_far(own_w, 1)
    from_x, from_y = to_x(own), to_y(own)
    own_other = to_core(own)
    from_x, from_y, own_other, w_one = barrier((from_x, from_y, own_other, w_one))
    tok_diag = to_y(from_x.reshape(2 * rows, feats)[: rows + EXTRA])
    cot_diag = to_x(from_y.reshape(2 * rows, feats)[rows - EXTRA :])
    x_other, y_other = to_core(from_x), to_core(from_y)
    w_three = to_far(w_two, 1)
    act_two, dpre_two, mixed_terms, grad_terms, tok, cot, w_in_three, w_out_three, bias = (
        pl.pallas_call(
            functools.partial(early_kernel, owned),
            out_shape=(
                bf16(early_rows, owned),
                bf16(early_rows, owned),
                f32(early_rows, width),
                f32(2 * owned, width),
                bf16(early_rows, width),
                bf16(early_rows, width),
                bf16(3 * owned, width),
                bf16(3 * owned, width),
                bf16(16, 3 * owned),
            ),
            in_specs=anywhere(9),
            out_specs=vmem(9),
            scratch_shapes=[
                pltpu.VMEM((early_rows, 2 * owned), jnp.bfloat16),
                dma((NEAR - 1, 2)),
                dma((NEAR - 1, 2)),
                dma((3, 3)),
            ],
            compiler_params=params,
            cost_estimate=cost(early_rows * units, early_rows),
            name="early",
        )(own, own_other, from_x, x_other, from_y, y_other, own_w, w_one, w_two)
    )
    tok_diag, cot_diag, act_two = barrier((tok_diag, cot_diag, act_two))
    tok_diag_other, cot_diag_other = to_core(tok_diag), to_core(cot_diag)

    mine, other, slope, w_in_all, w_out_all, bias = pl.pallas_call(
        functools.partial(output_kernel, owned),
        out_shape=(
            bf16(early_rows, feats),
            bf16(early_rows, feats),
            f32(early_rows, owned),
            bf16(units, width),
            bf16(units, width),
            bf16(16, units),
        ),
        in_specs=vmem(7),
        out_specs=vmem(6),
        scratch_shapes=[pltpu.VMEM((2 * owned, width), jnp.bfloat16), dma((4,))],
        compiler_params=params,
        cost_estimate=cost(8 * early_rows * units * width, 4 * count * width),
        name="output",
    )(act_two, tok, mixed_terms, w_in_three, w_out_three, bias, w_three)
    received = to_core(other)

    tok_diag_other, cot_diag_other, w_in_all = barrier((tok_diag_other, cot_diag_other, w_in_all))
    mine_diag, other_diag, slope_diag, tok_last = pl.pallas_call(
        diagonal_kernel,
        out_shape=(bf16(rows, feats), bf16(rows, feats), f32(rows, units), bf16(rows, width)),
        in_specs=vmem(3) + anywhere(2),
        out_specs=vmem(4),
        scratch_shapes=[dma((2,))],
        compiler_params=params,
        cost_estimate=cost(48 * rows * units * width, 4 * rows * width),
        name="diagonal",
    )(w_in_all, w_out_all, bias, tok_diag, tok_diag_other)
    received_diag = to_core(other_diag)

    mine, slope_diag = barrier((mine, slope_diag))
    sums = pl.pallas_call(
        functools.partial(pair_kernel, rows),
        out_shape=[bf16(rows, feats)] * (NEAR - 1),
        in_specs=vmem(2),
        out_specs=vmem(NEAR - 1),
        compiler_params=params,
        name="pair_sum",
    )(mine, received)
    mixed_x, mixed_y = to_x(sums[1]), to_y(sums[2])
    grad_terms, mixed_own = barrier((grad_terms, sums[0]))

    grad_own, grad_one, grad_two, grad_three = pl.pallas_call(
        functools.partial(gradient_kernel, owned),
        out_shape=[bf16(owned, width)] * 4,
        in_specs=vmem(8) + anywhere(2),
        out_specs=vmem(4),
        scratch_shapes=[
            pltpu.VMEM((rows, width), jnp.bfloat16),
            pltpu.VMEM((rows, units), jnp.bfloat16),
            dma((2,)),
        ],
        compiler_params=params,
        cost_estimate=cost(early_rows * units, early_rows),
        name="gradient",
    )(
        dpre_two, tok, cot, grad_terms, tok_last, slope, slope_diag, w_out_all,
        cot_diag, cot_diag_other,
    )
    relayed = to_far(grad_three, 1)
    from_one = to_far(grad_one, 1)

    mine_diag, grad_own = barrier((mine_diag, grad_own))
    (sum_diag,) = pl.pallas_call(
        functools.partial(pair_kernel, rows),
        out_shape=[bf16(rows, feats)],
        in_specs=vmem(2),
        out_specs=vmem(1),
        compiler_params=params,
        name="pair_sum_diagonal",
    )(mine_diag, received_diag)
    mixed_diag = to_diagonal(sum_diag)
    grad_two, _ = barrier((grad_two, sum_diag))
    from_two = to_far(
        (grad_two.astype(jnp.float32) + relayed.astype(jnp.float32)).astype(jnp.bfloat16), 2
    )
    total = (
        grad_own.astype(jnp.float32)
        + from_one.astype(jnp.float32)
        + from_two.astype(jnp.float32)
    )
    mixed = pl.pallas_call(
        plane_kernel,
        out_shape=f32(rows, feats),
        in_specs=vmem(3),
        out_specs=pl.BlockSpec(memory_space=pltpu.VMEM),
        compiler_params=params,
        cost_estimate=cost(PLANE_COST, rows),
        name="plane_sum",
    )(mixed_own, mixed_x, mixed_y)
    mixed = (mixed + mixed_diag.astype(jnp.float32)).astype(jnp.bfloat16)
    return (mixed, total * scale)


def solution(mesh):
    dp, tensor = mesh.shape["dp"], mesh.shape["tensor"]
    far = dp // NEAR
    if tensor == 2 and far == 4:
        fine = Mesh(mesh.devices.reshape(far, 2, 2, tensor), AXES)
        rows, owners, halves = ("far", "y", "x"), AXES, "core"
        body = on_device_lines
    else:
        fine = Mesh(mesh.devices.reshape(far, NEAR, tensor), ("far", "near", "tensor"))
        rows, owners, halves = ("far", "near"), ("far", "near", "tensor"), "tensor"
        body = on_device_any
    in_specs = (P(rows, halves), P(rows, halves), P(owners, None), P(owners), P(owners, None))
    out_specs = (P(rows, halves), P(owners, None))
    return jax.shard_map(
        body, mesh=fine, in_specs=in_specs, out_specs=out_specs, check_vma=False
    )
```

```python
import functools
import math

import jax
import jax.numpy as jnp
from jax import lax
from jax.experimental import pallas as pl
from jax.experimental.pallas import tpu as pltpu
from jax.sharding import Mesh, PartitionSpec as P

NEAR = 4
AXES = ("far", "y", "x", "core")
CONTRACT_LAST = (((1,), (1,)), ((), ()))
CONTRACT_FIRST = (((0,), (0,)), ((), ()))
VMEM_LIMIT = 28 * 1024 * 1024
PLANE_COST = 10**10
GRADIENT_COST = 10**10
DIAGONAL_COST = 10**6
EXTRA = 48
MORE = 16


def gelu_parts(value):
    coeff = 0.7978845608
    inner = coeff * (value + 0.044715 * value * value * value)
    tangent = jnp.tanh(inner)
    result = 0.5 * value * (1.0 + tangent)
    slope = 0.5 * (1.0 + tangent) + 0.5 * value * (1.0 - tangent * tangent) * coeff * (
        1.0 + 3.0 * 0.044715 * value * value
    )
    return (result, slope)


def on_device_any(tokens, cotangent, w_in, b_in, w_out):
    far, near, tensor = lax.axis_size("far"), lax.axis_size("near"), lax.axis_size("tensor")
    rows, feats = tokens.shape
    owned, width = w_in.shape
    scale = 1.0 / math.sqrt(rows * far * near)
    bias_rows = jnp.pad(b_in.reshape(1, owned), ((0, 15), (0, width - owned)))
    weights = lax.all_gather(jnp.concatenate([w_in, w_out, bias_rows], 0), "far", axis=0)
    in_rows = weights[:, :owned].reshape(far * owned, width)
    proj_rows = weights[:, owned : 2 * owned].reshape(far * owned, width)
    bias = weights[:, 2 * owned, :owned].reshape(far * owned).astype(jnp.float32)
    tok = lax.all_gather(tokens, ("near", "tensor"), axis=0).reshape(near, tensor, rows, feats)
    cot = lax.all_gather(cotangent, ("near", "tensor"), axis=0).reshape(near, tensor, rows, feats)
    tok_full = tok.transpose(0, 2, 1, 3).reshape(near * rows, width)
    cot_full = cot.transpose(0, 2, 1, 3).reshape(near * rows, width)
    pre = lax.dot_general(
        tok_full, in_rows, CONTRACT_LAST, preferred_element_type=jnp.float32
    ) + bias
    act_value, slope = gelu_parts(pre)
    act = act_value.astype(jnp.bfloat16)
    term = jnp.dot(act, proj_rows, preferred_element_type=jnp.float32).astype(jnp.bfloat16)
    term = term.reshape(near, rows, tensor, feats).transpose(0, 2, 1, 3)
    mixed = lax.psum_scatter(
        term.reshape(near * tensor, rows, feats), ("near", "tensor"), scatter_dimension=0
    )
    dact = lax.dot_general(cot_full, proj_rows, CONTRACT_LAST, preferred_element_type=jnp.float32)
    dpre = (dact * slope).astype(jnp.bfloat16)
    grad = lax.dot_general(dpre, tok_full, CONTRACT_FIRST, preferred_element_type=jnp.float32)
    grad_sum = lax.psum_scatter(grad.astype(jnp.bfloat16), "far", scatter_dimension=0, tiled=True)
    return (mixed, grad_sum.astype(jnp.float32) * scale)


def half_columns(core, shift, feats):
    return pl.ds(pl.multiple_of(lax.rem(core + shift, 2) * feats, feats), feats)


def side_by_side(core, pair, whole, start, sem):
    rows, feats = pair[0].shape
    return [
        pltpu.make_async_copy(
            pair[shift],
            whole.at[pl.ds(start, rows), half_columns(core, shift, feats)],
            sem.at[shift],
        )
        for shift in range(2)
    ]


def weight_copies(refs, owned, w_in, w_out, bias, sem):
    ins, outs = [], []
    for at, ref in enumerate(refs):
        spot = pl.ds(at * owned, owned)
        ins.append(pltpu.make_async_copy(ref.at[pl.ds(0, owned)], w_in.at[spot], sem.at[0, at]))
        ins.append(
            pltpu.make_async_copy(
                ref.at[pl.ds(2 * owned, 16), pl.ds(0, owned)], bias.at[:, spot], sem.at[1, at]
            )
        )
        outs.append(
            pltpu.make_async_copy(ref.at[pl.ds(owned, owned)], w_out.at[spot], sem.at[2, at])
        )
    return ins, outs


def run(copies, what):
    for copy in copies:
        getattr(copy, what)()


def activate(tok, w_in, bias):
    pre = lax.dot_general(
        tok, w_in, CONTRACT_LAST, preferred_element_type=jnp.float32
    ) + bias.astype(jnp.float32)
    return gelu_parts(pre)


def dot_last(left, right):
    return lax.dot_general(left, right, CONTRACT_LAST, preferred_element_type=jnp.float32)


def dot_first(left, right):
    return lax.dot_general(left, right, CONTRACT_FIRST, preferred_element_type=jnp.float32)


def early_block(start, step, tok, cot, w_in, w_out, bias, two, act_ref, dpre_ref, mixed_ref, dpre):
    @pl.loop(0, 2)
    def _(sub):
        spot = pl.ds(pl.multiple_of(start + sub * step, step), step)
        value, slope = activate(tok[spot, :], w_in[...], bias[0:1, :])
        act = value.astype(jnp.bfloat16)
        act_ref[spot, :] = act[:, two:]
        dact = dot_last(cot[spot, :], w_out[...])
        terms = (dact * slope).astype(jnp.bfloat16)
        dpre[spot, :] = terms[:, :two]
        dpre_ref[spot, :] = terms[:, two:]
        mixed_ref[spot, :] = jnp.dot(
            act[:, :two], w_out[:two, :], preferred_element_type=jnp.float32
        )


def early_kernel(owned, *refs):
    pair_refs, w_refs = refs[:6], refs[6:9]
    act_ref, dpre_ref, mixed_ref, grad_ref, tok, cot, w_in, w_out, bias = refs[9:18]
    dpre, tok_sem, cot_sem, w_sem = refs[18:]
    core = lax.axis_index("core")
    rows = pair_refs[0].shape[1]
    ins, outs = weight_copies(w_refs, owned, w_in, w_out, bias, w_sem)
    loads = []
    for block in range(NEAR - 1):
        first, second = pair_refs[2 * block], pair_refs[2 * block + 1]
        loads.append(
            side_by_side(core, (first.at[0], second.at[0]), tok, block * rows, tok_sem.at[block])
            + side_by_side(core, (first.at[1], second.at[1]), cot, block * rows, cot_sem.at[block])
        )
    run(ins + outs, "start")
    for load in loads:
        run(load, "start")
    run(ins + outs, "wait")
    for block, load in enumerate(loads):
        run(load, "wait")
        early_block(
            block * rows, rows // 2, tok, cot, w_in, w_out, bias, 2 * owned,
            act_ref, dpre_ref, mixed_ref, dpre,
        )
    grad_ref[...] = dot_first(dpre[...], tok[...])


def output_kernel(owned, *refs):
    act_two, tok, early_mixed, w_in, w_out, bias, w_three = refs[:7]
    mine_ref, other_ref, slope_ref, w_in_all, w_out_all, bias_all = refs[7:13]
    w_last, sem = refs[13:]
    core = lax.axis_index("core")
    feats = mine_ref.shape[1]
    two, three = 2 * owned, 3 * owned
    first, last = pl.ds(0, three), pl.ds(three, owned)
    copies = [
        pltpu.make_async_copy(w_in, w_in_all.at[first], sem.at[0]),
        pltpu.make_async_copy(w_three.at[pl.ds(0, owned)], w_in_all.at[last], sem.at[1]),
        pltpu.make_async_copy(w_out, w_out_all.at[first], sem.at[2]),
        pltpu.make_async_copy(w_three.at[pl.ds(owned, owned)], w_out_all.at[last], sem.at[3]),
    ]
    run(copies, "start")
    bias_last = w_three[two : two + 16, :owned]
    bias_all[:, :three] = bias[...]
    bias_all[:, three:] = bias_last
    w_last[:owned, :] = w_out[two:, :]
    w_last[owned:, :] = w_three[owned:two, :]
    step = tok.shape[0] // 3

    @pl.loop(0, 3)
    def _(block):
        spot = pl.ds(pl.multiple_of(block * step, step), step)
        value, slope = activate(tok[spot, :], w_three[:owned, :], bias_last[0:1, :])
        slope_ref[spot, :] = slope
        act = jnp.concatenate([act_two[spot, :], value.astype(jnp.bfloat16)], axis=1)
        for shift, ref in enumerate((mine_ref, other_ref)):
            half = half_columns(core, shift, feats)
            ref[spot, :] = (
                early_mixed[spot, half]
                + jnp.dot(act, w_last[:, half], preferred_element_type=jnp.float32)
            ).astype(jnp.bfloat16)

    run(copies, "wait")


def gradient_kernel(dpre_two, tok, cot, slope, w_three, grad_ref, dpre):
    owned = slope.shape[1]
    step = tok.shape[0] // 3

    @pl.loop(0, 3)
    def _(block):
        spot = pl.ds(pl.multiple_of(block * step, step), step)
        dact = dot_last(cot[spot, :], w_three[owned : 2 * owned, :])
        last = (dact * slope[spot, :]).astype(jnp.bfloat16)
        dpre[spot, :] = jnp.concatenate([dpre_two[spot, :], last], axis=1)

    grad_ref[...] = dot_first(dpre[...], tok[...])


def diagonal_kernel(owned, *refs):
    w_in, w_out, bias, grad_first, grad_last = refs[:5]
    mine_ref, other_ref, own_ref, one_ref, two_ref, three_ref = refs[9:15]
    tok, cot, dpre, tok_sem, cot_sem = refs[15:]
    core = lax.axis_index("core")
    rows, feats = mine_ref.shape
    two = 2 * owned
    load = side_by_side(core, [ref.at[pl.ds(0, rows)] for ref in refs[5:7]], tok, 0, tok_sem)
    load += side_by_side(core, [ref.at[pl.ds(EXTRA, rows)] for ref in refs[7:9]], cot, 0, cot_sem)
    run(load, "start")
    run(load, "wait")
    step = rows // 2

    @pl.loop(0, 2)
    def _(sub):
        spot = pl.ds(pl.multiple_of(sub * step, step), step)
        value, slope = activate(tok[spot, :], w_in[...], bias[0:1, :])
        act = value.astype(jnp.bfloat16)
        dact = dot_last(cot[spot, :], w_out[...])
        dpre[spot, :] = (dact * slope).astype(jnp.bfloat16)
        for shift, ref in enumerate((mine_ref, other_ref)):
            ref[spot, :] = jnp.dot(
                act, w_out[:, half_columns(core, shift, feats)], preferred_element_type=jnp.float32
            ).astype(jnp.bfloat16)

    grad = grad_last[...] + dot_first(dpre[:, two:], tok[...])
    two_ref[...] = grad[:owned].astype(jnp.bfloat16)
    three_ref[...] = grad[owned:].astype(jnp.bfloat16)
    grad = grad_first[...] + dot_first(dpre[:, :two], tok[...])
    own_ref[...] = grad[:owned].astype(jnp.bfloat16)
    one_ref[...] = grad[owned:].astype(jnp.bfloat16)


def pair_kernel(rows, mine_ref, other_ref, *out_refs):
    for block, ref in enumerate(out_refs):
        spot = pl.ds(block * rows, rows)
        ref[:rows, :] = (
            mine_ref[spot, :].astype(jnp.float32) + other_ref[spot, :].astype(jnp.float32)
        ).astype(jnp.bfloat16)
        if ref.shape[0] > rows:
            ref[rows:, :] = jnp.zeros_like(ref[rows:, :])


def plane_kernel(own_ref, x_ref, y_ref, out_ref):
    rows = own_ref.shape[0]
    out_ref[...] = (
        own_ref[...].astype(jnp.float32)
        + x_ref[:rows, :].astype(jnp.float32)
        + y_ref[:rows, :].astype(jnp.float32)
    )


def vmem(count):
    return [pl.BlockSpec(memory_space=pltpu.VMEM)] * count


def anywhere(count):
    return [pl.BlockSpec(memory_space=pl.ANY)] * count


def bf16(*shape):
    return jax.ShapeDtypeStruct(shape, jnp.bfloat16)


def permute(value, there):
    pairs = []
    for f in range(4):
        for y in range(2):
            for x in range(2):
                for c in range(2):
                    to = there(f, y, x, c)
                    here = ((f * 2 + y) * 2 + x) * 2 + c
                    pairs.append((here, ((to[0] * 2 + to[1]) * 2 + to[2]) * 2 + to[3]))
    return lax.ppermute(value, AXES, pairs)


def to_x(value):
    return permute(value, lambda f, y, x, c: (f, y, 1 - x, c))


def to_y(value):
    return permute(value, lambda f, y, x, c: (f, 1 - y, x, c))


def to_diagonal(value):
    return permute(value, lambda f, y, x, c: (f, 1 - y, 1 - x, c))


def to_core(value):
    return permute(value, lambda f, y, x, c: (f, y, x, 1 - c))


def to_far(value, flip):
    return permute(value, lambda f, y, x, c: (f ^ flip, y, x, c))


def on_device_lines(tokens, cotangent, w_in, b_in, w_out):
    rows, feats = tokens.shape
    owned, width = w_in.shape
    units = 4 * owned
    count = NEAR * rows
    scale = 1.0 / math.sqrt(4 * count)
    params = pltpu.CompilerParams(vmem_limit_bytes=VMEM_LIMIT)
    dma = pltpu.SemaphoreType.DMA
    barrier = lax.optimization_barrier
    early_rows = (NEAR - 1) * rows

    def f32(*shape):
        return jax.ShapeDtypeStruct(shape, jnp.float32)

    def cost(flops, traffic):
        return pl.CostEstimate(flops=flops, bytes_accessed=traffic, transcendentals=0)

    bias_rows = jnp.pad(b_in.reshape(1, owned), ((0, 15), (0, width - owned)))
    own_w = jnp.concatenate([w_in, w_out, bias_rows], 0)
    own_w, tokens, cotangent = barrier((own_w, tokens, cotangent))
    own = jnp.stack([tokens, cotangent])
    w_two, w_one = to_far(own_w, 2), to_far(own_w, 1)
    from_x, from_y = to_x(own), to_y(own)
    own_other = to_core(own)
    from_x, from_y, own_other = barrier((from_x, from_y, own_other))
    tok_diag = to_y(from_x.reshape(2 * rows, feats)[: rows + EXTRA])
    cot_diag = to_x(from_y.reshape(2 * rows, feats)[rows - EXTRA :])
    x_other, y_other = to_core(from_x), to_core(from_y)
    w_three = to_far(w_two, 1)
    act_two, dpre_two, mixed_terms, grad_terms, tok, cot, w_in_three, w_out_three, bias = (
        pl.pallas_call(
            functools.partial(early_kernel, owned),
            out_shape=(
                bf16(early_rows, owned),
                bf16(early_rows, owned),
                f32(early_rows, width),
                f32(2 * owned, width),
                bf16(early_rows, width),
                bf16(early_rows, width),
                bf16(3 * owned, width),
                bf16(3 * owned, width),
                bf16(16, 3 * owned),
            ),
            in_specs=anywhere(9),
            out_specs=vmem(9),
            scratch_shapes=[
                pltpu.VMEM((early_rows, 2 * owned), jnp.bfloat16),
                dma((NEAR - 1, 2)),
                dma((NEAR - 1, 2)),
                dma((3, 3)),
            ],
            compiler_params=params,
            cost_estimate=cost(early_rows * units, early_rows),
            name="early",
        )(own, own_other, from_x, x_other, from_y, y_other, own_w, w_one, w_two)
    )

    mine, other, slope, w_in_all, w_out_all, bias = pl.pallas_call(
        functools.partial(output_kernel, owned),
        out_shape=(
            bf16(early_rows, feats),
            bf16(early_rows, feats),
            f32(early_rows, owned),
            bf16(units, width),
            bf16(units, width),
            bf16(16, units),
        ),
        in_specs=vmem(7),
        out_specs=vmem(6),
        scratch_shapes=[pltpu.VMEM((2 * owned, width), jnp.bfloat16), dma((4,))],
        compiler_params=params,
        cost_estimate=cost(early_rows * units, early_rows),
        name="output",
    )(act_two, tok, mixed_terms, w_in_three, w_out_three, bias, w_three)
    tok_diag, cot_diag, other = barrier((tok_diag, cot_diag, other))
    received = to_core(other)
    tok_diag_other, cot_diag_other = to_core(tok_diag), to_core(cot_diag)
    slope, tok_diag = barrier((slope, tok_diag))
    grad_last = pl.pallas_call(
        gradient_kernel,
        out_shape=f32(2 * owned, width),
        in_specs=vmem(5),
        out_specs=pl.BlockSpec(memory_space=pltpu.VMEM),
        scratch_shapes=[pltpu.VMEM((early_rows, 2 * owned), jnp.bfloat16)],
        compiler_params=params,
        cost_estimate=cost(GRADIENT_COST, early_rows),
        name="gradient",
    )(dpre_two, tok, cot, slope, w_three)

    mine, grad_last = barrier((mine, grad_last))
    sums = pl.pallas_call(
        functools.partial(pair_kernel, rows),
        out_shape=[bf16(rows, feats)] + [bf16(rows + MORE, feats)] * 2,
        in_specs=vmem(2),
        out_specs=vmem(NEAR - 1),
        compiler_params=params,
        cost_estimate=cost(rows, rows),
        name="pair_sum",
    )(mine, received)
    mixed_x, mixed_y = to_x(sums[1]), to_y(sums[2])
    grad_terms, mixed_own = barrier((grad_terms, sums[0]))

    mine_diag, other_diag, grad_own, grad_one, grad_two, grad_three = pl.pallas_call(
        functools.partial(diagonal_kernel, owned),
        out_shape=[bf16(rows, feats)] * 2 + [bf16(owned, width)] * 4,
        in_specs=vmem(5) + anywhere(4),
        out_specs=vmem(6),
        scratch_shapes=[
            pltpu.VMEM((rows, width), jnp.bfloat16),
            pltpu.VMEM((rows, width), jnp.bfloat16),
            pltpu.VMEM((rows, units), jnp.bfloat16),
            dma((2,)),
            dma((2,)),
        ],
        compiler_params=params,
        cost_estimate=cost(DIAGONAL_COST, rows),
        name="diagonal",
    )(
        w_in_all, w_out_all, bias, grad_terms, grad_last,
        tok_diag, tok_diag_other, cot_diag, cot_diag_other,
    )
    received_diag = to_core(other_diag)
    relayed = to_far(grad_three, 1)
    from_one = to_far(grad_one, 1)

    (sum_diag,) = pl.pallas_call(
        functools.partial(pair_kernel, rows),
        out_shape=[bf16(rows, feats)],
        in_specs=vmem(2),
        out_specs=vmem(1),
        compiler_params=params,
        cost_estimate=cost(rows, rows),
        name="pair_sum_diagonal",
    )(mine_diag, received_diag)
    mixed_diag = to_diagonal(sum_diag)
    grad_two, _ = barrier((grad_two, sum_diag))
    (line_sum,) = pl.pallas_call(
        functools.partial(pair_kernel, owned),
        out_shape=[bf16(owned, width)],
        in_specs=vmem(2),
        out_specs=vmem(1),
        compiler_params=params,
        cost_estimate=cost(rows, rows),
        name="line_sum",
    )(grad_two, relayed)
    from_two = to_far(line_sum, 2)
    total = (
        grad_own.astype(jnp.float32)
        + from_one.astype(jnp.float32)
        + from_two.astype(jnp.float32)
    )
    mixed = pl.pallas_call(
        plane_kernel,
        out_shape=f32(rows, feats),
        in_specs=vmem(3),
        out_specs=pl.BlockSpec(memory_space=pltpu.VMEM),
        compiler_params=params,
        cost_estimate=cost(PLANE_COST, rows),
        name="plane_sum",
    )(mixed_own, mixed_x, mixed_y)
    mixed = (mixed + mixed_diag.astype(jnp.float32)).astype(jnp.bfloat16)
    return (mixed, total * scale)


def solution(mesh):
    dp, tensor = mesh.shape["dp"], mesh.shape["tensor"]
    far = dp // NEAR
    if tensor == 2 and far == 4:
        fine = Mesh(mesh.devices.reshape(far, 2, 2, tensor), AXES)
        rows, owners, halves = ("far", "y", "x"), AXES, "core"
        body = on_device_lines
    else:
        fine = Mesh(mesh.devices.reshape(far, NEAR, tensor), ("far", "near", "tensor"))
        rows, owners, halves = ("far", "near"), ("far", "near", "tensor"), "tensor"
        body = on_device_any
    in_specs = (P(rows, halves), P(rows, halves), P(owners, None), P(owners), P(owners, None))
    out_specs = (P(rows, halves), P(owners, None))
    return jax.shard_map(
        body, mesh=fine, in_specs=in_specs, out_specs=out_specs, check_vma=False
    )
```

```python
import functools
import math

import jax
import jax.numpy as jnp
from jax import lax
from jax.experimental import pallas as pl
from jax.experimental.pallas import tpu as pltpu
from jax.sharding import Mesh, PartitionSpec as P

NEAR = 4
AXES = ("far", "y", "x", "core")
CONTRACT_LAST = (((1,), (1,)), ((), ()))
CONTRACT_FIRST = (((0,), (0,)), ((), ()))
VMEM_LIMIT = 28 * 1024 * 1024
PLANE_COST = 10**10
GRADIENT_COST = 10**11
DIAGONAL_COST = 10**6
OUTPUT_COST = 10**6
EXTRA = 48
HAND_ON_COST = 2 * 10**10


def gelu_parts(value):
    coeff = 0.7978845608
    inner = coeff * (value + 0.044715 * value * value * value)
    tangent = jnp.tanh(inner)
    result = 0.5 * value * (1.0 + tangent)
    slope = 0.5 * (1.0 + tangent) + 0.5 * value * (1.0 - tangent * tangent) * coeff * (
        1.0 + 3.0 * 0.044715 * value * value
    )
    return (result, slope)


def on_device_any(tokens, cotangent, w_in, b_in, w_out):
    far, near, tensor = lax.axis_size("far"), lax.axis_size("near"), lax.axis_size("tensor")
    rows, feats = tokens.shape
    owned, width = w_in.shape
    scale = 1.0 / math.sqrt(rows * far * near)
    bias_rows = jnp.pad(b_in.reshape(1, owned), ((0, 15), (0, width - owned)))
    weights = lax.all_gather(jnp.concatenate([w_in, w_out, bias_rows], 0), "far", axis=0)
    in_rows = weights[:, :owned].reshape(far * owned, width)
    proj_rows = weights[:, owned : 2 * owned].reshape(far * owned, width)
    bias = weights[:, 2 * owned, :owned].reshape(far * owned).astype(jnp.float32)
    tok = lax.all_gather(tokens, ("near", "tensor"), axis=0).reshape(near, tensor, rows, feats)
    cot = lax.all_gather(cotangent, ("near", "tensor"), axis=0).reshape(near, tensor, rows, feats)
    tok_full = tok.transpose(0, 2, 1, 3).reshape(near * rows, width)
    cot_full = cot.transpose(0, 2, 1, 3).reshape(near * rows, width)
    pre = lax.dot_general(
        tok_full, in_rows, CONTRACT_LAST, preferred_element_type=jnp.float32
    ) + bias
    act_value, slope = gelu_parts(pre)
    act = act_value.astype(jnp.bfloat16)
    term = jnp.dot(act, proj_rows, preferred_element_type=jnp.float32).astype(jnp.bfloat16)
    term = term.reshape(near, rows, tensor, feats).transpose(0, 2, 1, 3)
    mixed = lax.psum_scatter(
        term.reshape(near * tensor, rows, feats), ("near", "tensor"), scatter_dimension=0
    )
    dact = lax.dot_general(cot_full, proj_rows, CONTRACT_LAST, preferred_element_type=jnp.float32)
    dpre = (dact * slope).astype(jnp.bfloat16)
    grad = lax.dot_general(dpre, tok_full, CONTRACT_FIRST, preferred_element_type=jnp.float32)
    grad_sum = lax.psum_scatter(grad.astype(jnp.bfloat16), "far", scatter_dimension=0, tiled=True)
    return (mixed, grad_sum.astype(jnp.float32) * scale)


def half_columns(core, shift, feats):
    return pl.ds(pl.multiple_of(lax.rem(core + shift, 2) * feats, feats), feats)


def side_by_side(core, pair, whole, start, sem):
    rows, feats = pair[0].shape
    return [
        pltpu.make_async_copy(
            pair[shift],
            whole.at[pl.ds(start, rows), half_columns(core, shift, feats)],
            sem.at[shift],
        )
        for shift in range(2)
    ]


def weight_copies(refs, owned, w_in, w_out, bias, sem):
    ins, outs = [], []
    for at, ref in enumerate(refs):
        spot = pl.ds(at * owned, owned)
        ins.append(pltpu.make_async_copy(ref.at[pl.ds(0, owned)], w_in.at[spot], sem.at[0, at]))
        ins.append(
            pltpu.make_async_copy(
                ref.at[pl.ds(2 * owned, 16), pl.ds(0, owned)], bias.at[:, spot], sem.at[1, at]
            )
        )
        outs.append(
            pltpu.make_async_copy(ref.at[pl.ds(owned, owned)], w_out.at[spot], sem.at[2, at])
        )
    return ins, outs


def run(copies, what):
    for copy in copies:
        getattr(copy, what)()


def activate(tok, w_in, bias):
    pre = lax.dot_general(
        tok, w_in, CONTRACT_LAST, preferred_element_type=jnp.float32
    ) + bias.astype(jnp.float32)
    return gelu_parts(pre)


def dot_last(left, right):
    return lax.dot_general(left, right, CONTRACT_LAST, preferred_element_type=jnp.float32)


def dot_first(left, right):
    return lax.dot_general(left, right, CONTRACT_FIRST, preferred_element_type=jnp.float32)


def early_block(start, step, tok, cot, w_in, w_out, bias, two, act_ref, dpre_ref, mixed_ref, dpre):
    @pl.loop(0, 2)
    def _(sub):
        spot = pl.ds(pl.multiple_of(start + sub * step, step), step)
        value, slope = activate(tok[spot, :], w_in[...], bias[0:1, :])
        act = value.astype(jnp.bfloat16)
        act_ref[spot, :] = act[:, two:]
        dact = dot_last(cot[spot, :], w_out[...])
        terms = (dact * slope).astype(jnp.bfloat16)
        dpre[spot, :] = terms[:, :two]
        dpre_ref[spot, :] = terms[:, two:]
        mixed_ref[spot, :] = jnp.dot(
            act[:, :two], w_out[:two, :], preferred_element_type=jnp.float32
        )


def early_kernel(owned, *refs):
    pair_refs, w_refs = refs[:6], refs[6:9]
    act_ref, dpre_ref, mixed_ref, grad_ref, tok, cot, w_in, w_out, bias = refs[9:18]
    dpre, tok_sem, cot_sem, w_sem = refs[18:]
    core = lax.axis_index("core")
    rows = pair_refs[0].shape[1]
    ins, outs = weight_copies(w_refs, owned, w_in, w_out, bias, w_sem)
    loads = []
    for block in range(NEAR - 1):
        first, second = pair_refs[2 * block], pair_refs[2 * block + 1]
        loads.append(
            side_by_side(core, (first.at[0], second.at[0]), tok, block * rows, tok_sem.at[block])
            + side_by_side(core, (first.at[1], second.at[1]), cot, block * rows, cot_sem.at[block])
        )
    run(ins + outs, "start")
    for load in loads:
        run(load, "start")
    run(ins + outs, "wait")
    for block, load in enumerate(loads):
        run(load, "wait")
        early_block(
            block * rows, rows // 2, tok, cot, w_in, w_out, bias, 2 * owned,
            act_ref, dpre_ref, mixed_ref, dpre,
        )
    grad_ref[...] = dot_first(dpre[...], tok[...])


def diagonal_kernel(owned, *refs):
    w_in, w_out, bias = refs[:3]
    act_ref, slope_ref, mixed_ref, tok, tok_sem = refs[5:]
    core = lax.axis_index("core")
    rows = tok.shape[0]
    two = 2 * owned
    load = side_by_side(core, (refs[3].at[pl.ds(0, rows)], refs[4]), tok, 0, tok_sem)
    run(load, "start")
    run(load, "wait")
    step = rows // 2

    @pl.loop(0, 2)
    def _(sub):
        spot = pl.ds(pl.multiple_of(sub * step, step), step)
        value, slope = activate(tok[spot, :], w_in[...], bias[0:1, :])
        slope_ref[spot, :] = slope
        act = value.astype(jnp.bfloat16)
        act_ref[spot, :] = act[:, two:]
        mixed_ref[spot, :] = jnp.dot(
            act[:, :two], w_out[:two, :], preferred_element_type=jnp.float32
        )


def output_kernel(owned, *refs):
    act_two, tok, early_mixed, act_diag, tok_diag, mixed_diag, w_out, w_three = refs[:8]
    mine_ref, other_ref, slope_ref, w_last = refs[8:]
    core = lax.axis_index("core")
    feats = mine_ref.shape[1]
    two = 2 * owned
    w_last[:owned, :] = w_out[two:, :]
    w_last[owned:, :] = w_three[owned:two, :]
    step = tok_diag.shape[0]

    def rows_of(here, spot, act_part, tok_part, mixed_part):
        value, slope = activate(
            tok_part[here, :], w_three[:owned, :], w_three[two : two + 16, :owned][0:1, :]
        )
        slope_ref[spot, :] = slope
        act = jnp.concatenate([act_part[here, :], value.astype(jnp.bfloat16)], axis=1)
        for shift, ref in enumerate((mine_ref, other_ref)):
            half = half_columns(core, shift, feats)
            ref[spot, :] = (
                mixed_part[here, half]
                + jnp.dot(act, w_last[:, half], preferred_element_type=jnp.float32)
            ).astype(jnp.bfloat16)

    @pl.loop(0, NEAR - 1)
    def _(block):
        spot = pl.ds(pl.multiple_of(block * step, step), step)
        rows_of(spot, spot, act_two, tok, early_mixed)

    rows_of(
        slice(None), pl.ds((NEAR - 1) * step, step), act_diag, tok_diag, mixed_diag
    )


def gradient_kernel(owned, *refs):
    dpre_two, tok, cot, slope, w_three, w_out, grad_first, tok_diag, slope_diag = refs[:9]
    own_ref, one_ref, two_ref, three_ref, cot_diag, dpre, dpre_diag, cot_sem = refs[11:]
    core = lax.axis_index("core")
    step = tok_diag.shape[0]
    two, three = 2 * owned, 3 * owned
    pair = (refs[9].at[pl.ds(EXTRA, step)], refs[10])
    load = side_by_side(core, pair, cot_diag, 0, cot_sem)
    run(load, "start")

    @pl.loop(0, NEAR - 1)
    def _(block):
        spot = pl.ds(pl.multiple_of(block * step, step), step)
        dact = dot_last(cot[spot, :], w_three[owned:two, :])
        last = (dact * slope[spot, :]).astype(jnp.bfloat16)
        dpre[spot, :] = jnp.concatenate([dpre_two[spot, :], last], axis=1)

    run(load, "wait")
    dact = dot_last(cot_diag[...], w_out[...])
    dpre_diag[:, :three] = (dact * slope_diag[...]).astype(jnp.bfloat16)
    dact = dot_last(cot_diag[...], w_three[owned:two, :])
    dpre_diag[:, three:] = (dact * slope[(NEAR - 1) * step :, :]).astype(jnp.bfloat16)
    grad = dot_first(dpre[...], tok[...]) + dot_first(dpre_diag[:, two:], tok_diag[...])
    two_ref[...] = grad[:owned].astype(jnp.bfloat16)
    three_ref[...] = grad[owned:].astype(jnp.bfloat16)
    grad = grad_first[...] + dot_first(dpre_diag[:, :two], tok_diag[...])
    own_ref[...] = grad[:owned].astype(jnp.bfloat16)
    one_ref[...] = grad[owned:].astype(jnp.bfloat16)


def pair_kernel(rows, mine_ref, other_ref, *out_refs):
    for block, ref in enumerate(out_refs):
        spot = pl.ds(block * rows, rows)
        ref[...] = (
            mine_ref[spot, :].astype(jnp.float32) + other_ref[spot, :].astype(jnp.float32)
        ).astype(jnp.bfloat16)


def hand_on_kernel(in_ref, out_ref):
    out_ref[...] = in_ref[...]


def plane_kernel(own_ref, x_ref, y_ref, diag_ref, out_ref):
    out_ref[...] = (
        own_ref[...].astype(jnp.float32)
        + x_ref[...].astype(jnp.float32)
        + y_ref[...].astype(jnp.float32)
        + diag_ref[...].astype(jnp.float32)
    ).astype(jnp.bfloat16)


def vmem(count):
    return [pl.BlockSpec(memory_space=pltpu.VMEM)] * count


def anywhere(count):
    return [pl.BlockSpec(memory_space=pl.ANY)] * count


def bf16(*shape):
    return jax.ShapeDtypeStruct(shape, jnp.bfloat16)


def permute(value, there):
    pairs = []
    for f in range(4):
        for y in range(2):
            for x in range(2):
                for c in range(2):
                    to = there(f, y, x, c)
                    here = ((f * 2 + y) * 2 + x) * 2 + c
                    pairs.append((here, ((to[0] * 2 + to[1]) * 2 + to[2]) * 2 + to[3]))
    return lax.ppermute(value, AXES, pairs)


def to_x(value):
    return permute(value, lambda f, y, x, c: (f, y, 1 - x, c))


def to_y(value):
    return permute(value, lambda f, y, x, c: (f, 1 - y, x, c))


def to_diagonal(value):
    return permute(value, lambda f, y, x, c: (f, 1 - y, 1 - x, c))


def to_core(value):
    return permute(value, lambda f, y, x, c: (f, y, x, 1 - c))


def to_far(value, flip):
    return permute(value, lambda f, y, x, c: (f ^ flip, y, x, c))


def on_device_lines(tokens, cotangent, w_in, b_in, w_out):
    rows, feats = tokens.shape
    owned, width = w_in.shape
    units = 4 * owned
    count = NEAR * rows
    scale = 1.0 / math.sqrt(4 * count)
    params = pltpu.CompilerParams(vmem_limit_bytes=VMEM_LIMIT)
    dma = pltpu.SemaphoreType.DMA
    barrier = lax.optimization_barrier
    early_rows = (NEAR - 1) * rows

    def f32(*shape):
        return jax.ShapeDtypeStruct(shape, jnp.float32)

    def cost(flops, traffic):
        return pl.CostEstimate(flops=flops, bytes_accessed=traffic, transcendentals=0)

    bias_rows = jnp.pad(b_in.reshape(1, owned), ((0, 15), (0, width - owned)))
    own_w = jnp.concatenate([w_in, w_out, bias_rows], 0)
    own_w, tokens, cotangent = barrier((own_w, tokens, cotangent))
    own = jnp.stack([tokens, cotangent])
    w_two, w_one = to_far(own_w, 2), to_far(own_w, 1)
    from_x, from_y = to_x(own), to_y(own)
    own_other = to_core(own)
    from_x, from_y, own_other = barrier((from_x, from_y, own_other))
    tok_diag = to_y(from_x.reshape(2 * rows, feats)[: rows + EXTRA])
    cot_diag = to_x(from_y.reshape(2 * rows, feats)[rows - EXTRA :])
    x_other, y_other = to_core(from_x), to_core(from_y)
    w_again = pl.pallas_call(
        hand_on_kernel,
        out_shape=bf16(*w_two.shape),
        in_specs=vmem(1),
        out_specs=pl.BlockSpec(memory_space=pltpu.VMEM),
        compiler_params=params,
        cost_estimate=cost(HAND_ON_COST, rows),
        name="hand_on",
    )(w_two)
    w_three = to_far(w_again, 1)
    act_two, dpre_two, mixed_terms, grad_terms, tok, cot, w_in_three, w_out_three, bias = (
        pl.pallas_call(
            functools.partial(early_kernel, owned),
            out_shape=(
                bf16(early_rows, owned),
                bf16(early_rows, owned),
                f32(early_rows, width),
                f32(2 * owned, width),
                bf16(early_rows, width),
                bf16(early_rows, width),
                bf16(3 * owned, width),
                bf16(3 * owned, width),
                bf16(16, 3 * owned),
            ),
            in_specs=anywhere(9),
            out_specs=vmem(9),
            scratch_shapes=[
                pltpu.VMEM((early_rows, 2 * owned), jnp.bfloat16),
                dma((NEAR - 1, 2)),
                dma((NEAR - 1, 2)),
                dma((3, 3)),
            ],
            compiler_params=params,
            cost_estimate=cost(early_rows * units, early_rows),
            name="early",
        )(own, own_other, from_x, x_other, from_y, y_other, own_w, w_one, w_two)
    )

    tok_diag, act_two = barrier((tok_diag, act_two))
    tok_diag_other = to_core(tok_diag[:rows])
    act_diag, slope_diag, mixed_terms_diag, tok_last = pl.pallas_call(
        functools.partial(diagonal_kernel, owned),
        out_shape=(
            bf16(rows, owned),
            f32(rows, 3 * owned),
            f32(rows, width),
            bf16(rows, width),
        ),
        in_specs=vmem(3) + anywhere(2),
        out_specs=vmem(4),
        scratch_shapes=[dma((2,))],
        compiler_params=params,
        cost_estimate=cost(DIAGONAL_COST, rows),
        name="diagonal",
    )(w_in_three, w_out_three, bias, tok_diag, tok_diag_other)
    cot_diag_other = to_core(cot_diag[EXTRA:])

    mine, other, slope = pl.pallas_call(
        functools.partial(output_kernel, owned),
        out_shape=(bf16(count, feats), bf16(count, feats), f32(count, owned)),
        in_specs=vmem(8),
        out_specs=vmem(3),
        scratch_shapes=[pltpu.VMEM((2 * owned, width), jnp.bfloat16)],
        compiler_params=params,
        cost_estimate=cost(OUTPUT_COST, early_rows),
        name="output",
    )(act_two, tok, mixed_terms, act_diag, tok_last, mixed_terms_diag, w_out_three, w_three)
    received = to_core(other)

    grad_own, grad_one, grad_two, grad_three = pl.pallas_call(
        functools.partial(gradient_kernel, owned),
        out_shape=[bf16(owned, width)] * 4,
        in_specs=vmem(9) + anywhere(2),
        out_specs=vmem(4),
        scratch_shapes=[
            pltpu.VMEM((rows, width), jnp.bfloat16),
            pltpu.VMEM((early_rows, 2 * owned), jnp.bfloat16),
            pltpu.VMEM((rows, units), jnp.bfloat16),
            dma((2,)),
        ],
        compiler_params=params,
        cost_estimate=cost(GRADIENT_COST, early_rows),
        name="gradient",
    )(
        dpre_two, tok, cot, slope, w_three, w_out_three, grad_terms, tok_last, slope_diag,
        cot_diag, cot_diag_other,
    )
    relayed = to_far(grad_three, 1)
    mine, grad_own = barrier((mine, grad_own))
    sums = pl.pallas_call(
        functools.partial(pair_kernel, rows),
        out_shape=[bf16(rows, feats)] * NEAR,
        in_specs=vmem(2),
        out_specs=vmem(NEAR),
        compiler_params=params,
        cost_estimate=cost(rows, rows),
        name="pair_sum",
    )(mine, received)
    mixed_own = sums[0]
    mixed_x, mixed_y, mixed_diag = to_x(sums[1]), to_y(sums[2]), to_diagonal(sums[3])
    grad_one, grad_two, _ = barrier((grad_one, grad_two, sums[0]))
    (line_sum,) = pl.pallas_call(
        functools.partial(pair_kernel, owned),
        out_shape=[bf16(owned, width)],
        in_specs=vmem(2),
        out_specs=vmem(1),
        compiler_params=params,
        cost_estimate=cost(rows, rows),
        name="line_sum",
    )(grad_two, relayed)
    from_two = to_far(line_sum, 2)
    from_one = to_far(grad_one, 1)
    total = (
        grad_own.astype(jnp.float32)
        + from_one.astype(jnp.float32)
        + from_two.astype(jnp.float32)
    )
    mixed = pl.pallas_call(
        plane_kernel,
        out_shape=bf16(rows, feats),
        in_specs=vmem(4),
        out_specs=pl.BlockSpec(memory_space=pltpu.VMEM),
        compiler_params=params,
        cost_estimate=cost(PLANE_COST, rows),
        name="plane_sum",
    )(mixed_own, mixed_x, mixed_y, mixed_diag)
    return (mixed, total * scale)


def solution(mesh):
    dp, tensor = mesh.shape["dp"], mesh.shape["tensor"]
    far = dp // NEAR
    if tensor == 2 and far == 4:
        fine = Mesh(mesh.devices.reshape(far, 2, 2, tensor), AXES)
        rows, owners, halves = ("far", "y", "x"), AXES, "core"
        body = on_device_lines
    else:
        fine = Mesh(mesh.devices.reshape(far, NEAR, tensor), ("far", "near", "tensor"))
        rows, owners, halves = ("far", "near"), ("far", "near", "tensor"), "tensor"
        body = on_device_any
    in_specs = (P(rows, halves), P(rows, halves), P(owners, None), P(owners), P(owners, None))
    out_specs = (P(rows, halves), P(owners, None))
    return jax.shard_map(
        body, mesh=fine, in_specs=in_specs, out_specs=out_specs, check_vma=False
    )
```

```python
import functools
import math

import jax
import jax.numpy as jnp
from jax import lax
from jax.experimental import pallas as pl
from jax.experimental.pallas import tpu as pltpu
from jax.sharding import Mesh, PartitionSpec as P

NEAR = 4
AXES = ("far", "y", "x", "core")
CONTRACT_LAST = (((1,), (1,)), ((), ()))
CONTRACT_FIRST = (((0,), (0,)), ((), ()))
VMEM_LIMIT = 28 * 1024 * 1024
PLANE_COST = 10**10
GRADIENT_COST = 10**10
DIAGONAL_COST = 10**6
EXTRA = 48
BIAS_ROWS = 8
MORE = 16


def gelu_parts(value):
    coeff = 0.7978845608
    inner = coeff * (value + 0.044715 * value * value * value)
    tangent = jnp.tanh(inner)
    result = 0.5 * value * (1.0 + tangent)
    slope = 0.5 * (1.0 + tangent) + 0.5 * value * (1.0 - tangent * tangent) * coeff * (
        1.0 + 3.0 * 0.044715 * value * value
    )
    return (result, slope)


def on_device_any(tokens, cotangent, w_in, b_in, w_out):
    far, near, tensor = lax.axis_size("far"), lax.axis_size("near"), lax.axis_size("tensor")
    rows, feats = tokens.shape
    owned, width = w_in.shape
    scale = 1.0 / math.sqrt(rows * far * near)
    bias_rows = jnp.pad(b_in.reshape(1, owned), ((0, 15), (0, width - owned)))
    weights = lax.all_gather(jnp.concatenate([w_in, w_out, bias_rows], 0), "far", axis=0)
    in_rows = weights[:, :owned].reshape(far * owned, width)
    proj_rows = weights[:, owned : 2 * owned].reshape(far * owned, width)
    bias = weights[:, 2 * owned, :owned].reshape(far * owned).astype(jnp.float32)
    tok = lax.all_gather(tokens, ("near", "tensor"), axis=0).reshape(near, tensor, rows, feats)
    cot = lax.all_gather(cotangent, ("near", "tensor"), axis=0).reshape(near, tensor, rows, feats)
    tok_full = tok.transpose(0, 2, 1, 3).reshape(near * rows, width)
    cot_full = cot.transpose(0, 2, 1, 3).reshape(near * rows, width)
    pre = lax.dot_general(
        tok_full, in_rows, CONTRACT_LAST, preferred_element_type=jnp.float32
    ) + bias
    act_value, slope = gelu_parts(pre)
    act = act_value.astype(jnp.bfloat16)
    term = jnp.dot(act, proj_rows, preferred_element_type=jnp.float32).astype(jnp.bfloat16)
    term = term.reshape(near, rows, tensor, feats).transpose(0, 2, 1, 3)
    mixed = lax.psum_scatter(
        term.reshape(near * tensor, rows, feats), ("near", "tensor"), scatter_dimension=0
    )
    dact = lax.dot_general(cot_full, proj_rows, CONTRACT_LAST, preferred_element_type=jnp.float32)
    dpre = (dact * slope).astype(jnp.bfloat16)
    grad = lax.dot_general(dpre, tok_full, CONTRACT_FIRST, preferred_element_type=jnp.float32)
    grad_sum = lax.psum_scatter(grad.astype(jnp.bfloat16), "far", scatter_dimension=0, tiled=True)
    return (mixed, grad_sum.astype(jnp.float32) * scale)


def half_columns(core, shift, feats):
    return pl.ds(pl.multiple_of(lax.rem(core + shift, 2) * feats, feats), feats)


def side_by_side(core, pair, whole, start, sem):
    rows, feats = pair[0].shape
    return [
        pltpu.make_async_copy(
            pair[shift],
            whole.at[pl.ds(start, rows), half_columns(core, shift, feats)],
            sem.at[shift],
        )
        for shift in range(2)
    ]


def weight_copies(refs, owned, w_in, w_out, sem):
    copies = []
    for at, ref in enumerate(refs):
        spot = pl.ds(at * owned, owned)
        copies.append(pltpu.make_async_copy(ref.at[pl.ds(0, owned)], w_in.at[spot], sem.at[0, at]))
        copies.append(
            pltpu.make_async_copy(ref.at[pl.ds(owned, owned)], w_out.at[spot], sem.at[1, at])
        )
    return copies


def bias_of(ref, owned):
    return ref[2 * owned : 2 * owned + BIAS_ROWS, :owned].astype(jnp.float32)


def run(copies, what):
    for copy in copies:
        getattr(copy, what)()


def activate(tok, w_in, bias):
    pre = lax.dot_general(
        tok, w_in, CONTRACT_LAST, preferred_element_type=jnp.float32
    ) + bias
    return gelu_parts(pre)


def dot_last(left, right):
    return lax.dot_general(left, right, CONTRACT_LAST, preferred_element_type=jnp.float32)


def dot_first(left, right):
    return lax.dot_general(left, right, CONTRACT_FIRST, preferred_element_type=jnp.float32)


def early_block(start, step, tok, cot, w_in, w_out, bias, two, act_ref, dpre_ref, mixed_ref, dpre):
    @pl.loop(0, 2)
    def _(sub):
        spot = pl.ds(pl.multiple_of(start + sub * step, step), step)
        value, slope = activate(tok[spot, :], w_in[...], bias[0:1, :])
        act = value.astype(jnp.bfloat16)
        act_ref[spot, :] = act[:, two:]
        dact = dot_last(cot[spot, :], w_out[...])
        terms = (dact * slope).astype(jnp.bfloat16)
        dpre[spot, :] = terms[:, :two]
        dpre_ref[spot, :] = terms[:, two:]
        mixed_ref[spot, :] = jnp.dot(
            act[:, :two], w_out[:two, :], preferred_element_type=jnp.float32
        )


def early_kernel(owned, *refs):
    pair_refs, w_refs = refs[:6], refs[6:9]
    act_ref, dpre_ref, mixed_ref, grad_ref, tok, cot, w_in, w_out, bias = refs[9:18]
    dpre, tok_sem, cot_sem, w_sem = refs[18:]
    core = lax.axis_index("core")
    rows = pair_refs[0].shape[1]
    w_copies = weight_copies(w_refs, owned, w_in, w_out, w_sem)
    loads = []
    for block in range(NEAR - 1):
        first, second = pair_refs[2 * block], pair_refs[2 * block + 1]
        loads.append(
            side_by_side(core, (first.at[0], second.at[0]), tok, block * rows, tok_sem.at[block])
            + side_by_side(core, (first.at[1], second.at[1]), cot, block * rows, cot_sem.at[block])
        )
    run(w_copies, "start")
    for load in loads:
        run(load, "start")
    for at, ref in enumerate(w_refs):
        bias[:, at * owned : (at + 1) * owned] = bias_of(ref, owned)
    run(w_copies, "wait")
    for block, load in enumerate(loads):
        run(load, "wait")
        early_block(
            block * rows, rows // 2, tok, cot, w_in, w_out, bias, 2 * owned,
            act_ref, dpre_ref, mixed_ref, dpre,
        )
    grad_ref[...] = dot_first(dpre[...], tok[...])


def output_kernel(owned, *refs):
    act_two, tok, early_mixed, w_in, w_out, bias, w_three = refs[:7]
    mine_ref, other_ref, slope_ref, w_in_all, w_out_all, bias_all = refs[7:13]
    w_last, sem = refs[13:]
    core = lax.axis_index("core")
    feats = mine_ref.shape[1]
    two, three = 2 * owned, 3 * owned
    first, last = pl.ds(0, three), pl.ds(three, owned)
    copies = [
        pltpu.make_async_copy(w_in, w_in_all.at[first], sem.at[0]),
        pltpu.make_async_copy(w_three.at[pl.ds(0, owned)], w_in_all.at[last], sem.at[1]),
        pltpu.make_async_copy(w_out, w_out_all.at[first], sem.at[2]),
        pltpu.make_async_copy(w_three.at[pl.ds(owned, owned)], w_out_all.at[last], sem.at[3]),
    ]
    run(copies, "start")
    bias_last = bias_of(w_three, owned)
    bias_all[:, :three] = bias[...]
    bias_all[:, three:] = bias_last
    w_last[:owned, :] = w_out[two:, :]
    w_last[owned:, :] = w_three[owned:two, :]
    step = tok.shape[0] // 3

    @pl.loop(0, 3)
    def _(block):
        spot = pl.ds(pl.multiple_of(block * step, step), step)
        value, slope = activate(tok[spot, :], w_three[:owned, :], bias_last[0:1, :])
        slope_ref[spot, :] = slope
        act = jnp.concatenate([act_two[spot, :], value.astype(jnp.bfloat16)], axis=1)
        for shift, ref in enumerate((mine_ref, other_ref)):
            half = half_columns(core, shift, feats)
            ref[spot, :] = (
                early_mixed[spot, half]
                + jnp.dot(act, w_last[:, half], preferred_element_type=jnp.float32)
            ).astype(jnp.bfloat16)

    run(copies, "wait")


def gradient_kernel(dpre_two, tok, cot, slope, w_three, grad_ref, dpre):
    owned = slope.shape[1]
    step = tok.shape[0] // 3

    @pl.loop(0, 3)
    def _(block):
        spot = pl.ds(pl.multiple_of(block * step, step), step)
        dact = dot_last(cot[spot, :], w_three[owned : 2 * owned, :])
        last = (dact * slope[spot, :]).astype(jnp.bfloat16)
        dpre[spot, :] = jnp.concatenate([dpre_two[spot, :], last], axis=1)

    grad_ref[...] = dot_first(dpre[...], tok[...])


def diagonal_kernel(owned, *refs):
    w_in, w_out, bias, grad_first, grad_last = refs[:5]
    tok_ref, cot_ref, far_ref = refs[5:8]
    mine_ref, other_ref, own_ref, one_ref, two_ref, three_ref = refs[8:14]
    tok, cot, dpre, tok_sem, cot_sem = refs[14:]
    core = lax.axis_index("core")
    rows, feats = mine_ref.shape
    two = 2 * owned
    first, second = pl.ds(0, rows), pl.ds(rows, rows)
    load = side_by_side(core, (tok_ref.at[first], far_ref.at[first]), tok, 0, tok_sem)
    load += side_by_side(
        core, (cot_ref.at[pl.ds(EXTRA, rows)], far_ref.at[second]), cot, 0, cot_sem
    )
    run(load, "start")
    run(load, "wait")
    step = rows // 2

    @pl.loop(0, 2)
    def _(sub):
        spot = pl.ds(pl.multiple_of(sub * step, step), step)
        value, slope = activate(tok[spot, :], w_in[...], bias[0:1, :])
        act = value.astype(jnp.bfloat16)
        dact = dot_last(cot[spot, :], w_out[...])
        dpre[spot, :] = (dact * slope).astype(jnp.bfloat16)
        for shift, ref in enumerate((mine_ref, other_ref)):
            ref[spot, :] = jnp.dot(
                act, w_out[:, half_columns(core, shift, feats)], preferred_element_type=jnp.float32
            ).astype(jnp.bfloat16)

    grad = grad_last[...] + dot_first(dpre[:, two:], tok[...])
    two_ref[...] = grad[:owned].astype(jnp.bfloat16)
    three_ref[...] = grad[owned:].astype(jnp.bfloat16)
    grad = grad_first[...] + dot_first(dpre[:, :two], tok[...])
    own_ref[...] = grad[:owned].astype(jnp.bfloat16)
    one_ref[...] = grad[owned:].astype(jnp.bfloat16)


def pair_kernel(rows, mine_ref, other_ref, *out_refs):
    for block, ref in enumerate(out_refs):
        spot = pl.ds(block * rows, rows)
        ref[:rows, :] = (
            mine_ref[spot, :].astype(jnp.float32) + other_ref[spot, :].astype(jnp.float32)
        ).astype(jnp.bfloat16)
        if ref.shape[0] > rows:
            ref[rows:, :] = jnp.zeros_like(ref[rows:, :])


def plane_kernel(own_ref, x_ref, y_ref, out_ref):
    rows = own_ref.shape[0]
    out_ref[...] = (
        own_ref[...].astype(jnp.float32)
        + x_ref[:rows, :].astype(jnp.float32)
        + y_ref[:rows, :].astype(jnp.float32)
    )


def vmem(count):
    return [pl.BlockSpec(memory_space=pltpu.VMEM)] * count


def anywhere(count):
    return [pl.BlockSpec(memory_space=pl.ANY)] * count


def bf16(*shape):
    return jax.ShapeDtypeStruct(shape, jnp.bfloat16)


def permute(value, there):
    pairs = []
    for f in range(4):
        for y in range(2):
            for x in range(2):
                for c in range(2):
                    to = there(f, y, x, c)
                    here = ((f * 2 + y) * 2 + x) * 2 + c
                    pairs.append((here, ((to[0] * 2 + to[1]) * 2 + to[2]) * 2 + to[3]))
    return lax.ppermute(value, AXES, pairs)


def to_x(value):
    return permute(value, lambda f, y, x, c: (f, y, 1 - x, c))


def to_y(value):
    return permute(value, lambda f, y, x, c: (f, 1 - y, x, c))


def to_diagonal(value):
    return permute(value, lambda f, y, x, c: (f, 1 - y, 1 - x, c))


def to_core(value):
    return permute(value, lambda f, y, x, c: (f, y, x, 1 - c))


def to_far(value, flip):
    return permute(value, lambda f, y, x, c: (f ^ flip, y, x, c))


def on_device_lines(tokens, cotangent, w_in, b_in, w_out):
    rows, feats = tokens.shape
    owned, width = w_in.shape
    units = 4 * owned
    count = NEAR * rows
    scale = 1.0 / math.sqrt(4 * count)
    params = pltpu.CompilerParams(vmem_limit_bytes=VMEM_LIMIT)
    dma = pltpu.SemaphoreType.DMA
    barrier = lax.optimization_barrier
    early_rows = (NEAR - 1) * rows

    def f32(*shape):
        return jax.ShapeDtypeStruct(shape, jnp.float32)

    def cost(flops, traffic):
        return pl.CostEstimate(flops=flops, bytes_accessed=traffic, transcendentals=0)

    bias_rows = jnp.pad(b_in.reshape(1, owned), ((0, BIAS_ROWS - 1), (0, width - owned)))
    own_w = jnp.concatenate([w_in, w_out, bias_rows], 0)
    own_w, tokens, cotangent = barrier((own_w, tokens, cotangent))
    own = jnp.stack([tokens, cotangent])
    w_two, w_one = to_far(own_w, 2), to_far(own_w, 1)
    from_x, from_y = to_x(own), to_y(own)
    own_other = to_core(own)
    from_x, from_y, own_other = barrier((from_x, from_y, own_other))
    tok_diag = to_y(from_x.reshape(2 * rows, feats)[: rows + EXTRA])
    cot_diag = to_x(from_y.reshape(2 * rows, feats)[rows - EXTRA :])
    x_other, y_other = to_core(from_x), to_core(from_y)
    w_three = to_far(w_two, 1)
    act_two, dpre_two, mixed_terms, grad_terms, tok, cot, w_in_three, w_out_three, bias = (
        pl.pallas_call(
            functools.partial(early_kernel, owned),
            out_shape=(
                bf16(early_rows, owned),
                bf16(early_rows, owned),
                f32(early_rows, width),
                f32(2 * owned, width),
                bf16(early_rows, width),
                bf16(early_rows, width),
                bf16(3 * owned, width),
                bf16(3 * owned, width),
                f32(BIAS_ROWS, 3 * owned),
            ),
            in_specs=anywhere(6) + vmem(3),
            out_specs=vmem(9),
            scratch_shapes=[
                pltpu.VMEM((early_rows, 2 * owned), jnp.bfloat16),
                dma((NEAR - 1, 2)),
                dma((NEAR - 1, 2)),
                dma((2, 3)),
            ],
            compiler_params=params,
            cost_estimate=cost(early_rows * units, early_rows),
            name="early",
        )(own, own_other, from_x, x_other, from_y, y_other, own_w, w_one, w_two)
    )

    mine, other, slope, w_in_all, w_out_all, bias = pl.pallas_call(
        functools.partial(output_kernel, owned),
        out_shape=(
            bf16(early_rows, feats),
            bf16(early_rows, feats),
            f32(early_rows, owned),
            bf16(units, width),
            bf16(units, width),
            f32(BIAS_ROWS, units),
        ),
        in_specs=vmem(7),
        out_specs=vmem(6),
        scratch_shapes=[pltpu.VMEM((2 * owned, width), jnp.bfloat16), dma((4,))],
        compiler_params=params,
        cost_estimate=cost(early_rows * units, early_rows),
        name="output",
    )(act_two, tok, mixed_terms, w_in_three, w_out_three, bias, w_three)
    tok_diag, cot_diag, other = barrier((tok_diag, cot_diag, other))
    received = to_core(other)
    diag_other = to_core(jnp.concatenate([tok_diag[:rows], cot_diag[EXTRA:]]))
    slope, tok_diag = barrier((slope, tok_diag))
    grad_last = pl.pallas_call(
        gradient_kernel,
        out_shape=f32(2 * owned, width),
        in_specs=vmem(5),
        out_specs=pl.BlockSpec(memory_space=pltpu.VMEM),
        scratch_shapes=[pltpu.VMEM((early_rows, 2 * owned), jnp.bfloat16)],
        compiler_params=params,
        cost_estimate=cost(GRADIENT_COST, early_rows),
        name="gradient",
    )(dpre_two, tok, cot, slope, w_three)

    mine, grad_last = barrier((mine, grad_last))
    sums = pl.pallas_call(
        functools.partial(pair_kernel, rows),
        out_shape=[bf16(rows, feats)] + [bf16(rows + MORE, feats)] * 2,
        in_specs=vmem(2),
        out_specs=vmem(NEAR - 1),
        compiler_params=params,
        cost_estimate=cost(rows, rows),
        name="pair_sum",
    )(mine, received)
    mixed_x, mixed_y = to_x(sums[1]), to_y(sums[2])
    grad_terms, mixed_own = barrier((grad_terms, sums[0]))

    mine_diag, other_diag, grad_own, grad_one, grad_two, grad_three = pl.pallas_call(
        functools.partial(diagonal_kernel, owned),
        out_shape=[bf16(rows, feats)] * 2 + [bf16(owned, width)] * 4,
        in_specs=vmem(5) + anywhere(3),
        out_specs=vmem(6),
        scratch_shapes=[
            pltpu.VMEM((rows, width), jnp.bfloat16),
            pltpu.VMEM((rows, width), jnp.bfloat16),
            pltpu.VMEM((rows, units), jnp.bfloat16),
            dma((2,)),
            dma((2,)),
        ],
        compiler_params=params,
        cost_estimate=cost(DIAGONAL_COST, rows),
        name="diagonal",
    )(
        w_in_all, w_out_all, bias, grad_terms, grad_last,
        tok_diag, cot_diag, diag_other,
    )
    received_diag = to_core(other_diag)
    relayed = to_far(grad_three, 1)
    (sum_diag,) = pl.pallas_call(
        functools.partial(pair_kernel, rows),
        out_shape=[bf16(rows, feats)],
        in_specs=vmem(2),
        out_specs=vmem(1),
        compiler_params=params,
        cost_estimate=cost(rows, rows),
        name="pair_sum_diagonal",
    )(mine_diag, received_diag)
    mixed_diag = to_diagonal(sum_diag)
    grad_one, grad_two, _ = barrier((grad_one, grad_two, sum_diag))
    from_one = to_far(grad_one, 1)
    (line_sum,) = pl.pallas_call(
        functools.partial(pair_kernel, owned),
        out_shape=[bf16(owned, width)],
        in_specs=vmem(2),
        out_specs=vmem(1),
        compiler_params=params,
        cost_estimate=cost(rows, rows),
        name="line_sum",
    )(grad_two, relayed)
    from_two = to_far(line_sum, 2)
    total = (
        grad_own.astype(jnp.float32)
        + from_one.astype(jnp.float32)
        + from_two.astype(jnp.float32)
    )
    mixed = pl.pallas_call(
        plane_kernel,
        out_shape=f32(rows, feats),
        in_specs=vmem(3),
        out_specs=pl.BlockSpec(memory_space=pltpu.VMEM),
        compiler_params=params,
        cost_estimate=cost(PLANE_COST, rows),
        name="plane_sum",
    )(mixed_own, mixed_x, mixed_y)
    mixed = (mixed + mixed_diag.astype(jnp.float32)).astype(jnp.bfloat16)
    return (mixed, total * scale)


def solution(mesh):
    dp, tensor = mesh.shape["dp"], mesh.shape["tensor"]
    far = dp // NEAR
    if tensor == 2 and far == 4:
        fine = Mesh(mesh.devices.reshape(far, 2, 2, tensor), AXES)
        rows, owners, halves = ("far", "y", "x"), AXES, "core"
        body = on_device_lines
    else:
        fine = Mesh(mesh.devices.reshape(far, NEAR, tensor), ("far", "near", "tensor"))
        rows, owners, halves = ("far", "near"), ("far", "near", "tensor"), "tensor"
        body = on_device_any
    in_specs = (P(rows, halves), P(rows, halves), P(owners, None), P(owners), P(owners, None))
    out_specs = (P(rows, halves), P(owners, None))
    return jax.shard_map(
        body, mesh=fine, in_specs=in_specs, out_specs=out_specs, check_vma=False
    )
```

```python
import functools
import math

import jax
import jax.numpy as jnp
from jax import lax
from jax.experimental import pallas as pl
from jax.experimental.pallas import tpu as pltpu
from jax.sharding import Mesh, PartitionSpec as P

NEAR = 4
AXES = ("far", "y", "x", "core")
CONTRACT_LAST = (((1,), (1,)), ((), ()))
CONTRACT_FIRST = (((0,), (0,)), ((), ()))
VMEM_LIMIT = 28 * 1024 * 1024
PLANE_COST = 10**10
GRADIENT_COST = 10**10
DIAGONAL_COST = 10**6
EXTRA = 48
BIAS_ROWS = 8
MORE = 16


def gelu_parts(value):
    coeff = 0.7978845608
    inner = coeff * (value + 0.044715 * value * value * value)
    tangent = jnp.tanh(inner)
    result = 0.5 * value * (1.0 + tangent)
    slope = 0.5 * (1.0 + tangent) + 0.5 * value * (1.0 - tangent * tangent) * coeff * (
        1.0 + 3.0 * 0.044715 * value * value
    )
    return (result, slope)


def on_device_any(tokens, cotangent, w_in, b_in, w_out):
    far, near, tensor = lax.axis_size("far"), lax.axis_size("near"), lax.axis_size("tensor")
    rows, feats = tokens.shape
    owned, width = w_in.shape
    scale = 1.0 / math.sqrt(rows * far * near)
    bias_rows = jnp.pad(b_in.reshape(1, owned), ((0, 15), (0, width - owned)))
    weights = lax.all_gather(jnp.concatenate([w_in, w_out, bias_rows], 0), "far", axis=0)
    in_rows = weights[:, :owned].reshape(far * owned, width)
    proj_rows = weights[:, owned : 2 * owned].reshape(far * owned, width)
    bias = weights[:, 2 * owned, :owned].reshape(far * owned).astype(jnp.float32)
    tok = lax.all_gather(tokens, ("near", "tensor"), axis=0).reshape(near, tensor, rows, feats)
    cot = lax.all_gather(cotangent, ("near", "tensor"), axis=0).reshape(near, tensor, rows, feats)
    tok_full = tok.transpose(0, 2, 1, 3).reshape(near * rows, width)
    cot_full = cot.transpose(0, 2, 1, 3).reshape(near * rows, width)
    pre = lax.dot_general(
        tok_full, in_rows, CONTRACT_LAST, preferred_element_type=jnp.float32
    ) + bias
    act_value, slope = gelu_parts(pre)
    act = act_value.astype(jnp.bfloat16)
    term = jnp.dot(act, proj_rows, preferred_element_type=jnp.float32).astype(jnp.bfloat16)
    term = term.reshape(near, rows, tensor, feats).transpose(0, 2, 1, 3)
    mixed = lax.psum_scatter(
        term.reshape(near * tensor, rows, feats), ("near", "tensor"), scatter_dimension=0
    )
    dact = lax.dot_general(cot_full, proj_rows, CONTRACT_LAST, preferred_element_type=jnp.float32)
    dpre = (dact * slope).astype(jnp.bfloat16)
    grad = lax.dot_general(dpre, tok_full, CONTRACT_FIRST, preferred_element_type=jnp.float32)
    grad_sum = lax.psum_scatter(grad.astype(jnp.bfloat16), "far", scatter_dimension=0, tiled=True)
    return (mixed, grad_sum.astype(jnp.float32) * scale)


def half_columns(core, shift, feats):
    return pl.ds(pl.multiple_of(lax.rem(core + shift, 2) * feats, feats), feats)


def side_by_side(core, pair, whole, start, sem):
    rows, feats = pair[0].shape
    return [
        pltpu.make_async_copy(
            pair[shift],
            whole.at[pl.ds(start, rows), half_columns(core, shift, feats)],
            sem.at[shift],
        )
        for shift in range(2)
    ]


def weight_copies(refs, owned, w_in, w_out, sem):
    copies = []
    for at, ref in enumerate(refs):
        spot = pl.ds(at * owned, owned)
        copies.append(pltpu.make_async_copy(ref.at[pl.ds(0, owned)], w_in.at[spot], sem.at[0, at]))
        copies.append(
            pltpu.make_async_copy(ref.at[pl.ds(owned, owned)], w_out.at[spot], sem.at[1, at])
        )
    return copies


def bias_of(ref, owned):
    return ref[2 * owned : 2 * owned + BIAS_ROWS, :owned].astype(jnp.float32)


def run(copies, what):
    for copy in copies:
        getattr(copy, what)()


def activate(tok, w_in, bias):
    pre = lax.dot_general(
        tok, w_in, CONTRACT_LAST, preferred_element_type=jnp.float32
    ) + bias
    return gelu_parts(pre)


def dot_last(left, right):
    return lax.dot_general(left, right, CONTRACT_LAST, preferred_element_type=jnp.float32)


def dot_first(left, right):
    return lax.dot_general(left, right, CONTRACT_FIRST, preferred_element_type=jnp.float32)


def early_block(start, step, tok, cot, w_in, w_out, bias, two, act_ref, dpre_ref, mixed_ref, dpre):
    @pl.loop(0, 2)
    def _(sub):
        spot = pl.ds(pl.multiple_of(start + sub * step, step), step)
        value, slope = activate(tok[spot, :], w_in[...], bias[0:1, :])
        act = value.astype(jnp.bfloat16)
        act_ref[spot, :] = act[:, two:]
        dact = dot_last(cot[spot, :], w_out[...])
        terms = (dact * slope).astype(jnp.bfloat16)
        dpre[spot, :] = terms[:, :two]
        dpre_ref[spot, :] = terms[:, two:]
        mixed_ref[spot, :] = jnp.dot(
            act[:, :two], w_out[:two, :], preferred_element_type=jnp.float32
        )


def early_kernel(owned, *refs):
    pair_refs, w_refs = refs[:6], refs[6:9]
    act_ref, dpre_ref, mixed_ref, grad_ref, tok, cot, w_in, w_out, bias = refs[9:18]
    dpre, tok_sem, cot_sem, w_sem = refs[18:]
    core = lax.axis_index("core")
    rows = pair_refs[0].shape[1]
    w_copies = weight_copies(w_refs, owned, w_in, w_out, w_sem)
    loads = []
    for block in range(NEAR - 1):
        first, second = pair_refs[2 * block], pair_refs[2 * block + 1]
        loads.append(
            side_by_side(core, (first.at[0], second.at[0]), tok, block * rows, tok_sem.at[block])
            + side_by_side(core, (first.at[1], second.at[1]), cot, block * rows, cot_sem.at[block])
        )
    run(w_copies, "start")
    for load in loads:
        run(load, "start")
    for at, ref in enumerate(w_refs):
        bias[:, at * owned : (at + 1) * owned] = bias_of(ref, owned)
    run(w_copies, "wait")
    for block, load in enumerate(loads):
        run(load, "wait")
        early_block(
            block * rows, rows // 2, tok, cot, w_in, w_out, bias, 2 * owned,
            act_ref, dpre_ref, mixed_ref, dpre,
        )
    grad_ref[...] = dot_first(dpre[...], tok[...])


def output_kernel(owned, *refs):
    act_two, tok, early_mixed, w_in, w_out, bias, w_three = refs[:7]
    mine_ref, other_ref, slope_ref, w_in_all, w_out_all, bias_all = refs[7:13]
    w_last, sem = refs[13:]
    core = lax.axis_index("core")
    feats = mine_ref.shape[1]
    two, three = 2 * owned, 3 * owned
    first, last = pl.ds(0, three), pl.ds(three, owned)
    copies = [
        pltpu.make_async_copy(w_in, w_in_all.at[first], sem.at[0]),
        pltpu.make_async_copy(w_three.at[pl.ds(0, owned)], w_in_all.at[last], sem.at[1]),
        pltpu.make_async_copy(w_out, w_out_all.at[first], sem.at[2]),
        pltpu.make_async_copy(w_three.at[pl.ds(owned, owned)], w_out_all.at[last], sem.at[3]),
    ]
    run(copies, "start")
    bias_last = bias_of(w_three, owned)
    bias_all[:, :three] = bias[...]
    bias_all[:, three:] = bias_last
    w_last[:owned, :] = w_out[two:, :]
    w_last[owned:, :] = w_three[owned:two, :]
    step = tok.shape[0] // 6
    for at in range(6):
        spot = slice(at * step, (at + 1) * step)
        value, slope = activate(tok[spot, :], w_three[:owned, :], bias_last[0:1, :])
        slope_ref[spot, :] = slope
        act = jnp.concatenate([act_two[spot, :], value.astype(jnp.bfloat16)], axis=1)
        for shift, ref in enumerate((mine_ref, other_ref)):
            half = half_columns(core, shift, feats)
            ref[spot, :] = (
                early_mixed[spot, half]
                + jnp.dot(act, w_last[:, half], preferred_element_type=jnp.float32)
            ).astype(jnp.bfloat16)

    run(copies, "wait")


def gradient_kernel(dpre_two, tok, cot, slope, w_three, grad_ref, dpre):
    owned = slope.shape[1]
    step = tok.shape[0] // 6
    for at in range(6):
        spot = slice(at * step, (at + 1) * step)
        dact = dot_last(cot[spot, :], w_three[owned : 2 * owned, :])
        last = (dact * slope[spot, :]).astype(jnp.bfloat16)
        dpre[spot, :] = jnp.concatenate([dpre_two[spot, :], last], axis=1)
    grad_ref[...] = dot_first(dpre[...], tok[...])


def diagonal_kernel(owned, *refs):
    w_in, w_out, bias, grad_first, grad_last = refs[:5]
    tok_ref, cot_ref, far_ref = refs[5:8]
    mine_ref, other_ref, own_ref, one_ref, two_ref, three_ref = refs[8:14]
    tok, cot, dpre, tok_sem, cot_sem = refs[14:]
    core = lax.axis_index("core")
    rows, feats = mine_ref.shape
    two = 2 * owned
    first, second = pl.ds(0, rows), pl.ds(rows, rows)
    load = side_by_side(core, (tok_ref.at[first], far_ref.at[first]), tok, 0, tok_sem)
    load += side_by_side(
        core, (cot_ref.at[pl.ds(EXTRA, rows)], far_ref.at[second]), cot, 0, cot_sem
    )
    run(load, "start")
    run(load, "wait")
    step = rows // 2

    for sub in range(2):
        spot = slice(sub * step, (sub + 1) * step)
        value, slope = activate(tok[spot, :], w_in[...], bias[0:1, :])
        act = value.astype(jnp.bfloat16)
        dact = dot_last(cot[spot, :], w_out[...])
        dpre[spot, :] = (dact * slope).astype(jnp.bfloat16)
        for shift, ref in enumerate((mine_ref, other_ref)):
            ref[spot, :] = jnp.dot(
                act, w_out[:, half_columns(core, shift, feats)], preferred_element_type=jnp.float32
            ).astype(jnp.bfloat16)

    grad = grad_last[...] + dot_first(dpre[:, two:], tok[...])
    two_ref[...] = grad[:owned].astype(jnp.bfloat16)
    three_ref[...] = grad[owned:].astype(jnp.bfloat16)
    grad = grad_first[...] + dot_first(dpre[:, :two], tok[...])
    own_ref[...] = grad[:owned].astype(jnp.bfloat16)
    one_ref[...] = grad[owned:].astype(jnp.bfloat16)


def pair_kernel(rows, mine_ref, other_ref, *out_refs):
    for block, ref in enumerate(out_refs):
        spot = pl.ds(block * rows, rows)
        ref[:rows, :] = (
            mine_ref[spot, :].astype(jnp.float32) + other_ref[spot, :].astype(jnp.float32)
        ).astype(jnp.bfloat16)
        if ref.shape[0] > rows:
            ref[rows:, :] = jnp.zeros_like(ref[rows:, :])


def plane_kernel(own_ref, x_ref, y_ref, out_ref):
    rows = own_ref.shape[0]
    out_ref[...] = (
        own_ref[...].astype(jnp.float32)
        + x_ref[:rows, :].astype(jnp.float32)
        + y_ref[:rows, :].astype(jnp.float32)
    )


def vmem(count):
    return [pl.BlockSpec(memory_space=pltpu.VMEM)] * count


def anywhere(count):
    return [pl.BlockSpec(memory_space=pl.ANY)] * count


def bf16(*shape):
    return jax.ShapeDtypeStruct(shape, jnp.bfloat16)


def permute(value, there):
    pairs = []
    for f in range(4):
        for y in range(2):
            for x in range(2):
                for c in range(2):
                    to = there(f, y, x, c)
                    here = ((f * 2 + y) * 2 + x) * 2 + c
                    pairs.append((here, ((to[0] * 2 + to[1]) * 2 + to[2]) * 2 + to[3]))
    return lax.ppermute(value, AXES, pairs)


def to_x(value):
    return permute(value, lambda f, y, x, c: (f, y, 1 - x, c))


def to_y(value):
    return permute(value, lambda f, y, x, c: (f, 1 - y, x, c))


def to_diagonal(value):
    return permute(value, lambda f, y, x, c: (f, 1 - y, 1 - x, c))


def to_core(value):
    return permute(value, lambda f, y, x, c: (f, y, x, 1 - c))


def to_far(value, flip):
    return permute(value, lambda f, y, x, c: (f ^ flip, y, x, c))


def on_device_lines(tokens, cotangent, w_in, b_in, w_out):
    rows, feats = tokens.shape
    owned, width = w_in.shape
    units = 4 * owned
    count = NEAR * rows
    scale = 1.0 / math.sqrt(4 * count)
    params = pltpu.CompilerParams(vmem_limit_bytes=VMEM_LIMIT)
    dma = pltpu.SemaphoreType.DMA
    barrier = lax.optimization_barrier
    early_rows = (NEAR - 1) * rows

    def f32(*shape):
        return jax.ShapeDtypeStruct(shape, jnp.float32)

    def cost(flops, traffic):
        return pl.CostEstimate(flops=flops, bytes_accessed=traffic, transcendentals=0)

    bias_rows = jnp.pad(b_in.reshape(1, owned), ((0, BIAS_ROWS - 1), (0, width - owned)))
    own_w = jnp.concatenate([w_in, w_out, bias_rows], 0)
    own = jnp.stack([tokens, cotangent])
    w_two, w_one = to_far(own_w, 2), to_far(own_w, 1)
    from_x, from_y = to_x(own), to_y(own)
    own_other = to_core(own)
    from_x, from_y, own_other = barrier((from_x, from_y, own_other))
    tok_diag = to_y(from_x.reshape(2 * rows, feats)[: rows + EXTRA])
    cot_diag = to_x(from_y.reshape(2 * rows, feats)[rows - EXTRA :])
    x_other, y_other = to_core(from_x), to_core(from_y)
    w_three = to_far(w_two, 1)
    act_two, dpre_two, mixed_terms, grad_terms, tok, cot, w_in_three, w_out_three, bias = (
        pl.pallas_call(
            functools.partial(early_kernel, owned),
            out_shape=(
                bf16(early_rows, owned),
                bf16(early_rows, owned),
                f32(early_rows, width),
                f32(2 * owned, width),
                bf16(early_rows, width),
                bf16(early_rows, width),
                bf16(3 * owned, width),
                bf16(3 * owned, width),
                f32(BIAS_ROWS, 3 * owned),
            ),
            in_specs=anywhere(6) + vmem(3),
            out_specs=vmem(9),
            scratch_shapes=[
                pltpu.VMEM((early_rows, 2 * owned), jnp.bfloat16),
                dma((NEAR - 1, 2)),
                dma((NEAR - 1, 2)),
                dma((2, 3)),
            ],
            compiler_params=params,
            cost_estimate=cost(early_rows * units, early_rows),
            name="early",
        )(own, own_other, from_x, x_other, from_y, y_other, own_w, w_one, w_two)
    )

    mine, other, slope, w_in_all, w_out_all, bias = pl.pallas_call(
        functools.partial(output_kernel, owned),
        out_shape=(
            bf16(early_rows, feats),
            bf16(early_rows, feats),
            f32(early_rows, owned),
            bf16(units, width),
            bf16(units, width),
            f32(BIAS_ROWS, units),
        ),
        in_specs=vmem(7),
        out_specs=vmem(6),
        scratch_shapes=[pltpu.VMEM((2 * owned, width), jnp.bfloat16), dma((4,))],
        compiler_params=params,
        cost_estimate=cost(early_rows * units, early_rows),
        name="output",
    )(act_two, tok, mixed_terms, w_in_three, w_out_three, bias, w_three)
    tok_diag, cot_diag, other = barrier((tok_diag, cot_diag, other))
    received = to_core(other)
    diag_other = to_core(jnp.concatenate([tok_diag[:rows], cot_diag[EXTRA:]]))
    slope, tok_diag = barrier((slope, tok_diag))
    grad_last = pl.pallas_call(
        gradient_kernel,
        out_shape=f32(2 * owned, width),
        in_specs=vmem(5),
        out_specs=pl.BlockSpec(memory_space=pltpu.VMEM),
        scratch_shapes=[pltpu.VMEM((early_rows, 2 * owned), jnp.bfloat16)],
        compiler_params=params,
        cost_estimate=cost(GRADIENT_COST, early_rows),
        name="gradient",
    )(dpre_two, tok, cot, slope, w_three)

    mine, grad_last = barrier((mine, grad_last))
    sums = pl.pallas_call(
        functools.partial(pair_kernel, rows),
        out_shape=[bf16(rows, feats)] + [bf16(rows + MORE, feats)] * 2,
        in_specs=vmem(2),
        out_specs=vmem(NEAR - 1),
        compiler_params=params,
        cost_estimate=cost(rows, rows),
        name="pair_sum",
    )(mine, received)
    mixed_x, mixed_y = to_x(sums[1]), to_y(sums[2])
    grad_terms, mixed_own = barrier((grad_terms, sums[0]))

    mine_diag, other_diag, grad_own, grad_one, grad_two, grad_three = pl.pallas_call(
        functools.partial(diagonal_kernel, owned),
        out_shape=[bf16(rows, feats)] * 2 + [bf16(owned, width)] * 4,
        in_specs=vmem(5) + anywhere(3),
        out_specs=vmem(6),
        scratch_shapes=[
            pltpu.VMEM((rows, width), jnp.bfloat16),
            pltpu.VMEM((rows, width), jnp.bfloat16),
            pltpu.VMEM((rows, units), jnp.bfloat16),
            dma((2,)),
            dma((2,)),
        ],
        compiler_params=params,
        cost_estimate=cost(DIAGONAL_COST, rows),
        name="diagonal",
    )(
        w_in_all, w_out_all, bias, grad_terms, grad_last,
        tok_diag, cot_diag, diag_other,
    )
    received_diag = to_core(other_diag)
    relayed = to_far(grad_three, 1)
    (sum_diag,) = pl.pallas_call(
        functools.partial(pair_kernel, rows),
        out_shape=[bf16(rows, feats)],
        in_specs=vmem(2),
        out_specs=vmem(1),
        compiler_params=params,
        cost_estimate=cost(rows, rows),
        name="pair_sum_diagonal",
    )(mine_diag, received_diag)
    mixed_diag = to_diagonal(sum_diag)
    grad_one, grad_two, _ = barrier((grad_one, grad_two, sum_diag))
    from_one = to_far(grad_one, 1)
    (line_sum,) = pl.pallas_call(
        functools.partial(pair_kernel, owned),
        out_shape=[bf16(owned, width)],
        in_specs=vmem(2),
        out_specs=vmem(1),
        compiler_params=params,
        cost_estimate=cost(rows, rows),
        name="line_sum",
    )(grad_two, relayed)
    from_two = to_far(line_sum, 2)
    total = (
        grad_own.astype(jnp.float32)
        + from_one.astype(jnp.float32)
        + from_two.astype(jnp.float32)
    )
    mixed = pl.pallas_call(
        plane_kernel,
        out_shape=f32(rows, feats),
        in_specs=vmem(3),
        out_specs=pl.BlockSpec(memory_space=pltpu.VMEM),
        compiler_params=params,
        cost_estimate=cost(PLANE_COST, rows),
        name="plane_sum",
    )(mixed_own, mixed_x, mixed_y)
    mixed = (mixed + mixed_diag.astype(jnp.float32)).astype(jnp.bfloat16)
    return (mixed, total * scale)


def solution(mesh):
    dp, tensor = mesh.shape["dp"], mesh.shape["tensor"]
    far = dp // NEAR
    if tensor == 2 and far == 4:
        fine = Mesh(mesh.devices.reshape(far, 2, 2, tensor), AXES)
        rows, owners, halves = ("far", "y", "x"), AXES, "core"
        body = on_device_lines
    else:
        fine = Mesh(mesh.devices.reshape(far, NEAR, tensor), ("far", "near", "tensor"))
        rows, owners, halves = ("far", "near"), ("far", "near", "tensor"), "tensor"
        body = on_device_any
    in_specs = (P(rows, halves), P(rows, halves), P(owners, None), P(owners), P(owners, None))
    out_specs = (P(rows, halves), P(owners, None))
    return jax.shard_map(
        body, mesh=fine, in_specs=in_specs, out_specs=out_specs, check_vma=False
    )
```

```python
import functools
import math

import jax
import jax.numpy as jnp
from jax import lax
from jax.experimental import pallas as pl
from jax.experimental.pallas import tpu as pltpu
from jax.sharding import Mesh, PartitionSpec as P

NEAR = 4
AXES = ("far", "y", "x", "core")
CONTRACT_LAST = (((1,), (1,)), ((), ()))
CONTRACT_FIRST = (((0,), (0,)), ((), ()))
VMEM_LIMIT = 28 * 1024 * 1024
PLANE_COST = 10**10
GRADIENT_COST = 10**10
DIAGONAL_COST = 10**6
EXTRA = 48
BIAS_ROWS = 8
MORE = 16


def gelu_parts(value):
    coeff = 0.7978845608
    inner = coeff * (value + 0.044715 * value * value * value)
    tangent = jnp.tanh(inner)
    result = 0.5 * value * (1.0 + tangent)
    slope = 0.5 * (1.0 + tangent) + 0.5 * value * (1.0 - tangent * tangent) * coeff * (
        1.0 + 3.0 * 0.044715 * value * value
    )
    return (result, slope)


def on_device_any(tokens, cotangent, w_in, b_in, w_out):
    far, near, tensor = lax.axis_size("far"), lax.axis_size("near"), lax.axis_size("tensor")
    rows, feats = tokens.shape
    owned, width = w_in.shape
    scale = 1.0 / math.sqrt(rows * far * near)
    bias_rows = jnp.pad(b_in.reshape(1, owned), ((0, 15), (0, width - owned)))
    weights = lax.all_gather(jnp.concatenate([w_in, w_out, bias_rows], 0), "far", axis=0)
    in_rows = weights[:, :owned].reshape(far * owned, width)
    proj_rows = weights[:, owned : 2 * owned].reshape(far * owned, width)
    bias = weights[:, 2 * owned, :owned].reshape(far * owned).astype(jnp.float32)
    tok = lax.all_gather(tokens, ("near", "tensor"), axis=0).reshape(near, tensor, rows, feats)
    cot = lax.all_gather(cotangent, ("near", "tensor"), axis=0).reshape(near, tensor, rows, feats)
    tok_full = tok.transpose(0, 2, 1, 3).reshape(near * rows, width)
    cot_full = cot.transpose(0, 2, 1, 3).reshape(near * rows, width)
    pre = lax.dot_general(
        tok_full, in_rows, CONTRACT_LAST, preferred_element_type=jnp.float32
    ) + bias
    act_value, slope = gelu_parts(pre)
    act = act_value.astype(jnp.bfloat16)
    term = jnp.dot(act, proj_rows, preferred_element_type=jnp.float32).astype(jnp.bfloat16)
    term = term.reshape(near, rows, tensor, feats).transpose(0, 2, 1, 3)
    mixed = lax.psum_scatter(
        term.reshape(near * tensor, rows, feats), ("near", "tensor"), scatter_dimension=0
    )
    dact = lax.dot_general(cot_full, proj_rows, CONTRACT_LAST, preferred_element_type=jnp.float32)
    dpre = (dact * slope).astype(jnp.bfloat16)
    grad = lax.dot_general(dpre, tok_full, CONTRACT_FIRST, preferred_element_type=jnp.float32)
    grad_sum = lax.psum_scatter(grad.astype(jnp.bfloat16), "far", scatter_dimension=0, tiled=True)
    return (mixed, grad_sum.astype(jnp.float32) * scale)


def half_columns(core, shift, feats):
    return pl.ds(pl.multiple_of(lax.rem(core + shift, 2) * feats, feats), feats)


def side_by_side(core, pair, whole, start, sem):
    rows, feats = pair[0].shape
    return [
        pltpu.make_async_copy(
            pair[shift],
            whole.at[pl.ds(start, rows), half_columns(core, shift, feats)],
            sem.at[shift],
        )
        for shift in range(2)
    ]


def weight_copies(refs, owned, w_in, w_out, sem):
    copies = []
    for at, ref in enumerate(refs):
        spot = pl.ds(at * owned, owned)
        copies.append(pltpu.make_async_copy(ref.at[pl.ds(0, owned)], w_in.at[spot], sem.at[0, at]))
        copies.append(
            pltpu.make_async_copy(ref.at[pl.ds(owned, owned)], w_out.at[spot], sem.at[1, at])
        )
    return copies


def bias_of(ref, owned):
    return ref[2 * owned : 2 * owned + BIAS_ROWS, :owned].astype(jnp.float32)


def run(copies, what):
    for copy in copies:
        getattr(copy, what)()


def activate(tok, w_in, bias):
    pre = lax.dot_general(
        tok, w_in, CONTRACT_LAST, preferred_element_type=jnp.float32
    ) + bias
    return gelu_parts(pre)


def dot_last(left, right):
    return lax.dot_general(left, right, CONTRACT_LAST, preferred_element_type=jnp.float32)


def dot_first(left, right):
    return lax.dot_general(left, right, CONTRACT_FIRST, preferred_element_type=jnp.float32)


def early_block(start, step, tok, cot, w_in, w_out, bias, two, act_ref, dpre_ref, mixed_ref, dpre):
    @pl.loop(0, 2)
    def _(sub):
        spot = pl.ds(pl.multiple_of(start + sub * step, step), step)
        value, slope = activate(tok[spot, :], w_in[...], bias[0:1, :])
        act = value.astype(jnp.bfloat16)
        act_ref[spot, :] = act[:, two:]
        dact = dot_last(cot[spot, :], w_out[...])
        terms = (dact * slope).astype(jnp.bfloat16)
        dpre[spot, :] = terms[:, :two]
        dpre_ref[spot, :] = terms[:, two:]
        mixed_ref[spot, :] = jnp.dot(
            act[:, :two], w_out[:two, :], preferred_element_type=jnp.float32
        )


def early_kernel(owned, *refs):
    pair_refs, w_refs = refs[:6], refs[6:9]
    act_ref, dpre_ref, mixed_ref, grad_ref, tok, cot, w_in, w_out, bias = refs[9:18]
    dpre, tok_sem, cot_sem, w_sem = refs[18:]
    core = lax.axis_index("core")
    rows = pair_refs[0].shape[1]
    w_copies = weight_copies(w_refs, owned, w_in, w_out, w_sem)
    loads = []
    for block in range(NEAR - 1):
        first, second = pair_refs[2 * block], pair_refs[2 * block + 1]
        loads.append(
            side_by_side(core, (first.at[0], second.at[0]), tok, block * rows, tok_sem.at[block])
            + side_by_side(core, (first.at[1], second.at[1]), cot, block * rows, cot_sem.at[block])
        )
    run(w_copies, "start")
    for load in loads:
        run(load, "start")
    for at, ref in enumerate(w_refs):
        bias[:, at * owned : (at + 1) * owned] = bias_of(ref, owned)
    run(w_copies, "wait")
    for block, load in enumerate(loads):
        run(load, "wait")
        early_block(
            block * rows, rows // 2, tok, cot, w_in, w_out, bias, 2 * owned,
            act_ref, dpre_ref, mixed_ref, dpre,
        )
    grad_ref[...] = dot_first(dpre[...], tok[...])


def output_kernel(owned, *refs):
    act_two, tok, early_mixed, w_in, w_out, bias, w_three = refs[:7]
    mine_ref, other_ref, slope_ref, w_in_all, w_out_all, bias_all = refs[7:13]
    w_last, sem = refs[13:]
    core = lax.axis_index("core")
    feats = mine_ref.shape[1]
    two, three = 2 * owned, 3 * owned
    first, last = pl.ds(0, three), pl.ds(three, owned)
    copies = [
        pltpu.make_async_copy(w_in, w_in_all.at[first], sem.at[0]),
        pltpu.make_async_copy(w_three.at[pl.ds(0, owned)], w_in_all.at[last], sem.at[1]),
        pltpu.make_async_copy(w_out, w_out_all.at[first], sem.at[2]),
        pltpu.make_async_copy(w_three.at[pl.ds(owned, owned)], w_out_all.at[last], sem.at[3]),
    ]
    run(copies, "start")
    bias_last = bias_of(w_three, owned)
    bias_all[:, :three] = bias[...]
    bias_all[:, three:] = bias_last
    w_last[:owned, :] = w_out[two:, :]
    w_last[owned:, :] = w_three[owned:two, :]
    step = tok.shape[0] // 6
    for at in range(6):
        spot = slice(at * step, (at + 1) * step)
        value, slope = activate(tok[spot, :], w_three[:owned, :], bias_last[0:1, :])
        slope_ref[spot, :] = slope
        act = jnp.concatenate([act_two[spot, :], value.astype(jnp.bfloat16)], axis=1)
        for shift, ref in enumerate((mine_ref, other_ref)):
            half = half_columns(core, shift, feats)
            ref[spot, :] = (
                early_mixed[spot, half]
                + jnp.dot(act, w_last[:, half], preferred_element_type=jnp.float32)
            ).astype(jnp.bfloat16)

    run(copies, "wait")


def gradient_kernel(dpre_two, tok, cot, slope, w_three, grad_ref, dpre):
    owned = slope.shape[1]
    step = tok.shape[0] // 6
    for at in range(6):
        spot = slice(at * step, (at + 1) * step)
        dact = dot_last(cot[spot, :], w_three[owned : 2 * owned, :])
        last = (dact * slope[spot, :]).astype(jnp.bfloat16)
        dpre[spot, :] = jnp.concatenate([dpre_two[spot, :], last], axis=1)
    grad_ref[...] = dot_first(dpre[...], tok[...])


def diagonal_kernel(owned, *refs):
    w_in, w_out, bias, grad_first, grad_last = refs[:5]
    tok_ref, cot_ref, far_ref = refs[5:8]
    mine_ref, other_ref, own_ref, one_ref, two_ref, three_ref = refs[8:14]
    tok, cot, dpre, tok_sem, cot_sem = refs[14:]
    core = lax.axis_index("core")
    rows, feats = mine_ref.shape
    two = 2 * owned
    first, second = pl.ds(0, rows), pl.ds(rows, rows)
    load = side_by_side(core, (tok_ref.at[first], far_ref.at[first]), tok, 0, tok_sem)
    cot_load = side_by_side(core, (cot_ref, far_ref.at[second]), cot, 0, cot_sem)
    run(load + cot_load, "start")
    run(load, "wait")
    step = rows // 2
    slopes = []
    for sub in range(2):
        spot = slice(sub * step, (sub + 1) * step)
        value, slope = activate(tok[spot, :], w_in[...], bias[0:1, :])
        slopes.append(slope)
        act = value.astype(jnp.bfloat16)
        for shift, ref in enumerate((mine_ref, other_ref)):
            ref[spot, :] = jnp.dot(
                act, w_out[:, half_columns(core, shift, feats)], preferred_element_type=jnp.float32
            ).astype(jnp.bfloat16)
    run(cot_load, "wait")
    for sub in range(2):
        spot = slice(sub * step, (sub + 1) * step)
        dpre[spot, :] = (dot_last(cot[spot, :], w_out[...]) * slopes[sub]).astype(jnp.bfloat16)

    grad = grad_last[...] + dot_first(dpre[:, two:], tok[...])
    two_ref[...] = grad[:owned].astype(jnp.bfloat16)
    three_ref[...] = grad[owned:].astype(jnp.bfloat16)
    grad = grad_first[...] + dot_first(dpre[:, :two], tok[...])
    own_ref[...] = grad[:owned].astype(jnp.bfloat16)
    one_ref[...] = grad[owned:].astype(jnp.bfloat16)


def pair_kernel(rows, mine_ref, other_ref, *out_refs):
    for block, ref in enumerate(out_refs):
        spot = pl.ds(block * rows, rows)
        ref[:rows, :] = (
            mine_ref[spot, :].astype(jnp.float32) + other_ref[spot, :].astype(jnp.float32)
        ).astype(jnp.bfloat16)
        if ref.shape[0] > rows:
            ref[rows:, :] = jnp.zeros_like(ref[rows:, :])


def plane_kernel(own_ref, x_ref, y_ref, out_ref):
    rows = own_ref.shape[0]
    out_ref[...] = (
        own_ref[...].astype(jnp.float32)
        + x_ref[:rows, :].astype(jnp.float32)
        + y_ref[:rows, :].astype(jnp.float32)
    )


def vmem(count):
    return [pl.BlockSpec(memory_space=pltpu.VMEM)] * count


def anywhere(count):
    return [pl.BlockSpec(memory_space=pl.ANY)] * count


def bf16(*shape):
    return jax.ShapeDtypeStruct(shape, jnp.bfloat16)


def permute(value, there):
    pairs = []
    for f in range(4):
        for y in range(2):
            for x in range(2):
                for c in range(2):
                    to = there(f, y, x, c)
                    here = ((f * 2 + y) * 2 + x) * 2 + c
                    pairs.append((here, ((to[0] * 2 + to[1]) * 2 + to[2]) * 2 + to[3]))
    return lax.ppermute(value, AXES, pairs)


def to_x(value):
    return permute(value, lambda f, y, x, c: (f, y, 1 - x, c))


def to_y(value):
    return permute(value, lambda f, y, x, c: (f, 1 - y, x, c))


def to_diagonal(value):
    return permute(value, lambda f, y, x, c: (f, 1 - y, 1 - x, c))


def to_core(value):
    return permute(value, lambda f, y, x, c: (f, y, x, 1 - c))


def to_far(value, flip):
    return permute(value, lambda f, y, x, c: (f ^ flip, y, x, c))


def on_device_lines(tokens, cotangent, w_in, b_in, w_out):
    rows, feats = tokens.shape
    owned, width = w_in.shape
    units = 4 * owned
    count = NEAR * rows
    scale = 1.0 / math.sqrt(4 * count)
    params = pltpu.CompilerParams(vmem_limit_bytes=VMEM_LIMIT)
    dma = pltpu.SemaphoreType.DMA
    barrier = lax.optimization_barrier
    early_rows = (NEAR - 1) * rows

    def f32(*shape):
        return jax.ShapeDtypeStruct(shape, jnp.float32)

    def cost(flops, traffic):
        return pl.CostEstimate(flops=flops, bytes_accessed=traffic, transcendentals=0)

    bias_rows = jnp.pad(b_in.reshape(1, owned), ((0, BIAS_ROWS - 1), (0, width - owned)))
    own_w = jnp.concatenate([w_in, w_out, bias_rows], 0)
    own = jnp.stack([tokens, cotangent])
    w_two, w_one = to_far(own_w, 2), to_far(own_w, 1)
    from_x, from_y = to_x(own), to_y(own)
    own_other = to_core(own)
    from_x, from_y, own_other = barrier((from_x, from_y, own_other))
    tok_diag = to_y(from_x.reshape(2 * rows, feats)[: rows + EXTRA])
    cot_diag = to_x(from_y[1])
    x_other, y_other = to_core(from_x), to_core(from_y)
    w_three = to_far(w_two, 1)
    act_two, dpre_two, mixed_terms, grad_terms, tok, cot, w_in_three, w_out_three, bias = (
        pl.pallas_call(
            functools.partial(early_kernel, owned),
            out_shape=(
                bf16(early_rows, owned),
                bf16(early_rows, owned),
                f32(early_rows, width),
                f32(2 * owned, width),
                bf16(early_rows, width),
                bf16(early_rows, width),
                bf16(3 * owned, width),
                bf16(3 * owned, width),
                f32(BIAS_ROWS, 3 * owned),
            ),
            in_specs=anywhere(6) + vmem(3),
            out_specs=vmem(9),
            scratch_shapes=[
                pltpu.VMEM((early_rows, 2 * owned), jnp.bfloat16),
                dma((NEAR - 1, 2)),
                dma((NEAR - 1, 2)),
                dma((2, 3)),
            ],
            compiler_params=params,
            cost_estimate=cost(early_rows * units, early_rows),
            name="early",
        )(own, own_other, from_x, x_other, from_y, y_other, own_w, w_one, w_two)
    )

    mine, other, slope, w_in_all, w_out_all, bias = pl.pallas_call(
        functools.partial(output_kernel, owned),
        out_shape=(
            bf16(early_rows, feats),
            bf16(early_rows, feats),
            f32(early_rows, owned),
            bf16(units, width),
            bf16(units, width),
            f32(BIAS_ROWS, units),
        ),
        in_specs=vmem(7),
        out_specs=vmem(6),
        scratch_shapes=[pltpu.VMEM((2 * owned, width), jnp.bfloat16), dma((4,))],
        compiler_params=params,
        cost_estimate=cost(early_rows * units, early_rows),
        name="output",
    )(act_two, tok, mixed_terms, w_in_three, w_out_three, bias, w_three)
    tok_diag, cot_diag, other = barrier((tok_diag, cot_diag, other))
    received = to_core(other)
    diag_other = to_core(jnp.concatenate([tok_diag[:rows], cot_diag]))
    slope, tok_diag = barrier((slope, tok_diag))
    grad_last = pl.pallas_call(
        gradient_kernel,
        out_shape=f32(2 * owned, width),
        in_specs=vmem(5),
        out_specs=pl.BlockSpec(memory_space=pltpu.VMEM),
        scratch_shapes=[pltpu.VMEM((early_rows, 2 * owned), jnp.bfloat16)],
        compiler_params=params,
        cost_estimate=cost(GRADIENT_COST, early_rows),
        name="gradient",
    )(dpre_two, tok, cot, slope, w_three)

    mine, grad_last = barrier((mine, grad_last))
    sums = pl.pallas_call(
        functools.partial(pair_kernel, rows),
        out_shape=[bf16(rows, feats)] + [bf16(rows + MORE, feats)] * 2,
        in_specs=vmem(2),
        out_specs=vmem(NEAR - 1),
        compiler_params=params,
        cost_estimate=cost(rows, rows),
        name="pair_sum",
    )(mine, received)
    mixed_x, mixed_y = to_x(sums[1]), to_y(sums[2])
    grad_terms, mixed_own = barrier((grad_terms, sums[0]))

    mine_diag, other_diag, grad_own, grad_one, grad_two, grad_three = pl.pallas_call(
        functools.partial(diagonal_kernel, owned),
        out_shape=[bf16(rows, feats)] * 2 + [bf16(owned, width)] * 4,
        in_specs=vmem(5) + anywhere(3),
        out_specs=vmem(6),
        scratch_shapes=[
            pltpu.VMEM((rows, width), jnp.bfloat16),
            pltpu.VMEM((rows, width), jnp.bfloat16),
            pltpu.VMEM((rows, units), jnp.bfloat16),
            dma((2,)),
            dma((2,)),
        ],
        compiler_params=params,
        cost_estimate=cost(DIAGONAL_COST, rows),
        name="diagonal",
    )(
        w_in_all, w_out_all, bias, grad_terms, grad_last,
        tok_diag, cot_diag, diag_other,
    )
    received_diag = to_core(other_diag)
    relayed = to_far(grad_three, 1)
    (sum_diag,) = pl.pallas_call(
        functools.partial(pair_kernel, rows),
        out_shape=[bf16(rows, feats)],
        in_specs=vmem(2),
        out_specs=vmem(1),
        compiler_params=params,
        cost_estimate=cost(rows, rows),
        name="pair_sum_diagonal",
    )(mine_diag, received_diag)
    mixed_diag = to_diagonal(sum_diag)
    grad_one, grad_two, _ = barrier((grad_one, grad_two, sum_diag))
    from_one = to_far(grad_one, 1)
    (line_sum,) = pl.pallas_call(
        functools.partial(pair_kernel, owned),
        out_shape=[bf16(owned, width)],
        in_specs=vmem(2),
        out_specs=vmem(1),
        compiler_params=params,
        cost_estimate=cost(rows, rows),
        name="line_sum",
    )(grad_two, relayed)
    from_two = to_far(line_sum, 2)
    mixed = pl.pallas_call(
        plane_kernel,
        out_shape=f32(rows, feats),
        in_specs=vmem(3),
        out_specs=pl.BlockSpec(memory_space=pltpu.VMEM),
        compiler_params=params,
        cost_estimate=cost(PLANE_COST, rows),
        name="plane_sum",
    )(mixed_own, mixed_x, mixed_y)
    mixed = (mixed + mixed_diag.astype(jnp.float32)).astype(jnp.bfloat16)
    from_two, mixed = barrier((from_two, mixed))
    total = (
        grad_own.astype(jnp.float32)
        + from_one.astype(jnp.float32)
        + from_two.astype(jnp.float32)
    )
    return (mixed, total * scale)


def solution(mesh):
    dp, tensor = mesh.shape["dp"], mesh.shape["tensor"]
    far = dp // NEAR
    if tensor == 2 and far == 4:
        fine = Mesh(mesh.devices.reshape(far, 2, 2, tensor), AXES)
        rows, owners, halves = ("far", "y", "x"), AXES, "core"
        body = on_device_lines
    else:
        fine = Mesh(mesh.devices.reshape(far, NEAR, tensor), ("far", "near", "tensor"))
        rows, owners, halves = ("far", "near"), ("far", "near", "tensor"), "tensor"
        body = on_device_any
    in_specs = (P(rows, halves), P(rows, halves), P(owners, None), P(owners), P(owners, None))
    out_specs = (P(rows, halves), P(owners, None))
    return jax.shard_map(
        body, mesh=fine, in_specs=in_specs, out_specs=out_specs, check_vma=False
    )
```

```python
import functools
import math

import jax
import jax.numpy as jnp
from jax import lax
from jax.experimental import pallas as pl
from jax.experimental.pallas import tpu as pltpu
from jax.sharding import Mesh, PartitionSpec as P

NEAR = 4
AXES = ("far", "y", "x", "core")
CONTRACT_LAST = (((1,), (1,)), ((), ()))
CONTRACT_FIRST = (((0,), (0,)), ((), ()))
VMEM_LIMIT = 28 * 1024 * 1024
PLANE_COST = 10**10
GRADIENT_COST = 10**10
DIAGONAL_COST = 10**6
EXTRA = 48
PARTS = 2
BIAS_ROWS = 8
MORE = 16


def gelu_parts(value):
    coeff = 0.7978845608
    inner = coeff * (value + 0.044715 * value * value * value)
    tangent = jnp.tanh(inner)
    result = 0.5 * value * (1.0 + tangent)
    slope = 0.5 * (1.0 + tangent) + 0.5 * value * (1.0 - tangent * tangent) * coeff * (
        1.0 + 3.0 * 0.044715 * value * value
    )
    return (result, slope)


def on_device_any(tokens, cotangent, w_in, b_in, w_out):
    far, near, tensor = lax.axis_size("far"), lax.axis_size("near"), lax.axis_size("tensor")
    rows, feats = tokens.shape
    owned, width = w_in.shape
    scale = 1.0 / math.sqrt(rows * far * near)
    bias_rows = jnp.pad(b_in.reshape(1, owned), ((0, 15), (0, width - owned)))
    weights = lax.all_gather(jnp.concatenate([w_in, w_out, bias_rows], 0), "far", axis=0)
    in_rows = weights[:, :owned].reshape(far * owned, width)
    proj_rows = weights[:, owned : 2 * owned].reshape(far * owned, width)
    bias = weights[:, 2 * owned, :owned].reshape(far * owned).astype(jnp.float32)
    tok = lax.all_gather(tokens, ("near", "tensor"), axis=0).reshape(near, tensor, rows, feats)
    cot = lax.all_gather(cotangent, ("near", "tensor"), axis=0).reshape(near, tensor, rows, feats)
    tok_full = tok.transpose(0, 2, 1, 3).reshape(near * rows, width)
    cot_full = cot.transpose(0, 2, 1, 3).reshape(near * rows, width)
    pre = lax.dot_general(
        tok_full, in_rows, CONTRACT_LAST, preferred_element_type=jnp.float32
    ) + bias
    act_value, slope = gelu_parts(pre)
    act = act_value.astype(jnp.bfloat16)
    term = jnp.dot(act, proj_rows, preferred_element_type=jnp.float32).astype(jnp.bfloat16)
    term = term.reshape(near, rows, tensor, feats).transpose(0, 2, 1, 3)
    mixed = lax.psum_scatter(
        term.reshape(near * tensor, rows, feats), ("near", "tensor"), scatter_dimension=0
    )
    dact = lax.dot_general(cot_full, proj_rows, CONTRACT_LAST, preferred_element_type=jnp.float32)
    dpre = (dact * slope).astype(jnp.bfloat16)
    grad = lax.dot_general(dpre, tok_full, CONTRACT_FIRST, preferred_element_type=jnp.float32)
    grad_sum = lax.psum_scatter(grad.astype(jnp.bfloat16), "far", scatter_dimension=0, tiled=True)
    return (mixed, grad_sum.astype(jnp.float32) * scale)


def half_columns(core, shift, feats):
    return pl.ds(pl.multiple_of(lax.rem(core + shift, 2) * feats, feats), feats)


def side_by_side(core, pair, whole, start, sem):
    rows, feats = pair[0].shape
    return [
        pltpu.make_async_copy(
            pair[shift],
            whole.at[pl.ds(start, rows), half_columns(core, shift, feats)],
            sem.at[shift],
        )
        for shift in range(2)
    ]


def weight_copies(refs, owned, w_in, w_out, sem):
    copies = []
    for at, ref in enumerate(refs):
        spot = pl.ds(at * owned, owned)
        copies.append(pltpu.make_async_copy(ref.at[pl.ds(0, owned)], w_in.at[spot], sem.at[0, at]))
        copies.append(
            pltpu.make_async_copy(ref.at[pl.ds(owned, owned)], w_out.at[spot], sem.at[1, at])
        )
    return copies


def bias_of(ref, owned):
    return ref[2 * owned : 2 * owned + BIAS_ROWS, :owned].astype(jnp.float32)


def run(copies, what):
    for copy in copies:
        getattr(copy, what)()


def activate(tok, w_in, bias):
    pre = lax.dot_general(
        tok, w_in, CONTRACT_LAST, preferred_element_type=jnp.float32
    ) + bias
    return gelu_parts(pre)


def dot_last(left, right):
    return lax.dot_general(left, right, CONTRACT_LAST, preferred_element_type=jnp.float32)


def dot_first(left, right):
    return lax.dot_general(left, right, CONTRACT_FIRST, preferred_element_type=jnp.float32)


def early_block(start, step, tok, cot, w_in, w_out, bias, two, act_ref, dpre_ref, mixed_ref, dpre):
    @pl.loop(0, 2)
    def _(sub):
        spot = pl.ds(pl.multiple_of(start + sub * step, step), step)
        value, slope = activate(tok[spot, :], w_in[...], bias[0:1, :])
        act = value.astype(jnp.bfloat16)
        act_ref[spot, :] = act[:, two:]
        dact = dot_last(cot[spot, :], w_out[...])
        terms = (dact * slope).astype(jnp.bfloat16)
        dpre[spot, :] = terms[:, :two]
        dpre_ref[spot, :] = terms[:, two:]
        mixed_ref[spot, :] = jnp.dot(
            act[:, :two], w_out[:two, :], preferred_element_type=jnp.float32
        )


def early_kernel(owned, *refs):
    pair_refs, w_refs = refs[:6], refs[6:9]
    act_ref, dpre_ref, mixed_ref, grad_ref, tok, cot, w_in, w_out, bias = refs[9:18]
    dpre, tok_sem, cot_sem, w_sem = refs[18:]
    core = lax.axis_index("core")
    rows = pair_refs[0].shape[1]
    w_copies = weight_copies(w_refs, owned, w_in, w_out, w_sem)
    loads = []
    for block in range(NEAR - 1):
        first, second = pair_refs[2 * block], pair_refs[2 * block + 1]
        loads.append(
            side_by_side(core, (first.at[0], second.at[0]), tok, block * rows, tok_sem.at[block])
            + side_by_side(core, (first.at[1], second.at[1]), cot, block * rows, cot_sem.at[block])
        )
    run(w_copies, "start")
    for load in loads:
        run(load, "start")
    for at, ref in enumerate(w_refs):
        bias[:, at * owned : (at + 1) * owned] = bias_of(ref, owned)
    run(w_copies, "wait")
    for block, load in enumerate(loads):
        run(load, "wait")
        early_block(
            block * rows, rows // 2, tok, cot, w_in, w_out, bias, 2 * owned,
            act_ref, dpre_ref, mixed_ref, dpre,
        )
    grad_ref[...] = dot_first(dpre[...], tok[...])


def output_kernel(owned, *refs):
    act_two, tok, early_mixed, w_in, w_out, bias, w_three = refs[:7]
    mine_ref, other_ref, slope_ref, w_in_all, w_out_all, bias_all = refs[7:13]
    w_last, sem = refs[13:]
    core = lax.axis_index("core")
    feats = mine_ref.shape[1]
    two, three = 2 * owned, 3 * owned
    first, last = pl.ds(0, three), pl.ds(three, owned)
    copies = [
        pltpu.make_async_copy(w_in, w_in_all.at[first], sem.at[0]),
        pltpu.make_async_copy(w_three.at[pl.ds(0, owned)], w_in_all.at[last], sem.at[1]),
        pltpu.make_async_copy(w_out, w_out_all.at[first], sem.at[2]),
        pltpu.make_async_copy(w_three.at[pl.ds(owned, owned)], w_out_all.at[last], sem.at[3]),
    ]
    run(copies, "start")
    bias_last = bias_of(w_three, owned)
    bias_all[:, :three] = bias[...]
    bias_all[:, three:] = bias_last
    w_last[:owned, :] = w_out[two:, :]
    w_last[owned:, :] = w_three[owned:two, :]
    step = tok.shape[0] // 6
    for at in range(6):
        spot = slice(at * step, (at + 1) * step)
        value, slope = activate(tok[spot, :], w_three[:owned, :], bias_last[0:1, :])
        slope_ref[spot, :] = slope
        act = jnp.concatenate([act_two[spot, :], value.astype(jnp.bfloat16)], axis=1)
        for shift, ref in enumerate((mine_ref, other_ref)):
            half = half_columns(core, shift, feats)
            ref[spot, :] = (
                early_mixed[spot, half]
                + jnp.dot(act, w_last[:, half], preferred_element_type=jnp.float32)
            ).astype(jnp.bfloat16)

    run(copies, "wait")


def gradient_kernel(dpre_two, tok, cot, slope, w_three, grad_ref, dpre):
    owned = slope.shape[1]
    step = tok.shape[0] // 6
    for at in range(6):
        spot = slice(at * step, (at + 1) * step)
        dact = dot_last(cot[spot, :], w_three[owned : 2 * owned, :])
        last = (dact * slope[spot, :]).astype(jnp.bfloat16)
        dpre[spot, :] = jnp.concatenate([dpre_two[spot, :], last], axis=1)
    grad_ref[...] = dot_first(dpre[...], tok[...])


def diagonal_kernel(owned, *refs):
    w_in, w_out, bias, grad_first, grad_last = refs[:5]
    tok_ref, cot_ref, far_ref = refs[5:8]
    mine_ref, other_ref, own_ref, one_ref = refs[8:12]
    two_refs, three_refs = refs[12 : 12 + PARTS], refs[12 + PARTS : 12 + 2 * PARTS]
    tok, cot, dpre, tok_sem, cot_sem = refs[12 + 2 * PARTS :]
    core = lax.axis_index("core")
    rows, feats = mine_ref.shape
    two = 2 * owned
    first, second = pl.ds(0, rows), pl.ds(rows, rows)
    load = side_by_side(core, (tok_ref.at[first], far_ref.at[first]), tok, 0, tok_sem)
    cot_load = side_by_side(core, (cot_ref, far_ref.at[second]), cot, 0, cot_sem)
    run(load + cot_load, "start")
    run(load, "wait")
    step = rows // 2
    for sub in range(2):
        spot = slice(sub * step, (sub + 1) * step)
        value, slope = activate(tok[spot, :], w_in[...], bias[0:1, :])
        act = value.astype(jnp.bfloat16)
        if sub == 0:
            run(cot_load, "wait")
        dact = dot_last(cot[spot, :], w_out[...])
        dpre[spot, :] = (dact * slope).astype(jnp.bfloat16)
        for shift, ref in enumerate((mine_ref, other_ref)):
            ref[spot, :] = jnp.dot(
                act, w_out[:, half_columns(core, shift, feats)], preferred_element_type=jnp.float32
            ).astype(jnp.bfloat16)

    grad = grad_last[...] + dot_first(dpre[:, two:], tok[...])
    part = owned // PARTS
    for at in range(PARTS):
        two_refs[at][...] = grad[at * part : (at + 1) * part].astype(jnp.bfloat16)
        three_refs[at][...] = grad[owned + at * part : owned + (at + 1) * part].astype(jnp.bfloat16)
    grad = grad_first[...] + dot_first(dpre[:, :two], tok[...])
    own_ref[...] = grad[:owned].astype(jnp.bfloat16)
    one_ref[...] = grad[owned:].astype(jnp.bfloat16)


def pair_kernel(rows, mine_ref, other_ref, *out_refs):
    for block, ref in enumerate(out_refs):
        spot = pl.ds(block * rows, rows)
        ref[:rows, :] = (
            mine_ref[spot, :].astype(jnp.float32) + other_ref[spot, :].astype(jnp.float32)
        ).astype(jnp.bfloat16)
        if ref.shape[0] > rows:
            ref[rows:, :] = jnp.zeros_like(ref[rows:, :])


def plane_kernel(own_ref, x_ref, y_ref, out_ref):
    rows = own_ref.shape[0]
    out_ref[...] = (
        own_ref[...].astype(jnp.float32)
        + x_ref[:rows, :].astype(jnp.float32)
        + y_ref[:rows, :].astype(jnp.float32)
    )


def vmem(count):
    return [pl.BlockSpec(memory_space=pltpu.VMEM)] * count


def anywhere(count):
    return [pl.BlockSpec(memory_space=pl.ANY)] * count


def bf16(*shape):
    return jax.ShapeDtypeStruct(shape, jnp.bfloat16)


def permute(value, there):
    pairs = []
    for f in range(4):
        for y in range(2):
            for x in range(2):
                for c in range(2):
                    to = there(f, y, x, c)
                    here = ((f * 2 + y) * 2 + x) * 2 + c
                    pairs.append((here, ((to[0] * 2 + to[1]) * 2 + to[2]) * 2 + to[3]))
    return lax.ppermute(value, AXES, pairs)


def to_x(value):
    return permute(value, lambda f, y, x, c: (f, y, 1 - x, c))


def to_y(value):
    return permute(value, lambda f, y, x, c: (f, 1 - y, x, c))


def to_diagonal(value):
    return permute(value, lambda f, y, x, c: (f, 1 - y, 1 - x, c))


def to_core(value):
    return permute(value, lambda f, y, x, c: (f, y, x, 1 - c))


def to_far(value, flip):
    return permute(value, lambda f, y, x, c: (f ^ flip, y, x, c))


def on_device_lines(tokens, cotangent, w_in, b_in, w_out):
    rows, feats = tokens.shape
    owned, width = w_in.shape
    units = 4 * owned
    count = NEAR * rows
    scale = 1.0 / math.sqrt(4 * count)
    params = pltpu.CompilerParams(vmem_limit_bytes=VMEM_LIMIT)
    dma = pltpu.SemaphoreType.DMA
    barrier = lax.optimization_barrier
    early_rows = (NEAR - 1) * rows

    def f32(*shape):
        return jax.ShapeDtypeStruct(shape, jnp.float32)

    def cost(flops, traffic):
        return pl.CostEstimate(flops=flops, bytes_accessed=traffic, transcendentals=0)

    bias_rows = jnp.pad(b_in.reshape(1, owned), ((0, BIAS_ROWS - 1), (0, width - owned)))
    own_w = jnp.concatenate([w_in, w_out, bias_rows], 0)
    own = jnp.stack([tokens, cotangent])
    w_two, w_one = to_far(own_w, 2), to_far(own_w, 1)
    from_x, from_y = to_x(own), to_y(own)
    own_other = to_core(own)
    from_x, from_y, own_other = barrier((from_x, from_y, own_other))
    tok_diag = to_y(from_x.reshape(2 * rows, feats)[: rows + EXTRA])
    cot_diag = to_x(from_y[1])
    x_other, y_other = to_core(from_x), to_core(from_y)
    w_three = to_far(w_two, 1)
    act_two, dpre_two, mixed_terms, grad_terms, tok, cot, w_in_three, w_out_three, bias = (
        pl.pallas_call(
            functools.partial(early_kernel, owned),
            out_shape=(
                bf16(early_rows, owned),
                bf16(early_rows, owned),
                f32(early_rows, width),
                f32(2 * owned, width),
                bf16(early_rows, width),
                bf16(early_rows, width),
                bf16(3 * owned, width),
                bf16(3 * owned, width),
                f32(BIAS_ROWS, 3 * owned),
            ),
            in_specs=anywhere(6) + vmem(3),
            out_specs=vmem(9),
            scratch_shapes=[
                pltpu.VMEM((early_rows, 2 * owned), jnp.bfloat16),
                dma((NEAR - 1, 2)),
                dma((NEAR - 1, 2)),
                dma((2, 3)),
            ],
            compiler_params=params,
            cost_estimate=cost(early_rows * units, early_rows),
            name="early",
        )(own, own_other, from_x, x_other, from_y, y_other, own_w, w_one, w_two)
    )

    mine, other, slope, w_in_all, w_out_all, bias = pl.pallas_call(
        functools.partial(output_kernel, owned),
        out_shape=(
            bf16(early_rows, feats),
            bf16(early_rows, feats),
            f32(early_rows, owned),
            bf16(units, width),
            bf16(units, width),
            f32(BIAS_ROWS, units),
        ),
        in_specs=vmem(7),
        out_specs=vmem(6),
        scratch_shapes=[pltpu.VMEM((2 * owned, width), jnp.bfloat16), dma((4,))],
        compiler_params=params,
        cost_estimate=cost(early_rows * units, early_rows),
        name="output",
    )(act_two, tok, mixed_terms, w_in_three, w_out_three, bias, w_three)
    tok_diag, cot_diag, other = barrier((tok_diag, cot_diag, other))
    received = to_core(other)
    diag_other = to_core(jnp.concatenate([tok_diag[:rows], cot_diag]))
    slope, tok_diag = barrier((slope, tok_diag))
    grad_last = pl.pallas_call(
        gradient_kernel,
        out_shape=f32(2 * owned, width),
        in_specs=vmem(5),
        out_specs=pl.BlockSpec(memory_space=pltpu.VMEM),
        scratch_shapes=[pltpu.VMEM((early_rows, 2 * owned), jnp.bfloat16)],
        compiler_params=params,
        cost_estimate=cost(GRADIENT_COST, early_rows),
        name="gradient",
    )(dpre_two, tok, cot, slope, w_three)

    mine, grad_last = barrier((mine, grad_last))
    sums = pl.pallas_call(
        functools.partial(pair_kernel, rows),
        out_shape=[bf16(rows, feats)] + [bf16(rows + MORE, feats)] * 2,
        in_specs=vmem(2),
        out_specs=vmem(NEAR - 1),
        compiler_params=params,
        cost_estimate=cost(rows, rows),
        name="pair_sum",
    )(mine, received)
    mixed_x, mixed_y = to_x(sums[1]), to_y(sums[2])
    grad_terms, mixed_own = barrier((grad_terms, sums[0]))

    mine_diag, other_diag, grad_own, grad_one, *grad_far = pl.pallas_call(
        functools.partial(diagonal_kernel, owned),
        out_shape=[bf16(rows, feats)] * 2
        + [bf16(owned, width)] * 2
        + [bf16(owned // PARTS, width)] * (2 * PARTS),
        in_specs=vmem(5) + anywhere(3),
        out_specs=vmem(4 + 2 * PARTS),
        scratch_shapes=[
            pltpu.VMEM((rows, width), jnp.bfloat16),
            pltpu.VMEM((rows, width), jnp.bfloat16),
            pltpu.VMEM((rows, units), jnp.bfloat16),
            dma((2,)),
            dma((2,)),
        ],
        compiler_params=params,
        cost_estimate=cost(DIAGONAL_COST, rows),
        name="diagonal",
    )(
        w_in_all, w_out_all, bias, grad_terms, grad_last,
        tok_diag, cot_diag, diag_other,
    )
    received_diag = to_core(other_diag)
    relayed = [to_far(piece, 1) for piece in grad_far[PARTS:]]
    (sum_diag,) = pl.pallas_call(
        functools.partial(pair_kernel, rows),
        out_shape=[bf16(rows, feats)],
        in_specs=vmem(2),
        out_specs=vmem(1),
        compiler_params=params,
        cost_estimate=cost(rows, rows),
        name="pair_sum_diagonal",
    )(mine_diag, received_diag)
    mixed_diag = to_diagonal(sum_diag)
    from_two = []
    for at in range(PARTS):
        piece, _ = barrier((grad_far[at], sum_diag))
        (line_sum,) = pl.pallas_call(
            functools.partial(pair_kernel, owned // PARTS),
            out_shape=[bf16(owned // PARTS, width)],
            in_specs=vmem(2),
            out_specs=vmem(1),
            compiler_params=params,
            cost_estimate=cost(rows, rows),
            name="line_sum",
        )(piece, relayed[at])
        from_two.append(to_far(line_sum, 2))
    grad_one, mixed_x = barrier((grad_one, mixed_x))
    from_one = to_far(grad_one, 1)
    mixed = pl.pallas_call(
        plane_kernel,
        out_shape=f32(rows, feats),
        in_specs=vmem(3),
        out_specs=pl.BlockSpec(memory_space=pltpu.VMEM),
        compiler_params=params,
        cost_estimate=cost(PLANE_COST, rows),
        name="plane_sum",
    )(mixed_own, mixed_x, mixed_y)
    mixed = (mixed + mixed_diag.astype(jnp.float32)).astype(jnp.bfloat16)
    *from_two, mixed = barrier((*from_two, mixed))
    from_two = jnp.concatenate(from_two)
    total = (
        grad_own.astype(jnp.float32)
        + from_one.astype(jnp.float32)
        + from_two.astype(jnp.float32)
    )
    return (mixed, total * scale)


def solution(mesh):
    dp, tensor = mesh.shape["dp"], mesh.shape["tensor"]
    far = dp // NEAR
    if tensor == 2 and far == 4:
        fine = Mesh(mesh.devices.reshape(far, 2, 2, tensor), AXES)
        rows, owners, halves = ("far", "y", "x"), AXES, "core"
        body = on_device_lines
    else:
        fine = Mesh(mesh.devices.reshape(far, NEAR, tensor), ("far", "near", "tensor"))
        rows, owners, halves = ("far", "near"), ("far", "near", "tensor"), "tensor"
        body = on_device_any
    in_specs = (P(rows, halves), P(rows, halves), P(owners, None), P(owners), P(owners, None))
    out_specs = (P(rows, halves), P(owners, None))
    return jax.shard_map(
        body, mesh=fine, in_specs=in_specs, out_specs=out_specs, check_vma=False
    )
```

```python
import functools
import math

import jax
import jax.numpy as jnp
from jax import lax
from jax.experimental import pallas as pl
from jax.experimental.pallas import tpu as pltpu
from jax.sharding import Mesh, PartitionSpec as P

NEAR = 4
AXES = ("far", "y", "x", "core")
CONTRACT_LAST = (((1,), (1,)), ((), ()))
CONTRACT_FIRST = (((0,), (0,)), ((), ()))
VMEM_LIMIT = 28 * 1024 * 1024
PLANE_COST = 10**10
GRADIENT_COST = 10**10
DIAGONAL_COST = 10**6
EXTRA = 48
PARTS = 2
BIAS_ROWS = 8
MORE = 16


def gelu_parts(value):
    coeff = 0.7978845608
    inner = coeff * (value + 0.044715 * value * value * value)
    tangent = jnp.tanh(inner)
    result = 0.5 * value * (1.0 + tangent)
    slope = 0.5 * (1.0 + tangent) + 0.5 * value * (1.0 - tangent * tangent) * coeff * (
        1.0 + 3.0 * 0.044715 * value * value
    )
    return (result, slope)


def on_device_any(tokens, cotangent, w_in, b_in, w_out):
    far, near, tensor = lax.axis_size("far"), lax.axis_size("near"), lax.axis_size("tensor")
    rows, feats = tokens.shape
    owned, width = w_in.shape
    scale = 1.0 / math.sqrt(rows * far * near)
    bias_rows = jnp.pad(b_in.reshape(1, owned), ((0, 15), (0, width - owned)))
    weights = lax.all_gather(jnp.concatenate([w_in, w_out, bias_rows], 0), "far", axis=0)
    in_rows = weights[:, :owned].reshape(far * owned, width)
    proj_rows = weights[:, owned : 2 * owned].reshape(far * owned, width)
    bias = weights[:, 2 * owned, :owned].reshape(far * owned).astype(jnp.float32)
    tok = lax.all_gather(tokens, ("near", "tensor"), axis=0).reshape(near, tensor, rows, feats)
    cot = lax.all_gather(cotangent, ("near", "tensor"), axis=0).reshape(near, tensor, rows, feats)
    tok_full = tok.transpose(0, 2, 1, 3).reshape(near * rows, width)
    cot_full = cot.transpose(0, 2, 1, 3).reshape(near * rows, width)
    pre = lax.dot_general(
        tok_full, in_rows, CONTRACT_LAST, preferred_element_type=jnp.float32
    ) + bias
    act_value, slope = gelu_parts(pre)
    act = act_value.astype(jnp.bfloat16)
    term = jnp.dot(act, proj_rows, preferred_element_type=jnp.float32).astype(jnp.bfloat16)
    term = term.reshape(near, rows, tensor, feats).transpose(0, 2, 1, 3)
    mixed = lax.psum_scatter(
        term.reshape(near * tensor, rows, feats), ("near", "tensor"), scatter_dimension=0
    )
    dact = lax.dot_general(cot_full, proj_rows, CONTRACT_LAST, preferred_element_type=jnp.float32)
    dpre = (dact * slope).astype(jnp.bfloat16)
    grad = lax.dot_general(dpre, tok_full, CONTRACT_FIRST, preferred_element_type=jnp.float32)
    grad_sum = lax.psum_scatter(grad.astype(jnp.bfloat16), "far", scatter_dimension=0, tiled=True)
    return (mixed, grad_sum.astype(jnp.float32) * scale)


def half_columns(core, shift, feats):
    return pl.ds(pl.multiple_of(lax.rem(core + shift, 2) * feats, feats), feats)


def side_by_side(core, pair, whole, start, sem):
    rows, feats = pair[0].shape
    return [
        pltpu.make_async_copy(
            pair[shift],
            whole.at[pl.ds(start, rows), half_columns(core, shift, feats)],
            sem.at[shift],
        )
        for shift in range(2)
    ]


def weight_copies(refs, owned, w_in, w_out, sem):
    copies = []
    for at, ref in enumerate(refs):
        spot = pl.ds(at * owned, owned)
        copies.append(pltpu.make_async_copy(ref.at[pl.ds(0, owned)], w_in.at[spot], sem.at[0, at]))
        copies.append(
            pltpu.make_async_copy(ref.at[pl.ds(owned, owned)], w_out.at[spot], sem.at[1, at])
        )
    return copies


def bias_of(ref, owned):
    return ref[2 * owned : 2 * owned + BIAS_ROWS, :owned].astype(jnp.float32)


def run(copies, what):
    for copy in copies:
        getattr(copy, what)()


def activate(tok, w_in, bias):
    pre = lax.dot_general(
        tok, w_in, CONTRACT_LAST, preferred_element_type=jnp.float32
    ) + bias
    return gelu_parts(pre)


def dot_last(left, right):
    return lax.dot_general(left, right, CONTRACT_LAST, preferred_element_type=jnp.float32)


def dot_first(left, right):
    return lax.dot_general(left, right, CONTRACT_FIRST, preferred_element_type=jnp.float32)


def early_block(start, step, tok, cot, w_in, w_out, bias, two, act_ref, dpre_ref, mixed_ref, dpre):
    @pl.loop(0, 2)
    def _(sub):
        spot = pl.ds(pl.multiple_of(start + sub * step, step), step)
        value, slope = activate(tok[spot, :], w_in[...], bias[0:1, :])
        act = value.astype(jnp.bfloat16)
        act_ref[spot, :] = act[:, two:]
        dact = dot_last(cot[spot, :], w_out[...])
        terms = (dact * slope).astype(jnp.bfloat16)
        dpre[spot, :] = terms[:, :two]
        dpre_ref[spot, :] = terms[:, two:]
        mixed_ref[spot, :] = jnp.dot(
            act[:, :two], w_out[:two, :], preferred_element_type=jnp.float32
        )


def early_kernel(owned, *refs):
    pair_refs, w_refs = refs[:6], refs[6:9]
    act_ref, dpre_ref, mixed_ref, grad_ref, tok, cot, w_in, w_out, bias = refs[9:18]
    dpre, tok_sem, cot_sem, w_sem = refs[18:]
    core = lax.axis_index("core")
    rows = pair_refs[0].shape[1]
    w_copies = weight_copies(w_refs, owned, w_in, w_out, w_sem)
    loads = []
    for block in range(NEAR - 1):
        first, second = pair_refs[2 * block], pair_refs[2 * block + 1]
        loads.append(
            side_by_side(core, (first.at[0], second.at[0]), tok, block * rows, tok_sem.at[block])
            + side_by_side(core, (first.at[1], second.at[1]), cot, block * rows, cot_sem.at[block])
        )
    run(w_copies, "start")
    for load in loads:
        run(load, "start")
    for at, ref in enumerate(w_refs):
        bias[:, at * owned : (at + 1) * owned] = bias_of(ref, owned)
    run(w_copies, "wait")
    for block, load in enumerate(loads):
        run(load, "wait")
        early_block(
            block * rows, rows // 2, tok, cot, w_in, w_out, bias, 2 * owned,
            act_ref, dpre_ref, mixed_ref, dpre,
        )
    grad_ref[...] = dot_first(dpre[...], tok[...])


def output_kernel(owned, *refs):
    act_two, tok, early_mixed, w_in, w_out, bias, w_three = refs[:7]
    mine_ref, near_ref, own_ref, slope_ref, w_in_all, w_out_all, bias_all = refs[7:14]
    w_last, sem = refs[14:]
    core = lax.axis_index("core")
    rows, feats = own_ref.shape
    two, three = 2 * owned, 3 * owned
    first, last = pl.ds(0, three), pl.ds(three, owned)
    copies = [
        pltpu.make_async_copy(w_in, w_in_all.at[first], sem.at[0]),
        pltpu.make_async_copy(w_three.at[pl.ds(0, owned)], w_in_all.at[last], sem.at[1]),
        pltpu.make_async_copy(w_out, w_out_all.at[first], sem.at[2]),
        pltpu.make_async_copy(w_three.at[pl.ds(owned, owned)], w_out_all.at[last], sem.at[3]),
    ]
    run(copies, "start")
    bias_last = bias_of(w_three, owned)
    bias_all[:, :three] = bias[...]
    bias_all[:, three:] = bias_last
    w_last[:owned, :] = w_out[two:, :]
    w_last[owned:, :] = w_three[owned:two, :]
    step = tok.shape[0] // 6
    for at in range(6):
        spot = slice(at * step, (at + 1) * step)
        value, slope = activate(tok[spot, :], w_three[:owned, :], bias_last[0:1, :])
        slope_ref[spot, :] = slope
        act = jnp.concatenate([act_two[spot, :], value.astype(jnp.bfloat16)], axis=1)
        if at * step < rows:
            far_ref, there = own_ref, spot
        else:
            far_ref, there = near_ref, slice(at * step - rows, (at + 1) * step - rows)
        for shift, ref, to in ((0, mine_ref, spot), (1, far_ref, there)):
            half = half_columns(core, shift, feats)
            ref[to, :] = (
                early_mixed[spot, half]
                + jnp.dot(act, w_last[:, half], preferred_element_type=jnp.float32)
            ).astype(jnp.bfloat16)

    run(copies, "wait")


def gradient_kernel(dpre_two, tok, cot, slope, w_three, grad_ref, dpre):
    owned = slope.shape[1]
    step = tok.shape[0] // 6
    for at in range(6):
        spot = slice(at * step, (at + 1) * step)
        dact = dot_last(cot[spot, :], w_three[owned : 2 * owned, :])
        last = (dact * slope[spot, :]).astype(jnp.bfloat16)
        dpre[spot, :] = jnp.concatenate([dpre_two[spot, :], last], axis=1)
    grad_ref[...] = dot_first(dpre[...], tok[...])


def diagonal_kernel(owned, *refs):
    w_in, w_out, bias, grad_first, grad_last = refs[:5]
    tok_ref, cot_ref, far_ref = refs[5:8]
    mine_ref, other_ref, own_ref, one_ref = refs[8:12]
    two_refs, three_refs = refs[12 : 12 + PARTS], refs[12 + PARTS : 12 + 2 * PARTS]
    tok, cot, dpre, tok_sem, cot_sem = refs[12 + 2 * PARTS :]
    core = lax.axis_index("core")
    rows, feats = mine_ref.shape
    two = 2 * owned
    first, second = pl.ds(0, rows), pl.ds(rows, rows)
    load = side_by_side(core, (tok_ref.at[first], far_ref.at[first]), tok, 0, tok_sem)
    cot_load = side_by_side(core, (cot_ref, far_ref.at[second]), cot, 0, cot_sem)
    run(load + cot_load, "start")
    run(load, "wait")
    step = rows // 2
    for sub in range(2):
        spot = slice(sub * step, (sub + 1) * step)
        value, slope = activate(tok[spot, :], w_in[...], bias[0:1, :])
        act = value.astype(jnp.bfloat16)
        if sub == 0:
            run(cot_load, "wait")
        dact = dot_last(cot[spot, :], w_out[...])
        dpre[spot, :] = (dact * slope).astype(jnp.bfloat16)
        for shift, ref in enumerate((mine_ref, other_ref)):
            ref[spot, :] = jnp.dot(
                act, w_out[:, half_columns(core, shift, feats)], preferred_element_type=jnp.float32
            ).astype(jnp.bfloat16)

    grad = grad_last[...] + dot_first(dpre[:, two:], tok[...])
    part = owned // PARTS
    for at in range(PARTS):
        two_refs[at][...] = grad[at * part : (at + 1) * part].astype(jnp.bfloat16)
        three_refs[at][...] = grad[owned + at * part : owned + (at + 1) * part].astype(jnp.bfloat16)
    grad = grad_first[...] + dot_first(dpre[:, :two], tok[...])
    own_ref[...] = grad[:owned].astype(jnp.bfloat16)
    one_ref[...] = grad[owned:].astype(jnp.bfloat16)


def pair_kernel(rows, first, mine_ref, other_ref, *out_refs):
    for block, ref in enumerate(out_refs):
        mine, other = pl.ds((first + block) * rows, rows), pl.ds(block * rows, rows)
        ref[:rows, :] = (
            mine_ref[mine, :].astype(jnp.float32) + other_ref[other, :].astype(jnp.float32)
        ).astype(jnp.bfloat16)
        if ref.shape[0] > rows:
            ref[rows:, :] = jnp.zeros_like(ref[rows:, :])


def last_pairs_kernel(mine_ref, far_ref, diag_ref, other_ref, own_sum_ref, diag_sum_ref):
    rows = diag_ref.shape[0]
    diag_sum_ref[...] = (
        diag_ref[...].astype(jnp.float32) + other_ref[...].astype(jnp.float32)
    ).astype(jnp.bfloat16)
    own_sum_ref[...] = (
        mine_ref[:rows, :].astype(jnp.float32)
        + far_ref[2 * rows : 3 * rows, :].astype(jnp.float32)
    ).astype(jnp.bfloat16)


def plane_kernel(own_ref, x_ref, y_ref, out_ref):
    rows = own_ref.shape[0]
    out_ref[...] = (
        own_ref[...].astype(jnp.float32)
        + x_ref[:rows, :].astype(jnp.float32)
        + y_ref[:rows, :].astype(jnp.float32)
    )


def vmem(count):
    return [pl.BlockSpec(memory_space=pltpu.VMEM)] * count


def anywhere(count):
    return [pl.BlockSpec(memory_space=pl.ANY)] * count


def bf16(*shape):
    return jax.ShapeDtypeStruct(shape, jnp.bfloat16)


def permute(value, there):
    pairs = []
    for f in range(4):
        for y in range(2):
            for x in range(2):
                for c in range(2):
                    to = there(f, y, x, c)
                    here = ((f * 2 + y) * 2 + x) * 2 + c
                    pairs.append((here, ((to[0] * 2 + to[1]) * 2 + to[2]) * 2 + to[3]))
    return lax.ppermute(value, AXES, pairs)


def to_x(value):
    return permute(value, lambda f, y, x, c: (f, y, 1 - x, c))


def to_y(value):
    return permute(value, lambda f, y, x, c: (f, 1 - y, x, c))


def to_diagonal(value):
    return permute(value, lambda f, y, x, c: (f, 1 - y, 1 - x, c))


def to_core(value):
    return permute(value, lambda f, y, x, c: (f, y, x, 1 - c))


def to_far(value, flip):
    return permute(value, lambda f, y, x, c: (f ^ flip, y, x, c))


def on_device_lines(tokens, cotangent, w_in, b_in, w_out):
    rows, feats = tokens.shape
    owned, width = w_in.shape
    units = 4 * owned
    count = NEAR * rows
    scale = 1.0 / math.sqrt(4 * count)
    params = pltpu.CompilerParams(vmem_limit_bytes=VMEM_LIMIT)
    dma = pltpu.SemaphoreType.DMA
    barrier = lax.optimization_barrier
    early_rows = (NEAR - 1) * rows

    def f32(*shape):
        return jax.ShapeDtypeStruct(shape, jnp.float32)

    def cost(flops, traffic):
        return pl.CostEstimate(flops=flops, bytes_accessed=traffic, transcendentals=0)

    bias_rows = jnp.pad(b_in.reshape(1, owned), ((0, BIAS_ROWS - 1), (0, width - owned)))
    own_w = jnp.concatenate([w_in, w_out, bias_rows], 0)
    own = jnp.stack([tokens, cotangent])
    w_two, w_one = to_far(own_w, 2), to_far(own_w, 1)
    from_x, from_y = to_x(own), to_y(own)
    own_other = to_core(own)
    from_x, from_y, own_other = barrier((from_x, from_y, own_other))
    tok_diag = to_y(from_x.reshape(2 * rows, feats)[: rows + EXTRA])
    cot_diag = to_x(from_y[1])
    x_other, y_other = to_core(from_x), to_core(from_y)
    w_three = to_far(w_two, 1)
    act_two, dpre_two, mixed_terms, grad_terms, tok, cot, w_in_three, w_out_three, bias = (
        pl.pallas_call(
            functools.partial(early_kernel, owned),
            out_shape=(
                bf16(early_rows, owned),
                bf16(early_rows, owned),
                f32(early_rows, width),
                f32(2 * owned, width),
                bf16(early_rows, width),
                bf16(early_rows, width),
                bf16(3 * owned, width),
                bf16(3 * owned, width),
                f32(BIAS_ROWS, 3 * owned),
            ),
            in_specs=anywhere(6) + vmem(3),
            out_specs=vmem(9),
            scratch_shapes=[
                pltpu.VMEM((early_rows, 2 * owned), jnp.bfloat16),
                dma((NEAR - 1, 2)),
                dma((NEAR - 1, 2)),
                dma((2, 3)),
            ],
            compiler_params=params,
            cost_estimate=cost(early_rows * units, early_rows),
            name="early",
        )(own, own_other, from_x, x_other, from_y, y_other, own_w, w_one, w_two)
    )

    mine, other, other_own, slope, w_in_all, w_out_all, bias = pl.pallas_call(
        functools.partial(output_kernel, owned),
        out_shape=(
            bf16(early_rows, feats),
            bf16(2 * rows, feats),
            bf16(rows, feats),
            f32(early_rows, owned),
            bf16(units, width),
            bf16(units, width),
            f32(BIAS_ROWS, units),
        ),
        in_specs=vmem(7),
        out_specs=vmem(7),
        scratch_shapes=[pltpu.VMEM((2 * owned, width), jnp.bfloat16), dma((4,))],
        compiler_params=params,
        cost_estimate=cost(early_rows * units, early_rows),
        name="output",
    )(act_two, tok, mixed_terms, w_in_three, w_out_three, bias, w_three)
    tok_diag, cot_diag, other = barrier((tok_diag, cot_diag, other))
    received = to_core(other)
    diag_other = to_core(jnp.concatenate([tok_diag[:rows], cot_diag, other_own]))
    slope, tok_diag = barrier((slope, tok_diag))
    grad_last = pl.pallas_call(
        gradient_kernel,
        out_shape=f32(2 * owned, width),
        in_specs=vmem(5),
        out_specs=pl.BlockSpec(memory_space=pltpu.VMEM),
        scratch_shapes=[pltpu.VMEM((early_rows, 2 * owned), jnp.bfloat16)],
        compiler_params=params,
        cost_estimate=cost(GRADIENT_COST, early_rows),
        name="gradient",
    )(dpre_two, tok, cot, slope, w_three)

    mine, grad_last = barrier((mine, grad_last))
    sums = pl.pallas_call(
        functools.partial(pair_kernel, rows, 1),
        out_shape=[bf16(rows + MORE, feats)] * 2,
        in_specs=vmem(2),
        out_specs=vmem(2),
        compiler_params=params,
        cost_estimate=cost(rows, rows),
        name="pair_sum",
    )(mine, received)
    mixed_x, mixed_y = to_x(sums[0]), to_y(sums[1])
    grad_terms, mixed_own = barrier((grad_terms, sums[0]))

    mine_diag, other_diag, grad_own, grad_one, *grad_far = pl.pallas_call(
        functools.partial(diagonal_kernel, owned),
        out_shape=[bf16(rows, feats)] * 2
        + [bf16(owned, width)] * 2
        + [bf16(owned // PARTS, width)] * (2 * PARTS),
        in_specs=vmem(5) + anywhere(3),
        out_specs=vmem(4 + 2 * PARTS),
        scratch_shapes=[
            pltpu.VMEM((rows, width), jnp.bfloat16),
            pltpu.VMEM((rows, width), jnp.bfloat16),
            pltpu.VMEM((rows, units), jnp.bfloat16),
            dma((2,)),
            dma((2,)),
        ],
        compiler_params=params,
        cost_estimate=cost(DIAGONAL_COST, rows),
        name="diagonal",
    )(
        w_in_all, w_out_all, bias, grad_terms, grad_last,
        tok_diag, cot_diag, diag_other,
    )
    received_diag = to_core(other_diag)
    relayed = [to_far(piece, 1) for piece in grad_far[PARTS:]]
    mixed_own, sum_diag = pl.pallas_call(
        last_pairs_kernel,
        out_shape=[bf16(rows, feats)] * 2,
        in_specs=vmem(4),
        out_specs=vmem(2),
        compiler_params=params,
        cost_estimate=cost(rows, rows),
        name="pair_sum_diagonal",
    )(mine, diag_other, mine_diag, received_diag)
    mixed_diag = to_diagonal(sum_diag)
    from_two = []
    for at in range(PARTS):
        piece, _ = barrier((grad_far[at], sum_diag))
        (line_sum,) = pl.pallas_call(
            functools.partial(pair_kernel, owned // PARTS, 0),
            out_shape=[bf16(owned // PARTS, width)],
            in_specs=vmem(2),
            out_specs=vmem(1),
            compiler_params=params,
            cost_estimate=cost(rows, rows),
            name="line_sum",
        )(piece, relayed[at])
        from_two.append(to_far(line_sum, 2))
    grad_one, mixed_x, _ = barrier((grad_one, mixed_x, line_sum))
    from_one = to_far(grad_one, 1)
    mixed = pl.pallas_call(
        plane_kernel,
        out_shape=f32(rows, feats),
        in_specs=vmem(3),
        out_specs=pl.BlockSpec(memory_space=pltpu.VMEM),
        compiler_params=params,
        cost_estimate=cost(PLANE_COST, rows),
        name="plane_sum",
    )(mixed_own, mixed_x, mixed_y)
    mixed = (mixed + mixed_diag.astype(jnp.float32)).astype(jnp.bfloat16)
    *from_two, mixed = barrier((*from_two, mixed))
    from_two = jnp.concatenate(from_two)
    total = (
        grad_own.astype(jnp.float32)
        + from_one.astype(jnp.float32)
        + from_two.astype(jnp.float32)
    )
    return (mixed, total * scale)


def solution(mesh):
    dp, tensor = mesh.shape["dp"], mesh.shape["tensor"]
    far = dp // NEAR
    if tensor == 2 and far == 4:
        fine = Mesh(mesh.devices.reshape(far, 2, 2, tensor), AXES)
        rows, owners, halves = ("far", "y", "x"), AXES, "core"
        body = on_device_lines
    else:
        fine = Mesh(mesh.devices.reshape(far, NEAR, tensor), ("far", "near", "tensor"))
        rows, owners, halves = ("far", "near"), ("far", "near", "tensor"), "tensor"
        body = on_device_any
    in_specs = (P(rows, halves), P(rows, halves), P(owners, None), P(owners), P(owners, None))
    out_specs = (P(rows, halves), P(owners, None))
    return jax.shard_map(
        body, mesh=fine, in_specs=in_specs, out_specs=out_specs, check_vma=False
    )
```

```python
import functools
import math

import jax
import jax.numpy as jnp
from jax import lax
from jax.experimental import pallas as pl
from jax.experimental.pallas import tpu as pltpu
from jax.sharding import Mesh, PartitionSpec as P

NEAR = 4
AXES = ("far", "y", "x", "core")
CONTRACT_LAST = (((1,), (1,)), ((), ()))
CONTRACT_FIRST = (((0,), (0,)), ((), ()))
VMEM_LIMIT = 28 * 1024 * 1024
PLANE_COST = 10**10
GRADIENT_COST = 10**10
DIAGONAL_COST = 10**6
EXTRA = 48
PAIR_COST = 10**10
PARTS = 2
BIAS_ROWS = 8
MORE = 16


def gelu_parts(value):
    coeff = 0.7978845608
    inner = coeff * (value + 0.044715 * value * value * value)
    tangent = jnp.tanh(inner)
    result = 0.5 * value * (1.0 + tangent)
    slope = 0.5 * (1.0 + tangent) + 0.5 * value * (1.0 - tangent * tangent) * coeff * (
        1.0 + 3.0 * 0.044715 * value * value
    )
    return (result, slope)


def on_device_any(tokens, cotangent, w_in, b_in, w_out):
    far, near, tensor = lax.axis_size("far"), lax.axis_size("near"), lax.axis_size("tensor")
    rows, feats = tokens.shape
    owned, width = w_in.shape
    scale = 1.0 / math.sqrt(rows * far * near)
    bias_rows = jnp.pad(b_in.reshape(1, owned), ((0, 15), (0, width - owned)))
    weights = lax.all_gather(jnp.concatenate([w_in, w_out, bias_rows], 0), "far", axis=0)
    in_rows = weights[:, :owned].reshape(far * owned, width)
    proj_rows = weights[:, owned : 2 * owned].reshape(far * owned, width)
    bias = weights[:, 2 * owned, :owned].reshape(far * owned).astype(jnp.float32)
    tok = lax.all_gather(tokens, ("near", "tensor"), axis=0).reshape(near, tensor, rows, feats)
    cot = lax.all_gather(cotangent, ("near", "tensor"), axis=0).reshape(near, tensor, rows, feats)
    tok_full = tok.transpose(0, 2, 1, 3).reshape(near * rows, width)
    cot_full = cot.transpose(0, 2, 1, 3).reshape(near * rows, width)
    pre = lax.dot_general(
        tok_full, in_rows, CONTRACT_LAST, preferred_element_type=jnp.float32
    ) + bias
    act_value, slope = gelu_parts(pre)
    act = act_value.astype(jnp.bfloat16)
    term = jnp.dot(act, proj_rows, preferred_element_type=jnp.float32).astype(jnp.bfloat16)
    term = term.reshape(near, rows, tensor, feats).transpose(0, 2, 1, 3)
    mixed = lax.psum_scatter(
        term.reshape(near * tensor, rows, feats), ("near", "tensor"), scatter_dimension=0
    )
    dact = lax.dot_general(cot_full, proj_rows, CONTRACT_LAST, preferred_element_type=jnp.float32)
    dpre = (dact * slope).astype(jnp.bfloat16)
    grad = lax.dot_general(dpre, tok_full, CONTRACT_FIRST, preferred_element_type=jnp.float32)
    grad_sum = lax.psum_scatter(grad.astype(jnp.bfloat16), "far", scatter_dimension=0, tiled=True)
    return (mixed, grad_sum.astype(jnp.float32) * scale)


def half_columns(core, shift, feats):
    return pl.ds(pl.multiple_of(lax.rem(core + shift, 2) * feats, feats), feats)


def side_by_side(core, pair, whole, start, sem):
    rows, feats = pair[0].shape
    return [
        pltpu.make_async_copy(
            pair[shift],
            whole.at[pl.ds(start, rows), half_columns(core, shift, feats)],
            sem.at[shift],
        )
        for shift in range(2)
    ]


def weight_copies(refs, owned, w_in, w_out, sem):
    copies = []
    for at, ref in enumerate(refs):
        spot = pl.ds(at * owned, owned)
        copies.append(pltpu.make_async_copy(ref.at[pl.ds(0, owned)], w_in.at[spot], sem.at[0, at]))
        copies.append(
            pltpu.make_async_copy(ref.at[pl.ds(owned, owned)], w_out.at[spot], sem.at[1, at])
        )
    return copies


def bias_of(ref, owned):
    return ref[2 * owned : 2 * owned + BIAS_ROWS, :owned].astype(jnp.float32)


def run(copies, what):
    for copy in copies:
        getattr(copy, what)()


def activate(tok, w_in, bias):
    pre = lax.dot_general(
        tok, w_in, CONTRACT_LAST, preferred_element_type=jnp.float32
    ) + bias
    return gelu_parts(pre)


def dot_last(left, right):
    return lax.dot_general(left, right, CONTRACT_LAST, preferred_element_type=jnp.float32)


def dot_first(left, right):
    return lax.dot_general(left, right, CONTRACT_FIRST, preferred_element_type=jnp.float32)


def early_block(start, step, tok, cot, w_in, w_out, bias, two, act_ref, dpre_ref, mixed_ref, dpre):
    @pl.loop(0, 2)
    def _(sub):
        spot = pl.ds(pl.multiple_of(start + sub * step, step), step)
        value, slope = activate(tok[spot, :], w_in[...], bias[0:1, :])
        act = value.astype(jnp.bfloat16)
        act_ref[spot, :] = act[:, two:]
        dact = dot_last(cot[spot, :], w_out[...])
        terms = (dact * slope).astype(jnp.bfloat16)
        dpre[spot, :] = terms[:, :two]
        dpre_ref[spot, :] = terms[:, two:]
        mixed_ref[spot, :] = jnp.dot(
            act[:, :two], w_out[:two, :], preferred_element_type=jnp.float32
        )


def early_kernel(owned, *refs):
    pair_refs, w_refs = refs[:6], refs[6:9]
    act_ref, dpre_ref, mixed_ref, grad_ref, tok, cot, w_in, w_out, bias = refs[9:18]
    dpre, tok_sem, cot_sem, w_sem = refs[18:]
    core = lax.axis_index("core")
    rows = pair_refs[0].shape[1]
    w_copies = weight_copies(w_refs, owned, w_in, w_out, w_sem)
    loads = []
    for block in range(NEAR - 1):
        first, second = pair_refs[2 * block], pair_refs[2 * block + 1]
        loads.append(
            side_by_side(core, (first.at[0], second.at[0]), tok, block * rows, tok_sem.at[block])
            + side_by_side(core, (first.at[1], second.at[1]), cot, block * rows, cot_sem.at[block])
        )
    run(w_copies, "start")
    for load in loads:
        run(load, "start")
    for at, ref in enumerate(w_refs):
        bias[:, at * owned : (at + 1) * owned] = bias_of(ref, owned)
    run(w_copies, "wait")
    for block, load in enumerate(loads):
        run(load, "wait")
        early_block(
            block * rows, rows // 2, tok, cot, w_in, w_out, bias, 2 * owned,
            act_ref, dpre_ref, mixed_ref, dpre,
        )
    grad_ref[...] = dot_first(dpre[...], tok[...])


def output_kernel(owned, *refs):
    act_two, tok, early_mixed, w_in, w_out, bias, w_three = refs[:7]
    mine_ref, near_ref, own_ref, slope_ref, w_in_all, w_out_all, bias_all = refs[7:14]
    w_last, sem = refs[14:]
    core = lax.axis_index("core")
    rows, feats = own_ref.shape
    two, three = 2 * owned, 3 * owned
    first, last = pl.ds(0, three), pl.ds(three, owned)
    copies = [
        pltpu.make_async_copy(w_in, w_in_all.at[first], sem.at[0]),
        pltpu.make_async_copy(w_three.at[pl.ds(0, owned)], w_in_all.at[last], sem.at[1]),
        pltpu.make_async_copy(w_out, w_out_all.at[first], sem.at[2]),
        pltpu.make_async_copy(w_three.at[pl.ds(owned, owned)], w_out_all.at[last], sem.at[3]),
    ]
    run(copies, "start")
    bias_last = bias_of(w_three, owned)
    bias_all[:, :three] = bias[...]
    bias_all[:, three:] = bias_last
    w_last[:owned, :] = w_out[two:, :]
    w_last[owned:, :] = w_three[owned:two, :]
    step = tok.shape[0] // 6
    for at in range(6):
        spot = slice(at * step, (at + 1) * step)
        value, slope = activate(tok[spot, :], w_three[:owned, :], bias_last[0:1, :])
        slope_ref[spot, :] = slope
        act = jnp.concatenate([act_two[spot, :], value.astype(jnp.bfloat16)], axis=1)
        if at * step < rows:
            far_ref, there = own_ref, spot
        else:
            far_ref, there = near_ref, slice(at * step - rows, (at + 1) * step - rows)
        for shift, ref, to in ((0, mine_ref, spot), (1, far_ref, there)):
            half = half_columns(core, shift, feats)
            ref[to, :] = (
                early_mixed[spot, half]
                + jnp.dot(act, w_last[:, half], preferred_element_type=jnp.float32)
            ).astype(jnp.bfloat16)

    run(copies, "wait")


def gradient_kernel(dpre_two, tok, cot, slope, w_three, grad_ref, dpre):
    owned = slope.shape[1]
    step = tok.shape[0] // 6
    for at in range(6):
        spot = slice(at * step, (at + 1) * step)
        dact = dot_last(cot[spot, :], w_three[owned : 2 * owned, :])
        last = (dact * slope[spot, :]).astype(jnp.bfloat16)
        dpre[spot, :] = jnp.concatenate([dpre_two[spot, :], last], axis=1)
    grad_ref[...] = dot_first(dpre[...], tok[...])


def diagonal_kernel(owned, *refs):
    w_in, w_out, bias, grad_first, grad_last = refs[:5]
    tok_ref, cot_ref, far_ref = refs[5:8]
    mine_ref, other_ref, own_ref, one_ref = refs[8:12]
    two_refs, three_refs = refs[12 : 12 + PARTS], refs[12 + PARTS : 12 + 2 * PARTS]
    tok, cot, dpre, tok_sem, cot_sem = refs[12 + 2 * PARTS :]
    core = lax.axis_index("core")
    rows, feats = mine_ref.shape
    two = 2 * owned
    first, second = pl.ds(0, rows), pl.ds(rows, rows)
    load = side_by_side(core, (tok_ref.at[first], far_ref.at[first]), tok, 0, tok_sem)
    cot_load = side_by_side(core, (cot_ref, far_ref.at[second]), cot, 0, cot_sem)
    run(load + cot_load, "start")
    run(load, "wait")
    step = rows // 2
    for sub in range(2):
        spot = slice(sub * step, (sub + 1) * step)
        value, slope = activate(tok[spot, :], w_in[...], bias[0:1, :])
        act = value.astype(jnp.bfloat16)
        if sub == 0:
            run(cot_load, "wait")
        dact = dot_last(cot[spot, :], w_out[...])
        dpre[spot, :] = (dact * slope).astype(jnp.bfloat16)
        for shift, ref in enumerate((mine_ref, other_ref)):
            ref[spot, :] = jnp.dot(
                act, w_out[:, half_columns(core, shift, feats)], preferred_element_type=jnp.float32
            ).astype(jnp.bfloat16)

    grad = grad_last[...] + dot_first(dpre[:, two:], tok[...])
    part = owned // PARTS
    for at in range(PARTS):
        two_refs[at][...] = grad[at * part : (at + 1) * part].astype(jnp.bfloat16)
        three_refs[at][...] = grad[owned + at * part : owned + (at + 1) * part].astype(jnp.bfloat16)
    grad = grad_first[...] + dot_first(dpre[:, :two], tok[...])
    own_ref[...] = grad[:owned].astype(jnp.bfloat16)
    one_ref[...] = grad[owned:].astype(jnp.bfloat16)


def pair_kernel(rows, first, mine_ref, other_ref, *out_refs):
    for block, ref in enumerate(out_refs):
        mine, other = pl.ds((first + block) * rows, rows), pl.ds(block * rows, rows)
        ref[:rows, :] = (
            mine_ref[mine, :].astype(jnp.float32) + other_ref[other, :].astype(jnp.float32)
        ).astype(jnp.bfloat16)
        if ref.shape[0] > rows:
            ref[rows:, :] = jnp.zeros_like(ref[rows:, :])


def last_pairs_kernel(mine_ref, far_ref, diag_ref, other_ref, own_sum_ref, diag_sum_ref):
    rows = diag_ref.shape[0]
    diag_sum_ref[...] = (
        diag_ref[...].astype(jnp.float32) + other_ref[...].astype(jnp.float32)
    ).astype(jnp.bfloat16)
    own_sum_ref[...] = (
        mine_ref[:rows, :].astype(jnp.float32)
        + far_ref[2 * rows : 3 * rows, :].astype(jnp.float32)
    ).astype(jnp.bfloat16)


def plane_kernel(own_ref, x_ref, y_ref, out_ref):
    rows = own_ref.shape[0]
    out_ref[...] = (
        own_ref[...].astype(jnp.float32)
        + x_ref[:rows, :].astype(jnp.float32)
        + y_ref[:rows, :].astype(jnp.float32)
    )


def vmem(count):
    return [pl.BlockSpec(memory_space=pltpu.VMEM)] * count


def anywhere(count):
    return [pl.BlockSpec(memory_space=pl.ANY)] * count


def bf16(*shape):
    return jax.ShapeDtypeStruct(shape, jnp.bfloat16)


def permute(value, there):
    pairs = []
    for f in range(4):
        for y in range(2):
            for x in range(2):
                for c in range(2):
                    to = there(f, y, x, c)
                    here = ((f * 2 + y) * 2 + x) * 2 + c
                    pairs.append((here, ((to[0] * 2 + to[1]) * 2 + to[2]) * 2 + to[3]))
    return lax.ppermute(value, AXES, pairs)


def to_x(value):
    return permute(value, lambda f, y, x, c: (f, y, 1 - x, c))


def to_y(value):
    return permute(value, lambda f, y, x, c: (f, 1 - y, x, c))


def to_diagonal(value):
    return permute(value, lambda f, y, x, c: (f, 1 - y, 1 - x, c))


def to_core(value):
    return permute(value, lambda f, y, x, c: (f, y, x, 1 - c))


def to_far(value, flip):
    return permute(value, lambda f, y, x, c: (f ^ flip, y, x, c))


def on_device_lines(tokens, cotangent, w_in, b_in, w_out):
    rows, feats = tokens.shape
    owned, width = w_in.shape
    units = 4 * owned
    count = NEAR * rows
    scale = 1.0 / math.sqrt(4 * count)
    params = pltpu.CompilerParams(vmem_limit_bytes=VMEM_LIMIT)
    dma = pltpu.SemaphoreType.DMA
    barrier = lax.optimization_barrier
    early_rows = (NEAR - 1) * rows

    def f32(*shape):
        return jax.ShapeDtypeStruct(shape, jnp.float32)

    def cost(flops, traffic):
        return pl.CostEstimate(flops=flops, bytes_accessed=traffic, transcendentals=0)

    bias_rows = jnp.pad(b_in.reshape(1, owned), ((0, BIAS_ROWS - 1), (0, width - owned)))
    own_w = jnp.concatenate([w_in, w_out, bias_rows], 0)
    own = jnp.stack([tokens, cotangent])
    w_two, w_one = to_far(own_w, 2), to_far(own_w, 1)
    from_x, from_y = to_x(own), to_y(own)
    own_other = to_core(own)
    from_x, from_y, own_other = barrier((from_x, from_y, own_other))
    tok_diag = to_y(from_x.reshape(2 * rows, feats)[: rows + EXTRA])
    cot_diag = to_x(from_y[1])
    x_other, y_other = to_core(from_x), to_core(from_y)
    w_three = to_far(w_two, 1)
    act_two, dpre_two, mixed_terms, grad_terms, tok, cot, w_in_three, w_out_three, bias = (
        pl.pallas_call(
            functools.partial(early_kernel, owned),
            out_shape=(
                bf16(early_rows, owned),
                bf16(early_rows, owned),
                f32(early_rows, width),
                f32(2 * owned, width),
                bf16(early_rows, width),
                bf16(early_rows, width),
                bf16(3 * owned, width),
                bf16(3 * owned, width),
                f32(BIAS_ROWS, 3 * owned),
            ),
            in_specs=anywhere(6) + vmem(3),
            out_specs=vmem(9),
            scratch_shapes=[
                pltpu.VMEM((early_rows, 2 * owned), jnp.bfloat16),
                dma((NEAR - 1, 2)),
                dma((NEAR - 1, 2)),
                dma((2, 3)),
            ],
            compiler_params=params,
            cost_estimate=cost(early_rows * units, early_rows),
            name="early",
        )(own, own_other, from_x, x_other, from_y, y_other, own_w, w_one, w_two)
    )

    mine, other, other_own, slope, w_in_all, w_out_all, bias = pl.pallas_call(
        functools.partial(output_kernel, owned),
        out_shape=(
            bf16(early_rows, feats),
            bf16(2 * rows, feats),
            bf16(rows, feats),
            f32(early_rows, owned),
            bf16(units, width),
            bf16(units, width),
            f32(BIAS_ROWS, units),
        ),
        in_specs=vmem(7),
        out_specs=vmem(7),
        scratch_shapes=[pltpu.VMEM((2 * owned, width), jnp.bfloat16), dma((4,))],
        compiler_params=params,
        cost_estimate=cost(early_rows * units, early_rows),
        name="output",
    )(act_two, tok, mixed_terms, w_in_three, w_out_three, bias, w_three)
    tok_diag, cot_diag, other = barrier((tok_diag, cot_diag, other))
    received = to_core(other)
    diag_other = to_core(jnp.concatenate([tok_diag[:rows], cot_diag, other_own]))
    slope, tok_diag = barrier((slope, tok_diag))
    grad_last = pl.pallas_call(
        gradient_kernel,
        out_shape=f32(2 * owned, width),
        in_specs=vmem(5),
        out_specs=pl.BlockSpec(memory_space=pltpu.VMEM),
        scratch_shapes=[pltpu.VMEM((early_rows, 2 * owned), jnp.bfloat16)],
        compiler_params=params,
        cost_estimate=cost(GRADIENT_COST, early_rows),
        name="gradient",
    )(dpre_two, tok, cot, slope, w_three)

    mine, grad_last = barrier((mine, grad_last))
    sums = pl.pallas_call(
        functools.partial(pair_kernel, rows, 1),
        out_shape=[bf16(rows + MORE, feats)] * 2,
        in_specs=vmem(2),
        out_specs=vmem(2),
        compiler_params=params,
        cost_estimate=cost(PAIR_COST, rows),
        name="pair_sum",
    )(mine, received)
    mixed_x, mixed_y = to_x(sums[0]), to_y(sums[1])
    grad_terms, _ = barrier((grad_terms, sums[0]))

    mine_diag, other_diag, grad_own, grad_one, *grad_far = pl.pallas_call(
        functools.partial(diagonal_kernel, owned),
        out_shape=[bf16(rows, feats)] * 2
        + [bf16(owned, width)] * 2
        + [bf16(owned // PARTS, width)] * (2 * PARTS),
        in_specs=vmem(5) + anywhere(3),
        out_specs=vmem(4 + 2 * PARTS),
        scratch_shapes=[
            pltpu.VMEM((rows, width), jnp.bfloat16),
            pltpu.VMEM((rows, width), jnp.bfloat16),
            pltpu.VMEM((rows, units), jnp.bfloat16),
            dma((2,)),
            dma((2,)),
        ],
        compiler_params=params,
        cost_estimate=cost(DIAGONAL_COST, rows),
        name="diagonal",
    )(
        w_in_all, w_out_all, bias, grad_terms, grad_last,
        tok_diag, cot_diag, diag_other,
    )
    received_diag = to_core(other_diag)
    relayed = [to_far(piece, 1) for piece in grad_far[PARTS:]]
    mixed_own, sum_diag = pl.pallas_call(
        last_pairs_kernel,
        out_shape=[bf16(rows, feats)] * 2,
        in_specs=vmem(4),
        out_specs=vmem(2),
        compiler_params=params,
        cost_estimate=cost(rows, rows),
        name="pair_sum_diagonal",
    )(mine, diag_other, mine_diag, received_diag)
    mixed_diag = to_diagonal(sum_diag)
    from_two = []
    for at in range(PARTS):
        piece, _ = barrier((grad_far[at], sum_diag))
        (line_sum,) = pl.pallas_call(
            functools.partial(pair_kernel, owned // PARTS, 0),
            out_shape=[bf16(owned // PARTS, width)],
            in_specs=vmem(2),
            out_specs=vmem(1),
            compiler_params=params,
            cost_estimate=cost(rows, rows),
            name="line_sum",
        )(piece, relayed[at])
        from_two.append(to_far(line_sum, 2))
    grad_one, mixed_x, _ = barrier((grad_one, mixed_x, line_sum))
    from_one = to_far(grad_one, 1)
    mixed = pl.pallas_call(
        plane_kernel,
        out_shape=f32(rows, feats),
        in_specs=vmem(3),
        out_specs=pl.BlockSpec(memory_space=pltpu.VMEM),
        compiler_params=params,
        cost_estimate=cost(PLANE_COST, rows),
        name="plane_sum",
    )(mixed_own, mixed_x, mixed_y)
    mixed = (mixed + mixed_diag.astype(jnp.float32)).astype(jnp.bfloat16)
    *from_two, mixed = barrier((*from_two, mixed))
    from_two = jnp.concatenate(from_two)
    total = (
        grad_own.astype(jnp.float32)
        + from_one.astype(jnp.float32)
        + from_two.astype(jnp.float32)
    )
    return (mixed, total * scale)


def solution(mesh):
    dp, tensor = mesh.shape["dp"], mesh.shape["tensor"]
    far = dp // NEAR
    if tensor == 2 and far == 4:
        fine = Mesh(mesh.devices.reshape(far, 2, 2, tensor), AXES)
        rows, owners, halves = ("far", "y", "x"), AXES, "core"
        body = on_device_lines
    else:
        fine = Mesh(mesh.devices.reshape(far, NEAR, tensor), ("far", "near", "tensor"))
        rows, owners, halves = ("far", "near"), ("far", "near", "tensor"), "tensor"
        body = on_device_any
    in_specs = (P(rows, halves), P(rows, halves), P(owners, None), P(owners), P(owners, None))
    out_specs = (P(rows, halves), P(owners, None))
    return jax.shard_map(
        body, mesh=fine, in_specs=in_specs, out_specs=out_specs, check_vma=False
    )
```

```python
import functools
import math

import jax
import jax.numpy as jnp
from jax import lax
from jax.experimental import pallas as pl
from jax.experimental.pallas import tpu as pltpu
from jax.sharding import Mesh, PartitionSpec as P

NEAR = 4
AXES = ("far", "y", "x", "core")
CONTRACT_LAST = (((1,), (1,)), ((), ()))
CONTRACT_FIRST = (((0,), (0,)), ((), ()))
VMEM_LIMIT = 28 * 1024 * 1024
PLANE_COST = 10**10
GRADIENT_COST = 10**10
DIAGONAL_COST = 10**6
EXTRA = 48
PAIR_COST = 10**10
PARTS = 2
BIAS_ROWS = 8
MORE = 16


def gelu_parts(value):
    coeff = 0.7978845608
    inner = coeff * (value + 0.044715 * value * value * value)
    tangent = jnp.tanh(inner)
    result = 0.5 * value * (1.0 + tangent)
    slope = 0.5 * (1.0 + tangent) + 0.5 * value * (1.0 - tangent * tangent) * coeff * (
        1.0 + 3.0 * 0.044715 * value * value
    )
    return (result, slope)


def on_device_any(tokens, cotangent, w_in, b_in, w_out):
    far, near, tensor = lax.axis_size("far"), lax.axis_size("near"), lax.axis_size("tensor")
    rows, feats = tokens.shape
    owned, width = w_in.shape
    scale = 1.0 / math.sqrt(rows * far * near)
    bias_rows = jnp.pad(b_in.reshape(1, owned), ((0, 15), (0, width - owned)))
    weights = lax.all_gather(jnp.concatenate([w_in, w_out, bias_rows], 0), "far", axis=0)
    in_rows = weights[:, :owned].reshape(far * owned, width)
    proj_rows = weights[:, owned : 2 * owned].reshape(far * owned, width)
    bias = weights[:, 2 * owned, :owned].reshape(far * owned).astype(jnp.float32)
    tok = lax.all_gather(tokens, ("near", "tensor"), axis=0).reshape(near, tensor, rows, feats)
    cot = lax.all_gather(cotangent, ("near", "tensor"), axis=0).reshape(near, tensor, rows, feats)
    tok_full = tok.transpose(0, 2, 1, 3).reshape(near * rows, width)
    cot_full = cot.transpose(0, 2, 1, 3).reshape(near * rows, width)
    pre = lax.dot_general(
        tok_full, in_rows, CONTRACT_LAST, preferred_element_type=jnp.float32
    ) + bias
    act_value, slope = gelu_parts(pre)
    act = act_value.astype(jnp.bfloat16)
    term = jnp.dot(act, proj_rows, preferred_element_type=jnp.float32).astype(jnp.bfloat16)
    term = term.reshape(near, rows, tensor, feats).transpose(0, 2, 1, 3)
    mixed = lax.psum_scatter(
        term.reshape(near * tensor, rows, feats), ("near", "tensor"), scatter_dimension=0
    )
    dact = lax.dot_general(cot_full, proj_rows, CONTRACT_LAST, preferred_element_type=jnp.float32)
    dpre = (dact * slope).astype(jnp.bfloat16)
    grad = lax.dot_general(dpre, tok_full, CONTRACT_FIRST, preferred_element_type=jnp.float32)
    grad_sum = lax.psum_scatter(grad.astype(jnp.bfloat16), "far", scatter_dimension=0, tiled=True)
    return (mixed, grad_sum.astype(jnp.float32) * scale)


def half_columns(core, shift, feats):
    return pl.ds(pl.multiple_of(lax.rem(core + shift, 2) * feats, feats), feats)


def side_by_side(core, pair, whole, start, sem):
    rows, feats = pair[0].shape
    return [
        pltpu.make_async_copy(
            pair[shift],
            whole.at[pl.ds(start, rows), half_columns(core, shift, feats)],
            sem.at[shift],
        )
        for shift in range(2)
    ]


def weight_copies(refs, owned, w_in, w_out, sem):
    copies = []
    for at, ref in enumerate(refs):
        spot = pl.ds(at * owned, owned)
        copies.append(pltpu.make_async_copy(ref.at[pl.ds(0, owned)], w_in.at[spot], sem.at[0, at]))
        copies.append(
            pltpu.make_async_copy(ref.at[pl.ds(owned, owned)], w_out.at[spot], sem.at[1, at])
        )
    return copies


def bias_of(ref, owned):
    return ref[2 * owned : 2 * owned + BIAS_ROWS, :owned].astype(jnp.float32)


def run(copies, what):
    for copy in copies:
        getattr(copy, what)()


def activate(tok, w_in, bias):
    pre = lax.dot_general(
        tok, w_in, CONTRACT_LAST, preferred_element_type=jnp.float32
    ) + bias
    return gelu_parts(pre)


def dot_last(left, right):
    return lax.dot_general(left, right, CONTRACT_LAST, preferred_element_type=jnp.float32)


def dot_first(left, right):
    return lax.dot_general(left, right, CONTRACT_FIRST, preferred_element_type=jnp.float32)


def early_block(start, step, tok, cot, w_in, w_out, bias, two, act_ref, dpre_ref, mixed_ref, dpre):
    @pl.loop(0, 2)
    def _(sub):
        spot = pl.ds(pl.multiple_of(start + sub * step, step), step)
        value, slope = activate(tok[spot, :], w_in[...], bias[0:1, :])
        act = value.astype(jnp.bfloat16)
        act_ref[spot, :] = act[:, two:]
        dact = dot_last(cot[spot, :], w_out[...])
        terms = (dact * slope).astype(jnp.bfloat16)
        dpre[spot, :] = terms[:, :two]
        dpre_ref[spot, :] = terms[:, two:]
        mixed_ref[spot, :] = jnp.dot(
            act[:, :two], w_out[:two, :], preferred_element_type=jnp.float32
        )


def early_kernel(owned, *refs):
    pair_refs, w_refs = refs[:6], refs[6:9]
    act_ref, dpre_ref, mixed_ref, grad_ref, tok, cot, w_in, w_out, bias = refs[9:18]
    dpre, tok_sem, cot_sem, w_sem = refs[18:]
    core = lax.axis_index("core")
    rows = pair_refs[0].shape[1]
    w_copies = weight_copies(w_refs, owned, w_in, w_out, w_sem)
    loads = []
    for block in range(NEAR - 1):
        first, second = pair_refs[2 * block], pair_refs[2 * block + 1]
        loads.append(
            side_by_side(core, (first.at[0], second.at[0]), tok, block * rows, tok_sem.at[block])
            + side_by_side(core, (first.at[1], second.at[1]), cot, block * rows, cot_sem.at[block])
        )
    run(w_copies, "start")
    for load in loads:
        run(load, "start")
    for at, ref in enumerate(w_refs):
        bias[:, at * owned : (at + 1) * owned] = bias_of(ref, owned)
    run(w_copies, "wait")
    for block, load in enumerate(loads):
        run(load, "wait")
        early_block(
            block * rows, rows // 2, tok, cot, w_in, w_out, bias, 2 * owned,
            act_ref, dpre_ref, mixed_ref, dpre,
        )
    grad_ref[...] = dot_first(dpre[...], tok[...])


def output_kernel(owned, *refs):
    act_two, tok, early_mixed, w_in, w_out, bias, w_three = refs[:7]
    mine_ref, near_ref, own_ref, slope_ref, w_in_all, w_out_all, bias_all = refs[7:14]
    w_last, sem = refs[14:]
    core = lax.axis_index("core")
    rows, feats = own_ref.shape
    two, three = 2 * owned, 3 * owned
    first, last = pl.ds(0, three), pl.ds(three, owned)
    copies = [
        pltpu.make_async_copy(w_in, w_in_all.at[first], sem.at[0]),
        pltpu.make_async_copy(w_three.at[pl.ds(0, owned)], w_in_all.at[last], sem.at[1]),
        pltpu.make_async_copy(w_out, w_out_all.at[first], sem.at[2]),
        pltpu.make_async_copy(w_three.at[pl.ds(owned, owned)], w_out_all.at[last], sem.at[3]),
    ]
    run(copies, "start")
    bias_last = bias_of(w_three, owned)
    bias_all[:, :three] = bias[...]
    bias_all[:, three:] = bias_last
    w_last[:owned, :] = w_out[two:, :]
    w_last[owned:, :] = w_three[owned:two, :]
    step = tok.shape[0] // 6
    for at in range(6):
        spot = slice(at * step, (at + 1) * step)
        value, slope = activate(tok[spot, :], w_three[:owned, :], bias_last[0:1, :])
        slope_ref[spot, :] = slope
        act = jnp.concatenate([act_two[spot, :], value.astype(jnp.bfloat16)], axis=1)
        if at * step < rows:
            far_ref, there = own_ref, spot
        else:
            far_ref, there = near_ref, slice(at * step - rows, (at + 1) * step - rows)
        for shift, ref, to in ((0, mine_ref, spot), (1, far_ref, there)):
            half = half_columns(core, shift, feats)
            ref[to, :] = (
                early_mixed[spot, half]
                + jnp.dot(act, w_last[:, half], preferred_element_type=jnp.float32)
            ).astype(jnp.bfloat16)

    run(copies, "wait")


def gradient_kernel(dpre_two, tok, cot, slope, w_three, grad_ref, dpre):
    owned = slope.shape[1]
    step = tok.shape[0] // 6
    for at in range(6):
        spot = slice(at * step, (at + 1) * step)
        dact = dot_last(cot[spot, :], w_three[owned : 2 * owned, :])
        last = (dact * slope[spot, :]).astype(jnp.bfloat16)
        dpre[spot, :] = jnp.concatenate([dpre_two[spot, :], last], axis=1)
    grad_ref[...] = dot_first(dpre[...], tok[...])


def diagonal_kernel(owned, *refs):
    w_in, w_out, bias, grad_first, grad_last = refs[:5]
    tok_ref, cot_ref, far_ref = refs[5:8]
    mine_ref, other_ref, own_ref, one_ref = refs[8:12]
    two_refs, three_refs = refs[12 : 12 + PARTS], refs[12 + PARTS : 12 + 2 * PARTS]
    tok, cot, dpre, tok_sem, cot_sem = refs[12 + 2 * PARTS :]
    core = lax.axis_index("core")
    rows, feats = mine_ref.shape
    two = 2 * owned
    first, second = pl.ds(0, rows), pl.ds(rows, rows)
    load = side_by_side(core, (tok_ref.at[first], far_ref.at[first]), tok, 0, tok_sem)
    cot_load = side_by_side(core, (cot_ref, far_ref.at[second]), cot, 0, cot_sem)
    run(load + cot_load, "start")
    run(load + cot_load, "wait")
    step = rows // 2
    for sub in range(2):
        spot = slice(sub * step, (sub + 1) * step)
        value, slope = activate(tok[spot, :], w_in[...], bias[0:1, :])
        act = value.astype(jnp.bfloat16)
        dact = dot_last(cot[spot, :], w_out[...])
        dpre[spot, :] = (dact * slope).astype(jnp.bfloat16)
        for shift, ref in enumerate((mine_ref, other_ref)):
            ref[spot, :] = jnp.dot(
                act, w_out[:, half_columns(core, shift, feats)], preferred_element_type=jnp.float32
            ).astype(jnp.bfloat16)

    grad = grad_last[...] + dot_first(dpre[:, two:], tok[...])
    part = owned // PARTS
    for at in range(PARTS):
        two_refs[at][...] = grad[at * part : (at + 1) * part].astype(jnp.bfloat16)
        three_refs[at][...] = grad[owned + at * part : owned + (at + 1) * part].astype(jnp.bfloat16)
    grad = grad_first[...] + dot_first(dpre[:, :two], tok[...])
    own_ref[...] = grad[:owned].astype(jnp.bfloat16)
    one_ref[...] = grad[owned:].astype(jnp.bfloat16)


def pair_kernel(rows, first, mine_ref, other_ref, *out_refs):
    for block, ref in enumerate(out_refs):
        mine, other = pl.ds((first + block) * rows, rows), pl.ds(block * rows, rows)
        ref[:rows, :] = (
            mine_ref[mine, :].astype(jnp.float32) + other_ref[other, :].astype(jnp.float32)
        ).astype(jnp.bfloat16)
        if ref.shape[0] > rows:
            ref[rows:, :] = jnp.zeros_like(ref[rows:, :])


def last_pairs_kernel(mine_ref, far_ref, diag_ref, other_ref, own_sum_ref, diag_sum_ref):
    rows = diag_ref.shape[0]
    diag_sum_ref[...] = (
        diag_ref[...].astype(jnp.float32) + other_ref[...].astype(jnp.float32)
    ).astype(jnp.bfloat16)
    own_sum_ref[...] = (
        mine_ref[:rows, :].astype(jnp.float32)
        + far_ref[2 * rows : 3 * rows, :].astype(jnp.float32)
    ).astype(jnp.bfloat16)


def plane_kernel(own_ref, x_ref, y_ref, out_ref):
    rows = own_ref.shape[0]
    out_ref[...] = (
        own_ref[...].astype(jnp.float32)
        + x_ref[:rows, :].astype(jnp.float32)
        + y_ref[:rows, :].astype(jnp.float32)
    )


def vmem(count):
    return [pl.BlockSpec(memory_space=pltpu.VMEM)] * count


def anywhere(count):
    return [pl.BlockSpec(memory_space=pl.ANY)] * count


def bf16(*shape):
    return jax.ShapeDtypeStruct(shape, jnp.bfloat16)


def permute(value, there):
    pairs = []
    for f in range(4):
        for y in range(2):
            for x in range(2):
                for c in range(2):
                    to = there(f, y, x, c)
                    here = ((f * 2 + y) * 2 + x) * 2 + c
                    pairs.append((here, ((to[0] * 2 + to[1]) * 2 + to[2]) * 2 + to[3]))
    return lax.ppermute(value, AXES, pairs)


def to_x(value):
    return permute(value, lambda f, y, x, c: (f, y, 1 - x, c))


def to_y(value):
    return permute(value, lambda f, y, x, c: (f, 1 - y, x, c))


def to_diagonal(value):
    return permute(value, lambda f, y, x, c: (f, 1 - y, 1 - x, c))


def to_core(value):
    return permute(value, lambda f, y, x, c: (f, y, x, 1 - c))


def to_far(value, flip):
    return permute(value, lambda f, y, x, c: (f ^ flip, y, x, c))


def on_device_lines(tokens, cotangent, w_in, b_in, w_out):
    rows, feats = tokens.shape
    owned, width = w_in.shape
    units = 4 * owned
    count = NEAR * rows
    scale = 1.0 / math.sqrt(4 * count)
    params = pltpu.CompilerParams(vmem_limit_bytes=VMEM_LIMIT)
    dma = pltpu.SemaphoreType.DMA
    barrier = lax.optimization_barrier
    early_rows = (NEAR - 1) * rows

    def f32(*shape):
        return jax.ShapeDtypeStruct(shape, jnp.float32)

    def cost(flops, traffic):
        return pl.CostEstimate(flops=flops, bytes_accessed=traffic, transcendentals=0)

    bias_rows = jnp.pad(b_in.reshape(1, owned), ((0, BIAS_ROWS - 1), (0, width - owned)))
    own_w = jnp.concatenate([w_in, w_out, bias_rows], 0)
    own = jnp.stack([tokens, cotangent])
    w_two, w_one = to_far(own_w, 2), to_far(own_w, 1)
    from_x, from_y = to_x(own), to_y(own)
    own_other = to_core(own)
    from_x, from_y, own_other = barrier((from_x, from_y, own_other))
    tok_diag = to_y(from_x.reshape(2 * rows, feats)[: rows + EXTRA])
    cot_diag = to_x(from_y[1])
    x_other, y_other = to_core(from_x), to_core(from_y)
    w_three = to_far(w_two, 1)
    act_two, dpre_two, mixed_terms, grad_terms, tok, cot, w_in_three, w_out_three, bias = (
        pl.pallas_call(
            functools.partial(early_kernel, owned),
            out_shape=(
                bf16(early_rows, owned),
                bf16(early_rows, owned),
                f32(early_rows, width),
                f32(2 * owned, width),
                bf16(early_rows, width),
                bf16(early_rows, width),
                bf16(3 * owned, width),
                bf16(3 * owned, width),
                f32(BIAS_ROWS, 3 * owned),
            ),
            in_specs=anywhere(6) + vmem(3),
            out_specs=vmem(9),
            scratch_shapes=[
                pltpu.VMEM((early_rows, 2 * owned), jnp.bfloat16),
                dma((NEAR - 1, 2)),
                dma((NEAR - 1, 2)),
                dma((2, 3)),
            ],
            compiler_params=params,
            cost_estimate=cost(early_rows * units, early_rows),
            name="early",
        )(own, own_other, from_x, x_other, from_y, y_other, own_w, w_one, w_two)
    )

    mine, other, other_own, slope, w_in_all, w_out_all, bias = pl.pallas_call(
        functools.partial(output_kernel, owned),
        out_shape=(
            bf16(early_rows, feats),
            bf16(2 * rows, feats),
            bf16(rows, feats),
            f32(early_rows, owned),
            bf16(units, width),
            bf16(units, width),
            f32(BIAS_ROWS, units),
        ),
        in_specs=vmem(7),
        out_specs=vmem(7),
        scratch_shapes=[pltpu.VMEM((2 * owned, width), jnp.bfloat16), dma((4,))],
        compiler_params=params,
        cost_estimate=cost(early_rows * units, early_rows),
        name="output",
    )(act_two, tok, mixed_terms, w_in_three, w_out_three, bias, w_three)
    tok_diag, cot_diag, other = barrier((tok_diag, cot_diag, other))
    received = to_core(other)
    diag_other = to_core(jnp.concatenate([tok_diag[:rows], cot_diag, other_own]))
    slope, tok_diag = barrier((slope, tok_diag))
    grad_last = pl.pallas_call(
        gradient_kernel,
        out_shape=f32(2 * owned, width),
        in_specs=vmem(5),
        out_specs=pl.BlockSpec(memory_space=pltpu.VMEM),
        scratch_shapes=[pltpu.VMEM((early_rows, 2 * owned), jnp.bfloat16)],
        compiler_params=params,
        cost_estimate=cost(GRADIENT_COST, early_rows),
        name="gradient",
    )(dpre_two, tok, cot, slope, w_three)

    mine, grad_last = barrier((mine, grad_last))
    sums = pl.pallas_call(
        functools.partial(pair_kernel, rows, 1),
        out_shape=[bf16(rows + MORE, feats)] * 2,
        in_specs=vmem(2),
        out_specs=vmem(2),
        compiler_params=params,
        cost_estimate=cost(PAIR_COST, rows),
        name="pair_sum",
    )(mine, received)
    mixed_x, mixed_y = to_x(sums[0]), to_y(sums[1])
    grad_terms, _ = barrier((grad_terms, sums[0]))

    mine_diag, other_diag, grad_own, grad_one, *grad_far = pl.pallas_call(
        functools.partial(diagonal_kernel, owned),
        out_shape=[bf16(rows, feats)] * 2
        + [bf16(owned, width)] * 2
        + [bf16(owned // PARTS, width)] * (2 * PARTS),
        in_specs=vmem(5) + anywhere(3),
        out_specs=vmem(4 + 2 * PARTS),
        scratch_shapes=[
            pltpu.VMEM((rows, width), jnp.bfloat16),
            pltpu.VMEM((rows, width), jnp.bfloat16),
            pltpu.VMEM((rows, units), jnp.bfloat16),
            dma((2,)),
            dma((2,)),
        ],
        compiler_params=params,
        cost_estimate=cost(DIAGONAL_COST, rows),
        name="diagonal",
    )(
        w_in_all, w_out_all, bias, grad_terms, grad_last,
        tok_diag, cot_diag, diag_other,
    )
    received_diag = to_core(other_diag)
    relayed = [to_far(piece, 1) for piece in grad_far[PARTS:]]
    mixed_own, sum_diag = pl.pallas_call(
        last_pairs_kernel,
        out_shape=[bf16(rows, feats)] * 2,
        in_specs=vmem(4),
        out_specs=vmem(2),
        compiler_params=params,
        cost_estimate=cost(rows, rows),
        name="pair_sum_diagonal",
    )(mine, diag_other, mine_diag, received_diag)
    mixed_diag = to_diagonal(sum_diag)
    from_two = []
    for at in range(PARTS):
        piece, _ = barrier((grad_far[at], sum_diag))
        (line_sum,) = pl.pallas_call(
            functools.partial(pair_kernel, owned // PARTS, 0),
            out_shape=[bf16(owned // PARTS, width)],
            in_specs=vmem(2),
            out_specs=vmem(1),
            compiler_params=params,
            cost_estimate=cost(rows, rows),
            name="line_sum",
        )(piece, relayed[at])
        from_two.append(to_far(line_sum, 2))
    grad_one, _ = barrier((grad_one, line_sum))
    from_one = to_far(grad_one, 1)
    mixed = pl.pallas_call(
        plane_kernel,
        out_shape=f32(rows, feats),
        in_specs=vmem(3),
        out_specs=pl.BlockSpec(memory_space=pltpu.VMEM),
        compiler_params=params,
        cost_estimate=cost(PLANE_COST, rows),
        name="plane_sum",
    )(mixed_own, mixed_x, mixed_y)
    mixed = (mixed + mixed_diag.astype(jnp.float32)).astype(jnp.bfloat16)
    *from_two, mixed = barrier((*from_two, mixed))
    from_two = jnp.concatenate(from_two)
    total = (
        grad_own.astype(jnp.float32)
        + from_one.astype(jnp.float32)
        + from_two.astype(jnp.float32)
    )
    return (mixed, total * scale)


def solution(mesh):
    dp, tensor = mesh.shape["dp"], mesh.shape["tensor"]
    far = dp // NEAR
    if tensor == 2 and far == 4:
        fine = Mesh(mesh.devices.reshape(far, 2, 2, tensor), AXES)
        rows, owners, halves = ("far", "y", "x"), AXES, "core"
        body = on_device_lines
    else:
        fine = Mesh(mesh.devices.reshape(far, NEAR, tensor), ("far", "near", "tensor"))
        rows, owners, halves = ("far", "near"), ("far", "near", "tensor"), "tensor"
        body = on_device_any
    in_specs = (P(rows, halves), P(rows, halves), P(owners, None), P(owners), P(owners, None))
    out_specs = (P(rows, halves), P(owners, None))
    return jax.shard_map(
        body, mesh=fine, in_specs=in_specs, out_specs=out_specs, check_vma=False
    )
```

```python
import functools
import math

import jax
import jax.numpy as jnp
from jax import lax
from jax.experimental import pallas as pl
from jax.experimental.pallas import tpu as pltpu
from jax.sharding import Mesh, PartitionSpec as P

NEAR = 4
AXES = ("far", "y", "x", "core")
CONTRACT_LAST = (((1,), (1,)), ((), ()))
CONTRACT_FIRST = (((0,), (0,)), ((), ()))
VMEM_LIMIT = 28 * 1024 * 1024
PLANE_COST = 10**10
GRADIENT_COST = 10**10
DIAGONAL_COST = 10**6
EXTRA = 48
PAIR_COST = 10**10
PARTS = 2
BIAS_ROWS = 8
MORE = 16


def gelu_parts(value):
    coeff = 0.7978845608
    inner = coeff * (value + 0.044715 * value * value * value)
    tangent = jnp.tanh(inner)
    result = 0.5 * value * (1.0 + tangent)
    slope = 0.5 * (1.0 + tangent) + 0.5 * value * (1.0 - tangent * tangent) * coeff * (
        1.0 + 3.0 * 0.044715 * value * value
    )
    return (result, slope)


def on_device_any(tokens, cotangent, w_in, b_in, w_out):
    far, near, tensor = lax.axis_size("far"), lax.axis_size("near"), lax.axis_size("tensor")
    rows, feats = tokens.shape
    owned, width = w_in.shape
    scale = 1.0 / math.sqrt(rows * far * near)
    bias_rows = jnp.pad(b_in.reshape(1, owned), ((0, 15), (0, width - owned)))
    weights = lax.all_gather(jnp.concatenate([w_in, w_out, bias_rows], 0), "far", axis=0)
    in_rows = weights[:, :owned].reshape(far * owned, width)
    proj_rows = weights[:, owned : 2 * owned].reshape(far * owned, width)
    bias = weights[:, 2 * owned, :owned].reshape(far * owned).astype(jnp.float32)
    tok = lax.all_gather(tokens, ("near", "tensor"), axis=0).reshape(near, tensor, rows, feats)
    cot = lax.all_gather(cotangent, ("near", "tensor"), axis=0).reshape(near, tensor, rows, feats)
    tok_full = tok.transpose(0, 2, 1, 3).reshape(near * rows, width)
    cot_full = cot.transpose(0, 2, 1, 3).reshape(near * rows, width)
    pre = lax.dot_general(
        tok_full, in_rows, CONTRACT_LAST, preferred_element_type=jnp.float32
    ) + bias
    act_value, slope = gelu_parts(pre)
    act = act_value.astype(jnp.bfloat16)
    term = jnp.dot(act, proj_rows, preferred_element_type=jnp.float32).astype(jnp.bfloat16)
    term = term.reshape(near, rows, tensor, feats).transpose(0, 2, 1, 3)
    mixed = lax.psum_scatter(
        term.reshape(near * tensor, rows, feats), ("near", "tensor"), scatter_dimension=0
    )
    dact = lax.dot_general(cot_full, proj_rows, CONTRACT_LAST, preferred_element_type=jnp.float32)
    dpre = (dact * slope).astype(jnp.bfloat16)
    grad = lax.dot_general(dpre, tok_full, CONTRACT_FIRST, preferred_element_type=jnp.float32)
    grad_sum = lax.psum_scatter(grad.astype(jnp.bfloat16), "far", scatter_dimension=0, tiled=True)
    return (mixed, grad_sum.astype(jnp.float32) * scale)


def half_columns(core, shift, feats):
    return pl.ds(pl.multiple_of(lax.rem(core + shift, 2) * feats, feats), feats)


def side_by_side(core, pair, whole, start, sem):
    rows, feats = pair[0].shape
    return [
        pltpu.make_async_copy(
            pair[shift],
            whole.at[pl.ds(start, rows), half_columns(core, shift, feats)],
            sem.at[shift],
        )
        for shift in range(2)
    ]


def weight_copies(refs, owned, w_in, w_out, sem):
    copies = []
    for at, ref in enumerate(refs):
        spot = pl.ds(at * owned, owned)
        copies.append(pltpu.make_async_copy(ref.at[pl.ds(0, owned)], w_in.at[spot], sem.at[0, at]))
        copies.append(
            pltpu.make_async_copy(ref.at[pl.ds(owned, owned)], w_out.at[spot], sem.at[1, at])
        )
    return copies


def bias_of(ref, owned):
    return ref[2 * owned : 2 * owned + BIAS_ROWS, :owned].astype(jnp.float32)


def run(copies, what):
    for copy in copies:
        getattr(copy, what)()


def activate(tok, w_in, bias):
    pre = lax.dot_general(
        tok, w_in, CONTRACT_LAST, preferred_element_type=jnp.float32
    ) + bias
    return gelu_parts(pre)


def dot_last(left, right):
    return lax.dot_general(left, right, CONTRACT_LAST, preferred_element_type=jnp.float32)


def dot_first(left, right):
    return lax.dot_general(left, right, CONTRACT_FIRST, preferred_element_type=jnp.float32)


def early_block(start, step, tok, cot, w_in, w_out, bias, mixed_ref, dpre):
    @pl.loop(0, 2)
    def _(sub):
        spot = pl.ds(pl.multiple_of(start + sub * step, step), step)
        value, slope = activate(tok[spot, :], w_in[...], bias[0:1, :])
        dact = dot_last(cot[spot, :], w_out[...])
        dpre[spot, :] = (dact * slope).astype(jnp.bfloat16)
        mixed_ref[spot, :] = jnp.dot(
            value.astype(jnp.bfloat16), w_out[...], preferred_element_type=jnp.float32
        )


def early_kernel(owned, *refs):
    pair_refs, w_refs = refs[:6], refs[6:9]
    mixed_ref, grad_ref, tok, cot, w_in, w_out, bias = refs[9:16]
    dpre, tok_sem, cot_sem, w_sem = refs[16:]
    core = lax.axis_index("core")
    rows = pair_refs[0].shape[1]
    w_copies = weight_copies(w_refs, owned, w_in, w_out, w_sem)
    loads = []
    for block in range(NEAR - 1):
        first, second = pair_refs[2 * block], pair_refs[2 * block + 1]
        loads.append(
            side_by_side(core, (first.at[0], second.at[0]), tok, block * rows, tok_sem.at[block])
            + side_by_side(core, (first.at[1], second.at[1]), cot, block * rows, cot_sem.at[block])
        )
    run(w_copies, "start")
    for load in loads:
        run(load, "start")
    for at, ref in enumerate(w_refs):
        bias[:, at * owned : (at + 1) * owned] = bias_of(ref, owned)
    run(w_copies, "wait")
    for block, load in enumerate(loads):
        run(load, "wait")
        early_block(
            block * rows, rows // 2, tok, cot, w_in, w_out, bias, mixed_ref, dpre
        )
    grad_ref[...] = dot_first(dpre[...], tok[...])


def output_kernel(owned, *refs):
    tok, early_mixed, w_in, w_out, bias, w_three = refs[:6]
    mine_ref, near_ref, own_ref, slope_ref, w_in_all, w_out_all, bias_all, sem = refs[6:]
    core = lax.axis_index("core")
    rows, feats = own_ref.shape
    two, three = 2 * owned, 3 * owned
    first, last = pl.ds(0, three), pl.ds(three, owned)
    copies = [
        pltpu.make_async_copy(w_in, w_in_all.at[first], sem.at[0]),
        pltpu.make_async_copy(w_three.at[pl.ds(0, owned)], w_in_all.at[last], sem.at[1]),
        pltpu.make_async_copy(w_out, w_out_all.at[first], sem.at[2]),
        pltpu.make_async_copy(w_three.at[pl.ds(owned, owned)], w_out_all.at[last], sem.at[3]),
    ]
    run(copies, "start")
    bias_last = bias_of(w_three, owned)
    bias_all[:, :three] = bias[...]
    bias_all[:, three:] = bias_last
    step = tok.shape[0] // 6
    for at in range(6):
        spot = slice(at * step, (at + 1) * step)
        value, slope = activate(tok[spot, :], w_three[:owned, :], bias_last[0:1, :])
        slope_ref[spot, :] = slope
        act = value.astype(jnp.bfloat16)
        if at * step < rows:
            far_ref, there = own_ref, spot
        else:
            far_ref, there = near_ref, slice(at * step - rows, (at + 1) * step - rows)
        for shift, ref, to in ((0, mine_ref, spot), (1, far_ref, there)):
            half = half_columns(core, shift, feats)
            ref[to, :] = (
                early_mixed[spot, half]
                + jnp.dot(act, w_three[owned:two, half], preferred_element_type=jnp.float32)
            ).astype(jnp.bfloat16)

    run(copies, "wait")


def gradient_kernel(tok, cot, slope, w_three, grad_ref, dpre):
    owned = slope.shape[1]
    step = tok.shape[0] // 6
    for at in range(6):
        spot = slice(at * step, (at + 1) * step)
        dact = dot_last(cot[spot, :], w_three[owned : 2 * owned, :])
        dpre[spot, :] = (dact * slope[spot, :]).astype(jnp.bfloat16)
    grad_ref[...] = dot_first(dpre[...], tok[...])


def diagonal_kernel(owned, *refs):
    w_in, w_out, bias, grad_first, grad_last = refs[:5]
    tok_ref, cot_ref, far_ref = refs[5:8]
    mine_ref, other_ref, own_ref, one_ref = refs[8:12]
    two_refs, three_refs = refs[12 : 12 + PARTS], refs[12 + PARTS : 12 + 2 * PARTS]
    tok, cot, dpre, tok_sem, cot_sem = refs[12 + 2 * PARTS :]
    core = lax.axis_index("core")
    rows, feats = mine_ref.shape
    two = 2 * owned
    first, second = pl.ds(0, rows), pl.ds(rows, rows)
    load = side_by_side(core, (tok_ref.at[first], far_ref.at[first]), tok, 0, tok_sem)
    cot_load = side_by_side(core, (cot_ref, far_ref.at[second]), cot, 0, cot_sem)
    run(load + cot_load, "start")
    run(load + cot_load, "wait")
    step = rows // 2
    for sub in range(2):
        spot = slice(sub * step, (sub + 1) * step)
        value, slope = activate(tok[spot, :], w_in[...], bias[0:1, :])
        act = value.astype(jnp.bfloat16)
        dact = dot_last(cot[spot, :], w_out[...])
        dpre[spot, :] = (dact * slope).astype(jnp.bfloat16)
        for shift, ref in enumerate((mine_ref, other_ref)):
            ref[spot, :] = jnp.dot(
                act, w_out[:, half_columns(core, shift, feats)], preferred_element_type=jnp.float32
            ).astype(jnp.bfloat16)

    grad = dot_first(dpre[:, two:], tok[...])
    middle, last = grad[:owned] + grad_first[two:, :], grad[owned:] + grad_last[...]
    part = owned // PARTS
    for at in range(PARTS):
        two_refs[at][...] = middle[at * part : (at + 1) * part].astype(jnp.bfloat16)
        three_refs[at][...] = last[at * part : (at + 1) * part].astype(jnp.bfloat16)
    grad = grad_first[:two, :] + dot_first(dpre[:, :two], tok[...])
    own_ref[...] = grad[:owned].astype(jnp.bfloat16)
    one_ref[...] = grad[owned:].astype(jnp.bfloat16)


def pair_kernel(rows, first, mine_ref, other_ref, *out_refs):
    for block, ref in enumerate(out_refs):
        mine, other = pl.ds((first + block) * rows, rows), pl.ds(block * rows, rows)
        ref[:rows, :] = (
            mine_ref[mine, :].astype(jnp.float32) + other_ref[other, :].astype(jnp.float32)
        ).astype(jnp.bfloat16)
        if ref.shape[0] > rows:
            ref[rows:, :] = jnp.zeros_like(ref[rows:, :])


def last_pairs_kernel(mine_ref, far_ref, diag_ref, other_ref, own_sum_ref, diag_sum_ref):
    rows = diag_ref.shape[0]
    diag_sum_ref[...] = (
        diag_ref[...].astype(jnp.float32) + other_ref[...].astype(jnp.float32)
    ).astype(jnp.bfloat16)
    own_sum_ref[...] = (
        mine_ref[:rows, :].astype(jnp.float32)
        + far_ref[2 * rows : 3 * rows, :].astype(jnp.float32)
    ).astype(jnp.bfloat16)


def plane_kernel(own_ref, x_ref, y_ref, out_ref):
    rows = own_ref.shape[0]
    out_ref[...] = (
        own_ref[...].astype(jnp.float32)
        + x_ref[:rows, :].astype(jnp.float32)
        + y_ref[:rows, :].astype(jnp.float32)
    )


def vmem(count):
    return [pl.BlockSpec(memory_space=pltpu.VMEM)] * count


def anywhere(count):
    return [pl.BlockSpec(memory_space=pl.ANY)] * count


def bf16(*shape):
    return jax.ShapeDtypeStruct(shape, jnp.bfloat16)


def permute(value, there):
    pairs = []
    for f in range(4):
        for y in range(2):
            for x in range(2):
                for c in range(2):
                    to = there(f, y, x, c)
                    here = ((f * 2 + y) * 2 + x) * 2 + c
                    pairs.append((here, ((to[0] * 2 + to[1]) * 2 + to[2]) * 2 + to[3]))
    return lax.ppermute(value, AXES, pairs)


def to_x(value):
    return permute(value, lambda f, y, x, c: (f, y, 1 - x, c))


def to_y(value):
    return permute(value, lambda f, y, x, c: (f, 1 - y, x, c))


def to_diagonal(value):
    return permute(value, lambda f, y, x, c: (f, 1 - y, 1 - x, c))


def to_core(value):
    return permute(value, lambda f, y, x, c: (f, y, x, 1 - c))


def to_far(value, flip):
    return permute(value, lambda f, y, x, c: (f ^ flip, y, x, c))


def on_device_lines(tokens, cotangent, w_in, b_in, w_out):
    rows, feats = tokens.shape
    owned, width = w_in.shape
    units = 4 * owned
    count = NEAR * rows
    scale = 1.0 / math.sqrt(4 * count)
    params = pltpu.CompilerParams(vmem_limit_bytes=VMEM_LIMIT)
    dma = pltpu.SemaphoreType.DMA
    barrier = lax.optimization_barrier
    early_rows = (NEAR - 1) * rows

    def f32(*shape):
        return jax.ShapeDtypeStruct(shape, jnp.float32)

    def cost(flops, traffic):
        return pl.CostEstimate(flops=flops, bytes_accessed=traffic, transcendentals=0)

    bias_rows = jnp.pad(b_in.reshape(1, owned), ((0, BIAS_ROWS - 1), (0, width - owned)))
    own_w = jnp.concatenate([w_in, w_out, bias_rows], 0)
    own = jnp.stack([tokens, cotangent])
    w_two, w_one = to_far(own_w, 2), to_far(own_w, 1)
    from_x, from_y = to_x(own), to_y(own)
    own_other = to_core(own)
    from_x, from_y, own_other = barrier((from_x, from_y, own_other))
    tok_diag = to_y(from_x.reshape(2 * rows, feats)[: rows + EXTRA])
    cot_diag = to_x(from_y[1])
    x_other, y_other = to_core(from_x), to_core(from_y)
    w_three = to_far(w_two, 1)
    mixed_terms, grad_terms, tok, cot, w_in_three, w_out_three, bias = (
        pl.pallas_call(
            functools.partial(early_kernel, owned),
            out_shape=(
                f32(early_rows, width),
                f32(3 * owned, width),
                bf16(early_rows, width),
                bf16(early_rows, width),
                bf16(3 * owned, width),
                bf16(3 * owned, width),
                f32(BIAS_ROWS, 3 * owned),
            ),
            in_specs=anywhere(6) + vmem(3),
            out_specs=vmem(7),
            scratch_shapes=[
                pltpu.VMEM((early_rows, 3 * owned), jnp.bfloat16),
                dma((NEAR - 1, 2)),
                dma((NEAR - 1, 2)),
                dma((2, 3)),
            ],
            compiler_params=params,
            cost_estimate=cost(early_rows * units, early_rows),
            name="early",
        )(own, own_other, from_x, x_other, from_y, y_other, own_w, w_one, w_two)
    )

    mine, other, other_own, slope, w_in_all, w_out_all, bias = pl.pallas_call(
        functools.partial(output_kernel, owned),
        out_shape=(
            bf16(early_rows, feats),
            bf16(2 * rows, feats),
            bf16(rows, feats),
            f32(early_rows, owned),
            bf16(units, width),
            bf16(units, width),
            f32(BIAS_ROWS, units),
        ),
        in_specs=vmem(6),
        out_specs=vmem(7),
        scratch_shapes=[dma((4,))],
        compiler_params=params,
        cost_estimate=cost(early_rows * units, early_rows),
        name="output",
    )(tok, mixed_terms, w_in_three, w_out_three, bias, w_three)
    tok_diag, cot_diag, other = barrier((tok_diag, cot_diag, other))
    received = to_core(other)
    diag_other = to_core(jnp.concatenate([tok_diag[:rows], cot_diag, other_own]))
    slope, tok_diag = barrier((slope, tok_diag))
    grad_last = pl.pallas_call(
        gradient_kernel,
        out_shape=f32(owned, width),
        in_specs=vmem(4),
        out_specs=pl.BlockSpec(memory_space=pltpu.VMEM),
        scratch_shapes=[pltpu.VMEM((early_rows, owned), jnp.bfloat16)],
        compiler_params=params,
        cost_estimate=cost(GRADIENT_COST, early_rows),
        name="gradient",
    )(tok, cot, slope, w_three)

    mine, grad_last = barrier((mine, grad_last))
    sums = pl.pallas_call(
        functools.partial(pair_kernel, rows, 1),
        out_shape=[bf16(rows + MORE, feats)] * 2,
        in_specs=vmem(2),
        out_specs=vmem(2),
        compiler_params=params,
        cost_estimate=cost(PAIR_COST, rows),
        name="pair_sum",
    )(mine, received)
    mixed_x, mixed_y = to_x(sums[0]), to_y(sums[1])
    grad_terms, _ = barrier((grad_terms, sums[0]))

    mine_diag, other_diag, grad_own, grad_one, *grad_far = pl.pallas_call(
        functools.partial(diagonal_kernel, owned),
        out_shape=[bf16(rows, feats)] * 2
        + [bf16(owned, width)] * 2
        + [bf16(owned // PARTS, width)] * (2 * PARTS),
        in_specs=vmem(5) + anywhere(3),
        out_specs=vmem(4 + 2 * PARTS),
        scratch_shapes=[
            pltpu.VMEM((rows, width), jnp.bfloat16),
            pltpu.VMEM((rows, width), jnp.bfloat16),
            pltpu.VMEM((rows, units), jnp.bfloat16),
            dma((2,)),
            dma((2,)),
        ],
        compiler_params=params,
        cost_estimate=cost(DIAGONAL_COST, rows),
        name="diagonal",
    )(
        w_in_all, w_out_all, bias, grad_terms, grad_last,
        tok_diag, cot_diag, diag_other,
    )
    received_diag = to_core(other_diag)
    relayed = [to_far(piece, 1) for piece in grad_far[PARTS:]]
    mixed_own, sum_diag = pl.pallas_call(
        last_pairs_kernel,
        out_shape=[bf16(rows, feats)] * 2,
        in_specs=vmem(4),
        out_specs=vmem(2),
        compiler_params=params,
        cost_estimate=cost(rows, rows),
        name="pair_sum_diagonal",
    )(mine, diag_other, mine_diag, received_diag)
    mixed_diag = to_diagonal(sum_diag)
    from_two = []
    for at in range(PARTS):
        piece, _ = barrier((grad_far[at], sum_diag))
        (line_sum,) = pl.pallas_call(
            functools.partial(pair_kernel, owned // PARTS, 0),
            out_shape=[bf16(owned // PARTS, width)],
            in_specs=vmem(2),
            out_specs=vmem(1),
            compiler_params=params,
            cost_estimate=cost(rows, rows),
            name="line_sum",
        )(piece, relayed[at])
        from_two.append(to_far(line_sum, 2))
    grad_one, _ = barrier((grad_one, line_sum))
    from_one = to_far(grad_one, 1)
    mixed = pl.pallas_call(
        plane_kernel,
        out_shape=f32(rows, feats),
        in_specs=vmem(3),
        out_specs=pl.BlockSpec(memory_space=pltpu.VMEM),
        compiler_params=params,
        cost_estimate=cost(PLANE_COST, rows),
        name="plane_sum",
    )(mixed_own, mixed_x, mixed_y)
    mixed = (mixed + mixed_diag.astype(jnp.float32)).astype(jnp.bfloat16)
    *from_two, mixed = barrier((*from_two, mixed))
    from_two = jnp.concatenate(from_two)
    total = (
        grad_own.astype(jnp.float32)
        + from_one.astype(jnp.float32)
        + from_two.astype(jnp.float32)
    )
    return (mixed, total * scale)


def solution(mesh):
    dp, tensor = mesh.shape["dp"], mesh.shape["tensor"]
    far = dp // NEAR
    if tensor == 2 and far == 4:
        fine = Mesh(mesh.devices.reshape(far, 2, 2, tensor), AXES)
        rows, owners, halves = ("far", "y", "x"), AXES, "core"
        body = on_device_lines
    else:
        fine = Mesh(mesh.devices.reshape(far, NEAR, tensor), ("far", "near", "tensor"))
        rows, owners, halves = ("far", "near"), ("far", "near", "tensor"), "tensor"
        body = on_device_any
    in_specs = (P(rows, halves), P(rows, halves), P(owners, None), P(owners), P(owners, None))
    out_specs = (P(rows, halves), P(owners, None))
    return jax.shard_map(
        body, mesh=fine, in_specs=in_specs, out_specs=out_specs, check_vma=False
    )
```

```python
import functools
import math

import jax
import jax.numpy as jnp
from jax import lax
from jax.experimental import pallas as pl
from jax.experimental.pallas import tpu as pltpu
from jax.sharding import Mesh, PartitionSpec as P

NEAR = 4
AXES = ("far", "y", "x", "core")
CONTRACT_LAST = (((1,), (1,)), ((), ()))
CONTRACT_FIRST = (((0,), (0,)), ((), ()))
VMEM_LIMIT = 28 * 1024 * 1024
PLANE_COST = 10**10
GRADIENT_COST = 10**10
DIAGONAL_COST = 10**6
EXTRA = 48
PAIR_COST = 10**10
PARTS = 2
BIAS_ROWS = 8
MORE = 16


def gelu_parts(value):
    coeff = 0.7978845608
    inner = coeff * (value + 0.044715 * value * value * value)
    tangent = jnp.tanh(inner)
    result = 0.5 * value * (1.0 + tangent)
    slope = 0.5 * (1.0 + tangent) + 0.5 * value * (1.0 - tangent * tangent) * coeff * (
        1.0 + 3.0 * 0.044715 * value * value
    )
    return (result, slope)


def on_device_any(tokens, cotangent, w_in, b_in, w_out):
    far, near, tensor = lax.axis_size("far"), lax.axis_size("near"), lax.axis_size("tensor")
    rows, feats = tokens.shape
    owned, width = w_in.shape
    scale = 1.0 / math.sqrt(rows * far * near)
    bias_rows = jnp.pad(b_in.reshape(1, owned), ((0, 15), (0, width - owned)))
    weights = lax.all_gather(jnp.concatenate([w_in, w_out, bias_rows], 0), "far", axis=0)
    in_rows = weights[:, :owned].reshape(far * owned, width)
    proj_rows = weights[:, owned : 2 * owned].reshape(far * owned, width)
    bias = weights[:, 2 * owned, :owned].reshape(far * owned).astype(jnp.float32)
    tok = lax.all_gather(tokens, ("near", "tensor"), axis=0).reshape(near, tensor, rows, feats)
    cot = lax.all_gather(cotangent, ("near", "tensor"), axis=0).reshape(near, tensor, rows, feats)
    tok_full = tok.transpose(0, 2, 1, 3).reshape(near * rows, width)
    cot_full = cot.transpose(0, 2, 1, 3).reshape(near * rows, width)
    pre = lax.dot_general(
        tok_full, in_rows, CONTRACT_LAST, preferred_element_type=jnp.float32
    ) + bias
    act_value, slope = gelu_parts(pre)
    act = act_value.astype(jnp.bfloat16)
    term = jnp.dot(act, proj_rows, preferred_element_type=jnp.float32).astype(jnp.bfloat16)
    term = term.reshape(near, rows, tensor, feats).transpose(0, 2, 1, 3)
    mixed = lax.psum_scatter(
        term.reshape(near * tensor, rows, feats), ("near", "tensor"), scatter_dimension=0
    )
    dact = lax.dot_general(cot_full, proj_rows, CONTRACT_LAST, preferred_element_type=jnp.float32)
    dpre = (dact * slope).astype(jnp.bfloat16)
    grad = lax.dot_general(dpre, tok_full, CONTRACT_FIRST, preferred_element_type=jnp.float32)
    grad_sum = lax.psum_scatter(grad.astype(jnp.bfloat16), "far", scatter_dimension=0, tiled=True)
    return (mixed, grad_sum.astype(jnp.float32) * scale)


def half_columns(core, shift, feats):
    return pl.ds(pl.multiple_of(lax.rem(core + shift, 2) * feats, feats), feats)


def side_by_side(core, pair, whole, start, sem):
    rows, feats = pair[0].shape
    return [
        pltpu.make_async_copy(
            pair[shift],
            whole.at[pl.ds(start, rows), half_columns(core, shift, feats)],
            sem.at[shift],
        )
        for shift in range(2)
    ]


def weight_copies(refs, owned, w_in, w_out, sem):
    copies = []
    for at, ref in enumerate(refs):
        spot = pl.ds(at * owned, owned)
        copies.append(pltpu.make_async_copy(ref.at[pl.ds(0, owned)], w_in.at[spot], sem.at[0, at]))
        copies.append(
            pltpu.make_async_copy(ref.at[pl.ds(owned, owned)], w_out.at[spot], sem.at[1, at])
        )
    return copies


def bias_of(ref, owned):
    return ref[2 * owned : 2 * owned + BIAS_ROWS, :owned].astype(jnp.float32)


def run(copies, what):
    for copy in copies:
        getattr(copy, what)()


def activate(tok, w_in, bias):
    pre = lax.dot_general(
        tok, w_in, CONTRACT_LAST, preferred_element_type=jnp.float32
    ) + bias
    return gelu_parts(pre)


def dot_last(left, right):
    return lax.dot_general(left, right, CONTRACT_LAST, preferred_element_type=jnp.float32)


def dot_first(left, right):
    return lax.dot_general(left, right, CONTRACT_FIRST, preferred_element_type=jnp.float32)


def early_block(start, step, tok, cot, w_in, w_out, bias, two, act_ref, dpre_ref, mixed_ref, dpre):
    @pl.loop(0, 2)
    def _(sub):
        spot = pl.ds(pl.multiple_of(start + sub * step, step), step)
        value, slope = activate(tok[spot, :], w_in[...], bias[0:1, :])
        act = value.astype(jnp.bfloat16)
        act_ref[spot, :] = act[:, two:]
        dact = dot_last(cot[spot, :], w_out[...])
        terms = (dact * slope).astype(jnp.bfloat16)
        dpre[spot, :] = terms[:, :two]
        dpre_ref[spot, :] = terms[:, two:]
        mixed_ref[spot, :] = jnp.dot(
            act[:, :two], w_out[:two, :], preferred_element_type=jnp.float32
        )


def early_kernel(owned, *refs):
    pair_refs, w_refs = refs[:6], refs[6:9]
    act_ref, dpre_ref, mixed_ref, grad_ref, tok, cot, w_in, w_out, bias = refs[9:18]
    dpre, tok_sem, cot_sem, w_sem = refs[18:]
    core = lax.axis_index("core")
    rows = pair_refs[0].shape[1]
    w_copies = weight_copies(w_refs, owned, w_in, w_out, w_sem)
    loads = []
    for block in range(NEAR - 1):
        first, second = pair_refs[2 * block], pair_refs[2 * block + 1]
        loads.append(
            side_by_side(core, (first.at[0], second.at[0]), tok, block * rows, tok_sem.at[block])
            + side_by_side(core, (first.at[1], second.at[1]), cot, block * rows, cot_sem.at[block])
        )
    run(w_copies, "start")
    for load in loads:
        run(load, "start")
    for at, ref in enumerate(w_refs):
        bias[:, at * owned : (at + 1) * owned] = bias_of(ref, owned)
    run(w_copies, "wait")
    for block, load in enumerate(loads):
        run(load, "wait")
        early_block(
            block * rows, rows // 2, tok, cot, w_in, w_out, bias, 2 * owned,
            act_ref, dpre_ref, mixed_ref, dpre,
        )
    grad_ref[...] = dot_first(dpre[...], tok[...])


def output_kernel(owned, *refs):
    act_two, tok, early_mixed, w_in, w_out, bias, w_three = refs[:7]
    mine_ref, near_ref, own_ref, slope_ref, w_in_all, w_out_all, bias_all = refs[7:14]
    w_last, sem = refs[14:]
    core = lax.axis_index("core")
    rows, feats = own_ref.shape
    two, three = 2 * owned, 3 * owned
    first, last = pl.ds(0, three), pl.ds(three, owned)
    copies = [
        pltpu.make_async_copy(w_in, w_in_all.at[first], sem.at[0]),
        pltpu.make_async_copy(w_three.at[pl.ds(0, owned)], w_in_all.at[last], sem.at[1]),
        pltpu.make_async_copy(w_out, w_out_all.at[first], sem.at[2]),
        pltpu.make_async_copy(w_three.at[pl.ds(owned, owned)], w_out_all.at[last], sem.at[3]),
    ]
    run(copies, "start")
    bias_last = bias_of(w_three, owned)
    bias_all[:, :three] = bias[...]
    bias_all[:, three:] = bias_last
    w_last[:owned, :] = w_out[two:, :]
    w_last[owned:, :] = w_three[owned:two, :]
    step = tok.shape[0] // 6
    for at in range(6):
        spot = slice(at * step, (at + 1) * step)
        value, slope = activate(tok[spot, :], w_three[:owned, :], bias_last[0:1, :])
        slope_ref[spot, :] = slope
        act = jnp.concatenate([act_two[spot, :], value.astype(jnp.bfloat16)], axis=1)
        if at * step < rows:
            far_ref, there = own_ref, spot
        else:
            far_ref, there = near_ref, slice(at * step - rows, (at + 1) * step - rows)
        for shift, ref, to in ((0, mine_ref, spot), (1, far_ref, there)):
            half = half_columns(core, shift, feats)
            ref[to, :] = (
                early_mixed[spot, half]
                + jnp.dot(act, w_last[:, half], preferred_element_type=jnp.float32)
            ).astype(jnp.bfloat16)

    run(copies, "wait")


def gradient_kernel(dpre_two, tok, cot, slope, w_three, grad_ref, dpre):
    owned = slope.shape[1]
    step = tok.shape[0] // 6
    for at in range(6):
        spot = slice(at * step, (at + 1) * step)
        dact = dot_last(cot[spot, :], w_three[owned : 2 * owned, :])
        last = (dact * slope[spot, :]).astype(jnp.bfloat16)
        dpre[spot, :] = jnp.concatenate([dpre_two[spot, :], last], axis=1)
    grad_ref[...] = dot_first(dpre[...], tok[...])


def diagonal_kernel(owned, *refs):
    w_in, w_out, bias, grad_first, grad_last = refs[:5]
    tok_ref, cot_ref, far_ref = refs[5:8]
    mine_ref, other_ref, own_ref, one_ref = refs[8:12]
    two_refs, three_refs = refs[12 : 12 + PARTS], refs[12 + PARTS : 12 + 2 * PARTS]
    tok, cot, dpre, tok_sem, cot_sem = refs[12 + 2 * PARTS :]
    core = lax.axis_index("core")
    rows, feats = mine_ref.shape
    two = 2 * owned
    first, second = pl.ds(0, rows), pl.ds(rows, rows)
    load = side_by_side(core, (tok_ref.at[first], far_ref.at[first]), tok, 0, tok_sem)
    cot_load = side_by_side(core, (cot_ref, far_ref.at[second]), cot, 0, cot_sem)
    run(load + cot_load, "start")
    run(load + cot_load, "wait")
    step = rows // 2
    for sub in range(2):
        spot = slice(sub * step, (sub + 1) * step)
        value, slope = activate(tok[spot, :], w_in[...], bias[0:1, :])
        act = value.astype(jnp.bfloat16)
        dact = dot_last(cot[spot, :], w_out[...])
        dpre[spot, :] = (dact * slope).astype(jnp.bfloat16)
        for shift, ref in enumerate((mine_ref, other_ref)):
            ref[spot, :] = jnp.dot(
                act, w_out[:, half_columns(core, shift, feats)], preferred_element_type=jnp.float32
            ).astype(jnp.bfloat16)

    grad = grad_last[...] + dot_first(dpre[:, two:], tok[...])
    part = owned // PARTS
    for at in range(PARTS):
        two_refs[at][...] = grad[at * part : (at + 1) * part].astype(jnp.bfloat16)
        three_refs[at][...] = grad[owned + at * part : owned + (at + 1) * part].astype(jnp.bfloat16)
    grad = grad_first[...] + dot_first(dpre[:, :two], tok[...])
    own_ref[...] = grad[:owned].astype(jnp.bfloat16)
    one_ref[...] = grad[owned:].astype(jnp.bfloat16)


def pair_kernel(rows, first, mine_ref, other_ref, *out_refs):
    for block, ref in enumerate(out_refs):
        mine, other = pl.ds((first + block) * rows, rows), pl.ds(block * rows, rows)
        ref[:rows, :] = (
            mine_ref[mine, :].astype(jnp.float32) + other_ref[other, :].astype(jnp.float32)
        ).astype(jnp.bfloat16)
        if ref.shape[0] > rows:
            ref[rows:, :] = jnp.zeros_like(ref[rows:, :])


def last_pairs_kernel(mine_ref, far_ref, diag_ref, other_ref, own_sum_ref, diag_sum_ref):
    rows = diag_ref.shape[0]
    diag_sum_ref[...] = (
        diag_ref[...].astype(jnp.float32) + other_ref[...].astype(jnp.float32)
    ).astype(jnp.bfloat16)
    own_sum_ref[...] = (
        mine_ref[:rows, :].astype(jnp.float32)
        + far_ref[2 * rows : 3 * rows, :].astype(jnp.float32)
    ).astype(jnp.bfloat16)


def plane_kernel(own_ref, x_ref, y_ref, out_ref):
    rows = own_ref.shape[0]
    out_ref[...] = (
        own_ref[...].astype(jnp.float32)
        + x_ref[:rows, :].astype(jnp.float32)
        + y_ref[:rows, :].astype(jnp.float32)
    )


def final_kernel(scale, plane_ref, diag_ref, own_ref, one_ref, *refs):
    two_refs, mixed_ref, grad_ref = refs[:-2], refs[-2], refs[-1]
    mixed_ref[...] = (plane_ref[...] + diag_ref[...].astype(jnp.float32)).astype(jnp.bfloat16)
    part = two_refs[0].shape[0]
    for at, ref in enumerate(two_refs):
        spot = slice(at * part, (at + 1) * part)
        grad_ref[spot, :] = scale * (
            own_ref[spot, :].astype(jnp.float32)
            + one_ref[spot, :].astype(jnp.float32)
            + ref[...].astype(jnp.float32)
        )


def vmem(count):
    return [pl.BlockSpec(memory_space=pltpu.VMEM)] * count


def anywhere(count):
    return [pl.BlockSpec(memory_space=pl.ANY)] * count


def bf16(*shape):
    return jax.ShapeDtypeStruct(shape, jnp.bfloat16)


def permute(value, there):
    pairs = []
    for f in range(4):
        for y in range(2):
            for x in range(2):
                for c in range(2):
                    to = there(f, y, x, c)
                    here = ((f * 2 + y) * 2 + x) * 2 + c
                    pairs.append((here, ((to[0] * 2 + to[1]) * 2 + to[2]) * 2 + to[3]))
    return lax.ppermute(value, AXES, pairs)


def to_x(value):
    return permute(value, lambda f, y, x, c: (f, y, 1 - x, c))


def to_y(value):
    return permute(value, lambda f, y, x, c: (f, 1 - y, x, c))


def to_diagonal(value):
    return permute(value, lambda f, y, x, c: (f, 1 - y, 1 - x, c))


def to_core(value):
    return permute(value, lambda f, y, x, c: (f, y, x, 1 - c))


def to_far(value, flip):
    return permute(value, lambda f, y, x, c: (f ^ flip, y, x, c))


def on_device_lines(tokens, cotangent, w_in, b_in, w_out):
    rows, feats = tokens.shape
    owned, width = w_in.shape
    units = 4 * owned
    count = NEAR * rows
    scale = 1.0 / math.sqrt(4 * count)
    params = pltpu.CompilerParams(vmem_limit_bytes=VMEM_LIMIT)
    dma = pltpu.SemaphoreType.DMA
    barrier = lax.optimization_barrier
    early_rows = (NEAR - 1) * rows

    def f32(*shape):
        return jax.ShapeDtypeStruct(shape, jnp.float32)

    def cost(flops, traffic):
        return pl.CostEstimate(flops=flops, bytes_accessed=traffic, transcendentals=0)

    bias_rows = jnp.pad(b_in.reshape(1, owned), ((0, BIAS_ROWS - 1), (0, width - owned)))
    own_w = jnp.concatenate([w_in, w_out, bias_rows], 0)
    own = jnp.stack([tokens, cotangent])
    w_two, w_one = to_far(own_w, 2), to_far(own_w, 1)
    from_x, from_y = to_x(own), to_y(own)
    own_other = to_core(own)
    from_x, from_y, own_other = barrier((from_x, from_y, own_other))
    tok_diag = to_y(from_x.reshape(2 * rows, feats)[: rows + EXTRA])
    cot_diag = to_x(from_y[1])
    x_other, y_other = to_core(from_x), to_core(from_y)
    w_three = to_far(w_two, 1)
    act_two, dpre_two, mixed_terms, grad_terms, tok, cot, w_in_three, w_out_three, bias = (
        pl.pallas_call(
            functools.partial(early_kernel, owned),
            out_shape=(
                bf16(early_rows, owned),
                bf16(early_rows, owned),
                f32(early_rows, width),
                f32(2 * owned, width),
                bf16(early_rows, width),
                bf16(early_rows, width),
                bf16(3 * owned, width),
                bf16(3 * owned, width),
                f32(BIAS_ROWS, 3 * owned),
            ),
            in_specs=anywhere(6) + vmem(3),
            out_specs=vmem(9),
            scratch_shapes=[
                pltpu.VMEM((early_rows, 2 * owned), jnp.bfloat16),
                dma((NEAR - 1, 2)),
                dma((NEAR - 1, 2)),
                dma((2, 3)),
            ],
            compiler_params=params,
            cost_estimate=cost(early_rows * units, early_rows),
            name="early",
        )(own, own_other, from_x, x_other, from_y, y_other, own_w, w_one, w_two)
    )

    mine, other, other_own, slope, w_in_all, w_out_all, bias = pl.pallas_call(
        functools.partial(output_kernel, owned),
        out_shape=(
            bf16(early_rows, feats),
            bf16(2 * rows, feats),
            bf16(rows, feats),
            f32(early_rows, owned),
            bf16(units, width),
            bf16(units, width),
            f32(BIAS_ROWS, units),
        ),
        in_specs=vmem(7),
        out_specs=vmem(7),
        scratch_shapes=[pltpu.VMEM((2 * owned, width), jnp.bfloat16), dma((4,))],
        compiler_params=params,
        cost_estimate=cost(early_rows * units, early_rows),
        name="output",
    )(act_two, tok, mixed_terms, w_in_three, w_out_three, bias, w_three)
    tok_diag, cot_diag, other = barrier((tok_diag, cot_diag, other))
    received = to_core(other)
    diag_other = to_core(jnp.concatenate([tok_diag[:rows], cot_diag, other_own]))
    slope, tok_diag = barrier((slope, tok_diag))
    grad_last = pl.pallas_call(
        gradient_kernel,
        out_shape=f32(2 * owned, width),
        in_specs=vmem(5),
        out_specs=pl.BlockSpec(memory_space=pltpu.VMEM),
        scratch_shapes=[pltpu.VMEM((early_rows, 2 * owned), jnp.bfloat16)],
        compiler_params=params,
        cost_estimate=cost(GRADIENT_COST, early_rows),
        name="gradient",
    )(dpre_two, tok, cot, slope, w_three)

    mine, grad_last = barrier((mine, grad_last))
    sums = pl.pallas_call(
        functools.partial(pair_kernel, rows, 1),
        out_shape=[bf16(rows + MORE, feats)] * 2,
        in_specs=vmem(2),
        out_specs=vmem(2),
        compiler_params=params,
        cost_estimate=cost(PAIR_COST, rows),
        name="pair_sum",
    )(mine, received)
    mixed_x, mixed_y = to_x(sums[0]), to_y(sums[1])
    grad_terms, _ = barrier((grad_terms, sums[0]))

    mine_diag, other_diag, grad_own, grad_one, *grad_far = pl.pallas_call(
        functools.partial(diagonal_kernel, owned),
        out_shape=[bf16(rows, feats)] * 2
        + [bf16(owned, width)] * 2
        + [bf16(owned // PARTS, width)] * (2 * PARTS),
        in_specs=vmem(5) + anywhere(3),
        out_specs=vmem(4 + 2 * PARTS),
        scratch_shapes=[
            pltpu.VMEM((rows, width), jnp.bfloat16),
            pltpu.VMEM((rows, width), jnp.bfloat16),
            pltpu.VMEM((rows, units), jnp.bfloat16),
            dma((2,)),
            dma((2,)),
        ],
        compiler_params=params,
        cost_estimate=cost(DIAGONAL_COST, rows),
        name="diagonal",
    )(
        w_in_all, w_out_all, bias, grad_terms, grad_last,
        tok_diag, cot_diag, diag_other,
    )
    received_diag = to_core(other_diag)
    relayed = [to_far(piece, 1) for piece in grad_far[PARTS:]]
    mixed_own, sum_diag = pl.pallas_call(
        last_pairs_kernel,
        out_shape=[bf16(rows, feats)] * 2,
        in_specs=vmem(4),
        out_specs=vmem(2),
        compiler_params=params,
        cost_estimate=cost(rows, rows),
        name="pair_sum_diagonal",
    )(mine, diag_other, mine_diag, received_diag)
    mixed_diag = to_diagonal(sum_diag)
    from_two = []
    for at in range(PARTS):
        piece, _ = barrier((grad_far[at], sum_diag))
        (line_sum,) = pl.pallas_call(
            functools.partial(pair_kernel, owned // PARTS, 0),
            out_shape=[bf16(owned // PARTS, width)],
            in_specs=vmem(2),
            out_specs=vmem(1),
            compiler_params=params,
            cost_estimate=cost(rows, rows),
            name="line_sum",
        )(piece, relayed[at])
        from_two.append(to_far(line_sum, 2))
    grad_one, _ = barrier((grad_one, line_sum))
    from_one = to_far(grad_one, 1)
    mixed = pl.pallas_call(
        plane_kernel,
        out_shape=f32(rows, feats),
        in_specs=vmem(3),
        out_specs=pl.BlockSpec(memory_space=pltpu.VMEM),
        compiler_params=params,
        cost_estimate=cost(PLANE_COST, rows),
        name="plane_sum",
    )(mixed_own, mixed_x, mixed_y)
    *from_two, from_one, mixed = barrier((*from_two, from_one, mixed))
    return pl.pallas_call(
        functools.partial(final_kernel, scale),
        out_shape=(bf16(rows, feats), f32(owned, width)),
        in_specs=vmem(4 + PARTS),
        out_specs=(vmem(1)[0], vmem(1)[0]),
        compiler_params=params,
        cost_estimate=cost(rows, rows),
        name="results",
    )(mixed, mixed_diag, grad_own, from_one, *from_two)


def solution(mesh):
    dp, tensor = mesh.shape["dp"], mesh.shape["tensor"]
    far = dp // NEAR
    if tensor == 2 and far == 4:
        fine = Mesh(mesh.devices.reshape(far, 2, 2, tensor), AXES)
        rows, owners, halves = ("far", "y", "x"), AXES, "core"
        body = on_device_lines
    else:
        fine = Mesh(mesh.devices.reshape(far, NEAR, tensor), ("far", "near", "tensor"))
        rows, owners, halves = ("far", "near"), ("far", "near", "tensor"), "tensor"
        body = on_device_any
    in_specs = (P(rows, halves), P(rows, halves), P(owners, None), P(owners), P(owners, None))
    out_specs = (P(rows, halves), P(owners, None))
    return jax.shard_map(
        body, mesh=fine, in_specs=in_specs, out_specs=out_specs, check_vma=False
    )
```

```python
import functools
import math

import jax
import jax.numpy as jnp
from jax import lax
from jax.experimental import pallas as pl
from jax.experimental.pallas import tpu as pltpu
from jax.sharding import Mesh, PartitionSpec as P

NEAR = 4
AXES = ("far", "y", "x", "core")
CONTRACT_LAST = (((1,), (1,)), ((), ()))
CONTRACT_FIRST = (((0,), (0,)), ((), ()))
VMEM_LIMIT = 28 * 1024 * 1024
PLANE_COST = 10**10
GRADIENT_COST = 10**10
DIAGONAL_COST = 10**6
EXTRA = 48
PAIR_COST = 10**10
PARTS = 2
BIAS_ROWS = 8
MORE = 16


def gelu_parts(value):
    coeff = 0.7978845608
    inner = coeff * (value + 0.044715 * value * value * value)
    tangent = jnp.tanh(inner)
    result = 0.5 * value * (1.0 + tangent)
    slope = 0.5 * (1.0 + tangent) + 0.5 * value * (1.0 - tangent * tangent) * coeff * (
        1.0 + 3.0 * 0.044715 * value * value
    )
    return (result, slope)


def on_device_any(tokens, cotangent, w_in, b_in, w_out):
    far, near, tensor = lax.axis_size("far"), lax.axis_size("near"), lax.axis_size("tensor")
    rows, feats = tokens.shape
    owned, width = w_in.shape
    scale = 1.0 / math.sqrt(rows * far * near)
    bias_rows = jnp.pad(b_in.reshape(1, owned), ((0, 15), (0, width - owned)))
    weights = lax.all_gather(jnp.concatenate([w_in, w_out, bias_rows], 0), "far", axis=0)
    in_rows = weights[:, :owned].reshape(far * owned, width)
    proj_rows = weights[:, owned : 2 * owned].reshape(far * owned, width)
    bias = weights[:, 2 * owned, :owned].reshape(far * owned).astype(jnp.float32)
    tok = lax.all_gather(tokens, ("near", "tensor"), axis=0).reshape(near, tensor, rows, feats)
    cot = lax.all_gather(cotangent, ("near", "tensor"), axis=0).reshape(near, tensor, rows, feats)
    tok_full = tok.transpose(0, 2, 1, 3).reshape(near * rows, width)
    cot_full = cot.transpose(0, 2, 1, 3).reshape(near * rows, width)
    pre = lax.dot_general(
        tok_full, in_rows, CONTRACT_LAST, preferred_element_type=jnp.float32
    ) + bias
    act_value, slope = gelu_parts(pre)
    act = act_value.astype(jnp.bfloat16)
    term = jnp.dot(act, proj_rows, preferred_element_type=jnp.float32).astype(jnp.bfloat16)
    term = term.reshape(near, rows, tensor, feats).transpose(0, 2, 1, 3)
    mixed = lax.psum_scatter(
        term.reshape(near * tensor, rows, feats), ("near", "tensor"), scatter_dimension=0
    )
    dact = lax.dot_general(cot_full, proj_rows, CONTRACT_LAST, preferred_element_type=jnp.float32)
    dpre = (dact * slope).astype(jnp.bfloat16)
    grad = lax.dot_general(dpre, tok_full, CONTRACT_FIRST, preferred_element_type=jnp.float32)
    grad_sum = lax.psum_scatter(grad.astype(jnp.bfloat16), "far", scatter_dimension=0, tiled=True)
    return (mixed, grad_sum.astype(jnp.float32) * scale)


def half_columns(core, shift, feats):
    return pl.ds(pl.multiple_of(lax.rem(core + shift, 2) * feats, feats), feats)


def side_by_side(core, pair, whole, start, sem):
    rows, feats = pair[0].shape
    return [
        pltpu.make_async_copy(
            pair[shift],
            whole.at[pl.ds(start, rows), half_columns(core, shift, feats)],
            sem.at[shift],
        )
        for shift in range(2)
    ]


def weight_copies(refs, owned, w_in, w_out, sem):
    copies = []
    for at, ref in enumerate(refs):
        spot = pl.ds(at * owned, owned)
        copies.append(pltpu.make_async_copy(ref.at[pl.ds(0, owned)], w_in.at[spot], sem.at[0, at]))
        copies.append(
            pltpu.make_async_copy(ref.at[pl.ds(owned, owned)], w_out.at[spot], sem.at[1, at])
        )
    return copies


def bias_of(ref, owned):
    return ref[2 * owned : 2 * owned + BIAS_ROWS, :owned].astype(jnp.float32)


def run(copies, what):
    for copy in copies:
        getattr(copy, what)()


def activate(tok, w_in, bias):
    pre = lax.dot_general(
        tok, w_in, CONTRACT_LAST, preferred_element_type=jnp.float32
    ) + bias
    return gelu_parts(pre)


def dot_last(left, right):
    return lax.dot_general(left, right, CONTRACT_LAST, preferred_element_type=jnp.float32)


def dot_first(left, right):
    return lax.dot_general(left, right, CONTRACT_FIRST, preferred_element_type=jnp.float32)


def early_block(start, step, tok, cot, w_in, w_out, bias, two, act_ref, dpre_ref, mixed_ref, dpre):
    @pl.loop(0, 2)
    def _(sub):
        spot = pl.ds(pl.multiple_of(start + sub * step, step), step)
        value, slope = activate(tok[spot, :], w_in[...], bias[0:1, :])
        act = value.astype(jnp.bfloat16)
        act_ref[spot, :] = act[:, two:]
        dact = dot_last(cot[spot, :], w_out[...])
        terms = (dact * slope).astype(jnp.bfloat16)
        dpre[spot, :] = terms[:, :two]
        dpre_ref[spot, :] = terms[:, two:]
        mixed_ref[spot, :] = jnp.dot(
            act[:, :two], w_out[:two, :], preferred_element_type=jnp.float32
        )


def early_kernel(owned, *refs):
    pair_refs, w_refs = refs[:6], refs[6:9]
    act_ref, dpre_ref, mixed_ref, grad_ref, tok, cot, w_in, w_out, bias = refs[9:18]
    dpre, tok_sem, cot_sem, w_sem = refs[18:]
    core = lax.axis_index("core")
    rows = pair_refs[0].shape[1]
    w_copies = weight_copies(w_refs, owned, w_in, w_out, w_sem)
    loads = []
    for block in range(NEAR - 1):
        first, second = pair_refs[2 * block], pair_refs[2 * block + 1]
        loads.append(
            side_by_side(core, (first.at[0], second.at[0]), tok, block * rows, tok_sem.at[block])
            + side_by_side(core, (first.at[1], second.at[1]), cot, block * rows, cot_sem.at[block])
        )
    run(w_copies, "start")
    for load in loads:
        run(load, "start")
    for at, ref in enumerate(w_refs):
        bias[:, at * owned : (at + 1) * owned] = bias_of(ref, owned)
    run(w_copies, "wait")
    for block, load in enumerate(loads):
        run(load, "wait")
        early_block(
            block * rows, rows // 2, tok, cot, w_in, w_out, bias, 2 * owned,
            act_ref, dpre_ref, mixed_ref, dpre,
        )
    grad_ref[...] = dot_first(dpre[...], tok[...])


def output_kernel(owned, *refs):
    act_two, tok, early_mixed, w_in, w_out, bias, w_three = refs[:7]
    mine_ref, near_ref, own_ref, slope_ref, w_in_all, w_out_all, bias_all = refs[7:14]
    w_last, sem = refs[14:]
    core = lax.axis_index("core")
    rows, feats = own_ref.shape
    two, three = 2 * owned, 3 * owned
    first, last = pl.ds(0, three), pl.ds(three, owned)
    copies = [
        pltpu.make_async_copy(w_in, w_in_all.at[first], sem.at[0]),
        pltpu.make_async_copy(w_three.at[pl.ds(0, owned)], w_in_all.at[last], sem.at[1]),
        pltpu.make_async_copy(w_out, w_out_all.at[first], sem.at[2]),
        pltpu.make_async_copy(w_three.at[pl.ds(owned, owned)], w_out_all.at[last], sem.at[3]),
    ]
    run(copies, "start")
    bias_last = bias_of(w_three, owned)
    bias_all[:, :three] = bias[...]
    bias_all[:, three:] = bias_last
    w_last[:owned, :] = w_out[two:, :]
    w_last[owned:, :] = w_three[owned:two, :]
    step = tok.shape[0] // 6
    for at in range(6):
        spot = slice(at * step, (at + 1) * step)
        value, slope = activate(tok[spot, :], w_three[:owned, :], bias_last[0:1, :])
        slope_ref[spot, :] = slope
        act = jnp.concatenate([act_two[spot, :], value.astype(jnp.bfloat16)], axis=1)
        if at * step < rows:
            far_ref, there = own_ref, spot
        else:
            far_ref, there = near_ref, slice(at * step - rows, (at + 1) * step - rows)
        for shift, ref, to in ((0, mine_ref, spot), (1, far_ref, there)):
            half = half_columns(core, shift, feats)
            ref[to, :] = (
                early_mixed[spot, half]
                + jnp.dot(act, w_last[:, half], preferred_element_type=jnp.float32)
            ).astype(jnp.bfloat16)

    run(copies, "wait")


def gradient_kernel(dpre_two, tok, cot, slope, w_three, grad_ref, dpre):
    owned = slope.shape[1]
    step = tok.shape[0] // 6
    for at in range(6):
        spot = slice(at * step, (at + 1) * step)
        dact = dot_last(cot[spot, :], w_three[owned : 2 * owned, :])
        last = (dact * slope[spot, :]).astype(jnp.bfloat16)
        dpre[spot, :] = jnp.concatenate([dpre_two[spot, :], last], axis=1)
    grad_ref[...] = dot_first(dpre[...], tok[...])


def diagonal_kernel(owned, *refs):
    w_in, w_out, bias, grad_first, grad_last = refs[:5]
    tok_ref, cot_ref, far_ref = refs[5:8]
    mine_ref, other_ref, own_ref, one_ref = refs[8:12]
    two_refs, three_refs = refs[12 : 12 + PARTS], refs[12 + PARTS : 12 + 2 * PARTS]
    tok, cot, dpre, tok_sem, cot_sem = refs[12 + 2 * PARTS :]
    core = lax.axis_index("core")
    rows, feats = mine_ref.shape
    two = 2 * owned
    first, second = pl.ds(0, rows), pl.ds(rows, rows)
    load = side_by_side(core, (tok_ref.at[first], far_ref.at[first]), tok, 0, tok_sem)
    cot_load = side_by_side(core, (cot_ref, far_ref.at[second]), cot, 0, cot_sem)
    run(load + cot_load, "start")
    run(load + cot_load, "wait")
    step = rows // 2
    for sub in range(2):
        spot = slice(sub * step, (sub + 1) * step)
        value, slope = activate(tok[spot, :], w_in[...], bias[0:1, :])
        act = value.astype(jnp.bfloat16)
        dact = dot_last(cot[spot, :], w_out[...])
        dpre[spot, :] = (dact * slope).astype(jnp.bfloat16)
        for shift, ref in enumerate((mine_ref, other_ref)):
            ref[spot, :] = jnp.dot(
                act, w_out[:, half_columns(core, shift, feats)], preferred_element_type=jnp.float32
            ).astype(jnp.bfloat16)

    grad = grad_last[...] + dot_first(dpre[:, two:], tok[...])
    part = owned // PARTS
    for at in range(PARTS):
        two_refs[at][...] = grad[at * part : (at + 1) * part].astype(jnp.bfloat16)
        three_refs[at][...] = grad[owned + at * part : owned + (at + 1) * part].astype(jnp.bfloat16)
    grad = grad_first[...] + dot_first(dpre[:, :two], tok[...])
    own_ref[...] = grad[:owned].astype(jnp.bfloat16)
    one_ref[...] = grad[owned:].astype(jnp.bfloat16)


def pair_kernel(rows, first, mine_ref, other_ref, *out_refs):
    for block, ref in enumerate(out_refs):
        mine, other = pl.ds((first + block) * rows, rows), pl.ds(block * rows, rows)
        ref[:rows, :] = (
            mine_ref[mine, :].astype(jnp.float32) + other_ref[other, :].astype(jnp.float32)
        ).astype(jnp.bfloat16)
        if ref.shape[0] > rows:
            ref[rows:, :] = jnp.zeros_like(ref[rows:, :])


def last_pairs_kernel(mine_ref, far_ref, diag_ref, other_ref, own_sum_ref, diag_sum_ref):
    rows = diag_ref.shape[0]
    diag_sum_ref[...] = (
        diag_ref[...].astype(jnp.float32) + other_ref[...].astype(jnp.float32)
    ).astype(jnp.bfloat16)
    own_sum_ref[...] = (
        mine_ref[:rows, :].astype(jnp.float32)
        + far_ref[2 * rows : 3 * rows, :].astype(jnp.float32)
    ).astype(jnp.bfloat16)


def plane_kernel(own_ref, x_ref, y_ref, out_ref):
    rows = own_ref.shape[0]
    out_ref[...] = (
        own_ref[...].astype(jnp.float32)
        + x_ref[:rows, :].astype(jnp.float32)
        + y_ref[:rows, :].astype(jnp.float32)
    )


def final_kernel(scale, plane_ref, diag_ref, own_ref, one_ref, *refs):
    two_refs, mixed_ref, grad_ref = refs[:-2], refs[-2], refs[-1]
    mixed_ref[...] = (plane_ref[...] + diag_ref[...].astype(jnp.float32)).astype(jnp.bfloat16)
    part = two_refs[0].shape[0]
    for at, ref in enumerate(two_refs):
        spot = slice(at * part, (at + 1) * part)
        grad_ref[spot, :] = scale * (
            own_ref[spot, :].astype(jnp.float32)
            + one_ref[spot, :].astype(jnp.float32)
            + ref[...].astype(jnp.float32)
        )


def vmem(count):
    return [pl.BlockSpec(memory_space=pltpu.VMEM)] * count


def anywhere(count):
    return [pl.BlockSpec(memory_space=pl.ANY)] * count


def bf16(*shape):
    return jax.ShapeDtypeStruct(shape, jnp.bfloat16)


def permute(value, there):
    pairs = []
    for f in range(4):
        for y in range(2):
            for x in range(2):
                for c in range(2):
                    to = there(f, y, x, c)
                    here = ((f * 2 + y) * 2 + x) * 2 + c
                    pairs.append((here, ((to[0] * 2 + to[1]) * 2 + to[2]) * 2 + to[3]))
    return lax.ppermute(value, AXES, pairs)


def to_x(value):
    return permute(value, lambda f, y, x, c: (f, y, 1 - x, c))


def to_y(value):
    return permute(value, lambda f, y, x, c: (f, 1 - y, x, c))


def to_diagonal(value):
    return permute(value, lambda f, y, x, c: (f, 1 - y, 1 - x, c))


def to_core(value):
    return permute(value, lambda f, y, x, c: (f, y, x, 1 - c))


def to_far(value, flip):
    return permute(value, lambda f, y, x, c: (f ^ flip, y, x, c))


def on_device_lines(tokens, cotangent, w_in, b_in, w_out):
    rows, feats = tokens.shape
    owned, width = w_in.shape
    units = 4 * owned
    count = NEAR * rows
    scale = 1.0 / math.sqrt(4 * count)
    params = pltpu.CompilerParams(vmem_limit_bytes=VMEM_LIMIT)
    dma = pltpu.SemaphoreType.DMA
    barrier = lax.optimization_barrier
    early_rows = (NEAR - 1) * rows

    def f32(*shape):
        return jax.ShapeDtypeStruct(shape, jnp.float32)

    def cost(flops, traffic):
        return pl.CostEstimate(flops=flops, bytes_accessed=traffic, transcendentals=0)

    bias_rows = jnp.pad(b_in.reshape(1, owned), ((0, BIAS_ROWS - 1), (0, width - owned)))
    own_w = jnp.concatenate([w_in, w_out, bias_rows], 0)
    own = jnp.stack([tokens, cotangent])
    w_two, w_one = to_far(own_w, 2), to_far(own_w, 1)
    from_x, from_y = to_x(own), to_y(own)
    own_other = to_core(own)
    from_x, from_y, own_other = barrier((from_x, from_y, own_other))
    tok_diag = to_y(from_x.reshape(2 * rows, feats)[: rows + EXTRA])
    cot_diag = to_x(from_y[1])
    x_other, y_other = to_core(from_x), to_core(from_y)
    w_three = to_far(w_two, 1)
    act_two, dpre_two, mixed_terms, grad_terms, tok, cot, w_in_three, w_out_three, bias = (
        pl.pallas_call(
            functools.partial(early_kernel, owned),
            out_shape=(
                bf16(early_rows, owned),
                bf16(early_rows, owned),
                f32(early_rows, width),
                f32(2 * owned, width),
                bf16(early_rows, width),
                bf16(early_rows, width),
                bf16(3 * owned, width),
                bf16(3 * owned, width),
                f32(BIAS_ROWS, 3 * owned),
            ),
            in_specs=anywhere(6) + vmem(3),
            out_specs=vmem(9),
            scratch_shapes=[
                pltpu.VMEM((early_rows, 2 * owned), jnp.bfloat16),
                dma((NEAR - 1, 2)),
                dma((NEAR - 1, 2)),
                dma((2, 3)),
            ],
            compiler_params=params,
            cost_estimate=cost(early_rows * units, early_rows),
            name="early",
        )(own, own_other, from_x, x_other, from_y, y_other, own_w, w_one, w_two)
    )

    mine, other, other_own, slope, w_in_all, w_out_all, bias = pl.pallas_call(
        functools.partial(output_kernel, owned),
        out_shape=(
            bf16(early_rows, feats),
            bf16(2 * rows, feats),
            bf16(rows, feats),
            f32(early_rows, owned),
            bf16(units, width),
            bf16(units, width),
            f32(BIAS_ROWS, units),
        ),
        in_specs=vmem(7),
        out_specs=vmem(7),
        scratch_shapes=[pltpu.VMEM((2 * owned, width), jnp.bfloat16), dma((4,))],
        compiler_params=params,
        cost_estimate=cost(early_rows * units, early_rows),
        name="output",
    )(act_two, tok, mixed_terms, w_in_three, w_out_three, bias, w_three)
    tok_diag, cot_diag, other = barrier((tok_diag, cot_diag, other))
    received = to_core(other)
    diag_other = to_core(jnp.concatenate([tok_diag[:rows], cot_diag, other_own]))
    slope, tok_diag = barrier((slope, tok_diag))
    grad_last = pl.pallas_call(
        gradient_kernel,
        out_shape=f32(2 * owned, width),
        in_specs=vmem(5),
        out_specs=pl.BlockSpec(memory_space=pltpu.VMEM),
        scratch_shapes=[pltpu.VMEM((early_rows, 2 * owned), jnp.bfloat16)],
        compiler_params=params,
        cost_estimate=cost(GRADIENT_COST, early_rows),
        name="gradient",
    )(dpre_two, tok, cot, slope, w_three)

    mine, grad_last = barrier((mine, grad_last))
    sums = pl.pallas_call(
        functools.partial(pair_kernel, rows, 1),
        out_shape=[bf16(rows + MORE, feats), bf16(rows + 2 * MORE, feats)],
        in_specs=vmem(2),
        out_specs=vmem(2),
        compiler_params=params,
        cost_estimate=cost(PAIR_COST, rows),
        name="pair_sum",
    )(mine, received)
    mixed_x, mixed_y = to_x(sums[0]), to_y(sums[1])
    grad_terms, _ = barrier((grad_terms, sums[0]))

    mine_diag, other_diag, grad_own, grad_one, *grad_far = pl.pallas_call(
        functools.partial(diagonal_kernel, owned),
        out_shape=[bf16(rows, feats)] * 2
        + [bf16(owned, width)] * 2
        + [bf16(owned // PARTS, width)] * (2 * PARTS),
        in_specs=vmem(5) + anywhere(3),
        out_specs=vmem(4 + 2 * PARTS),
        scratch_shapes=[
            pltpu.VMEM((rows, width), jnp.bfloat16),
            pltpu.VMEM((rows, width), jnp.bfloat16),
            pltpu.VMEM((rows, units), jnp.bfloat16),
            dma((2,)),
            dma((2,)),
        ],
        compiler_params=params,
        cost_estimate=cost(DIAGONAL_COST, rows),
        name="diagonal",
    )(
        w_in_all, w_out_all, bias, grad_terms, grad_last,
        tok_diag, cot_diag, diag_other,
    )
    received_diag = to_core(other_diag)
    relayed = [to_far(piece, 1) for piece in grad_far[PARTS:]]
    mixed_own, sum_diag = pl.pallas_call(
        last_pairs_kernel,
        out_shape=[bf16(rows, feats)] * 2,
        in_specs=vmem(4),
        out_specs=vmem(2),
        compiler_params=params,
        cost_estimate=cost(rows, rows),
        name="pair_sum_diagonal",
    )(mine, diag_other, mine_diag, received_diag)
    mixed_diag = to_diagonal(sum_diag)
    from_two = []
    for at in range(PARTS):
        piece, _ = barrier((grad_far[at], sum_diag))
        (line_sum,) = pl.pallas_call(
            functools.partial(pair_kernel, owned // PARTS, 0),
            out_shape=[bf16(owned // PARTS, width)],
            in_specs=vmem(2),
            out_specs=vmem(1),
            compiler_params=params,
            cost_estimate=cost(rows, rows),
            name="line_sum",
        )(piece, relayed[at])
        from_two.append(to_far(line_sum, 2))
    grad_one, _ = barrier((grad_one, line_sum))
    from_one = to_far(grad_one, 1)
    mixed = pl.pallas_call(
        plane_kernel,
        out_shape=f32(rows, feats),
        in_specs=vmem(3),
        out_specs=pl.BlockSpec(memory_space=pltpu.VMEM),
        compiler_params=params,
        cost_estimate=cost(PLANE_COST, rows),
        name="plane_sum",
    )(mixed_own, mixed_x, mixed_y)
    *from_two, from_one, mixed = barrier((*from_two, from_one, mixed))
    return pl.pallas_call(
        functools.partial(final_kernel, scale),
        out_shape=(bf16(rows, feats), f32(owned, width)),
        in_specs=vmem(4 + PARTS),
        out_specs=(vmem(1)[0], vmem(1)[0]),
        compiler_params=params,
        cost_estimate=cost(rows, rows),
        name="results",
    )(mixed, mixed_diag, grad_own, from_one, *from_two)


def solution(mesh):
    dp, tensor = mesh.shape["dp"], mesh.shape["tensor"]
    far = dp // NEAR
    if tensor == 2 and far == 4:
        fine = Mesh(mesh.devices.reshape(far, 2, 2, tensor), AXES)
        rows, owners, halves = ("far", "y", "x"), AXES, "core"
        body = on_device_lines
    else:
        fine = Mesh(mesh.devices.reshape(far, NEAR, tensor), ("far", "near", "tensor"))
        rows, owners, halves = ("far", "near"), ("far", "near", "tensor"), "tensor"
        body = on_device_any
    in_specs = (P(rows, halves), P(rows, halves), P(owners, None), P(owners), P(owners, None))
    out_specs = (P(rows, halves), P(owners, None))
    return jax.shard_map(
        body, mesh=fine, in_specs=in_specs, out_specs=out_specs, check_vma=False
    )
```

```python
import functools
import math

import jax
import jax.numpy as jnp
from jax import lax
from jax.experimental import pallas as pl
from jax.experimental.pallas import tpu as pltpu
from jax.sharding import Mesh, PartitionSpec as P

NEAR = 4
AXES = ("far", "y", "x", "core")
CONTRACT_LAST = (((1,), (1,)), ((), ()))
CONTRACT_FIRST = (((0,), (0,)), ((), ()))
VMEM_LIMIT = 28 * 1024 * 1024
PLANE_COST = 10**10
GRADIENT_COST = 10**10
DIAGONAL_COST = 10**6
EXTRA = 48
PAIR_COST = 10**10
PARTS = 2
BIAS_ROWS = 8
MORE = 16


def gelu_parts(value):
    coeff = 0.7978845608
    inner = coeff * (value + 0.044715 * value * value * value)
    tangent = jnp.tanh(inner)
    result = 0.5 * value * (1.0 + tangent)
    slope = 0.5 * (1.0 + tangent) + 0.5 * value * (1.0 - tangent * tangent) * coeff * (
        1.0 + 3.0 * 0.044715 * value * value
    )
    return (result, slope)


def on_device_any(tokens, cotangent, w_in, b_in, w_out):
    far, near, tensor = lax.axis_size("far"), lax.axis_size("near"), lax.axis_size("tensor")
    rows, feats = tokens.shape
    owned, width = w_in.shape
    scale = 1.0 / math.sqrt(rows * far * near)
    bias_rows = jnp.pad(b_in.reshape(1, owned), ((0, 15), (0, width - owned)))
    weights = lax.all_gather(jnp.concatenate([w_in, w_out, bias_rows], 0), "far", axis=0)
    in_rows = weights[:, :owned].reshape(far * owned, width)
    proj_rows = weights[:, owned : 2 * owned].reshape(far * owned, width)
    bias = weights[:, 2 * owned, :owned].reshape(far * owned).astype(jnp.float32)
    tok = lax.all_gather(tokens, ("near", "tensor"), axis=0).reshape(near, tensor, rows, feats)
    cot = lax.all_gather(cotangent, ("near", "tensor"), axis=0).reshape(near, tensor, rows, feats)
    tok_full = tok.transpose(0, 2, 1, 3).reshape(near * rows, width)
    cot_full = cot.transpose(0, 2, 1, 3).reshape(near * rows, width)
    pre = lax.dot_general(
        tok_full, in_rows, CONTRACT_LAST, preferred_element_type=jnp.float32
    ) + bias
    act_value, slope = gelu_parts(pre)
    act = act_value.astype(jnp.bfloat16)
    term = jnp.dot(act, proj_rows, preferred_element_type=jnp.float32).astype(jnp.bfloat16)
    term = term.reshape(near, rows, tensor, feats).transpose(0, 2, 1, 3)
    mixed = lax.psum_scatter(
        term.reshape(near * tensor, rows, feats), ("near", "tensor"), scatter_dimension=0
    )
    dact = lax.dot_general(cot_full, proj_rows, CONTRACT_LAST, preferred_element_type=jnp.float32)
    dpre = (dact * slope).astype(jnp.bfloat16)
    grad = lax.dot_general(dpre, tok_full, CONTRACT_FIRST, preferred_element_type=jnp.float32)
    grad_sum = lax.psum_scatter(grad.astype(jnp.bfloat16), "far", scatter_dimension=0, tiled=True)
    return (mixed, grad_sum.astype(jnp.float32) * scale)


def half_columns(core, shift, feats):
    return pl.ds(pl.multiple_of(lax.rem(core + shift, 2) * feats, feats), feats)


def side_by_side(core, pair, whole, start, sem):
    rows, feats = pair[0].shape
    return [
        pltpu.make_async_copy(
            pair[shift],
            whole.at[pl.ds(start, rows), half_columns(core, shift, feats)],
            sem.at[shift],
        )
        for shift in range(2)
    ]


def weight_copies(refs, owned, w_in, w_out, sem):
    copies = []
    for at, ref in enumerate(refs):
        spot = pl.ds(at * owned, owned)
        copies.append(pltpu.make_async_copy(ref.at[pl.ds(0, owned)], w_in.at[spot], sem.at[0, at]))
        copies.append(
            pltpu.make_async_copy(ref.at[pl.ds(owned, owned)], w_out.at[spot], sem.at[1, at])
        )
    return copies


def bias_of(ref, owned):
    return ref[2 * owned : 2 * owned + BIAS_ROWS, :owned].astype(jnp.float32)


def run(copies, what):
    for copy in copies:
        getattr(copy, what)()


def activate(tok, w_in, bias):
    pre = lax.dot_general(
        tok, w_in, CONTRACT_LAST, preferred_element_type=jnp.float32
    ) + bias
    return gelu_parts(pre)


def dot_last(left, right):
    return lax.dot_general(left, right, CONTRACT_LAST, preferred_element_type=jnp.float32)


def dot_first(left, right):
    return lax.dot_general(left, right, CONTRACT_FIRST, preferred_element_type=jnp.float32)


def early_block(start, step, tok, cot, w_in, w_out, bias, two, act_ref, dpre_ref, mixed_ref, dpre):
    @pl.loop(0, 2)
    def _(sub):
        spot = pl.ds(pl.multiple_of(start + sub * step, step), step)
        value, slope = activate(tok[spot, :], w_in[...], bias[0:1, :])
        act = value.astype(jnp.bfloat16)
        act_ref[spot, :] = act[:, two:]
        dact = dot_last(cot[spot, :], w_out[...])
        terms = (dact * slope).astype(jnp.bfloat16)
        dpre[spot, :] = terms[:, :two]
        dpre_ref[spot, :] = terms[:, two:]
        mixed_ref[spot, :] = jnp.dot(
            act[:, :two], w_out[:two, :], preferred_element_type=jnp.float32
        )


def early_kernel(owned, *refs):
    pair_refs, w_refs = refs[:6], refs[6:9]
    act_ref, dpre_ref, mixed_ref, grad_ref, tok, cot, w_in, w_out, bias = refs[9:18]
    dpre, tok_sem, cot_sem, w_sem = refs[18:]
    core = lax.axis_index("core")
    rows = pair_refs[0].shape[1]
    w_copies = weight_copies(w_refs, owned, w_in, w_out, w_sem)
    loads = []
    for block in range(NEAR - 1):
        first, second = pair_refs[2 * block], pair_refs[2 * block + 1]
        loads.append(
            side_by_side(core, (first.at[0], second.at[0]), tok, block * rows, tok_sem.at[block])
            + side_by_side(core, (first.at[1], second.at[1]), cot, block * rows, cot_sem.at[block])
        )
    run(w_copies, "start")
    for load in loads:
        run(load, "start")
    for at, ref in enumerate(w_refs):
        bias[:, at * owned : (at + 1) * owned] = bias_of(ref, owned)
    run(w_copies, "wait")
    for block, load in enumerate(loads):
        run(load, "wait")
        early_block(
            block * rows, rows // 2, tok, cot, w_in, w_out, bias, 2 * owned,
            act_ref, dpre_ref, mixed_ref, dpre,
        )
    grad_ref[...] = dot_first(dpre[...], tok[...])


def output_kernel(owned, *refs):
    act_two, tok, early_mixed, w_in, w_out, bias, w_three = refs[:7]
    mine_ref, near_ref, own_ref, slope_ref, w_in_all, w_out_all, bias_all = refs[7:14]
    w_last, sem = refs[14:]
    core = lax.axis_index("core")
    rows, feats = own_ref.shape
    two, three = 2 * owned, 3 * owned
    first, last = pl.ds(0, three), pl.ds(three, owned)
    copies = [
        pltpu.make_async_copy(w_in, w_in_all.at[first], sem.at[0]),
        pltpu.make_async_copy(w_three.at[pl.ds(0, owned)], w_in_all.at[last], sem.at[1]),
        pltpu.make_async_copy(w_out, w_out_all.at[first], sem.at[2]),
        pltpu.make_async_copy(w_three.at[pl.ds(owned, owned)], w_out_all.at[last], sem.at[3]),
    ]
    run(copies, "start")
    bias_last = bias_of(w_three, owned)
    bias_all[:, :three] = bias[...]
    bias_all[:, three:] = bias_last
    w_last[:owned, :] = w_out[two:, :]
    w_last[owned:, :] = w_three[owned:two, :]
    step = tok.shape[0] // 6
    acts = {}

    def mix(at):
        spot = slice(at * step, (at + 1) * step)
        if at * step < rows:
            far_ref, there = own_ref, spot
        else:
            far_ref, there = near_ref, slice(at * step - rows, (at + 1) * step - rows)
        for shift, ref, to in ((0, mine_ref, spot), (1, far_ref, there)):
            half = half_columns(core, shift, feats)
            ref[to, :] = (
                early_mixed[spot, half]
                + jnp.dot(acts[at], w_last[:, half], preferred_element_type=jnp.float32)
            ).astype(jnp.bfloat16)

    for at in range(6):
        spot = slice(at * step, (at + 1) * step)
        value, slope = activate(tok[spot, :], w_three[:owned, :], bias_last[0:1, :])
        slope_ref[spot, :] = slope
        acts[at] = jnp.concatenate([act_two[spot, :], value.astype(jnp.bfloat16)], axis=1)
        if at:
            mix(at - 1)
    mix(5)
    run(copies, "wait")


def gradient_kernel(dpre_two, tok, cot, slope, w_three, grad_ref, dpre):
    owned = slope.shape[1]
    step = tok.shape[0] // 6
    for at in range(6):
        spot = slice(at * step, (at + 1) * step)
        dact = dot_last(cot[spot, :], w_three[owned : 2 * owned, :])
        last = (dact * slope[spot, :]).astype(jnp.bfloat16)
        dpre[spot, :] = jnp.concatenate([dpre_two[spot, :], last], axis=1)
    grad_ref[...] = dot_first(dpre[...], tok[...])


def diagonal_kernel(owned, *refs):
    w_in, w_out, bias, grad_first, grad_last = refs[:5]
    tok_ref, cot_ref, far_ref = refs[5:8]
    mine_ref, other_ref, own_ref, one_ref = refs[8:12]
    two_refs, three_refs = refs[12 : 12 + PARTS], refs[12 + PARTS : 12 + 2 * PARTS]
    tok, cot, dpre, tok_sem, cot_sem = refs[12 + 2 * PARTS :]
    core = lax.axis_index("core")
    rows, feats = mine_ref.shape
    two = 2 * owned
    first, second = pl.ds(0, rows), pl.ds(rows, rows)
    load = side_by_side(core, (tok_ref.at[first], far_ref.at[first]), tok, 0, tok_sem)
    cot_load = side_by_side(core, (cot_ref, far_ref.at[second]), cot, 0, cot_sem)
    run(load + cot_load, "start")
    run(load + cot_load, "wait")
    step = rows // 2
    for sub in range(2):
        spot = slice(sub * step, (sub + 1) * step)
        value, slope = activate(tok[spot, :], w_in[...], bias[0:1, :])
        act = value.astype(jnp.bfloat16)
        dact = dot_last(cot[spot, :], w_out[...])
        dpre[spot, :] = (dact * slope).astype(jnp.bfloat16)
        for shift, ref in enumerate((mine_ref, other_ref)):
            ref[spot, :] = jnp.dot(
                act, w_out[:, half_columns(core, shift, feats)], preferred_element_type=jnp.float32
            ).astype(jnp.bfloat16)

    grad = grad_last[...] + dot_first(dpre[:, two:], tok[...])
    part = owned // PARTS
    for at in range(PARTS):
        two_refs[at][...] = grad[at * part : (at + 1) * part].astype(jnp.bfloat16)
        three_refs[at][...] = grad[owned + at * part : owned + (at + 1) * part].astype(jnp.bfloat16)
    grad = grad_first[...] + dot_first(dpre[:, :two], tok[...])
    own_ref[...] = grad[:owned].astype(jnp.bfloat16)
    one_ref[...] = grad[owned:].astype(jnp.bfloat16)


def pair_kernel(rows, first, mine_ref, other_ref, *out_refs):
    for block, ref in enumerate(out_refs):
        mine, other = pl.ds((first + block) * rows, rows), pl.ds(block * rows, rows)
        ref[:rows, :] = (
            mine_ref[mine, :].astype(jnp.float32) + other_ref[other, :].astype(jnp.float32)
        ).astype(jnp.bfloat16)
        if ref.shape[0] > rows:
            ref[rows:, :] = jnp.zeros_like(ref[rows:, :])


def last_pairs_kernel(mine_ref, far_ref, diag_ref, other_ref, own_sum_ref, diag_sum_ref):
    rows = diag_ref.shape[0]
    diag_sum_ref[...] = (
        diag_ref[...].astype(jnp.float32) + other_ref[...].astype(jnp.float32)
    ).astype(jnp.bfloat16)
    own_sum_ref[...] = (
        mine_ref[:rows, :].astype(jnp.float32)
        + far_ref[2 * rows : 3 * rows, :].astype(jnp.float32)
    ).astype(jnp.bfloat16)


def plane_kernel(own_ref, x_ref, y_ref, out_ref):
    rows = own_ref.shape[0]
    out_ref[...] = (
        own_ref[...].astype(jnp.float32)
        + x_ref[:rows, :].astype(jnp.float32)
        + y_ref[:rows, :].astype(jnp.float32)
    )


def final_kernel(scale, plane_ref, diag_ref, own_ref, one_ref, *refs):
    two_refs, mixed_ref, grad_ref = refs[:-2], refs[-2], refs[-1]
    mixed_ref[...] = (plane_ref[...] + diag_ref[...].astype(jnp.float32)).astype(jnp.bfloat16)
    part = two_refs[0].shape[0]
    for at, ref in enumerate(two_refs):
        spot = slice(at * part, (at + 1) * part)
        grad_ref[spot, :] = scale * (
            own_ref[spot, :].astype(jnp.float32)
            + one_ref[spot, :].astype(jnp.float32)
            + ref[...].astype(jnp.float32)
        )


def vmem(count):
    return [pl.BlockSpec(memory_space=pltpu.VMEM)] * count


def anywhere(count):
    return [pl.BlockSpec(memory_space=pl.ANY)] * count


def bf16(*shape):
    return jax.ShapeDtypeStruct(shape, jnp.bfloat16)


def permute(value, there):
    pairs = []
    for f in range(4):
        for y in range(2):
            for x in range(2):
                for c in range(2):
                    to = there(f, y, x, c)
                    here = ((f * 2 + y) * 2 + x) * 2 + c
                    pairs.append((here, ((to[0] * 2 + to[1]) * 2 + to[2]) * 2 + to[3]))
    return lax.ppermute(value, AXES, pairs)


def to_x(value):
    return permute(value, lambda f, y, x, c: (f, y, 1 - x, c))


def to_y(value):
    return permute(value, lambda f, y, x, c: (f, 1 - y, x, c))


def to_diagonal(value):
    return permute(value, lambda f, y, x, c: (f, 1 - y, 1 - x, c))


def to_core(value):
    return permute(value, lambda f, y, x, c: (f, y, x, 1 - c))


def to_far(value, flip):
    return permute(value, lambda f, y, x, c: (f ^ flip, y, x, c))


def on_device_lines(tokens, cotangent, w_in, b_in, w_out):
    rows, feats = tokens.shape
    owned, width = w_in.shape
    units = 4 * owned
    count = NEAR * rows
    scale = 1.0 / math.sqrt(4 * count)
    params = pltpu.CompilerParams(vmem_limit_bytes=VMEM_LIMIT)
    dma = pltpu.SemaphoreType.DMA
    barrier = lax.optimization_barrier
    early_rows = (NEAR - 1) * rows

    def f32(*shape):
        return jax.ShapeDtypeStruct(shape, jnp.float32)

    def cost(flops, traffic):
        return pl.CostEstimate(flops=flops, bytes_accessed=traffic, transcendentals=0)

    bias_rows = jnp.pad(b_in.reshape(1, owned), ((0, BIAS_ROWS - 1), (0, width - owned)))
    own_w = jnp.concatenate([w_in, w_out, bias_rows], 0)
    own = jnp.stack([tokens, cotangent])
    w_two, w_one = to_far(own_w, 2), to_far(own_w, 1)
    from_x, from_y = to_x(own), to_y(own)
    own_other = to_core(own)
    from_x, from_y, own_other = barrier((from_x, from_y, own_other))
    tok_diag = to_y(from_x.reshape(2 * rows, feats)[: rows + EXTRA])
    cot_diag = to_x(from_y[1])
    x_other, y_other = to_core(from_x), to_core(from_y)
    w_three = to_far(w_two, 1)
    act_two, dpre_two, mixed_terms, grad_terms, tok, cot, w_in_three, w_out_three, bias = (
        pl.pallas_call(
            functools.partial(early_kernel, owned),
            out_shape=(
                bf16(early_rows, owned),
                bf16(early_rows, owned),
                f32(early_rows, width),
                f32(2 * owned, width),
                bf16(early_rows, width),
                bf16(early_rows, width),
                bf16(3 * owned, width),
                bf16(3 * owned, width),
                f32(BIAS_ROWS, 3 * owned),
            ),
            in_specs=anywhere(6) + vmem(3),
            out_specs=vmem(9),
            scratch_shapes=[
                pltpu.VMEM((early_rows, 2 * owned), jnp.bfloat16),
                dma((NEAR - 1, 2)),
                dma((NEAR - 1, 2)),
                dma((2, 3)),
            ],
            compiler_params=params,
            cost_estimate=cost(early_rows * units, early_rows),
            name="early",
        )(own, own_other, from_x, x_other, from_y, y_other, own_w, w_one, w_two)
    )

    mine, other, other_own, slope, w_in_all, w_out_all, bias = pl.pallas_call(
        functools.partial(output_kernel, owned),
        out_shape=(
            bf16(early_rows, feats),
            bf16(2 * rows, feats),
            bf16(rows, feats),
            f32(early_rows, owned),
            bf16(units, width),
            bf16(units, width),
            f32(BIAS_ROWS, units),
        ),
        in_specs=vmem(7),
        out_specs=vmem(7),
        scratch_shapes=[pltpu.VMEM((2 * owned, width), jnp.bfloat16), dma((4,))],
        compiler_params=params,
        cost_estimate=cost(early_rows * units, early_rows),
        name="output",
    )(act_two, tok, mixed_terms, w_in_three, w_out_three, bias, w_three)
    tok_diag, cot_diag, other = barrier((tok_diag, cot_diag, other))
    received = to_core(other)
    diag_other = to_core(jnp.concatenate([tok_diag[:rows], cot_diag, other_own]))
    slope, tok_diag = barrier((slope, tok_diag))
    grad_last = pl.pallas_call(
        gradient_kernel,
        out_shape=f32(2 * owned, width),
        in_specs=vmem(5),
        out_specs=pl.BlockSpec(memory_space=pltpu.VMEM),
        scratch_shapes=[pltpu.VMEM((early_rows, 2 * owned), jnp.bfloat16)],
        compiler_params=params,
        cost_estimate=cost(GRADIENT_COST, early_rows),
        name="gradient",
    )(dpre_two, tok, cot, slope, w_three)

    mine, grad_last = barrier((mine, grad_last))
    sums = pl.pallas_call(
        functools.partial(pair_kernel, rows, 1),
        out_shape=[bf16(rows + MORE, feats)] * 2,
        in_specs=vmem(2),
        out_specs=vmem(2),
        compiler_params=params,
        cost_estimate=cost(PAIR_COST, rows),
        name="pair_sum",
    )(mine, received)
    mixed_x, mixed_y = to_x(sums[0]), to_y(sums[1])
    grad_terms, _ = barrier((grad_terms, sums[0]))

    mine_diag, other_diag, grad_own, grad_one, *grad_far = pl.pallas_call(
        functools.partial(diagonal_kernel, owned),
        out_shape=[bf16(rows, feats)] * 2
        + [bf16(owned, width)] * 2
        + [bf16(owned // PARTS, width)] * (2 * PARTS),
        in_specs=vmem(5) + anywhere(3),
        out_specs=vmem(4 + 2 * PARTS),
        scratch_shapes=[
            pltpu.VMEM((rows, width), jnp.bfloat16),
            pltpu.VMEM((rows, width), jnp.bfloat16),
            pltpu.VMEM((rows, units), jnp.bfloat16),
            dma((2,)),
            dma((2,)),
        ],
        compiler_params=params,
        cost_estimate=cost(DIAGONAL_COST, rows),
        name="diagonal",
    )(
        w_in_all, w_out_all, bias, grad_terms, grad_last,
        tok_diag, cot_diag, diag_other,
    )
    received_diag = to_core(other_diag)
    relayed = [to_far(piece, 1) for piece in grad_far[PARTS:]]
    mixed_own, sum_diag = pl.pallas_call(
        last_pairs_kernel,
        out_shape=[bf16(rows, feats)] * 2,
        in_specs=vmem(4),
        out_specs=vmem(2),
        compiler_params=params,
        cost_estimate=cost(rows, rows),
        name="pair_sum_diagonal",
    )(mine, diag_other, mine_diag, received_diag)
    mixed_diag = to_diagonal(sum_diag)
    from_two = []
    for at in range(PARTS):
        piece, _ = barrier((grad_far[at], sum_diag))
        (line_sum,) = pl.pallas_call(
            functools.partial(pair_kernel, owned // PARTS, 0),
            out_shape=[bf16(owned // PARTS, width)],
            in_specs=vmem(2),
            out_specs=vmem(1),
            compiler_params=params,
            cost_estimate=cost(rows, rows),
            name="line_sum",
        )(piece, relayed[at])
        from_two.append(to_far(line_sum, 2))
    grad_one, _ = barrier((grad_one, line_sum))
    from_one = to_far(grad_one, 1)
    mixed = pl.pallas_call(
        plane_kernel,
        out_shape=f32(rows, feats),
        in_specs=vmem(3),
        out_specs=pl.BlockSpec(memory_space=pltpu.VMEM),
        compiler_params=params,
        cost_estimate=cost(PLANE_COST, rows),
        name="plane_sum",
    )(mixed_own, mixed_x, mixed_y)
    *from_two, from_one, mixed = barrier((*from_two, from_one, mixed))
    return pl.pallas_call(
        functools.partial(final_kernel, scale),
        out_shape=(bf16(rows, feats), f32(owned, width)),
        in_specs=vmem(4 + PARTS),
        out_specs=(vmem(1)[0], vmem(1)[0]),
        compiler_params=params,
        cost_estimate=cost(rows, rows),
        name="results",
    )(mixed, mixed_diag, grad_own, from_one, *from_two)


def solution(mesh):
    dp, tensor = mesh.shape["dp"], mesh.shape["tensor"]
    far = dp // NEAR
    if tensor == 2 and far == 4:
        fine = Mesh(mesh.devices.reshape(far, 2, 2, tensor), AXES)
        rows, owners, halves = ("far", "y", "x"), AXES, "core"
        body = on_device_lines
    else:
        fine = Mesh(mesh.devices.reshape(far, NEAR, tensor), ("far", "near", "tensor"))
        rows, owners, halves = ("far", "near"), ("far", "near", "tensor"), "tensor"
        body = on_device_any
    in_specs = (P(rows, halves), P(rows, halves), P(owners, None), P(owners), P(owners, None))
    out_specs = (P(rows, halves), P(owners, None))
    return jax.shard_map(
        body, mesh=fine, in_specs=in_specs, out_specs=out_specs, check_vma=False
    )
```
